32 devices in a mesh: fsdp: 16 (over z, y, x), dp: 2 (over core).
Axes of the slice: x: 2, y: 2, z: 4, core: 2. Of those that a mesh axis runs over, the one named last changes fastest.
Arguments:
- tokens: bfloat16 [256, 257, 384], P(('fsdp', 'dp')), may hold values from -6 to 6
- duplicate: int32 [256, 257], P(('fsdp', 'dp')), may hold values 0 or 1
- targets: float32 [256, 384], P(('fsdp', 'dp')), may hold values from -6 to 6
- ln1_gain: bfloat16 [384], P('fsdp'), may hold values from 0.5 to 1.5
- ln1_bias: bfloat16 [384], P('fsdp'), may hold values from -1.796875 to 1.796875
- qkv_weight: bfloat16 [384, 1152], P('fsdp'), may hold values from -0.3125 to 0.3125
- qv_bias: bfloat16 [768], P('fsdp'), may hold values from -1.796875 to 1.796875
- out_weight: bfloat16 [384, 384], P('fsdp'), may hold values from -1.25 to 1.25
- out_bias: bfloat16 [384], P('fsdp'), may hold values from -1.796875 to 1.796875
- ln2_gain: bfloat16 [384], P('fsdp'), may hold values from 0.5 to 1.5
- ln2_bias: bfloat16 [384], P('fsdp'), may hold values from -1.796875 to 1.796875
- fc1_weight: bfloat16 [384, 1536], P('fsdp'), may hold values from -0.3125 to 0.3125
- fc1_bias: bfloat16 [1536], P('fsdp'), may hold values from -1.796875 to 1.796875
- fc2_weight: bfloat16 [1536, 384], P('fsdp'), may hold values from -0.15625 to 0.15625
- fc2_bias: bfloat16 [384], P('fsdp'), may hold values from -1.796875 to 1.796875
Outputs:
- block_output: bfloat16 [256, 257, 384], P(('fsdp', 'dp'))
- input_grad: float32 [256, 257, 384], P(('fsdp', 'dp'))
- ln1_gain_grad: float32 [384], P('fsdp')
- ln1_bias_grad: float32 [384], P('fsdp')
- qkv_weight_grad: float32 [384, 1152], P('fsdp')
- qv_bias_grad: float32 [768], P('fsdp')
- out_weight_grad: float32 [384, 384], P('fsdp')
- out_bias_grad: float32 [384], P('fsdp')
- ln2_gain_grad: float32 [384], P('fsdp')
- ln2_bias_grad: float32 [384], P('fsdp')
- fc1_weight_grad: float32 [384, 1536], P('fsdp')
- fc1_bias_grad: float32 [1536], P('fsdp')
- fc2_weight_grad: float32 [1536, 384], P('fsdp')
- fc2_bias_grad: float32 [384], P('fsdp')
The draws below stay inside these ranges and needn't reach their ends.
Inputs may be any that keep to these rules, and one draw needn't show every extreme that they name: 1 marks a duplicate patch; the entry at position 0, the class token, is not read.
All inputs are finite; a program needn't handle non-finite values. No bound on the sum of `duplicate` on one device may be relied on, other than what follows from the above.
Results may differ from the reference program's by a relative error of at most 0.009.
Values may be sent and summed in bfloat16 or wider, within the bound.
A program may use at most 128 MiB of HBM per device.

```python
import jax
import jax.numpy as jnp
from jax import lax

D = 384
FF = 1536
HEADS = 6
HEAD_DIM = 64
SEQ = 257
IMG_DEV = 8
IMAGES = 256


def with_ends(values, rng, smallest, high):
    longest = values.shape.index(max(values.shape))
    spots = []
    for shift in (0, 1):
        where = [jax.random.randint(jax.random.fold_in(rng, axis), (), 0, length) for axis, length in enumerate(values.shape)]
        where[longest] = (where[longest] + shift) % values.shape[longest]
        spots.append(tuple(where))
    return values.at[spots[0]].set(smallest).at[spots[1]].set(high)


def shard_levels(own_key, extent, shards, smallest, top_value):
    level, own = 1.0, jax.random.fold_in(own_key, 6)
    for dim, shards_of in shards:
        steps = jnp.exp(jax.random.uniform(jax.random.fold_in(own, dim), (shards_of,), jnp.float32, smallest / len(shards), top_value / len(shards)))
        level = level * jnp.repeat(steps, extent[dim] // shards_of).reshape([-1 if axis == dim else 1 for axis in range(len(extent))])
    return level


def noise(stream_key, extent, width, limit, shards=(), dtype=jnp.bfloat16):
    entries = jax.random.normal(stream_key, extent, jnp.float32) * width
    if len(shards) > 0:
        entries = shard_levels(stream_key, extent, shards, -0.22, 0.18) * entries
    return jnp.clip(entries, min=-limit, max=limit).astype(dtype)


def setup_inputs(seed: int = 0) -> dict:
    key_list = jax.random.split(jax.random.key(seed), 16)
    return {
        "tokens": noise(key_list[0], (IMAGES, SEQ, D), 1.0, 6.0, ((0, 32),)),
        "duplicate": with_ends((jax.random.randint(key_list[1], (IMAGES, SEQ), 0, 4) < 1).astype(jnp.int32), jax.random.fold_in(key_list[1], 1), 0, 1),
        "targets": noise(key_list[2], (IMAGES, D), 1.0, 6.0, ((0, 32),), jnp.float32),
        "ln1_gain": jnp.clip(1.0 + 0.1 * jax.random.normal(key_list[3], (D,), jnp.float32), 0.5, 1.5).astype(jnp.bfloat16),
        "ln1_bias": noise(key_list[4], (D,), 0.3, 1.796875, ((0, 16),)),
        "qkv_weight": noise(key_list[5], (D, 3 * D), D ** -0.5, 0.3125, ((0, 16),)),
        "qv_bias": noise(key_list[6], (2 * D,), 0.3, 1.796875, ((0, 16),)),
        "out_weight": noise(key_list[7], (D, D), (D // 16) ** -0.5, 1.25, ((0, 16),)),
        "out_bias": noise(key_list[8], (D,), 0.3, 1.796875, ((0, 16),)),
        "ln2_gain": jnp.clip(1.0 + 0.1 * jax.random.normal(key_list[9], (D,), jnp.float32), 0.5, 1.5).astype(jnp.bfloat16),
        "ln2_bias": noise(key_list[10], (D,), 0.3, 1.796875, ((0, 16),)),
        "fc1_weight": noise(key_list[11], (D, FF), D ** -0.5, 0.3125, ((0, 16),)),
        "fc1_bias": noise(key_list[12], (FF,), 0.3, 1.796875, ((0, 16),)),
        "fc2_weight": noise(key_list[13], (FF, D), FF ** -0.5, 0.15625, ((0, 16),)),
        "fc2_bias": noise(key_list[14], (D,), 0.3, 1.796875, ((0, 16),)),
    }


@jax.custom_vjp
def low(v):
    return lax.optimization_barrier(v.astype(jnp.bfloat16)).astype(jnp.float32)

@jax.custom_vjp
def low_back(v):
    return v

def low_keep(v):
    return (low(v), None)

def low_pass(kept, grad):
    return (grad,)

def back_keep(v):
    return (v, None)

def back_low(kept, grad):
    return (low(grad),)
low.defvjp(low_keep, low_pass)
low_back.defvjp(back_keep, back_low)
EPSILON = 1e-06
HIGHEST = lax.Precision.HIGHEST

def layer_norm(values, gain, shift):
    centre = lax.optimization_barrier(jnp.mean(values, -1, keepdims=True))
    centred = values - centre
    spread = lax.optimization_barrier(jnp.mean(centred * centred, -1, keepdims=True))
    return centred * lax.rsqrt(spread + EPSILON) * gain + shift

def gelu_exact(values):
    return jax.nn.gelu(values, approximate=False)

def block(tok_in, params):
    ln1_gain, ln1_bias, qkv_weight, qv_bias, out_weight, out_bias, ln2_gain, ln2_bias, fc1_weight, fc1_bias, fc2_weight, fc2_bias = params
    image_count, seq_len, feature_width = tok_in.shape
    tok_rows = tok_in.reshape(image_count * seq_len, feature_width)
    normed1 = low(layer_norm(tok_rows, ln1_gain, ln1_bias))
    bias_full = jnp.concatenate([qv_bias[:feature_width], jnp.zeros((feature_width,), jnp.float32), qv_bias[feature_width:]])
    qkv = low_back(low(jnp.dot(normed1, qkv_weight, precision=HIGHEST) + bias_full))
    qkv = qkv.reshape(image_count, seq_len, 3, HEADS, HEAD_DIM)
    queries = qkv[:, :, 0]
    key_heads = qkv[:, :, 1]
    value_heads = qkv[:, :, 2]
    score_scale = HEAD_DIM ** (-0.5)
    scores = low_back(jnp.einsum('bqhd,bkhd->bhqk', queries, key_heads, precision=HIGHEST) * score_scale)
    shares = low(jax.nn.softmax(scores, -1))
    attended = jnp.einsum('bhqk,bkhd->bqhd', shares, value_heads, precision=HIGHEST)
    attended = low_back(low(attended.reshape(image_count * seq_len, feature_width)))
    middle = tok_rows + low_back(jnp.dot(attended, out_weight, precision=HIGHEST) + out_bias)
    normed2 = low(layer_norm(middle, ln2_gain, ln2_bias))
    hidden_pre = low_back(jnp.dot(normed2, fc1_weight, precision=HIGHEST) + fc1_bias)
    activated = low(gelu_exact(hidden_pre))
    final = middle + low_back(jnp.dot(activated, fc2_weight, precision=HIGHEST) + fc2_bias)
    return final.reshape(image_count, seq_len, feature_width)

def keep_weights(duplicate):
    position = jnp.arange(duplicate.shape[-1])[None, :]
    return jnp.where(position == 0, jnp.float32(1.0), jnp.float32(1.0) - duplicate.astype(jnp.float32))

def group_loss(tok_in, target_rows, keep, params):
    final = block(tok_in, params)
    count = lax.optimization_barrier(jnp.sum(keep, -1))
    pooled = lax.optimization_barrier(jnp.sum(keep[:, :, None] * final, 1)) / count[:, None]
    return (SEQ * jnp.sum(pooled * target_rows), final)

def reference(tokens, duplicate, targets, ln1_gain, ln1_bias, qkv_weight, qv_bias, out_weight, out_bias, ln2_gain, ln2_bias, fc1_weight, fc1_bias, fc2_weight, fc2_bias):
    params = tuple((weight.astype(jnp.float32) for weight in (ln1_gain, ln1_bias, qkv_weight, qv_bias, out_weight, out_bias, ln2_gain, ln2_bias, fc1_weight, fc1_bias, fc2_weight, fc2_bias)))
    groups = IMAGES // IMG_DEV
    tok_groups = tokens.reshape(groups, IMG_DEV, SEQ, D)
    dup_groups = duplicate.reshape(groups, IMG_DEV, SEQ)
    target_groups = targets.reshape(groups, IMG_DEV, D)

    def step(carry, inputs_block):
        tok_block, dup_block, target_block = inputs_block
        keep = keep_weights(dup_block)

        def loss_of(tok_in, *weights):
            return group_loss(tok_in, target_block, keep, weights)
        loss_value, pullback, final = jax.vjp(loss_of, tok_block.astype(jnp.float32), *params, has_aux=True)
        grads = pullback(jnp.ones_like(loss_value))
        updated = tuple((total + grad for total, grad in zip(carry, grads[1:])))
        return (updated, (final.astype(jnp.bfloat16), grads[0]))
    start = tuple((jnp.zeros_like(weight) for weight in params))
    totals, (outputs, input_grads) = lax.scan(step, start, (tok_groups, dup_groups, target_groups))
    block_output = outputs.reshape(IMAGES, SEQ, D)
    input_grad = input_grads.reshape(IMAGES, SEQ, D)
    return (block_output, input_grad, totals[0], totals[1], totals[2], totals[3], totals[4], totals[5], totals[6], totals[7], totals[8], totals[9], totals[10], totals[11])
```

```python
import functools
import jax
import jax.numpy as jnp
from jax import lax
from jax.experimental import pallas as pl
from jax.experimental.pallas import tpu as pltpu
from jax.sharding import PartitionSpec as P

HEADS = 6
HD = 64
EPS = 1e-06
F32 = jnp.float32
BF16 = jnp.bfloat16

NN = (((1,), (0,)), ((), ()))
NT = (((1,), (1,)), ((), ()))


def mm(a, b, dims=NN):
    return lax.dot_general(a, b, dims, preferred_element_type=F32)


def normalise(v):
    mu = jnp.mean(v, 0, keepdims=True)
    c = v - mu
    r = lax.rsqrt(jnp.mean(c * c, 0, keepdims=True) + EPS)
    return c * r, r


def norm_back(dn, u, r, gain):
    e = dn * gain
    me = jnp.mean(e, 0, keepdims=True)
    meu = jnp.mean(e * u, 0, keepdims=True)
    return r * (e - me - u * meu)


def fold(v):
    lanes = v.shape[1]
    total = v[:, :128]
    for k in range(1, lanes // 128):
        total = total + v[:, 128 * k : 128 * (k + 1)]
    return total


def wide(col, lanes):
    if lanes == 128:
        return col
    return jnp.concatenate([col] * (lanes // 128), 1)


def gelu_pair(x):
    e = jnp.exp(x * x * -0.5)
    d = 1.0 + 0.231641888 * jnp.abs(x)
    t = pl.reciprocal(d, approx=True)
    t = t * (2.0 - d * t)
    poly = t * (0.127414796 + t * (-0.142248368 + t * (0.710706871 + t * (-0.726576014 + t * 0.530702715))))
    h = poly * e
    phi = jnp.where(x >= 0.0, 1.0 - h, h)
    return x * phi, phi + x * (e * 0.3989422804014327)


def rows_of(values):
    return jnp.concatenate(values, 0)


MESH_ID = pl.DeviceIdType.MESH
NZ = 4


def place():
    p = lax.axis_index("fsdp")
    c = lax.axis_index("dp")
    x = lax.rem(p, 2)
    y = lax.rem(lax.div(p, 2), 2)
    z = lax.div(p, 4)
    return x, y, z, c


def index_of(x, y, z):
    return (z * 2 + y) * 2 + x


def greet(x, y, z, c):
    barrier = pltpu.get_barrier_semaphore()
    pl.semaphore_signal(barrier, inc=1, device_id=(index_of(1 - x, y, z), c), device_id_type=MESH_ID)
    pl.semaphore_signal(barrier, inc=1, device_id=(index_of(x, 1 - y, z), c), device_id_type=MESH_ID)
    pl.semaphore_signal(barrier, inc=1, device_id=(index_of(x, y, z), 1 - c), device_id_type=MESH_ID)
    for step in range(1, NZ):
        other = lax.rem(z + step, NZ)
        pl.semaphore_signal(barrier, inc=1, device_id=(index_of(x, y, other), c), device_id_type=MESH_ID)
    pl.semaphore_wait(barrier, 3 + NZ - 1)


def remote(src, dst, sems, k, device):
    return pltpu.make_async_remote_copy(
        src_ref=src, dst_ref=dst, send_sem=sems.at[0, k], recv_sem=sems.at[1, k],
        device_id=device, device_id_type=MESH_ID,
    )


def gather_body(qkv, outw, fc1, fc2, vec, slots1, slots2, slots_v, sems1, sems2, semsv, sib):
    x, y, z, c = place()
    d = outw.shape[1]

    f = fc1[...].astype(F32)
    q = qkv[...].astype(F32)

    @pl.when(c == 0)
    def _():
        slots1[0, y, x, z] = jnp.concatenate([q[:, :d], q[:, d : 2 * d]], 0).astype(BF16)
        slots2[0, y, x, z] = jnp.concatenate([f[:, k * d : (k + 1) * d] for k in range(4)], 0).astype(BF16)

    @pl.when(c == 1)
    def _():
        slots1[1, y, x, z] = jnp.concatenate([q[:, 2 * d :], outw[...].astype(F32)], 0).astype(BF16)
        slots2[1, y, x, z] = fc2[...]

    slots_v[y, x, z] = vec[...]
    greet(x, y, z, c)

    def line(buf, sems):
        copies = []
        for step in range(1, NZ):
            other = lax.rem(z + step, NZ)
            copy = remote(buf.at[y, x, z], buf.at[y, x, z], sems, step - 1, (index_of(x, y, other), c))
            copy.start()
            copies.append(copy)
        return copies

    def across(buf, sems, first):
        copies = []
        if first == "x":
            copies.append(remote(buf.at[y, x], buf.at[y, x], sems, 3, (index_of(1 - x, y, z), c)))
            copies[-1].start()
            copies[-1].wait()
            copies.append(remote(buf.at[y], buf.at[y], sems, 4, (index_of(x, 1 - y, z), c)))
            copies[-1].start()
            copies[-1].wait()
        else:
            copies.append(remote(buf.at[y, x], buf.at[y, x], sems, 3, (index_of(x, 1 - y, z), c)))
            copies[-1].start()
            copies[-1].wait()
            pair = [
                remote(buf.at[k, x], buf.at[k, x], sems, 4 + k, (index_of(1 - x, y, z), c)) for k in range(2)
            ]
            for copy in pair:
                copy.start()
            for copy in pair:
                copy.wait()

    def path(group, first):
        one, two = slots1.at[group], slots2.at[group]
        flights = line(slots_v, semsv) + line(one, sems1) + line(two, sems2)
        for copy in flights[:3]:
            copy.wait()
        for copy in flights[3:6]:
            copy.wait()
        across(slots_v, semsv, first)
        across(one, sems1, first)
        swap = remote(one, one, sib, 0, (index_of(x, y, z), 1 - c))
        swap.start()
        for copy in flights[6:]:
            copy.wait()
        across(two, sems2, first)
        swap2 = remote(two, two, sib, 1, (index_of(x, y, z), 1 - c))
        swap2.start()
        swap.wait()
        swap2.wait()

    @pl.when(c == 0)
    def _():
        path(0, "x")

    @pl.when(c == 1)
    def _():
        path(1, "y")


def reduce_body(
    gqkv, gout, g1, g2, gvec,
    oqkv, oout, o1, o2, ovec,
    t1, t2, u1, u2, a1, a2, b1, b2, z1, z2, f1, f2, va, vz, sems1, sems2, semsv,
):
    x, y, z, c = place()
    d = gout.shape[1]
    rows = gout.shape[0] // 16

    def stage(buf, group, blocks):
        for p in range(16):
            part = [b[rows * p : rows * (p + 1)] for b in blocks]
            buf[group, (p // 2) % 2, p % 2, p // 4] = jnp.concatenate(part, 0).astype(BF16)

    q = gqkv[...].astype(F32)
    stage(t1, 0, [q[:, :d], q[:, d : 2 * d]])
    stage(t1, 1, [q[:, 2 * d :], gout[...].astype(F32)])
    f = g1[...].astype(F32)
    stage(t2, 0, [f[:, k * d : (k + 1) * d] for k in range(4)])
    for p in range(16):
        t2[1, (p // 2) % 2, p % 2, p // 4] = g2[4 * rows * p : 4 * rows * (p + 1), :]
    va[0] = gvec[...]
    greet(x, y, z, c)

    sibling = (index_of(x, y, z), 1 - c)
    xn = (index_of(1 - x, y, z), c)
    yn = (index_of(x, 1 - y, z), c)

    def add(dst, src):
        dst[...] = (dst[...].astype(F32) + src[...].astype(F32)).astype(BF16)

    def send_all(copies):
        for copy in copies:
            copy.start()
        return copies

    def wait_all(copies):
        for copy in copies:
            copy.wait()

    def z_copies(src, dst, sems, base):
        copies = []
        for step in range(1, NZ):
            other = lax.rem(z + step, NZ)
            copies.append(remote(src(other), dst.at[step - 1], sems, base + step - 1, (index_of(x, y, other), c)))
        return copies

    def path(group, order):
        units = ((t1.at[group], u1, a1, b1, z1, f1, sems1), (t2.at[group], u2, a2, b2, z2, f2, sems2))
        swaps = [
            send_all([remote(full.at[1 - group], got, sems, 0, sibling)])
            for full, got, sems in ((t1, u1, sems1), (t2, u2, sems2))
        ]
        for (buf, got, *_), copies in zip(units, swaps):
            wait_all(copies)
            add(buf, got)
        flights = []
        for buf, got, ra, rb, rz, fin, sems in units:
            if order == "yx":
                flights.append(send_all([remote(buf.at[1 - y], ra, sems, 1, yn)]))
            else:
                flights.append(
                    send_all([remote(buf.at[k, 1 - x], ra.at[k], sems, 1 + k, xn) for k in range(2)])
                )
        for (buf, got, ra, rb, rz, fin, sems), copies in zip(units, flights):
            wait_all(copies)
            if order == "yx":
                add(buf.at[y], ra)
            else:
                for k in range(2):
                    add(buf.at[k, x], ra.at[k])
        flights = []
        for buf, got, ra, rb, rz, fin, sems in units:
            if order == "yx":
                flights.append(send_all([remote(buf.at[y, 1 - x], rb, sems, 3, xn)]))
            else:
                flights.append(send_all([remote(buf.at[1 - y, x], rb, sems, 3, yn)]))
        for (buf, got, ra, rb, rz, fin, sems), copies in zip(units, flights):
            wait_all(copies)
            add(buf.at[y, x], rb)
        flights = []
        for buf, got, ra, rb, rz, fin, sems in units:
            flights.append(send_all(z_copies(lambda k, buf=buf: buf.at[y, x, k], rz, sems, 4)))
        flights2 = []
        for (buf, got, ra, rb, rz, fin, sems), copies in zip(units, flights):
            wait_all(copies)
            total = buf[y, x, z].astype(F32)
            for k in range(NZ - 1):
                total = total + rz[k].astype(F32)
            fin[group] = total
            flights2.append(send_all([remote(fin.at[group], fin.at[group], sems, 7, sibling)]))
        for copies in flights2:
            wait_all(copies)

    for k, device in enumerate((sibling, xn, yn)):
        copy = remote(va.at[2 * k], va.at[2 * k + 1], semsv, k, device)
        copy.start()
        copy.wait()
        va[2 * k + 2] = va[2 * k] + va[2 * k + 1]
    vz[z] = va[6]
    copies = [
        remote(vz.at[z], vz.at[z], semsv, 2 + step, (index_of(x, y, lax.rem(z + step, NZ)), c))
        for step in range(1, NZ)
    ]
    send_all(copies)
    wait_all(copies)
    ovec[...] = vz[0] + vz[1] + vz[2] + vz[3]

    @pl.when(c == 0)
    def _():
        path(0, "yx")

    @pl.when(c == 1)
    def _():
        path(1, "xy")

    oqkv[:, :d] = f1[0, :rows]
    oqkv[:, d : 2 * d] = f1[0, rows:]
    oqkv[:, 2 * d :] = f1[1, :rows]
    oout[...] = f1[1, rows:]
    for k in range(4):
        o1[:, k * d : (k + 1) * d] = f2[0, rows * k : rows * (k + 1)]
    o2[...] = f2[1]


def gather_call(qkv, outw, fc1, fc2, vec):
    rows, d = outw.shape
    dma = pltpu.SemaphoreType.DMA
    spec = pl.BlockSpec(memory_space=pltpu.VMEM)
    return pl.pallas_call(
        gather_body,
        out_shape=(
            jax.ShapeDtypeStruct((2, 2, 2, NZ, 2 * rows, d), BF16),
            jax.ShapeDtypeStruct((2, 2, 2, NZ, 4 * rows, d), BF16),
            jax.ShapeDtypeStruct((2, 2, NZ) + vec.shape, vec.dtype),
        ),
        in_specs=[spec] * 5,
        out_specs=(spec,) * 3,
        scratch_shapes=[dma((2, 6)), dma((2, 6)), dma((2, 6)), dma((2, 2))],
        compiler_params=pltpu.CompilerParams(collective_id=0, has_side_effects=True, vmem_limit_bytes=48 * 1024 * 1024),
        name="gather",
    )(qkv, outw, fc1, fc2, vec)


def reduce_call(gqkv, gout, g1, g2, gvec):
    d = gout.shape[1]
    rows = d // 16
    dma = pltpu.SemaphoreType.DMA
    vm = pltpu.VMEM
    spec = pl.BlockSpec(memory_space=pltpu.VMEM)

    def pair(lead, dtype=BF16):
        return [vm(lead + (2 * rows, d), dtype), vm(lead + (4 * rows, d), dtype)]

    return pl.pallas_call(
        reduce_body,
        out_shape=(
            jax.ShapeDtypeStruct((rows, 3 * d), F32),
            jax.ShapeDtypeStruct((rows, d), F32),
            jax.ShapeDtypeStruct((rows, 4 * d), F32),
            jax.ShapeDtypeStruct((4 * rows, d), F32),
            jax.ShapeDtypeStruct(gvec.shape, F32),
        ),
        in_specs=[spec] * 5,
        out_specs=(spec,) * 5,
        scratch_shapes=pair((2, 2, 2, NZ)) + pair((2, 2, NZ)) + pair((2, NZ)) + pair((NZ,)) + pair((NZ - 1,))
        + pair((2,), F32) + [vm((7,) + gvec.shape, F32), vm((NZ,) + gvec.shape, F32)]
        + [dma((2, 8)), dma((2, 8)), dma((2, 8))],
        compiler_params=pltpu.CompilerParams(collective_id=1, has_side_effects=True, vmem_limit_bytes=48 * 1024 * 1024),
        name="reduce",
    )(gqkv, gout, g1, g2, gvec)


LN1G, LN1B, BQKV, BOUT, LN2G, LN2B, BFC1, BFC2 = range(8)


def to_columns(vec, row, count):
    return jnp.broadcast_to(vec[row : row + 1, :count], (128, count)).T


def compute_body(
    tok, dup, tgt, vec, wqkv, wout, w1, w2,
    out, gin, gqkv, gout, g1, g2, gvec,
    xs, n1, qkv, att, n2, act, dpre, db2, db1, dos, dmid, probs,
    wqkv_t, wout_t, w1_t, w2_t,
    c_ln1g, c_ln1b, c_bqkv, c_bout, c_ln2g, c_ln2b, c_b1, c_b2,
    rl_s, ex_s, exq_s, rlx_s, exx_s, attx, dqkvx, a_g1, a_b1, a_g2, a_b2, tgt_t, stage, gin_sem,
):
    images, seq = dup.shape
    d = tok.shape[1]
    t = seq - 1
    x0 = images * t
    ff = w1.shape[1]
    w = x0 + 128
    dqkv = act.at[: 3 * d]

    blocks = d // 128

    def load_image(i):
        return jnp.concatenate([stage[b, pl.ds(i, t, stride=images), :] for b in range(blocks)], 1)

    def store_image(i, values):
        for b in range(blocks):
            stage[b, pl.ds(i, t, stride=images), :] = values[:, 128 * b : 128 * (b + 1)]

    def store_last(values):
        for b in range(blocks):
            stage[b, x0:, :] = values[:images, 128 * b : 128 * (b + 1)]

    def lanes_of(i):
        return pl.ds(pl.multiple_of(i * t, 128), t)

    extra_lanes = pl.ds(x0, 128)

    wqkv_t[...] = wqkv[...].T
    wout_t[...] = wout[...].T
    w1_t[...] = w1[...].T
    w2_t[...] = w2[...].T
    c_ln1g[...] = to_columns(vec, LN1G, d)
    c_ln1b[...] = to_columns(vec, LN1B, d)
    c_bqkv[...] = to_columns(vec, BQKV, 3 * d)
    c_bout[...] = to_columns(vec, BOUT, d)
    c_ln2g[...] = to_columns(vec, LN2G, d)
    c_ln2b[...] = to_columns(vec, LN2B, d)
    c_b1[...] = to_columns(vec, BFC1, ff)
    c_b2[...] = to_columns(vec, BFC2, d)
    tgt_t[...] = jnp.concatenate([tgt[...], jnp.zeros((128 - images, d), F32)], 0).T
    ones_row = jnp.where(lax.broadcasted_iota(jnp.int32, (16, w), 0) == 0, 1.0, 0.0).astype(BF16)
    n1[d : d + 16, :] = ones_row
    n2[d : d + 16, :] = ones_row
    att[d : d + 16, :] = ones_row
    act[ff : ff + 16, :] = ones_row
    attx[...] = jnp.zeros_like(attx)
    dqkvx[...] = jnp.zeros_like(dqkvx)
    for acc in (a_g1, a_b1, a_g2, a_b2):
        acc[...] = jnp.zeros_like(acc)

    def project(x_t, lanes, count):
        x = x_t.astype(F32)
        xs[:, lanes] = x_t
        u, r = normalise(x)
        n = (u * wide(c_ln1g[...], count) + wide(c_ln1b[...], count)).astype(BF16)
        n1[:d, lanes] = n
        for k in range(3):
            rows = slice(k * d, (k + 1) * d)
            y = mm(wqkv_t[rows, :], n) + wide(c_bqkv[rows, :], count)
            y = y.astype(BF16)
            if k == 0:
                y = y * jnp.asarray(HD**-0.5, BF16)
            qkv[rows, lanes] = y

    def project_image(i, carry):
        project(load_image(i).astype(BF16).T, lanes_of(i), t)
        return carry

    for b in range(blocks):
        stage[b] = tok[:, 128 * b : 128 * (b + 1)].astype(F32)

    lax.fori_loop(0, images, project_image, 0)
    last = jnp.concatenate([tok[x0:, :].astype(F32), jnp.zeros((128 - images, d), F32)], 0)
    project(last.astype(BF16).T, extra_lanes, 128)

    lane_ids = lax.broadcasted_iota(jnp.int32, (HD, 128), 1)

    def pick(ref, row, i):
        block = ref[row : row + HD, extra_lanes].astype(F32)
        return jnp.sum(jnp.where(lane_ids == i, block, 0.0), 1, keepdims=True)

    def attend_image(i, carry):
        lanes = lanes_of(i)
        for h in range(HEADS):
            r0 = h * HD
            q = qkv[r0 : r0 + HD, lanes]
            k = qkv[d + r0 : d + r0 + HD, lanes]
            v = qkv[2 * d + r0 : 2 * d + r0 + HD, lanes]
            qx, kx, vx = pick(qkv, r0, i), pick(qkv, d + r0, i), pick(qkv, 2 * d + r0, i)
            s = mm(k.T, q)
            sx = jnp.sum(q.astype(F32) * kx, 0, keepdims=True)
            top = jnp.maximum(jnp.max(s, 0, keepdims=True), sx)
            e = jnp.exp(s - top)
            ex = jnp.exp(sx - top)
            rl = 1.0 / (jnp.sum(e, 0, keepdims=True) + ex)
            e = e.astype(BF16)
            probs[i * HEADS + h] = e
            o = (mm(v, e) + vx * ex) * rl
            att[r0 : r0 + HD, lanes] = o.astype(BF16)
            rl_s[i, h : h + 1, :] = rl
            ex_s[i, h : h + 1, :] = ex
            sq = jnp.sum(k.astype(F32) * qx, 0, keepdims=True)
            sxx = jnp.sum(kx * qx, 0, keepdims=True)
            topx = jnp.maximum(jnp.max(sq, 1, keepdims=True), sxx)
            eq = jnp.exp(sq - topx)
            exx = jnp.exp(sxx - topx)
            rlx = 1.0 / (jnp.sum(eq, 1, keepdims=True) + exx)
            ox = (jnp.sum(v.astype(F32) * eq, 1, keepdims=True) + vx * exx) * rlx
            attx[r0 : r0 + HD, :] = jnp.where(lane_ids == i, ox, attx[r0 : r0 + HD, :])
            exq_s[i, h : h + 1, :] = eq
            rlx_s[i, h : h + 1, :] = jnp.broadcast_to(rlx, (1, 128))
            exx_s[i, h : h + 1, :] = jnp.broadcast_to(exx, (1, 128))
        return carry

    lax.fori_loop(0, images, attend_image, 0)
    att[:d, extra_lanes] = attx[...].astype(BF16)

    def feed(lanes, count, d_final):
        mid = xs[:, lanes].astype(F32) + mm(wout_t[...], att[:d, lanes]) + wide(c_bout[...], count)
        u, r = normalise(mid)
        n = (u * wide(c_ln2g[...], count) + wide(c_ln2b[...], count)).astype(BF16)
        n2[:d, lanes] = n
        db = d_final.astype(BF16)
        db2[:, lanes] = db
        for j in range(ff // 256):
            rows = slice(256 * j, 256 * (j + 1))
            pre = mm(w1_t[rows, :], n) + wide(c_b1[rows, :], count)
            da = mm(w2[rows, :], db)
            value, slope = gelu_pair(pre)
            act[rows, lanes] = value.astype(BF16)
            dpre[rows, lanes] = (slope * da).astype(BF16)
        final = mid + mm(w2_t[...], act[:ff, lanes]) + wide(c_b2[...], count)
        dn = mm(w1[...], dpre[:, lanes])
        a_g2[...] += fold(dn * u)
        a_b2[...] += fold(dn)
        dm = d_final + norm_back(dn, u, r, wide(c_ln2g[...], count))
        dmid[:, lanes] = dm
        low = dm.astype(BF16)
        db1[:, lanes] = low
        dos[:, lanes] = mm(wout[...], low).astype(BF16)
        return final.T

    def keep_row(row):
        first = lax.broadcasted_iota(jnp.int32, row.shape, 1) == 0
        return jnp.where(first, 1.0, 1.0 - row.astype(F32))

    def feed_image(i, carry):
        keep = keep_row(dup[pl.ds(i, 1), :])
        count = jnp.sum(keep, 1, keepdims=True)
        scale = seq * keep[:, :t] / count
        ids = lax.broadcasted_iota(jnp.int32, (d, 128), 1)
        target = jnp.sum(jnp.where(ids == i, tgt_t[...], 0.0), 1, keepdims=True)
        store_image(i, feed(lanes_of(i), t, target * scale))
        return carry

    lax.fori_loop(0, images, feed_image, 0)
    keep_all = keep_row(dup[...])
    scale_x = seq * keep_all[:, t:] / jnp.sum(keep_all, 1, keepdims=True)
    scale_x = jnp.broadcast_to(scale_x, (images, 128))
    scale_x = jnp.concatenate([scale_x, jnp.zeros((128 - images, 128), F32)], 0).T[:1, :]
    store_last(feed(extra_lanes, 128, tgt_t[...] * scale_x))
    for b in range(blocks):
        out[:, 128 * b : 128 * (b + 1)] = stage[b].astype(BF16)

    for j in range(ff // 256):
        rows = slice(256 * j, 256 * (j + 1))
        g = mm(n2[...], dpre[rows, :], NT)
        g1[:, rows] = g[:d].astype(BF16)
        gvec[BFC1 : BFC1 + 1, rows] = g[d : d + 1]
        g2[rows, :] = mm(act[rows, :], db2[...], NT).astype(BF16)
    g = mm(act[ff : ff + 16, :], db2[...], NT)
    gvec[BFC2 : BFC2 + 1, :d] = g[:1]

    def attend_back(i, carry):
        lanes = lanes_of(i)
        for h in range(HEADS):
            r0 = h * HD
            q = qkv[r0 : r0 + HD, lanes]
            k = qkv[d + r0 : d + r0 + HD, lanes]
            v = qkv[2 * d + r0 : 2 * d + r0 + HD, lanes]
            qx, kx, vx = pick(qkv, r0, i), pick(qkv, d + r0, i), pick(qkv, 2 * d + r0, i)
            rl = rl_s[i, h : h + 1, :]
            ex = ex_s[i, h : h + 1, :]
            do = dos[r0 : r0 + HD, lanes].astype(F32) * rl
            dot_o = jnp.sum(do * att[r0 : r0 + HD, lanes].astype(F32), 0, keepdims=True)
            dol = do.astype(BF16)
            p = probs[i * HEADS + h]
            ds = (p.astype(F32) * (mm(v.T, dol) - dot_o)).astype(BF16)
            dsx = ex * (jnp.sum(do * vx, 0, keepdims=True) - dot_o)
            dq = mm(k, ds) + kx * dsx
            dk = mm(q, ds, NT)
            dv = mm(dol, p, NT)
            qf = q.astype(F32)
            kf = k.astype(F32)
            vf = v.astype(F32)
            dkx = jnp.sum(qf * dsx, 1, keepdims=True)
            dvx = jnp.sum(do * ex, 1, keepdims=True)
            eq = exq_s[i, h : h + 1, :]
            rlx = rlx_s[i, h : h + 1, :1]
            exx = exx_s[i, h : h + 1, :1]
            dox = pick(dos, r0, i) * rlx
            dotx = jnp.sum(dox * pick(att, r0, i), 0, keepdims=True)
            dsq = eq * (jnp.sum(vf * dox, 0, keepdims=True) - dotx)
            dsxx = exx * (jnp.sum(vx * dox, 0, keepdims=True) - dotx)
            dqx = jnp.sum(kf * dsq, 1, keepdims=True) + kx * dsxx
            dk = dk + qx * dsq
            dv = dv + dox * eq
            dkx = dkx + qx * dsxx
            dvx = dvx + dox * exx
            scale = HD**-0.5
            for base, main, tail in ((0, dq * scale, dqx * scale), (d, dk, dkx), (2 * d, dv, dvx)):
                rows = slice(base + r0, base + r0 + HD)
                dqkv[rows, lanes] = main.astype(BF16)
                dqkvx[rows, :] = jnp.where(lane_ids == i, tail, dqkvx[rows, :])
        return carry

    lax.fori_loop(0, images, attend_back, 0)
    dqkv[:, extra_lanes] = dqkvx[...].astype(BF16)

    for k in range(3):
        rows = slice(k * d, (k + 1) * d)
        g = mm(n1[...], dqkv[rows, :], NT)
        gqkv[:, rows] = g[:d].astype(BF16)
        gvec[BQKV : BQKV + 1, rows] = g[d : d + 1]
    g = mm(att[...], db1[...], NT)
    gout[...] = g[:d].astype(BF16)
    gvec[BOUT : BOUT + 1, :d] = g[d : d + 1]

    def finish(lanes, count):
        u, r = normalise(xs[:, lanes].astype(F32))
        dn = mm(wqkv[...], dqkv[:, lanes])
        a_g1[...] += fold(dn * u)
        a_b1[...] += fold(dn)
        return (dmid[:, lanes] + norm_back(dn, u, r, wide(c_ln1g[...], count))).T

    def finish_image(i, carry):
        store_image(i, finish(lanes_of(i), t))
        return carry

    lax.fori_loop(0, images, finish_image, 0)
    store_last(finish(extra_lanes, 128))
    copies = [
        pltpu.make_async_copy(stage.at[b], gin.at[:, pl.ds(128 * b, 128)], gin_sem.at[b]) for b in range(blocks)
    ]
    for copy in copies:
        copy.start()

    for row, acc in ((LN1G, a_g1), (LN1B, a_b1), (LN2G, a_g2), (LN2B, a_b2)):
        gvec[row : row + 1, :d] = jnp.sum(acc[...].T, 0, keepdims=True)
    for copy in copies:
        copy.wait()


def compute(tok, dup, tgt, vec, wqkv, wout, w1, w2):
    images, seq = dup.shape
    d = tok.shape[1]
    ff = w1.shape[1]
    t = seq - 1
    w = images * t + 128
    vm = pltpu.VMEM
    scratch = [
        vm((d, w), BF16),
        vm((d + 16, w), BF16),
        vm((3 * d, w), BF16),
        vm((d + 16, w), BF16),
        vm((d + 16, w), BF16),
        vm((ff + 16, w), BF16),
        vm((ff, w), BF16),
        vm((d, w), BF16),
        vm((d, w), BF16),
        vm((d, w), BF16),
        vm((d, w), F32),
        vm((images * HEADS, t, t), BF16),
        vm((3 * d, d), BF16),
        vm((d, d), BF16),
        vm((ff, d), BF16),
        vm((d, ff), BF16),
        vm((d, 128), F32), vm((d, 128), F32), vm((3 * d, 128), F32), vm((d, 128), F32),
        vm((d, 128), F32), vm((d, 128), F32), vm((ff, 128), F32), vm((d, 128), F32),
        vm((images, 8, t), F32),
        vm((images, 8, t), F32),
        vm((images, 8, t), F32),
        vm((images, 8, 128), F32),
        vm((images, 8, 128), F32),
        vm((d, 128), F32),
        vm((3 * d, 128), F32),
        vm((d, 128), F32), vm((d, 128), F32), vm((d, 128), F32), vm((d, 128), F32),
        vm((d, 128), F32),
        vm((d // 128, images * seq, 128), F32),
        pltpu.SemaphoreType.DMA((d // 128,)),
    ]
    outs = (
        jax.ShapeDtypeStruct(tok.shape, BF16),
        jax.ShapeDtypeStruct(tok.shape, F32),
        jax.ShapeDtypeStruct((d, 3 * d), BF16),
        jax.ShapeDtypeStruct((d, d), BF16),
        jax.ShapeDtypeStruct((d, ff), BF16),
        jax.ShapeDtypeStruct((ff, d), BF16),
        jax.ShapeDtypeStruct((8, ff), F32),
    )
    spec = pl.BlockSpec(memory_space=pltpu.VMEM)
    return pl.pallas_call(
        compute_body,
        out_shape=outs,
        in_specs=[spec] * 8,
        out_specs=(spec, pl.BlockSpec(memory_space=pl.ANY)) + (spec,) * 5,
        scratch_shapes=scratch,
        compiler_params=pltpu.CompilerParams(vmem_limit_bytes=64 * 1024 * 1024),
        name="block",
    )(tok, dup, tgt, vec, wqkv, wout, w1, w2)

def gather_all(value):
    return lax.all_gather(value, "fsdp", axis=0, tiled=True)


def pack_rows(ln1_gain, ln1_bias, qv_bias, out_bias, ln2_gain, ln2_bias, fc1_bias, fc2_bias):
    n = ln1_gain.shape[0]
    rows = [ln1_gain, ln1_bias, qv_bias[:n], qv_bias[n:], out_bias, ln2_gain, ln2_bias, fc2_bias]
    rows += [fc1_bias[n * k : n * (k + 1)] for k in range(4)]
    table = jnp.stack(rows, 0)
    return jnp.pad(table, ((0, 4), (0, 128 - n)))


def vectors(full):
    ln1_gain, ln1_bias, qv_bias, out_bias, ln2_gain, ln2_bias, fc1_bias, fc2_bias = full
    d = ln1_gain.shape[0]
    bias = jnp.concatenate([qv_bias[:d], jnp.zeros((d,), qv_bias.dtype), qv_bias[d:]])
    rows = (ln1_gain, ln1_bias, bias, out_bias, ln2_gain, ln2_bias, fc1_bias, fc2_bias)
    width = fc1_bias.shape[0]
    return jnp.stack([jnp.pad(row.astype(F32), (0, width - row.shape[0])) for row in rows], 0)


def per_device(
    tokens, duplicate, targets,
    ln1_gain, ln1_bias, qkv_weight, qv_bias, out_weight, out_bias,
    ln2_gain, ln2_bias, fc1_weight, fc1_bias, fc2_weight, fc2_bias,
    block16,
):
    images, seq, d = tokens.shape
    small = (ln1_gain, ln1_bias, qv_bias, out_bias, ln2_gain, ln2_bias, fc1_bias, fc2_bias)
    rows = tokens.transpose(1, 0, 2).reshape(seq * images, d)
    if block16:
        n = d // 16
        slots1, slots2, slots_v = gather_call(
            qkv_weight, out_weight, fc1_weight, fc2_weight, pack_rows(*small).astype(BF16)
        )
        def whole(slots):
            return slots.transpose((2, 0, 1) + tuple(range(3, slots.ndim))).reshape((16,) + slots.shape[3:])

        g0, g1 = whole(slots1[0]), whole(slots1[1])
        wqkv = jnp.concatenate([g0[:, :n], g0[:, n:], g1[:, :n]], 2).reshape(d, 3 * d)
        wout = g1[:, n:].reshape(d, d)
        w1 = whole(slots2[0]).reshape(16, 4, n, d).transpose(0, 2, 1, 3).reshape(d, 4 * d)
        w2 = whole(slots2[1]).reshape(4 * d, d)
        table = whole(slots_v)[:, :12, :n]
        line = lambda k: table[:, k].reshape(d)
        qv = table[:, 2:4].reshape(2 * d)
        b1 = table[:, 8:12].reshape(4 * d)
        vec = vectors((line(0), line(1), qv, line(4), line(5), line(6), b1, line(7)))
    else:
        wqkv, wout, w1, w2 = map(gather_all, (qkv_weight, out_weight, fc1_weight, fc2_weight))
        vec = vectors(tuple(map(gather_all, small)))
    out, gin, gqkv, gout, g1, g2, gvec = compute(rows, duplicate, targets, vec, wqkv, wout, w1, w2)
    if block16:
        gqkv, gout, g1, g2, gvec = reduce_call(gqkv, gout, g1, g2, gvec)
        p = lax.axis_index("fsdp")
    else:
        def scatter(value):
            value = lax.psum_scatter(value.astype(F32), "fsdp", scatter_dimension=0, tiled=True)
            return lax.psum(value, "dp")

        gqkv, gout, g1, g2 = map(scatter, (gqkv, gout, g1, g2))
        gvec = lax.psum(gvec, ("fsdp", "dp"))
        p = lax.axis_index("fsdp")

    def shard(value, whole_size):
        count = whole_size // lax.axis_size("fsdp")
        return lax.dynamic_slice(value, (p * count,), (count,))

    qv_grad = jnp.concatenate([gvec[2, :d], gvec[2, 2 * d : 3 * d]])
    back = lambda v: v.reshape(seq, images, d).transpose(1, 0, 2)
    return (
        back(out), back(gin),
        shard(gvec[0], d), shard(gvec[1], d), gqkv, shard(qv_grad, 2 * d), gout, shard(gvec[3], d),
        shard(gvec[4], d), shard(gvec[5], d), g1, shard(gvec[6], 4 * d), g2, shard(gvec[7], d),
    )


def solution(mesh):
    block16 = mesh.shape["fsdp"] == 16 and mesh.shape["dp"] == 2
    both = ("fsdp", "dp")
    vector, matrix = P("fsdp"), P("fsdp", None)
    weights = (vector, vector, matrix, vector, matrix, vector, vector, vector, matrix, vector, matrix, vector)
    return jax.shard_map(
        functools.partial(per_device, block16=block16),
        mesh=mesh,
        in_specs=(P(both, None, None), P(both, None), P(both, None)) + weights,
        out_specs=(P(both, None, None), P(both, None, None)) + weights,
        check_vma=False,
    )
```

```python
import functools
import jax
import jax.numpy as jnp
from jax import lax
from jax.experimental import pallas as pl
from jax.experimental.pallas import tpu as pltpu
from jax.sharding import PartitionSpec as P

HEADS = 6
HD = 64
EPS = 1e-06
F32 = jnp.float32
BF16 = jnp.bfloat16

NN = (((1,), (0,)), ((), ()))
NT = (((1,), (1,)), ((), ()))


def mm(a, b, dims=NN):
    return lax.dot_general(a, b, dims, preferred_element_type=F32)


def normalise(v):
    mu = jnp.mean(v, 0, keepdims=True)
    c = v - mu
    r = lax.rsqrt(jnp.mean(c * c, 0, keepdims=True) + EPS)
    return c * r, r


def norm_back(dn, u, r, gain):
    e = dn * gain
    me = jnp.mean(e, 0, keepdims=True)
    meu = jnp.mean(e * u, 0, keepdims=True)
    return r * (e - me - u * meu)


def fold(v):
    lanes = v.shape[1]
    total = v[:, :128]
    for k in range(1, lanes // 128):
        total = total + v[:, 128 * k : 128 * (k + 1)]
    return total


def wide(col, lanes):
    if lanes == 128:
        return col
    return jnp.concatenate([col] * (lanes // 128), 1)


def gelu_pair(x):
    e = jnp.exp(x * x * -0.5)
    d = 1.0 + 0.231641888 * jnp.abs(x)
    t = pl.reciprocal(d, approx=True)
    t = t * (2.0 - d * t)
    poly = t * (0.127414796 + t * (-0.142248368 + t * (0.710706871 + t * (-0.726576014 + t * 0.530702715))))
    h = poly * e
    phi = jnp.where(x >= 0.0, 1.0 - h, h)
    return x * phi, phi + x * (e * 0.3989422804014327)


def rows_of(values):
    return jnp.concatenate(values, 0)


LN1G, LN1B, BQKV, BOUT, LN2G, LN2B, BFC1, BFC2 = range(8)


def to_columns(vec, row, count):
    return jnp.broadcast_to(vec[row : row + 1, :count], (128, count)).T


def compute_body(
    tok, dup, tgt, vec, wqkv, wout, w1, w2,
    out, gin, gqkv, gout, g1, g2, gvec,
    xs, n1, qkv, att, n2, act, dpre, db2, db1, dos, dmid, probs,
    wqkv_t, wout_t, w1_t, w2_t,
    c_ln1g, c_ln1b, c_bqkv, c_bout, c_ln2g, c_ln2b, c_b1, c_b2,
    rl_s, ex_s, exq_s, rlx_s, exx_s, attx, dqkvx, a_g1, a_b1, a_g2, a_b2, tgt_t, stage, gin_sem,
):
    images, seq = dup.shape
    d = tok.shape[1]
    t = seq - 1
    x0 = images * t
    ff = w1.shape[1]
    w = x0 + 128
    dqkv = act.at[: 3 * d]

    blocks = d // 128

    def load_image(i):
        return jnp.concatenate([stage[b, pl.ds(i, t, stride=images), :] for b in range(blocks)], 1)

    def store_image(i, values):
        for b in range(blocks):
            stage[b, pl.ds(i, t, stride=images), :] = values[:, 128 * b : 128 * (b + 1)]

    def store_last(values):
        for b in range(blocks):
            stage[b, x0:, :] = values[:images, 128 * b : 128 * (b + 1)]

    def lanes_of(i):
        return pl.ds(pl.multiple_of(i * t, 128), t)

    extra_lanes = pl.ds(x0, 128)

    wqkv_t[...] = wqkv[...].T
    wout_t[...] = wout[...].T
    w1_t[...] = w1[...].T
    w2_t[...] = w2[...].T
    c_ln1g[...] = to_columns(vec, LN1G, d)
    c_ln1b[...] = to_columns(vec, LN1B, d)
    c_bqkv[...] = to_columns(vec, BQKV, 3 * d)
    c_bout[...] = to_columns(vec, BOUT, d)
    c_ln2g[...] = to_columns(vec, LN2G, d)
    c_ln2b[...] = to_columns(vec, LN2B, d)
    c_b1[...] = to_columns(vec, BFC1, ff)
    c_b2[...] = to_columns(vec, BFC2, d)
    tgt_t[...] = jnp.concatenate([tgt[...], jnp.zeros((128 - images, d), F32)], 0).T
    ones_row = jnp.where(lax.broadcasted_iota(jnp.int32, (16, w), 0) == 0, 1.0, 0.0).astype(BF16)
    n1[d : d + 16, :] = ones_row
    n2[d : d + 16, :] = ones_row
    att[d : d + 16, :] = ones_row
    act[ff : ff + 16, :] = ones_row
    attx[...] = jnp.zeros_like(attx)
    dqkvx[...] = jnp.zeros_like(dqkvx)
    for acc in (a_g1, a_b1, a_g2, a_b2):
        acc[...] = jnp.zeros_like(acc)

    def project(x_t, lanes, count):
        x = x_t.astype(F32)
        xs[:, lanes] = x_t
        u, r = normalise(x)
        n = (u * wide(c_ln1g[...], count) + wide(c_ln1b[...], count)).astype(BF16)
        n1[:d, lanes] = n
        for k in range(3):
            rows = slice(k * d, (k + 1) * d)
            y = mm(wqkv_t[rows, :], n) + wide(c_bqkv[rows, :], count)
            y = y.astype(BF16)
            if k == 0:
                y = y * jnp.asarray(HD**-0.5, BF16)
            qkv[rows, lanes] = y

    def project_image(i, carry):
        project(load_image(i).astype(BF16).T, lanes_of(i), t)
        return carry

    for b in range(blocks):
        stage[b] = tok[:, 128 * b : 128 * (b + 1)].astype(F32)

    lax.fori_loop(0, images, project_image, 0)
    last = jnp.concatenate([tok[x0:, :].astype(F32), jnp.zeros((128 - images, d), F32)], 0)
    project(last.astype(BF16).T, extra_lanes, 128)

    lane_ids = lax.broadcasted_iota(jnp.int32, (HD, 128), 1)

    def pick(ref, row, i):
        block = ref[row : row + HD, extra_lanes].astype(F32)
        return jnp.sum(jnp.where(lane_ids == i, block, 0.0), 1, keepdims=True)

    def attend_image(i, carry):
        lanes = lanes_of(i)
        for h in range(HEADS):
            r0 = h * HD
            q = qkv[r0 : r0 + HD, lanes]
            k = qkv[d + r0 : d + r0 + HD, lanes]
            v = qkv[2 * d + r0 : 2 * d + r0 + HD, lanes]
            qx, kx, vx = pick(qkv, r0, i), pick(qkv, d + r0, i), pick(qkv, 2 * d + r0, i)
            s = mm(k.T, q)
            sx = jnp.sum(q.astype(F32) * kx, 0, keepdims=True)
            top = jnp.maximum(jnp.max(s, 0, keepdims=True), sx)
            e = jnp.exp(s - top)
            ex = jnp.exp(sx - top)
            rl = 1.0 / (jnp.sum(e, 0, keepdims=True) + ex)
            e = e.astype(BF16)
            probs[i * HEADS + h] = e
            o = (mm(v, e) + vx * ex) * rl
            att[r0 : r0 + HD, lanes] = o.astype(BF16)
            rl_s[i, h : h + 1, :] = rl
            ex_s[i, h : h + 1, :] = ex
            sq = jnp.sum(k.astype(F32) * qx, 0, keepdims=True)
            sxx = jnp.sum(kx * qx, 0, keepdims=True)
            topx = jnp.maximum(jnp.max(sq, 1, keepdims=True), sxx)
            eq = jnp.exp(sq - topx)
            exx = jnp.exp(sxx - topx)
            rlx = 1.0 / (jnp.sum(eq, 1, keepdims=True) + exx)
            ox = (jnp.sum(v.astype(F32) * eq, 1, keepdims=True) + vx * exx) * rlx
            attx[r0 : r0 + HD, :] = jnp.where(lane_ids == i, ox, attx[r0 : r0 + HD, :])
            exq_s[i, h : h + 1, :] = eq
            rlx_s[i, h : h + 1, :] = jnp.broadcast_to(rlx, (1, 128))
            exx_s[i, h : h + 1, :] = jnp.broadcast_to(exx, (1, 128))
        return carry

    lax.fori_loop(0, images, attend_image, 0)
    att[:d, extra_lanes] = attx[...].astype(BF16)

    def feed(lanes, count, d_final):
        mid = xs[:, lanes].astype(F32) + mm(wout_t[...], att[:d, lanes]) + wide(c_bout[...], count)
        u, r = normalise(mid)
        n = (u * wide(c_ln2g[...], count) + wide(c_ln2b[...], count)).astype(BF16)
        n2[:d, lanes] = n
        db = d_final.astype(BF16)
        db2[:, lanes] = db
        for j in range(ff // 256):
            rows = slice(256 * j, 256 * (j + 1))
            pre = mm(w1_t[rows, :], n) + wide(c_b1[rows, :], count)
            da = mm(w2[rows, :], db)
            value, slope = gelu_pair(pre)
            act[rows, lanes] = value.astype(BF16)
            dpre[rows, lanes] = (slope * da).astype(BF16)
        final = mid + mm(w2_t[...], act[:ff, lanes]) + wide(c_b2[...], count)
        dn = mm(w1[...], dpre[:, lanes])
        a_g2[...] += fold(dn * u)
        a_b2[...] += fold(dn)
        dm = d_final + norm_back(dn, u, r, wide(c_ln2g[...], count))
        dmid[:, lanes] = dm
        low = dm.astype(BF16)
        db1[:, lanes] = low
        dos[:, lanes] = mm(wout[...], low).astype(BF16)
        return final.T

    def keep_row(row):
        first = lax.broadcasted_iota(jnp.int32, row.shape, 1) == 0
        return jnp.where(first, 1.0, 1.0 - row.astype(F32))

    def feed_image(i, carry):
        keep = keep_row(dup[pl.ds(i, 1), :])
        count = jnp.sum(keep, 1, keepdims=True)
        scale = seq * keep[:, :t] / count
        ids = lax.broadcasted_iota(jnp.int32, (d, 128), 1)
        target = jnp.sum(jnp.where(ids == i, tgt_t[...], 0.0), 1, keepdims=True)
        store_image(i, feed(lanes_of(i), t, target * scale))
        return carry

    lax.fori_loop(0, images, feed_image, 0)
    keep_all = keep_row(dup[...])
    scale_x = seq * keep_all[:, t:] / jnp.sum(keep_all, 1, keepdims=True)
    scale_x = jnp.broadcast_to(scale_x, (images, 128))
    scale_x = jnp.concatenate([scale_x, jnp.zeros((128 - images, 128), F32)], 0).T[:1, :]
    store_last(feed(extra_lanes, 128, tgt_t[...] * scale_x))
    for b in range(blocks):
        out[:, 128 * b : 128 * (b + 1)] = stage[b].astype(BF16)

    for j in range(ff // 256):
        rows = slice(256 * j, 256 * (j + 1))
        g = mm(n2[...], dpre[rows, :], NT)
        g1[:, rows] = g[:d].astype(BF16)
        gvec[BFC1 : BFC1 + 1, rows] = g[d : d + 1]
        g2[rows, :] = mm(act[rows, :], db2[...], NT).astype(BF16)
    g = mm(act[ff : ff + 16, :], db2[...], NT)
    gvec[BFC2 : BFC2 + 1, :d] = g[:1]

    def attend_back(i, carry):
        lanes = lanes_of(i)
        for h in range(HEADS):
            r0 = h * HD
            q = qkv[r0 : r0 + HD, lanes]
            k = qkv[d + r0 : d + r0 + HD, lanes]
            v = qkv[2 * d + r0 : 2 * d + r0 + HD, lanes]
            qx, kx, vx = pick(qkv, r0, i), pick(qkv, d + r0, i), pick(qkv, 2 * d + r0, i)
            rl = rl_s[i, h : h + 1, :]
            ex = ex_s[i, h : h + 1, :]
            do = dos[r0 : r0 + HD, lanes].astype(F32) * rl
            dot_o = jnp.sum(do * att[r0 : r0 + HD, lanes].astype(F32), 0, keepdims=True)
            dol = do.astype(BF16)
            p = probs[i * HEADS + h]
            ds = (p.astype(F32) * (mm(v.T, dol) - dot_o)).astype(BF16)
            dsx = ex * (jnp.sum(do * vx, 0, keepdims=True) - dot_o)
            dq = mm(k, ds) + kx * dsx
            dk = mm(q, ds, NT)
            dv = mm(dol, p, NT)
            qf = q.astype(F32)
            kf = k.astype(F32)
            vf = v.astype(F32)
            dkx = jnp.sum(qf * dsx, 1, keepdims=True)
            dvx = jnp.sum(do * ex, 1, keepdims=True)
            eq = exq_s[i, h : h + 1, :]
            rlx = rlx_s[i, h : h + 1, :1]
            exx = exx_s[i, h : h + 1, :1]
            dox = pick(dos, r0, i) * rlx
            dotx = jnp.sum(dox * pick(att, r0, i), 0, keepdims=True)
            dsq = eq * (jnp.sum(vf * dox, 0, keepdims=True) - dotx)
            dsxx = exx * (jnp.sum(vx * dox, 0, keepdims=True) - dotx)
            dqx = jnp.sum(kf * dsq, 1, keepdims=True) + kx * dsxx
            dk = dk + qx * dsq
            dv = dv + dox * eq
            dkx = dkx + qx * dsxx
            dvx = dvx + dox * exx
            scale = HD**-0.5
            for base, main, tail in ((0, dq * scale, dqx * scale), (d, dk, dkx), (2 * d, dv, dvx)):
                rows = slice(base + r0, base + r0 + HD)
                dqkv[rows, lanes] = main.astype(BF16)
                dqkvx[rows, :] = jnp.where(lane_ids == i, tail, dqkvx[rows, :])
        return carry

    lax.fori_loop(0, images, attend_back, 0)
    dqkv[:, extra_lanes] = dqkvx[...].astype(BF16)

    for k in range(3):
        rows = slice(k * d, (k + 1) * d)
        g = mm(n1[...], dqkv[rows, :], NT)
        gqkv[:, rows] = g[:d].astype(BF16)
        gvec[BQKV : BQKV + 1, rows] = g[d : d + 1]
    g = mm(att[...], db1[...], NT)
    gout[...] = g[:d].astype(BF16)
    gvec[BOUT : BOUT + 1, :d] = g[d : d + 1]

    def finish(lanes, count):
        u, r = normalise(xs[:, lanes].astype(F32))
        dn = mm(wqkv[...], dqkv[:, lanes])
        a_g1[...] += fold(dn * u)
        a_b1[...] += fold(dn)
        return (dmid[:, lanes] + norm_back(dn, u, r, wide(c_ln1g[...], count))).T

    def finish_image(i, carry):
        store_image(i, finish(lanes_of(i), t))
        return carry

    lax.fori_loop(0, images, finish_image, 0)
    store_last(finish(extra_lanes, 128))
    copies = [
        pltpu.make_async_copy(stage.at[b], gin.at[:, pl.ds(128 * b, 128)], gin_sem.at[b]) for b in range(blocks)
    ]
    for copy in copies:
        copy.start()

    for row, acc in ((LN1G, a_g1), (LN1B, a_b1), (LN2G, a_g2), (LN2B, a_b2)):
        gvec[row : row + 1, :d] = jnp.sum(acc[...].T, 0, keepdims=True)
    for copy in copies:
        copy.wait()


def compute(tok, dup, tgt, vec, wqkv, wout, w1, w2):
    images, seq = dup.shape
    d = tok.shape[1]
    ff = w1.shape[1]
    t = seq - 1
    w = images * t + 128
    vm = pltpu.VMEM
    scratch = [
        vm((d, w), BF16),
        vm((d + 16, w), BF16),
        vm((3 * d, w), BF16),
        vm((d + 16, w), BF16),
        vm((d + 16, w), BF16),
        vm((ff + 16, w), BF16),
        vm((ff, w), BF16),
        vm((d, w), BF16),
        vm((d, w), BF16),
        vm((d, w), BF16),
        vm((d, w), F32),
        vm((images * HEADS, t, t), BF16),
        vm((3 * d, d), BF16),
        vm((d, d), BF16),
        vm((ff, d), BF16),
        vm((d, ff), BF16),
        vm((d, 128), F32), vm((d, 128), F32), vm((3 * d, 128), F32), vm((d, 128), F32),
        vm((d, 128), F32), vm((d, 128), F32), vm((ff, 128), F32), vm((d, 128), F32),
        vm((images, 8, t), F32),
        vm((images, 8, t), F32),
        vm((images, 8, t), F32),
        vm((images, 8, 128), F32),
        vm((images, 8, 128), F32),
        vm((d, 128), F32),
        vm((3 * d, 128), F32),
        vm((d, 128), F32), vm((d, 128), F32), vm((d, 128), F32), vm((d, 128), F32),
        vm((d, 128), F32),
        vm((d // 128, images * seq, 128), F32),
        pltpu.SemaphoreType.DMA((d // 128,)),
    ]
    outs = (
        jax.ShapeDtypeStruct(tok.shape, BF16),
        jax.ShapeDtypeStruct(tok.shape, F32),
        jax.ShapeDtypeStruct((d, 3 * d), BF16),
        jax.ShapeDtypeStruct((d, d), BF16),
        jax.ShapeDtypeStruct((d, ff), BF16),
        jax.ShapeDtypeStruct((ff, d), BF16),
        jax.ShapeDtypeStruct((8, ff), F32),
    )
    spec = pl.BlockSpec(memory_space=pltpu.VMEM)
    return pl.pallas_call(
        compute_body,
        out_shape=outs,
        in_specs=[spec] * 8,
        out_specs=(spec, pl.BlockSpec(memory_space=pl.ANY)) + (spec,) * 5,
        scratch_shapes=scratch,
        compiler_params=pltpu.CompilerParams(vmem_limit_bytes=64 * 1024 * 1024),
        name="block",
    )(tok, dup, tgt, vec, wqkv, wout, w1, w2)

MESH_ID = pl.DeviceIdType.MESH
NZ = 4


class Place:
    def __init__(self):
        p = lax.axis_index("fsdp")
        self.p = p
        self.c = lax.axis_index("dp")
        self.x = lax.rem(p, 2)
        self.y = lax.rem(lax.div(p, 2), 2)
        self.z = lax.div(p, 4)
        self.a = self.y + self.c * (self.x - self.y)
        self.b = self.x + self.c * (self.y - self.x)

    def device(self, x, y, z):
        return ((z * 2 + y) * 2 + x, self.c)

    def along_a(self):
        c = self.c
        return self.device(self.x + c * (1 - 2 * self.x), self.y + (1 - c) * (1 - 2 * self.y), self.z)

    def along_b(self):
        c = self.c
        return self.device(self.x + (1 - c) * (1 - 2 * self.x), self.y + c * (1 - 2 * self.y), self.z)

    def along_z(self, step):
        return lax.rem(self.z + step, NZ)

    def sibling(self):
        return (self.p, 1 - self.c)


def slot_of(p, group):
    x, y, z = p % 2, (p // 2) % 2, p // 4
    a, b = (y, x) if group == 0 else (x, y)
    return (a * 2 + b) * NZ + z


def greet(at):
    barrier = pltpu.get_barrier_semaphore()
    others = [at.along_a(), at.along_b(), at.sibling()]
    others += [at.device(at.x, at.y, at.along_z(step)) for step in range(1, NZ)]
    for device in others:
        pl.semaphore_signal(barrier, inc=1, device_id=device, device_id_type=MESH_ID)
    pl.semaphore_wait(barrier, len(others))


def remote(src, dst, sems, k, device):
    return pltpu.make_async_remote_copy(
        src_ref=src, dst_ref=dst, send_sem=sems.at[0, k], recv_sem=sems.at[1, k],
        device_id=device, device_id_type=MESH_ID,
    )


def span(start, size):
    return pl.ds(pl.multiple_of(start, size), size)


class Gather:
    def __init__(self, at, buf, r, sems, swap):
        self.at, self.buf, self.r, self.sems, self.shared = at, buf, r, sems, swap

    def part(self, rows, k, device):
        piece = self.buf.at[rows]
        return remote(piece, piece, self.sems, k, device)

    def line(self):
        at, r = self.at, self.r
        rows = span(((at.a * 2 + at.b) * NZ + at.z) * r, r)
        return [
            self.part(rows, step - 1, at.device(at.x, at.y, at.along_z(step))) for step in range(1, NZ)
        ]

    def over_b(self):
        at, r = self.at, self.r
        return [self.part(span((at.a * 2 + at.b) * NZ * r, NZ * r), 3, at.along_b())]

    def over_a(self):
        at, r = self.at, self.r
        return [self.part(span(at.a * 2 * NZ * r, 2 * NZ * r), 4, at.along_a())]

    def swap(self):
        return [remote(self.buf, self.buf, self.sems, 5, self.at.sibling())] if self.shared else []

    def go(self, step):
        steps = (self.line, self.over_b, self.over_a, self.swap)
        if step > 0:
            for copy in steps[step - 1]():
                copy.wait()
        if step < 4:
            for copy in steps[step]():
                copy.start()


class Reduce:
    def __init__(self, at, full, got, from_a, from_b, from_z, total, r, sems):
        self.at, self.full, self.got = at, full, got
        self.from_a, self.from_b, self.from_z, self.total = from_a, from_b, from_z, total
        self.r, self.sems = r, sems

    def first(self):
        return [remote(self.full.at[1 - self.at.c], self.got, self.sems, 0, self.at.sibling())]

    def over_a(self):
        at, r = self.at, self.r
        rows = span((1 - at.a) * 2 * NZ * r, 2 * NZ * r)
        return [remote(self.full.at[at.c, rows], self.from_a, self.sems, 1, at.along_a())]

    def over_b(self):
        at, r = self.at, self.r
        rows = span((at.a * 2 + 1 - at.b) * NZ * r, NZ * r)
        return [remote(self.full.at[at.c, rows], self.from_b, self.sems, 2, at.along_b())]

    def line(self):
        at, r = self.at, self.r
        copies = []
        for step in range(1, NZ):
            other = at.along_z(step)
            rows = span(((at.a * 2 + at.b) * NZ + other) * r, r)
            copies.append(
                remote(self.full.at[at.c, rows], self.from_z.at[pl.ds((step - 1) * r, r)], self.sems, 2 + step, at.device(at.x, at.y, other))
            )
        return copies

    def last(self):
        piece = self.total.at[self.at.c]
        return [remote(piece, piece, self.sems, 6, self.at.sibling())]

    def add(self, rows, values):
        ref = self.full.at[self.at.c, rows]
        ref[...] = (ref[...].astype(F32) + values.astype(F32)).astype(ref.dtype)

    def go(self, step):
        at, r = self.at, self.r
        steps = (self.first, self.over_a, self.over_b, self.line, self.last)
        if step > 0:
            for copy in steps[step - 1]():
                copy.wait()
        if step == 1:
            for half in range(2):
                rows = pl.ds(half * 2 * NZ * r, 2 * NZ * r)
                self.add(rows, self.got[rows, :])
        elif step == 2:
            self.add(span(at.a * 2 * NZ * r, 2 * NZ * r), self.from_a[...])
        elif step == 3:
            self.add(span((at.a * 2 + at.b) * NZ * r, NZ * r), self.from_b[...])
        elif step == 4:
            total = self.full[at.c, span(((at.a * 2 + at.b) * NZ + at.z) * r, r), :].astype(F32)
            for k in range(NZ - 1):
                total = total + self.from_z[k * r : (k + 1) * r, :].astype(F32)
            self.total[at.c] = total
        if step < 5:
            for copy in steps[step]():
                copy.start()


V_LN1G, V_LN1B, V_QV, V_BOUT, V_LN2G, V_LN2B, V_BFC2, V_BFC1 = 0, 1, 2, 4, 5, 6, 7, 8


def block_body(
    tok, dup, tgt, s_ln1g, s_ln1b, s_qkv, s_qvb, s_out, s_bout, s_ln2g, s_ln2b, s_fc1, s_b1, s_fc2, s_b2,
    out, gin, oqkv, oout, o1, o2, ovec,
    tokb, stage, xs, n1, qkv, att, n2, act, dpre, db2, db1, dos, dmid, probs,
    wqkv, wout, w1, w2_t, wt_a, wf,
    c_ln1g, c_ln1b, c_bqkv, c_bout, c_ln2g, c_ln2b, c_b1, c_b2,
    stat_s, rl_s, ex_s, exq_s, rlx_s, exx_s, attx, dqkvx, a_g2, a_b2, tgt_t, gvec, allc,
    sv, tv, uv, av, bv, zv, f1, f2, fv,
    loc_sem, gsem1, gsem2, gsemv, rsem1, rsem2, rsemv, ready,
):
    images, seq = dup.shape
    d = tok.shape[1]
    t = seq - 1
    x0 = images * t
    ff = w1.shape[1]
    w = x0 + 128
    shard = d // 16
    blocks = d // 128
    at = Place()

    def lanes_of(i):
        return pl.ds(pl.multiple_of(i * t, 128), t)

    extra_lanes = pl.ds(x0, 128)

    def load_image(i):
        return jnp.concatenate([stage[b, pl.ds(i, t, stride=images), :] for b in range(blocks)], 1)

    def store_image(i, values):
        for b in range(blocks):
            stage[b, pl.ds(i, t, stride=images), :] = values[:, 128 * b : 128 * (b + 1)]

    def store_last(values):
        for b in range(blocks):
            stage[b, x0:, :] = values[:images, 128 * b : 128 * (b + 1)]

    tok_copy = pltpu.make_async_copy(tok, tokb, loc_sem.at[0])
    tok_copy.start()

    own = span(((at.a * 2 + at.b) * NZ + at.z) * 16, 16)
    table = jnp.zeros((16, 128), F32)
    sv[own, :] = table
    base = ((at.a * 2 + at.b) * NZ + at.z) * 16
    flat = [s_ln1g[...], s_ln1b[...], s_qvb[:shard], s_qvb[shard:], s_bout[...], s_ln2g[...], s_ln2b[...], s_b2[...]]
    flat += [s_b1[shard * k : shard * (k + 1)] for k in range(4)]
    for k, line in enumerate(flat):
        sv[pl.ds(base + k, 1), :shard] = line.astype(F32).reshape(1, shard)
    halves = (pl.ds(0, d), pl.ds(d, d))
    mine = pl.ds(pl.multiple_of(at.c * d, 128), d)
    own1 = span(((at.a * 2 + at.b) * NZ + at.z) * 2 * shard, 2 * shard)
    own2 = span(((at.a * 2 + at.b) * NZ + at.z) * 4 * shard, 4 * shard)
    slots1 = act.at[: 16 * 2 * shard]
    slots2 = dpre

    @pl.when(at.c == 0)
    def _():
        q = s_qkv[...].astype(F32)
        f = s_fc1[...].astype(F32)
        slots1[own1, halves[0]] = jnp.concatenate([q[:, :d], q[:, d : 2 * d]], 0).astype(BF16)
        slots2[own2, halves[0]] = jnp.concatenate([f[:, k * d : (k + 1) * d] for k in range(4)], 0).astype(BF16)

    @pl.when(at.c == 1)
    def _():
        q = s_qkv[...].astype(F32)
        slots1[own1, halves[1]] = jnp.concatenate([q[:, 2 * d :], s_out[...].astype(F32)], 0).astype(BF16)
        slots2[own2, halves[1]] = s_fc2[...]

    greet(at)
    gather_v = Gather(at, sv, 16, gsemv, False)
    gather1 = Gather(at, slots1.at[:, mine], 2 * shard, gsem1, True)
    gather2 = Gather(at, slots2.at[:, mine], 4 * shard, gsem2, True)
    gather_v.go(0)
    gather1.go(0)

    tok_copy.wait()
    for b in range(blocks):
        stage[b] = tokb[:, 128 * b : 128 * (b + 1)].astype(F32)

    def statistics(x):
        mu = jnp.mean(x, 0, keepdims=True)
        c = x - mu
        return mu, lax.rsqrt(jnp.mean(c * c, 0, keepdims=True) + EPS)

    def turn(i, carry):
        x = load_image(i).astype(BF16).T
        xs[:, lanes_of(i)] = x
        mu, r = statistics(x.astype(F32))
        stat_s[i, 0:1, :] = mu
        stat_s[i, 1:2, :] = r
        return carry

    gather_v.go(1)
    gather1.go(1)
    gather2.go(0)
    lax.fori_loop(0, images // 2, turn, 0)
    gather_v.go(2)
    gather1.go(2)
    lax.fori_loop(images // 2, images, turn, 0)
    last = jnp.concatenate([tokb[x0:, :].astype(F32), jnp.zeros((128 - images, d), F32)], 0)
    x = last.astype(BF16).T
    xs[:, extra_lanes] = x
    mu, r = statistics(x.astype(F32))
    stat_s[images, 0:1, :128] = mu
    stat_s[images, 1:2, :128] = r
    tgt_t[...] = jnp.concatenate([tgt[...], jnp.zeros((128 - images, d), F32)], 0).T
    ones_row = jnp.where(lax.broadcasted_iota(jnp.int32, (16, w), 0) == 0, 1.0, 0.0).astype(BF16)
    n1[d : d + 16, :] = ones_row
    n2[d : d + 16, :] = ones_row
    att[d : d + 16, :] = ones_row
    attx[...] = jnp.zeros_like(attx)
    dqkvx[...] = jnp.zeros_like(dqkvx)
    a_g2[...] = jnp.zeros_like(a_g2)
    a_b2[...] = jnp.zeros_like(a_b2)
    gather_v.go(3)
    gather1.go(3)

    def slot_v(p):
        px, py, pz = p % 2, (p // 2) % 2, p // 4
        pa = py + at.c * (px - py)
        pb = px + at.c * (py - px)
        return sv[span(((pa * 2 + pb) * NZ + pz) * 16, 16), :]

    for half in range(2):
        allc[half] = jnp.concatenate([slot_v(p) for p in range(8 * half, 8 * half + 8)], 0).T

    def column(ref, entries):
        runs = []
        ids = lax.broadcasted_iota(jnp.int32, (shard, 128), 1)
        for p, k in entries:
            runs.append(jnp.where(ids == 16 * (p % 8) + k, allc[p // 8, :shard, :], 0.0))
        block = jnp.sum(jnp.concatenate(runs, 0), 1, keepdims=True)
        ref[...] = jnp.broadcast_to(block, (len(entries) * shard, 128))

    every = range(16)
    column(c_ln1g, [(p, V_LN1G) for p in every])
    column(c_ln1b, [(p, V_LN1B) for p in every])
    column(c_bqkv.at[:d], [(p, V_QV + k) for p in range(8) for k in range(2)])
    c_bqkv[d : 2 * d, :] = jnp.zeros((d, 128), F32)
    column(c_bqkv.at[2 * d :], [(p, V_QV + k) for p in range(8, 16) for k in range(2)])
    column(c_bout, [(p, V_BOUT) for p in every])
    column(c_ln2g, [(p, V_LN2G) for p in every])
    column(c_ln2b, [(p, V_LN2B) for p in every])
    column(c_b2, [(p, V_BFC2) for p in every])
    column(c_b1, [(p, V_BFC1 + k) for p in every for k in range(4)])

    gather1.go(4)
    gather2.go(1)

    def unpack(slots, group, r, k):
        part = slots[:, halves[group]]
        runs = []
        for p in every:
            s = slot_of(p, group)
            runs.append(slots[r * s : r * (s + 1), halves[group]].astype(F32)[k * shard : (k + 1) * shard])
        return jnp.concatenate(runs, 0).astype(BF16)

    for k in range(4):
        block = unpack(slots1, k // 2, 2 * shard, k % 2)
        if k < 3:
            wqkv[:, k * d : (k + 1) * d] = block
        else:
            wout[...] = block
        wt_a[k // 2, (k % 2) * d : (k % 2 + 1) * d, :] = block.T

    def project(lanes, count, mu, r):
        u = (xs[:, lanes].astype(F32) - mu) * r
        n = (u * wide(c_ln1g[...], count) + wide(c_ln1b[...], count)).astype(BF16)
        n1[:d, lanes] = n
        for k in range(3):
            rows = slice(k * d, (k + 1) * d)
            y = mm(wt_a[k // 2, (k % 2) * d : (k % 2 + 1) * d, :], n) + wide(c_bqkv[rows, :], count)
            y = y.astype(BF16)
            if k == 0:
                y = y * jnp.asarray(HD**-0.5, BF16)
            qkv[rows, lanes] = y

    def project_image(i, carry):
        project(lanes_of(i), t, stat_s[i, 0:1, :], stat_s[i, 1:2, :])
        return carry

    lax.fori_loop(0, images, project_image, 0)
    project(extra_lanes, 128, stat_s[images, 0:1, :128], stat_s[images, 1:2, :128])
    gather2.go(2)

    lane_ids = lax.broadcasted_iota(jnp.int32, (HD, 128), 1)

    def pick(ref, row, i):
        block = ref[row : row + HD, extra_lanes].astype(F32)
        return jnp.sum(jnp.where(lane_ids == i, block, 0.0), 1, keepdims=True)

    def attend_image(i, carry):
        lanes = lanes_of(i)
        for h in range(HEADS):
            r0 = h * HD
            q = qkv[r0 : r0 + HD, lanes]
            k = qkv[d + r0 : d + r0 + HD, lanes]
            v = qkv[2 * d + r0 : 2 * d + r0 + HD, lanes]
            qx, kx, vx = pick(qkv, r0, i), pick(qkv, d + r0, i), pick(qkv, 2 * d + r0, i)
            s = mm(k.T, q)
            sx = jnp.sum(q.astype(F32) * kx, 0, keepdims=True)
            top = jnp.maximum(jnp.max(s, 0, keepdims=True), sx)
            e = jnp.exp(s - top)
            ex = jnp.exp(sx - top)
            rl = 1.0 / (jnp.sum(e, 0, keepdims=True) + ex)
            e = e.astype(BF16)
            probs[i * HEADS + h] = e
            o = (mm(v, e) + vx * ex) * rl
            att[r0 : r0 + HD, lanes] = o.astype(BF16)
            rl_s[i, h : h + 1, :] = rl
            ex_s[i, h : h + 1, :] = ex
            sq = jnp.sum(k.astype(F32) * qx, 0, keepdims=True)
            sxx = jnp.sum(kx * qx, 0, keepdims=True)
            topx = jnp.maximum(jnp.max(sq, 1, keepdims=True), sxx)
            eq = jnp.exp(sq - topx)
            exx = jnp.exp(sxx - topx)
            rlx = 1.0 / (jnp.sum(eq, 1, keepdims=True) + exx)
            ox = (jnp.sum(v.astype(F32) * eq, 1, keepdims=True) + vx * exx) * rlx
            attx[r0 : r0 + HD, :] = jnp.where(lane_ids == i, ox, attx[r0 : r0 + HD, :])
            exq_s[i, h : h + 1, :] = eq
            rlx_s[i, h : h + 1, :] = jnp.broadcast_to(rlx, (1, 128))
            exx_s[i, h : h + 1, :] = jnp.broadcast_to(exx, (1, 128))

        @pl.when(i == images // 2)
        def _():
            gather2.go(3)

        return carry

    lax.fori_loop(0, images, attend_image, 0)
    att[:d, extra_lanes] = attx[...].astype(BF16)
    gather2.go(4)
    for k in range(4):
        block = unpack(slots2, 0, 4 * shard, k)
        w1[:, k * d : (k + 1) * d] = block
        wf[0, k * d : (k + 1) * d, :] = block.T
    for p in every:
        s = slot_of(p, 1)
        wf[1, 4 * shard * p : 4 * shard * (p + 1), :] = slots2[4 * shard * s : 4 * shard * (s + 1), halves[1]]
    w2_t[...] = wf[1].T
    act[ff : ff + 16, :] = ones_row

    def feed(lanes, count, d_final):
        mid = xs[:, lanes].astype(F32) + mm(wt_a[1, d:, :], att[:d, lanes]) + wide(c_bout[...], count)
        u, r = normalise(mid)
        n = (u * wide(c_ln2g[...], count) + wide(c_ln2b[...], count)).astype(BF16)
        n2[:d, lanes] = n
        db = d_final.astype(BF16)
        db2[:, lanes] = db
        for j in range(ff // 256):
            rows = slice(256 * j, 256 * (j + 1))
            pre = mm(wf[0, rows, :], n) + wide(c_b1[rows, :], count)
            da = mm(wf[1, rows, :], db)
            value, slope = gelu_pair(pre)
            act[rows, lanes] = value.astype(BF16)
            dpre[rows, lanes] = (slope * da).astype(BF16)
        final = mid + mm(w2_t[...], act[:ff, lanes]) + wide(c_b2[...], count)
        dn = mm(w1[...], dpre[:, lanes])
        a_g2[...] += fold(dn * u)
        a_b2[...] += fold(dn)
        dm = d_final + norm_back(dn, u, r, wide(c_ln2g[...], count))
        dmid[:, lanes] = dm
        low = dm.astype(BF16)
        db1[:, lanes] = low
        dos[:, lanes] = mm(wout[...], low).astype(BF16)
        return final.T

    def keep_row(row):
        first = lax.broadcasted_iota(jnp.int32, row.shape, 1) == 0
        return jnp.where(first, 1.0, 1.0 - row.astype(F32))

    def feed_image(i, carry):
        keep = keep_row(dup[pl.ds(i, 1), :])
        count = jnp.sum(keep, 1, keepdims=True)
        scale = seq * keep[:, :t] / count
        ids = lax.broadcasted_iota(jnp.int32, (d, 128), 1)
        target = jnp.sum(jnp.where(ids == i, tgt_t[...], 0.0), 1, keepdims=True)
        store_image(i, feed(lanes_of(i), t, target * scale))
        return carry

    lax.fori_loop(0, images, feed_image, 0)
    keep_all = keep_row(dup[...])
    scale_x = seq * keep_all[:, t:] / jnp.sum(keep_all, 1, keepdims=True)
    scale_x = jnp.broadcast_to(scale_x, (images, 128))
    scale_x = jnp.concatenate([scale_x, jnp.zeros((128 - images, 128), F32)], 0).T[:1, :]
    store_last(feed(extra_lanes, 128, tgt_t[...] * scale_x))
    for b in range(blocks):
        tokb[:, 128 * b : 128 * (b + 1)] = stage[b].astype(BF16)
    out_copy = pltpu.make_async_copy(tokb, out, loc_sem.at[0])
    out_copy.start()

    for j in range(2):
        rows = slice(2 * d * j, 2 * d * (j + 1))
        g = mm(n2[...], dpre[rows, :], NT)
        gvec[BFC1 : BFC1 + 1, rows] = g[d : d + 1]
        for k in range(2):
            part = g[:d, d * k : d * (k + 1)].astype(BF16)
            for p in every:
                start = 4 * shard * slot_of(p, 0) + shard * (2 * j + k)
                wf[0, start : start + shard, :] = part[shard * p : shard * (p + 1)]
    for j in range(ff // 256):
        rows = slice(256 * j, 256 * (j + 1))
        g = mm(act[rows, :], db2[...], NT).astype(BF16)
        step = 4 * shard
        lo = 256 * j
        while lo < 256 * (j + 1):
            p = lo // step
            hi = min(256 * (j + 1), (p + 1) * step)
            start = step * slot_of(p, 1) + lo - p * step
            wf[1, start : start + hi - lo, :] = g[lo - 256 * j : hi - 256 * j]
            lo = hi
    g = mm(act[ff : ff + 16, :], db2[...], NT)
    gvec[BFC2 : BFC2 + 1, :d] = g[:1]

    partners = [at.sibling(), at.along_a(), at.along_b()]
    partners += [at.device(at.x, at.y, at.along_z(step)) for step in range(1, NZ)]
    for k, device in enumerate(partners):
        pl.semaphore_signal(ready.at[min(k, 3)], inc=1, device_id=device, device_id_type=MESH_ID)

    def area(row, count, column):
        return dpre.at[row : row + count, d * column : d * (column + 1)]

    r2, r1 = 4 * shard, 2 * shard
    reduce2 = Reduce(
        at, wf, area(0, 16 * r2, 0), area(0, 8 * r2, 1), area(8 * r2, 4 * r2, 1), area(12 * r2, 3 * r2, 1), f2, r2, rsem2
    )
    reduce1 = Reduce(
        at, wt_a, area(0, 16 * r1, 2), area(16 * r1, 8 * r1, 2), area(24 * r1, 4 * r1, 2), area(28 * r1, 3 * r1, 2), f1, r1, rsem1
    )
    pl.semaphore_wait(ready.at[0], 1)
    reduce2.go(0)

    def attend_back(i, carry):
        lanes = lanes_of(i)
        for h in range(HEADS):
            r0 = h * HD
            q = qkv[r0 : r0 + HD, lanes]
            k = qkv[d + r0 : d + r0 + HD, lanes]
            v = qkv[2 * d + r0 : 2 * d + r0 + HD, lanes]
            qx, kx, vx = pick(qkv, r0, i), pick(qkv, d + r0, i), pick(qkv, 2 * d + r0, i)
            rl = rl_s[i, h : h + 1, :]
            ex = ex_s[i, h : h + 1, :]
            do = dos[r0 : r0 + HD, lanes].astype(F32) * rl
            dot_o = jnp.sum(do * att[r0 : r0 + HD, lanes].astype(F32), 0, keepdims=True)
            dol = do.astype(BF16)
            p = probs[i * HEADS + h]
            ds = (p.astype(F32) * (mm(v.T, dol) - dot_o)).astype(BF16)
            dsx = ex * (jnp.sum(do * vx, 0, keepdims=True) - dot_o)
            dq = mm(k, ds) + kx * dsx
            dk = mm(q, ds, NT)
            dv = mm(dol, p, NT)
            qf = q.astype(F32)
            kf = k.astype(F32)
            vf = v.astype(F32)
            dkx = jnp.sum(qf * dsx, 1, keepdims=True)
            dvx = jnp.sum(do * ex, 1, keepdims=True)
            eq = exq_s[i, h : h + 1, :]
            rlx = rlx_s[i, h : h + 1, :1]
            exx = exx_s[i, h : h + 1, :1]
            dox = pick(dos, r0, i) * rlx
            dotx = jnp.sum(dox * pick(att, r0, i), 0, keepdims=True)
            dsq = eq * (jnp.sum(vf * dox, 0, keepdims=True) - dotx)
            dsxx = exx * (jnp.sum(vx * dox, 0, keepdims=True) - dotx)
            dqx = jnp.sum(kf * dsq, 1, keepdims=True) + kx * dsxx
            dk = dk + qx * dsq
            dv = dv + dox * eq
            dkx = dkx + qx * dsxx
            dvx = dvx + dox * exx
            scale = HD**-0.5
            for base, main, tail in ((0, dq * scale, dqx * scale), (d, dk, dkx), (2 * d, dv, dvx)):
                rows = slice(base + r0, base + r0 + HD)
                qkv[rows, lanes] = main.astype(BF16)
                dqkvx[rows, :] = jnp.where(lane_ids == i, tail, dqkvx[rows, :])

        for step, when in ((1, 1), (2, 3), (3, 5), (4, 7)):

            @pl.when(i == when)
            def _(step=step):
                if step < 4:
                    pl.semaphore_wait(ready.at[step], 1 if step < 3 else NZ - 1)
                reduce2.go(step)

        return carry

    lax.fori_loop(0, images, attend_back, 0)
    qkv[:, extra_lanes] = dqkvx[...].astype(BF16)

    scale1 = jnp.zeros((d, 128), F32)
    shift1 = jnp.zeros((d, 128), F32)
    gain1, bias1 = c_ln1g[:, :1], c_ln1b[:, :1]

    def put(group, k, part):
        part = part.astype(BF16)
        for p in every:
            start = 2 * shard * slot_of(p, group) + shard * k
            wt_a[group, start : start + shard, :] = part[shard * p : shard * (p + 1)]

    for k in range(3):
        rows = slice(k * d, (k + 1) * d)
        g = mm(n1[...], qkv[rows, :], NT)
        sums = g[d : d + 1]
        gvec[BQKV : BQKV + 1, rows] = sums
        weight = wqkv[:, rows].astype(F32)
        scale1 = scale1 + fold(weight * (g[:d] - bias1 * sums))
        shift1 = shift1 + fold(weight * sums)
        put(k // 2, k % 2, g[:d])
    g = mm(att[...], db1[...], NT)
    put(1, 1, g[:d])
    gvec[BOUT : BOUT + 1, :d] = g[d : d + 1]
    scale1 = scale1 * (1.0 / c_ln1g[...])
    for row, acc in ((LN1G, scale1), (LN1B, shift1), (LN2G, a_g2[...]), (LN2B, a_b2[...])):
        gvec[row : row + 1, :d] = jnp.sum(acc.T, 0, keepdims=True)
    tv[...] = jnp.zeros_like(tv)
    for p in every:
        s0 = 8 * slot_of(p, 0)
        tv[0, s0 : s0 + 8, :shard] = gvec[:, shard * p : shard * (p + 1)]
        s1 = 8 * slot_of(p, 1)
        lo = 2 * shard * p if p < 8 else 2 * d + 2 * shard * (p - 8)
        parts = [gvec[BQKV : BQKV + 1, lo + shard * k : lo + shard * (k + 1)] for k in range(2)]
        lo = 4 * shard * p
        parts += [gvec[BFC1 : BFC1 + 1, lo + shard * k : lo + shard * (k + 1)] for k in range(4)]
        tv[1, s1 : s1 + 6, :shard] = jnp.concatenate(parts, 0)

    reduce_v = Reduce(at, tv, uv, av, bv, zv, fv, 8, rsemv)
    reduce1.go(0)
    reduce_v.go(0)
    reduce2.go(5)

    def finish(lanes, count, mu, r):
        u = (xs[:, lanes].astype(F32) - mu) * r
        dn = mm(wqkv[...], qkv[:, lanes])
        return (dmid[:, lanes] + norm_back(dn, u, r, wide(c_ln1g[...], count))).T

    def finish_image(i, carry):
        store_image(i, finish(lanes_of(i), t, stat_s[i, 0:1, :], stat_s[i, 1:2, :]))
        for step, when in ((1, 2), (2, 6)):

            @pl.when(i == when)
            def _(step=step):
                reduce_v.go(step)
                reduce1.go(step)

        return carry

    lax.fori_loop(0, images, finish_image, 0)
    store_last(finish(extra_lanes, 128, stat_s[images, 0:1, :128], stat_s[images, 1:2, :128]))
    copies = [
        pltpu.make_async_copy(stage.at[b], gin.at[:, pl.ds(128 * b, 128)], loc_sem.at[1 + b]) for b in range(blocks)
    ]
    for copy in copies:
        copy.start()
    o1[...] = jnp.concatenate([f2[0, shard * k : shard * (k + 1)] for k in range(4)], 1)
    o2[...] = f2[1]
    for step in (3, 4, 5):
        reduce_v.go(step)
        reduce1.go(step)
    oqkv[:, :d] = f1[0, :shard]
    oqkv[:, d : 2 * d] = f1[0, shard:]
    oqkv[:, 2 * d :] = f1[1, :shard]
    oout[...] = f1[1, shard:]
    ovec[...] = fv[...]
    for copy in copies:
        copy.wait()
    out_copy.wait()


def block_call(tok, dup, tgt, weights):
    images, seq = dup.shape
    d = tok.shape[1]
    n = d // 16
    ff = 4 * d
    t = seq - 1
    w = images * t + 128
    vm = pltpu.VMEM
    dma = pltpu.SemaphoreType.DMA
    sd = jax.ShapeDtypeStruct
    scratch = [
        vm((seq * images, d), BF16),
        vm((d // 128, seq * images, 128), F32),
        vm((d, w), BF16),
        vm((d + 16, w), BF16),
        vm((3 * d, w), BF16),
        vm((d + 16, w), BF16),
        vm((d + 16, w), BF16),
        vm((ff + 16, w), BF16),
        vm((ff, w), BF16),
        vm((d, w), BF16),
        vm((d, w), BF16),
        vm((d, w), BF16),
        vm((d, w), F32),
        vm((images * HEADS, t, t), BF16),
        vm((d, 3 * d), BF16),
        vm((d, d), BF16),
        vm((d, ff), BF16),
        vm((d, ff), BF16),
        vm((2, 2 * d, d), BF16),
        vm((2, ff, d), BF16),
        vm((d, 128), F32), vm((d, 128), F32), vm((3 * d, 128), F32), vm((d, 128), F32),
        vm((d, 128), F32), vm((d, 128), F32), vm((ff, 128), F32), vm((d, 128), F32),
        vm((images + 1, 8, t), F32),
        vm((images, 8, t), F32),
        vm((images, 8, t), F32),
        vm((images, 8, t), F32),
        vm((images, 8, 128), F32),
        vm((images, 8, 128), F32),
        vm((d, 128), F32),
        vm((3 * d, 128), F32),
        vm((d, 128), F32), vm((d, 128), F32),
        vm((d, 128), F32),
        vm((8, ff), F32),
        vm((2, 128, 128), F32),
        vm((256, 128), F32),
        vm((2, 128, 128), F32),
    ]
    for slots in (16, 8, 4):
        scratch += [vm((slots * 8, 128), F32)]
    scratch += [vm((24, 128), F32)]
    scratch += [vm((2, 2 * n, d), F32), vm((2, 4 * n, d), F32), vm((2, 8, 128), F32)]
    scratch += [dma((4,))] + [dma((2, 7))] * 6 + [pltpu.SemaphoreType.REGULAR((4,))]
    spec = pl.BlockSpec(memory_space=pltpu.VMEM)
    any_spec = pl.BlockSpec(memory_space=pl.ANY)
    return pl.pallas_call(
        block_body,
        out_shape=(
            sd(tok.shape, BF16), sd(tok.shape, F32),
            sd((n, 3 * d), F32), sd((n, d), F32), sd((n, ff), F32), sd((4 * n, d), F32), sd((2, 8, 128), F32),
        ),
        in_specs=[any_spec] + [spec] * 14,
        out_specs=(any_spec, any_spec) + (spec,) * 5,
        scratch_shapes=scratch,
        compiler_params=pltpu.CompilerParams(
            collective_id=0, has_side_effects=True, vmem_limit_bytes=64 * 1024 * 1024
        ),
        name="block16",
    )(tok, dup, tgt, *weights)


def deliver_body(out, gin, gqkv, gout, g1, g2, gv, *refs):
    o_out, o_gin, o_ln1g, o_ln1b, o_qkv, o_qvb, o_w, o_bout, o_ln2g, o_ln2b, o_fc1, o_b1, o_fc2, o_b2 = refs[:14]
    buf_out, buf_gin, sems = refs[14:]
    n = gqkv.shape[0]
    pieces = []
    for k, (src, buf, dst) in enumerate(((out, buf_out, o_out), (gin, buf_gin, o_gin))):
        count = 1 + 3 * k
        size = (src.shape[0] // count) // 16 * 16
        for m in range(count):
            rows = pl.ds(m * size, size if m < count - 1 else src.shape[0] - m * size)
            s = k + m
            pieces.append((
                pltpu.make_async_copy(src.at[rows], buf.at[rows], sems.at[0, s]),
                pltpu.make_async_copy(buf.at[rows], dst.at[rows], sems.at[1, s]),
            ))
    for load, store in pieces:
        load.start()
    o_qkv[...] = gqkv[...]
    o_w[...] = gout[...]
    o_fc1[...] = g1[...]
    o_fc2[...] = g2[...]
    for ref, row in ((o_ln1g, LN1G), (o_ln1b, LN1B), (o_bout, BOUT), (o_ln2g, LN2G), (o_ln2b, LN2B), (o_b2, BFC2)):
        ref[...] = gv[0, row, :n]
    o_qvb[...] = jnp.concatenate([gv[1, k, :n] for k in range(2)], 0)
    o_b1[...] = jnp.concatenate([gv[1, 2 + k, :n] for k in range(4)], 0)
    for load, store in pieces:
        load.wait()
        store.start()
    for load, store in pieces:
        store.wait()


def deliver_call(out, gin, gqkv, gout, g1, g2, gv):
    n, d = gout.shape
    sd = jax.ShapeDtypeStruct
    spec = pl.BlockSpec(memory_space=pltpu.VMEM)
    any_spec = pl.BlockSpec(memory_space=pl.ANY)
    vec = sd((n,), F32)
    return pl.pallas_call(
        deliver_body,
        out_shape=(
            sd(out.shape, BF16), sd(gin.shape, F32), vec, vec, sd((n, 3 * d), F32), sd((2 * n,), F32),
            sd((n, d), F32), vec, vec, vec, sd((n, 4 * d), F32), sd((4 * n,), F32), sd((4 * n, d), F32), vec,
        ),
        in_specs=[any_spec, any_spec] + [spec] * 5,
        out_specs=(any_spec, any_spec) + (spec,) * 12,
        scratch_shapes=[
            pltpu.VMEM(out.shape, BF16), pltpu.VMEM(gin.shape, F32), pltpu.SemaphoreType.DMA((2, 6)),
        ],
        compiler_params=pltpu.CompilerParams(vmem_limit_bytes=24 * 1024 * 1024),
        name="deliver",
    )(out, gin, gqkv, gout, g1, g2, gv)


def gather_all(value):
    return lax.all_gather(value, "fsdp", axis=0, tiled=True)


def vectors(full):
    ln1_gain, ln1_bias, qv_bias, out_bias, ln2_gain, ln2_bias, fc1_bias, fc2_bias = full
    d = ln1_gain.shape[0]
    bias = jnp.concatenate([qv_bias[:d], jnp.zeros((d,), qv_bias.dtype), qv_bias[d:]])
    rows = (ln1_gain, ln1_bias, bias, out_bias, ln2_gain, ln2_bias, fc1_bias, fc2_bias)
    width = fc1_bias.shape[0]
    return jnp.stack([jnp.pad(row.astype(F32), (0, width - row.shape[0])) for row in rows], 0)


def per_device(tokens, duplicate, targets, *weights, block16):
    images, seq, d = tokens.shape
    rows = tokens.transpose(1, 0, 2).reshape(seq * images, d)
    back = lambda v: v.reshape(seq, images, d).transpose(1, 0, 2)
    if block16:
        results = deliver_call(*block_call(rows, duplicate, targets, weights))
        return (back(results[0]), back(results[1])) + tuple(results[2:])

    (
        ln1_gain, ln1_bias, qkv_weight, qv_bias, out_weight, out_bias,
        ln2_gain, ln2_bias, fc1_weight, fc1_bias, fc2_weight, fc2_bias,
    ) = weights
    small = (ln1_gain, ln1_bias, qv_bias, out_bias, ln2_gain, ln2_bias, fc1_bias, fc2_bias)
    wqkv, wout, w1, w2 = map(gather_all, (qkv_weight, out_weight, fc1_weight, fc2_weight))
    vec = vectors(tuple(map(gather_all, small)))
    out, gin, gqkv, gout, g1, g2, gvec = compute(rows, duplicate, targets, vec, wqkv, wout, w1, w2)

    def scatter(value):
        value = lax.psum_scatter(value.astype(F32), "fsdp", scatter_dimension=0, tiled=True)
        return lax.psum(value, "dp")

    gqkv, gout, g1, g2 = map(scatter, (gqkv, gout, g1, g2))
    gvec = lax.psum(gvec, ("fsdp", "dp"))
    p = lax.axis_index("fsdp")

    def shard(value, whole_size):
        count = whole_size // lax.axis_size("fsdp")
        return lax.dynamic_slice(value, (p * count,), (count,))

    qv_grad = jnp.concatenate([gvec[2, :d], gvec[2, 2 * d : 3 * d]])
    return (
        back(out), back(gin),
        shard(gvec[0], d), shard(gvec[1], d), gqkv, shard(qv_grad, 2 * d), gout, shard(gvec[3], d),
        shard(gvec[4], d), shard(gvec[5], d), g1, shard(gvec[6], 4 * d), g2, shard(gvec[7], d),
    )


def solution(mesh):
    block16 = mesh.shape["fsdp"] == 16 and mesh.shape["dp"] == 2
    both = ("fsdp", "dp")
    vector, matrix = P("fsdp"), P("fsdp", None)
    weights = (vector, vector, matrix, vector, matrix, vector, vector, vector, matrix, vector, matrix, vector)
    return jax.shard_map(
        functools.partial(per_device, block16=block16),
        mesh=mesh,
        in_specs=(P(both, None, None), P(both, None), P(both, None)) + weights,
        out_specs=(P(both, None, None), P(both, None, None)) + weights,
        check_vma=False,
    )
```

```python
import functools
import jax
import jax.numpy as jnp
from jax import lax
from jax.experimental import pallas as pl
from jax.experimental.pallas import tpu as pltpu
from jax.sharding import PartitionSpec as P

HEADS = 6
HD = 64
EPS = 1e-06
F32 = jnp.float32
BF16 = jnp.bfloat16

NN = (((1,), (0,)), ((), ()))
NT = (((1,), (1,)), ((), ()))


def mm(a, b, dims=NN):
    return lax.dot_general(a, b, dims, preferred_element_type=F32)


def normalise(v):
    mu = jnp.mean(v, 0, keepdims=True)
    c = v - mu
    r = lax.rsqrt(jnp.mean(c * c, 0, keepdims=True) + EPS)
    return c * r, r


def norm_back(dn, u, r, gain):
    e = dn * gain
    me = jnp.mean(e, 0, keepdims=True)
    meu = jnp.mean(e * u, 0, keepdims=True)
    return r * (e - me - u * meu)


def fold(v):
    lanes = v.shape[1]
    total = v[:, :128]
    for k in range(1, lanes // 128):
        total = total + v[:, 128 * k : 128 * (k + 1)]
    return total


def wide(col, lanes):
    if lanes == 128:
        return col
    return jnp.concatenate([col] * (lanes // 128), 1)


def gelu_pair(x):
    z = x * 0.7071067811865476
    bell = jnp.exp(-(z * z))
    tail = lax.erf(z)
    half = 0.5 * x
    return half + half * tail, 0.5 + (0.5 * tail + (x * 0.3989422804014327) * bell)


LN1G, LN1B, BQKV, BOUT, LN2G, LN2B, BFC1, BFC2 = range(8)


def to_columns(vec, row, count):
    return jnp.broadcast_to(vec[row : row + 1, :count], (128, count)).T


def compute_body(
    tok, dup, tgt, vec, wqkv, wout, w1, w2,
    out, gin, gqkv, gout, g1, g2, gvec,
    xs, n1, qkv, att, n2, act, dpre, db2, db1, dos, dmid, probs,
    wqkv_t, wout_t, w1_t, w2_t,
    c_ln1g, c_ln1b, c_bqkv, c_bout, c_ln2g, c_ln2b, c_b1, c_b2,
    rl_s, ex_s, exq_s, rlx_s, exx_s, attx, dqkvx, a_g1, a_b1, a_g2, a_b2, tgt_t, stage, gin_sem,
):
    images, seq = dup.shape
    d = tok.shape[1]
    t = seq - 1
    x0 = images * t
    ff = w1.shape[1]
    w = x0 + 128
    dqkv = act.at[: 3 * d]

    blocks = d // 128

    def load_image(i):
        return jnp.concatenate([stage[b, pl.ds(i, t, stride=images), :] for b in range(blocks)], 1)

    def store_image(i, values):
        for b in range(blocks):
            stage[b, pl.ds(i, t, stride=images), :] = values[:, 128 * b : 128 * (b + 1)]

    def store_last(values):
        for b in range(blocks):
            stage[b, x0:, :] = values[:images, 128 * b : 128 * (b + 1)]

    def lanes_of(i):
        return pl.ds(pl.multiple_of(i * t, 128), t)

    extra_lanes = pl.ds(x0, 128)

    tok_copy = pltpu.make_async_copy(tok, out, gin_sem.at[0])
    tok_copy.start()
    tok_copy.wait()
    wqkv_t[...] = wqkv[...].T
    wout_t[...] = wout[...].T
    w1_t[...] = w1[...].T
    w2_t[...] = w2[...].T
    c_ln1g[...] = to_columns(vec, LN1G, d)
    c_ln1b[...] = to_columns(vec, LN1B, d)
    c_bqkv[...] = to_columns(vec, BQKV, 3 * d)
    c_bout[...] = to_columns(vec, BOUT, d)
    c_ln2g[...] = to_columns(vec, LN2G, d)
    c_ln2b[...] = to_columns(vec, LN2B, d)
    c_b1[...] = to_columns(vec, BFC1, ff)
    c_b2[...] = to_columns(vec, BFC2, d)
    tgt_t[...] = jnp.concatenate([tgt[...], jnp.zeros((128 - images, d), F32)], 0).T
    ones_row = jnp.where(lax.broadcasted_iota(jnp.int32, (16, w), 0) == 0, 1.0, 0.0).astype(BF16)
    n1[d : d + 16, :] = ones_row
    n2[d : d + 16, :] = ones_row
    att[d : d + 16, :] = ones_row
    act[ff : ff + 16, :] = ones_row
    attx[...] = jnp.zeros_like(attx)
    dqkvx[...] = jnp.zeros_like(dqkvx)
    for acc in (a_g1, a_b1, a_g2, a_b2):
        acc[...] = jnp.zeros_like(acc)

    def project(x_t, lanes, count):
        x = x_t.astype(F32)
        xs[:, lanes] = x_t
        u, r = normalise(x)
        n = (u * wide(c_ln1g[...], count) + wide(c_ln1b[...], count)).astype(BF16)
        n1[:d, lanes] = n
        for k in range(3):
            rows = slice(k * d, (k + 1) * d)
            y = mm(wqkv_t[rows, :], n) + wide(c_bqkv[rows, :], count)
            y = y.astype(BF16)
            if k == 0:
                y = y * jnp.asarray(HD**-0.5, BF16)
            qkv[rows, lanes] = y

    def project_image(i, carry):
        project(load_image(i).astype(BF16).T, lanes_of(i), t)
        return carry

    for b in range(blocks):
        stage[b] = out[:, 128 * b : 128 * (b + 1)].astype(F32)

    lax.fori_loop(0, images, project_image, 0)
    last = jnp.concatenate([out[x0:, :].astype(F32), jnp.zeros((128 - images, d), F32)], 0)
    project(last.astype(BF16).T, extra_lanes, 128)

    lane_ids = lax.broadcasted_iota(jnp.int32, (HD, 128), 1)

    def pick(ref, row, i):
        block = ref[row : row + HD, extra_lanes].astype(F32)
        return jnp.sum(jnp.where(lane_ids == i, block, 0.0), 1, keepdims=True)

    def attend_image(i, carry):
        lanes = lanes_of(i)
        for h in range(HEADS):
            r0 = h * HD
            q = qkv[r0 : r0 + HD, lanes]
            k = qkv[d + r0 : d + r0 + HD, lanes]
            v = qkv[2 * d + r0 : 2 * d + r0 + HD, lanes]
            qx, kx, vx = pick(qkv, r0, i), pick(qkv, d + r0, i), pick(qkv, 2 * d + r0, i)
            s = mm(k.T, q)
            sx = jnp.sum(q.astype(F32) * kx, 0, keepdims=True)
            top = jnp.maximum(jnp.max(s, 0, keepdims=True), sx)
            e = jnp.exp(s - top)
            ex = jnp.exp(sx - top)
            rl = 1.0 / (jnp.sum(e, 0, keepdims=True) + ex)
            e = e.astype(BF16)
            probs[i * HEADS + h] = e
            o = (mm(v, e) + vx * ex) * rl
            att[r0 : r0 + HD, lanes] = o.astype(BF16)
            rl_s[i, h : h + 1, :] = rl
            ex_s[i, h : h + 1, :] = ex
            sq = jnp.sum(k.astype(F32) * qx, 0, keepdims=True)
            sxx = jnp.sum(kx * qx, 0, keepdims=True)
            topx = jnp.maximum(jnp.max(sq, 1, keepdims=True), sxx)
            eq = jnp.exp(sq - topx)
            exx = jnp.exp(sxx - topx)
            rlx = 1.0 / (jnp.sum(eq, 1, keepdims=True) + exx)
            ox = (jnp.sum(v.astype(F32) * eq, 1, keepdims=True) + vx * exx) * rlx
            attx[r0 : r0 + HD, :] = jnp.where(lane_ids == i, ox, attx[r0 : r0 + HD, :])
            exq_s[i, h : h + 1, :] = eq
            rlx_s[i, h : h + 1, :] = jnp.broadcast_to(rlx, (1, 128))
            exx_s[i, h : h + 1, :] = jnp.broadcast_to(exx, (1, 128))
        return carry

    lax.fori_loop(0, images, attend_image, 0)
    att[:d, extra_lanes] = attx[...].astype(BF16)

    def feed(lanes, count, d_final):
        mid = xs[:, lanes].astype(F32) + mm(wout_t[...], att[:d, lanes]) + wide(c_bout[...], count)
        u, r = normalise(mid)
        n = (u * wide(c_ln2g[...], count) + wide(c_ln2b[...], count)).astype(BF16)
        n2[:d, lanes] = n
        db = d_final.astype(BF16)
        db2[:, lanes] = db
        for j in range(ff // 256):
            rows = slice(256 * j, 256 * (j + 1))
            pre = mm(w1_t[rows, :], n) + wide(c_b1[rows, :], count)
            da = mm(w2[rows, :], db)
            value, slope = gelu_pair(pre)
            act[rows, lanes] = value.astype(BF16)
            dpre[rows, lanes] = (slope * da).astype(BF16)
        final = mid + mm(w2_t[...], act[:ff, lanes]) + wide(c_b2[...], count)
        dn = mm(w1[...], dpre[:, lanes])
        a_g2[...] += fold(dn * u)
        a_b2[...] += fold(dn)
        dm = d_final + norm_back(dn, u, r, wide(c_ln2g[...], count))
        dmid[:, lanes] = dm
        low = dm.astype(BF16)
        db1[:, lanes] = low
        dos[:, lanes] = mm(wout[...], low).astype(BF16)
        return final.T

    def keep_row(row):
        first = lax.broadcasted_iota(jnp.int32, row.shape, 1) == 0
        return jnp.where(first, 1.0, 1.0 - row.astype(F32))

    def feed_image(i, carry):
        keep = keep_row(dup[pl.ds(i, 1), :])
        count = jnp.sum(keep, 1, keepdims=True)
        scale = seq * keep[:, :t] / count
        ids = lax.broadcasted_iota(jnp.int32, (d, 128), 1)
        target = jnp.sum(jnp.where(ids == i, tgt_t[...], 0.0), 1, keepdims=True)
        store_image(i, feed(lanes_of(i), t, target * scale))
        return carry

    lax.fori_loop(0, images, feed_image, 0)
    keep_all = keep_row(dup[...])
    scale_x = seq * keep_all[:, t:] / jnp.sum(keep_all, 1, keepdims=True)
    scale_x = jnp.broadcast_to(scale_x, (images, 128))
    scale_x = jnp.concatenate([scale_x, jnp.zeros((128 - images, 128), F32)], 0).T[:1, :]
    store_last(feed(extra_lanes, 128, tgt_t[...] * scale_x))
    for b in range(blocks):
        out[:, 128 * b : 128 * (b + 1)] = stage[b].astype(BF16)

    for j in range(ff // 256):
        rows = slice(256 * j, 256 * (j + 1))
        g = mm(n2[...], dpre[rows, :], NT)
        g1[:, rows] = g[:d].astype(BF16)
        gvec[BFC1 : BFC1 + 1, rows] = g[d : d + 1]
        g2[rows, :] = mm(act[rows, :], db2[...], NT).astype(BF16)
    g = mm(act[ff : ff + 16, :], db2[...], NT)
    gvec[BFC2 : BFC2 + 1, :d] = g[:1]

    def attend_back(i, carry):
        lanes = lanes_of(i)
        for h in range(HEADS):
            r0 = h * HD
            q = qkv[r0 : r0 + HD, lanes]
            k = qkv[d + r0 : d + r0 + HD, lanes]
            v = qkv[2 * d + r0 : 2 * d + r0 + HD, lanes]
            qx, kx, vx = pick(qkv, r0, i), pick(qkv, d + r0, i), pick(qkv, 2 * d + r0, i)
            rl = rl_s[i, h : h + 1, :]
            ex = ex_s[i, h : h + 1, :]
            do = dos[r0 : r0 + HD, lanes].astype(F32) * rl
            dot_o = jnp.sum(do * att[r0 : r0 + HD, lanes].astype(F32), 0, keepdims=True)
            dol = do.astype(BF16)
            p = probs[i * HEADS + h]
            ds = (p.astype(F32) * (mm(v.T, dol) - dot_o)).astype(BF16)
            dsx = ex * (jnp.sum(do * vx, 0, keepdims=True) - dot_o)
            dq = mm(k, ds) + kx * dsx
            dk = mm(q, ds, NT)
            dv = mm(dol, p, NT)
            qf = q.astype(F32)
            kf = k.astype(F32)
            vf = v.astype(F32)
            dkx = jnp.sum(qf * dsx, 1, keepdims=True)
            dvx = jnp.sum(do * ex, 1, keepdims=True)
            eq = exq_s[i, h : h + 1, :]
            rlx = rlx_s[i, h : h + 1, :1]
            exx = exx_s[i, h : h + 1, :1]
            dox = pick(dos, r0, i) * rlx
            dotx = jnp.sum(dox * pick(att, r0, i), 0, keepdims=True)
            dsq = eq * (jnp.sum(vf * dox, 0, keepdims=True) - dotx)
            dsxx = exx * (jnp.sum(vx * dox, 0, keepdims=True) - dotx)
            dqx = jnp.sum(kf * dsq, 1, keepdims=True) + kx * dsxx
            dk = dk + qx * dsq
            dv = dv + dox * eq
            dkx = dkx + qx * dsxx
            dvx = dvx + dox * exx
            scale = HD**-0.5
            for base, main, tail in ((0, dq * scale, dqx * scale), (d, dk, dkx), (2 * d, dv, dvx)):
                rows = slice(base + r0, base + r0 + HD)
                dqkv[rows, lanes] = main.astype(BF16)
                dqkvx[rows, :] = jnp.where(lane_ids == i, tail, dqkvx[rows, :])
        return carry

    lax.fori_loop(0, images, attend_back, 0)
    dqkv[:, extra_lanes] = dqkvx[...].astype(BF16)

    for k in range(3):
        rows = slice(k * d, (k + 1) * d)
        g = mm(n1[...], dqkv[rows, :], NT)
        gqkv[:, rows] = g[:d].astype(BF16)
        gvec[BQKV : BQKV + 1, rows] = g[d : d + 1]
    g = mm(att[...], db1[...], NT)
    gout[...] = g[:d].astype(BF16)
    gvec[BOUT : BOUT + 1, :d] = g[d : d + 1]

    def finish(lanes, count):
        u, r = normalise(xs[:, lanes].astype(F32))
        dn = mm(wqkv[...], dqkv[:, lanes])
        a_g1[...] += fold(dn * u)
        a_b1[...] += fold(dn)
        return (dmid[:, lanes] + norm_back(dn, u, r, wide(c_ln1g[...], count))).T

    def finish_image(i, carry):
        store_image(i, finish(lanes_of(i), t))
        return carry

    lax.fori_loop(0, images, finish_image, 0)
    store_last(finish(extra_lanes, 128))
    copies = [
        pltpu.make_async_copy(stage.at[b], gin.at[:, pl.ds(128 * b, 128)], gin_sem.at[b]) for b in range(blocks)
    ]
    for copy in copies:
        copy.start()

    for row, acc in ((LN1G, a_g1), (LN1B, a_b1), (LN2G, a_g2), (LN2B, a_b2)):
        gvec[row : row + 1, :d] = jnp.sum(acc[...].T, 0, keepdims=True)
    for copy in copies:
        copy.wait()


def compute(tok, dup, tgt, vec, wqkv, wout, w1, w2):
    images, seq = dup.shape
    d = tok.shape[1]
    ff = w1.shape[1]
    t = seq - 1
    w = images * t + 128
    vm = pltpu.VMEM
    scratch = [
        vm((d, w), BF16),
        vm((d + 16, w), BF16),
        vm((3 * d, w), BF16),
        vm((d + 16, w), BF16),
        vm((d + 16, w), BF16),
        vm((ff + 16, w), BF16),
        vm((ff, w), BF16),
        vm((d, w), BF16),
        vm((d, w), BF16),
        vm((d, w), BF16),
        vm((d, w), F32),
        vm((images * HEADS, t, t), BF16),
        vm((3 * d, d), BF16),
        vm((d, d), BF16),
        vm((ff, d), BF16),
        vm((d, ff), BF16),
        vm((d, 128), F32), vm((d, 128), F32), vm((3 * d, 128), F32), vm((d, 128), F32),
        vm((d, 128), F32), vm((d, 128), F32), vm((ff, 128), F32), vm((d, 128), F32),
        vm((images, 8, t), F32),
        vm((images, 8, t), F32),
        vm((images, 8, t), F32),
        vm((images, 8, 128), F32),
        vm((images, 8, 128), F32),
        vm((d, 128), F32),
        vm((3 * d, 128), F32),
        vm((d, 128), F32), vm((d, 128), F32), vm((d, 128), F32), vm((d, 128), F32),
        vm((d, 128), F32),
        vm((d // 128, images * seq, 128), F32),
        pltpu.SemaphoreType.DMA((d // 128,)),
    ]
    outs = (
        jax.ShapeDtypeStruct(tok.shape, BF16),
        jax.ShapeDtypeStruct(tok.shape, F32),
        jax.ShapeDtypeStruct((d, 3 * d), BF16),
        jax.ShapeDtypeStruct((d, d), BF16),
        jax.ShapeDtypeStruct((d, ff), BF16),
        jax.ShapeDtypeStruct((ff, d), BF16),
        jax.ShapeDtypeStruct((8, ff), F32),
    )
    spec = pl.BlockSpec(memory_space=pltpu.VMEM)
    return pl.pallas_call(
        compute_body,
        out_shape=outs,
        in_specs=[pl.BlockSpec(memory_space=pl.ANY)] + [spec] * 7,
        out_specs=(spec, pl.BlockSpec(memory_space=pl.ANY)) + (spec,) * 5,
        scratch_shapes=scratch,
        compiler_params=pltpu.CompilerParams(vmem_limit_bytes=64 * 1024 * 1024),
        name="block",
    )(tok, dup, tgt, vec, wqkv, wout, w1, w2)

MESH_ID = pl.DeviceIdType.MESH
NZ = 4
PAD = 16


class Place:
    def __init__(self):
        p = lax.axis_index("fsdp")
        self.p = p
        self.c = lax.axis_index("dp")
        self.x = lax.rem(p, 2)
        self.y = lax.rem(lax.div(p, 2), 2)
        self.z = lax.div(p, 4)
        self.a = self.y + self.c * (self.x - self.y)
        self.b = self.x + self.c * (self.y - self.x)

    def device(self, x, y, z):
        return ((z * 2 + y) * 2 + x, self.c)

    def along_a(self):
        c = self.c
        return self.device(self.x + c * (1 - 2 * self.x), self.y + (1 - c) * (1 - 2 * self.y), self.z)

    def along_b(self):
        c = self.c
        return self.device(self.x + (1 - c) * (1 - 2 * self.x), self.y + c * (1 - 2 * self.y), self.z)

    def along_z(self, step):
        return lax.rem(self.z + step, NZ)

    def sibling(self):
        return (self.p, 1 - self.c)


def slot_of(p, group):
    x, y, z = p % 2, (p // 2) % 2, p // 4
    a, b = (y, x) if group == 0 else (x, y)
    return (a * 2 + b) * NZ + z


def greet(at):
    barrier = pltpu.get_barrier_semaphore()
    others = [at.along_a(), at.along_b(), at.sibling()]
    others += [at.device(at.x, at.y, at.along_z(step)) for step in range(1, NZ)]
    for device in others:
        pl.semaphore_signal(barrier, inc=1, device_id=device, device_id_type=MESH_ID)
    pl.semaphore_wait(barrier, len(others))


def remote(src, dst, sems, k, device):
    return pltpu.make_async_remote_copy(
        src_ref=src, dst_ref=dst, send_sem=sems.at[0, k], recv_sem=sems.at[1, k],
        device_id=device, device_id_type=MESH_ID,
    )


def span(start, size):
    return pl.ds(pl.multiple_of(start, size), size)


class Gather:
    def __init__(self, at, buf, r, sems, swap):
        self.at, self.buf, self.r, self.sems, self.shared = at, buf, r, sems, swap

    def part(self, rows, k, device):
        piece = self.buf.at[rows]
        return remote(piece, piece, self.sems, k, device)

    def line(self):
        at, r = self.at, self.r
        rows = span(((at.a * 2 + at.b) * NZ + at.z) * r, r)
        return [
            self.part(rows, step - 1, at.device(at.x, at.y, at.along_z(step))) for step in range(1, NZ)
        ]

    def over_b(self):
        at, r = self.at, self.r
        return [self.part(span((at.a * 2 + at.b) * NZ * r, NZ * r), 3, at.along_b())]

    def over_a(self):
        at, r = self.at, self.r
        return [self.part(span(at.a * 2 * NZ * r, 2 * NZ * r), 4, at.along_a())]

    def swap(self):
        return [remote(self.buf, self.buf, self.sems, 5, self.at.sibling())] if self.shared else []

    def go(self, step):
        steps = (self.line, self.over_b, self.over_a, self.swap)
        if step > 0:
            for copy in steps[step - 1]():
                copy.wait()
        if step < 4:
            for copy in steps[step]():
                copy.start()


class Reduce:
    def __init__(self, at, full, got, from_a, from_b, from_z, total, r, sems):
        self.at, self.full, self.got = at, full, got
        self.from_a, self.from_b, self.from_z, self.total = from_a, from_b, from_z, total
        self.r, self.sems = r, sems

    def first(self):
        return [remote(self.full.at[1 - self.at.c], self.got, self.sems, 0, self.at.sibling())]

    def over_a(self):
        at, r = self.at, self.r
        rows = span((1 - at.a) * 2 * NZ * r, 2 * NZ * r)
        return [remote(self.full.at[at.c, rows], self.from_a, self.sems, 1, at.along_a())]

    def over_b(self):
        at, r = self.at, self.r
        rows = span((at.a * 2 + 1 - at.b) * NZ * r, NZ * r)
        return [remote(self.full.at[at.c, rows], self.from_b, self.sems, 2, at.along_b())]

    def line(self):
        at, r = self.at, self.r
        copies = []
        for step in range(1, NZ):
            other = at.along_z(step)
            rows = span(((at.a * 2 + at.b) * NZ + other) * r, r)
            copies.append(
                remote(self.full.at[at.c, rows], self.from_z.at[pl.ds((step - 1) * r, r)], self.sems, 2 + step, at.device(at.x, at.y, other))
            )
        return copies

    def last(self):
        piece = self.total.at[self.at.c]
        return [remote(piece, piece, self.sems, 6, self.at.sibling())]

    def add(self, rows, values):
        ref = self.full.at[self.at.c, rows]
        ref[...] = (ref[...].astype(F32) + values.astype(F32)).astype(ref.dtype)

    def go(self, step):
        at, r = self.at, self.r
        steps = (self.first, self.over_a, self.over_b, self.line, self.last)
        if step > 0:
            for copy in steps[step - 1]():
                copy.wait()
        if step == 1:
            for half in range(2):
                rows = pl.ds(half * 2 * NZ * r, 2 * NZ * r)
                self.add(rows, self.got[rows, :])
        elif step == 2:
            self.add(span(at.a * 2 * NZ * r, 2 * NZ * r), self.from_a[...])
        elif step == 3:
            self.add(span((at.a * 2 + at.b) * NZ * r, NZ * r), self.from_b[...])
        elif step == 4:
            total = self.full[at.c, span(((at.a * 2 + at.b) * NZ + at.z) * r, r), :].astype(F32)
            for k in range(NZ - 1):
                total = total + self.from_z[k * r : (k + 1) * r, :].astype(F32)
            self.total[at.c] = total
        if step < 5:
            for copy in steps[step]():
                copy.start()


V_LN1G, V_LN1B, V_QV, V_BOUT, V_LN2G, V_LN2B, V_BFC2, V_BFC1 = 0, 1, 2, 4, 5, 6, 7, 8


def block_body(
    tok, dup, tgt, s_ln1g, s_ln1b, s_qkv, s_qvb, s_out, s_bout, s_ln2g, s_ln2b, s_fc1, s_b1, s_fc2, s_b2,
    out, gin, oqkv, oout, o1, o2, ovec,
    tokb, stage, xs, n1, qkv, att, n2, act, dpre, db2, db1, dos, dmid, probs,
    wqkv, wout, w1, w2_t, wt_a, wf,
    c_ln1g, c_ln1b, c_bqkv, c_bout, c_ln2g, c_ln2b, c_b1, c_b2,
    stat_s, rl_s, exq, qxn, kxn, vxn, oxn, attx, dqkvx, a_g2, a_b2, tgt_t, gvec, allc,
    sv, tv, uv, av, bv, zv, f1, f2, fv,
    loc_sem, gsem1, gsem2, gsemv, rsem1, rsem2, rsemv, ready,
):
    images, seq = dup.shape
    d = tok.shape[1]
    t = seq - 1
    x0 = images * t
    ff = w1.shape[1]
    w = x0 + 128
    shard = d // 16
    blocks = d // 128
    at = Place()

    def lanes_of(i):
        return pl.ds(pl.multiple_of(i * t, 128), t)

    extra_lanes = pl.ds(x0, 128)

    def load_image(i):
        return jnp.concatenate([stage[b, pl.ds(i, t, stride=images), :] for b in range(blocks)], 1)

    def store_image(i, values):
        for b in range(blocks):
            stage[b, pl.ds(i, t, stride=images), :] = values[:, 128 * b : 128 * (b + 1)]

    def store_last(values):
        for b in range(blocks):
            stage[b, x0:, :] = values[:images, 128 * b : 128 * (b + 1)]

    tok_copy = pltpu.make_async_copy(tok, tokb, loc_sem.at[0])
    tok_copy.start()

    own = span(((at.a * 2 + at.b) * NZ + at.z) * 16, 16)
    table = jnp.zeros((16, 128), F32)
    sv[own, :] = table
    base = ((at.a * 2 + at.b) * NZ + at.z) * 16
    flat = [s_ln1g[...], s_ln1b[...], s_qvb[:shard], s_qvb[shard:], s_bout[...], s_ln2g[...], s_ln2b[...], s_b2[...]]
    flat += [s_b1[shard * k : shard * (k + 1)] for k in range(4)]
    for k, line in enumerate(flat):
        sv[pl.ds(base + k, 1), :shard] = line.astype(F32).reshape(1, shard)
    halves = (pl.ds(0, d), pl.ds(d, d))
    mine = pl.ds(pl.multiple_of(at.c * d, 128), d)
    own1 = span(((at.a * 2 + at.b) * NZ + at.z) * 2 * shard, 2 * shard)
    own2 = span(((at.a * 2 + at.b) * NZ + at.z) * 4 * shard, 4 * shard)
    slots1 = act.at[: 16 * 2 * shard]
    slots2 = dpre

    @pl.when(at.c == 0)
    def _():
        q = s_qkv[...].astype(F32)
        f = s_fc1[...].astype(F32)
        slots1[own1, halves[0]] = jnp.concatenate([q[:, :d], q[:, d : 2 * d]], 0).astype(BF16)
        slots2[own2, halves[0]] = jnp.concatenate([f[:, k * d : (k + 1) * d] for k in range(4)], 0).astype(BF16)

    @pl.when(at.c == 1)
    def _():
        q = s_qkv[...].astype(F32)
        slots1[own1, halves[1]] = jnp.concatenate([q[:, 2 * d :], s_out[...].astype(F32)], 0).astype(BF16)
        slots2[own2, halves[1]] = s_fc2[...]

    greet(at)
    gather_v = Gather(at, sv, 16, gsemv, False)
    gather1 = Gather(at, slots1.at[:, mine], 2 * shard, gsem1, True)
    gather2 = Gather(at, slots2.at[:, mine], 4 * shard, gsem2, True)
    gather_v.go(0)
    gather1.go(0)

    tok_copy.wait()
    for b in range(blocks):
        stage[b] = tokb[:, 128 * b : 128 * (b + 1)].astype(F32)

    def statistics(x):
        mu = jnp.mean(x, 0, keepdims=True)
        c = x - mu
        return mu, lax.rsqrt(jnp.mean(c * c, 0, keepdims=True) + EPS)

    def turn(i, carry):
        x = load_image(i).astype(BF16).T
        xs[:, lanes_of(i)] = x
        mu, r = statistics(x.astype(F32))
        stat_s[i, 0:1, :] = mu
        stat_s[i, 1:2, :] = r
        return carry

    gather_v.go(1)
    gather1.go(1)
    gather2.go(0)
    lax.fori_loop(0, images // 2, turn, 0)
    gather_v.go(2)
    gather1.go(2)
    lax.fori_loop(images // 2, images, turn, 0)
    last = jnp.concatenate([tokb[x0:, :].astype(F32), jnp.zeros((128 - images, d), F32)], 0)
    x = last.astype(BF16).T
    xs[:, extra_lanes] = x
    mu, r = statistics(x.astype(F32))
    stat_s[images, 0:1, :128] = mu
    stat_s[images, 1:2, :128] = r
    tgt_t[...] = jnp.concatenate([tgt[...], jnp.zeros((128 - images, d), F32)], 0).T
    ones_row = jnp.where(lax.broadcasted_iota(jnp.int32, (16, w), 0) == 0, 1.0, 0.0).astype(BF16)
    n1[d : d + 16, :] = ones_row
    n2[d : d + 16, :] = ones_row
    att[d : d + 16, :] = ones_row
    attx[...] = jnp.zeros_like(attx)
    dqkvx[...] = jnp.zeros_like(dqkvx)
    a_g2[...] = jnp.zeros_like(a_g2)
    a_b2[...] = jnp.zeros_like(a_b2)
    gather_v.go(3)
    gather1.go(3)

    def slot_v(p):
        px, py, pz = p % 2, (p // 2) % 2, p // 4
        pa = py + at.c * (px - py)
        pb = px + at.c * (py - px)
        return sv[span(((pa * 2 + pb) * NZ + pz) * 16, 16), :]

    for half in range(2):
        allc[half] = jnp.concatenate([slot_v(p) for p in range(8 * half, 8 * half + 8)], 0).T

    def column(ref, entries):
        runs = []
        ids = lax.broadcasted_iota(jnp.int32, (shard, 128), 1)
        for p, k in entries:
            runs.append(jnp.where(ids == 16 * (p % 8) + k, allc[p // 8, :shard, :], 0.0))
        block = jnp.sum(jnp.concatenate(runs, 0), 1, keepdims=True)
        ref[...] = jnp.broadcast_to(block, (len(entries) * shard, 128))

    every = range(16)
    column(c_ln1g, [(p, V_LN1G) for p in every])
    column(c_ln1b, [(p, V_LN1B) for p in every])
    column(c_bqkv.at[:d], [(p, V_QV + k) for p in range(8) for k in range(2)])
    c_bqkv[d : 2 * d, :] = jnp.zeros((d, 128), F32)
    column(c_bqkv.at[2 * d :], [(p, V_QV + k) for p in range(8, 16) for k in range(2)])
    column(c_bout, [(p, V_BOUT) for p in every])
    column(c_ln2g, [(p, V_LN2G) for p in every])
    column(c_ln2b, [(p, V_LN2B) for p in every])
    column(c_b2, [(p, V_BFC2) for p in every])
    column(c_b1, [(p, V_BFC1 + k) for p in every for k in range(4)])

    gather1.go(4)
    gather2.go(1)

    def unpack(slots, group, r, k):
        part = slots[:, halves[group]]
        runs = []
        for p in every:
            s = slot_of(p, group)
            runs.append(slots[r * s : r * (s + 1), halves[group]].astype(F32)[k * shard : (k + 1) * shard])
        return jnp.concatenate(runs, 0).astype(BF16)

    for k in range(4):
        block = unpack(slots1, k // 2, 2 * shard, k % 2)
        if k < 3:
            wqkv[:, k * d : (k + 1) * d] = block
        else:
            wout[...] = block
        wt_a[k // 2, (k % 2) * d : (k % 2 + 1) * d, :] = block.T

    def project(lanes, count, mu, r):
        u = (xs[:, lanes].astype(F32) - mu) * r
        n = (u * wide(c_ln1g[...], count) + wide(c_ln1b[...], count)).astype(BF16)
        n1[:d, lanes] = n
        for k in range(3):
            rows = slice(k * d, (k + 1) * d)
            y = mm(wt_a[k // 2, (k % 2) * d : (k % 2 + 1) * d, :], n) + wide(c_bqkv[rows, :], count)
            y = y.astype(BF16)
            if k == 0:
                y = y * jnp.asarray(HD**-0.5, BF16)
            qkv[rows, lanes] = y

    def project_image(i, carry):
        project(lanes_of(i), t, stat_s[i, 0:1, :], stat_s[i, 1:2, :])
        return carry

    lax.fori_loop(0, images, project_image, 0)
    project(extra_lanes, 128, stat_s[images, 0:1, :128], stat_s[images, 1:2, :128])
    gather2.go(2)

    last = pl.ds(x0, PAD)
    tail = t + PAD

    def split(values, ref):
        rows = values.T[:PAD]
        for h in range(HEADS):
            ref[h] = rows[:, h * HD : (h + 1) * HD].astype(BF16)

    for k, ref in enumerate((qxn, kxn, vxn)):
        split(qkv[k * d : (k + 1) * d, extra_lanes].astype(F32), ref)

    def heads_of(base, lanes, h):
        r0 = base + h * HD
        return jnp.concatenate([qkv[r0 : r0 + HD, lanes], qkv[r0 : r0 + HD, last]], 1)

    def attend_image(i, carry):
        lanes = lanes_of(i)
        own_row = lax.broadcasted_iota(jnp.int32, (PAD, t), 0) == i
        lane = lax.broadcasted_iota(jnp.int32, (PAD, tail), 1)
        own_key = (lane < t) | (lane == t + i)
        own_query = lax.broadcasted_iota(jnp.int32, (PAD, tail), 0) == i

        def score(h):
            q = qkv[h * HD : (h + 1) * HD, lanes]
            k = heads_of(d, lanes, h)
            s = mm(jnp.concatenate([k[:, :t].T, kxn[h]], 0), q)
            return s, mm(qxn[h], k)

        def share(h, s, sq):
            s = jnp.concatenate([s[:t], jnp.where(own_row, s[t:], -1e30)], 0)
            e = jnp.exp(s - jnp.max(s, 0, keepdims=True))
            rl = 1.0 / jnp.sum(e, 0, keepdims=True)
            e = e.astype(BF16)
            probs[i * HEADS + h] = e
            rl_s[i, h : h + 1, :] = rl
            sq = jnp.where(own_key, sq, -1e30)
            eq = jnp.exp(sq - jnp.max(sq, 1, keepdims=True))
            eq = eq * (1.0 / jnp.sum(eq, 1, keepdims=True))
            eq = jnp.where(own_query, eq, 0.0).astype(BF16)
            exq[i * HEADS + h] = eq
            return e, rl, eq

        def mix(h, e, rl, eq):
            v = heads_of(2 * d, lanes, h)
            rows = slice(h * HD, (h + 1) * HD)
            att[rows, lanes] = (mm(v, e) * rl).astype(BF16)
            attx[rows, :PAD] += mm(v, eq, NT)

        ready_scores = [score(0)]
        shares = []
        for h in range(HEADS):
            if h + 1 < HEADS:
                ready_scores.append(score(h + 1))
            shares.append(share(h, *ready_scores[h]))
            if h >= 1:
                mix(h - 1, *shares[h - 1])
        mix(HEADS - 1, *shares[HEADS - 1])

        @pl.when(i == images // 2)
        def _():
            gather2.go(3)

        return carry

    lax.fori_loop(0, images, attend_image, 0)
    att[:d, extra_lanes] = attx[...].astype(BF16)
    gather2.go(4)
    for k in range(4):
        block = unpack(slots2, 0, 4 * shard, k)
        w1[:, k * d : (k + 1) * d] = block
        wf[0, k * d : (k + 1) * d, :] = block.T
    for p in every:
        s = slot_of(p, 1)
        wf[1, 4 * shard * p : 4 * shard * (p + 1), :] = slots2[4 * shard * s : 4 * shard * (s + 1), halves[1]]
    w2_t[...] = wf[1].T
    act[ff : ff + 16, :] = ones_row

    def feed(lanes, count, d_final):
        mid = xs[:, lanes].astype(F32) + mm(wt_a[1, d:, :], att[:d, lanes]) + wide(c_bout[...], count)
        u, r = normalise(mid)
        n = (u * wide(c_ln2g[...], count) + wide(c_ln2b[...], count)).astype(BF16)
        n2[:d, lanes] = n
        db = d_final.astype(BF16)
        db2[:, lanes] = db
        for j in range(ff // 256):
            rows = slice(256 * j, 256 * (j + 1))
            pre = mm(wf[0, rows, :], n) + wide(c_b1[rows, :], count)
            da = mm(wf[1, rows, :], db)
            value, slope = gelu_pair(pre)
            act[rows, lanes] = value.astype(BF16)
            dpre[rows, lanes] = (slope * da).astype(BF16)
        final = mid + mm(w2_t[...], act[:ff, lanes]) + wide(c_b2[...], count)
        dn = mm(w1[...], dpre[:, lanes])
        a_g2[...] += fold(dn * u)
        a_b2[...] += fold(dn)
        dm = d_final + norm_back(dn, u, r, wide(c_ln2g[...], count))
        dmid[:, lanes] = dm
        low = dm.astype(BF16)
        db1[:, lanes] = low
        dos[:, lanes] = mm(wout[...], low).astype(BF16)
        return final.T

    def keep_row(row):
        first = lax.broadcasted_iota(jnp.int32, row.shape, 1) == 0
        return jnp.where(first, 1.0, 1.0 - row.astype(F32))

    def feed_image(i, carry):
        keep = keep_row(dup[pl.ds(i, 1), :])
        count = jnp.sum(keep, 1, keepdims=True)
        scale = seq * keep[:, :t] / count
        ids = lax.broadcasted_iota(jnp.int32, (d, 128), 1)
        target = jnp.sum(jnp.where(ids == i, tgt_t[...], 0.0), 1, keepdims=True)
        store_image(i, feed(lanes_of(i), t, target * scale))
        return carry

    lax.fori_loop(0, images, feed_image, 0)
    keep_all = keep_row(dup[...])
    scale_x = seq * keep_all[:, t:] / jnp.sum(keep_all, 1, keepdims=True)
    scale_x = jnp.broadcast_to(scale_x, (images, 128))
    scale_x = jnp.concatenate([scale_x, jnp.zeros((128 - images, 128), F32)], 0).T[:1, :]
    store_last(feed(extra_lanes, 128, tgt_t[...] * scale_x))
    for b in range(blocks):
        tokb[:, 128 * b : 128 * (b + 1)] = stage[b].astype(BF16)
    out_copy = pltpu.make_async_copy(tokb, out, loc_sem.at[0])
    out_copy.start()

    for j in range(2):
        rows = slice(2 * d * j, 2 * d * (j + 1))
        g = mm(n2[...], dpre[rows, :], NT)
        gvec[BFC1 : BFC1 + 1, rows] = g[d : d + 1]
        for k in range(2):
            part = g[:d, d * k : d * (k + 1)].astype(BF16)
            for p in every:
                start = 4 * shard * slot_of(p, 0) + shard * (2 * j + k)
                wf[0, start : start + shard, :] = part[shard * p : shard * (p + 1)]
    for j in range(ff // 256):
        rows = slice(256 * j, 256 * (j + 1))
        g = mm(act[rows, :], db2[...], NT).astype(BF16)
        step = 4 * shard
        lo = 256 * j
        while lo < 256 * (j + 1):
            p = lo // step
            hi = min(256 * (j + 1), (p + 1) * step)
            start = step * slot_of(p, 1) + lo - p * step
            wf[1, start : start + hi - lo, :] = g[lo - 256 * j : hi - 256 * j]
            lo = hi
    g = mm(act[ff : ff + 16, :], db2[...], NT)
    gvec[BFC2 : BFC2 + 1, :d] = g[:1]

    partners = [at.sibling(), at.along_a(), at.along_b()]
    partners += [at.device(at.x, at.y, at.along_z(step)) for step in range(1, NZ)]
    for k, device in enumerate(partners):
        pl.semaphore_signal(ready.at[min(k, 3)], inc=1, device_id=device, device_id_type=MESH_ID)

    def area(row, count, column):
        return dpre.at[row : row + count, d * column : d * (column + 1)]

    r2, r1 = 4 * shard, 2 * shard
    reduce2 = Reduce(
        at, wf, area(0, 16 * r2, 0), area(0, 8 * r2, 1), area(8 * r2, 4 * r2, 1), area(12 * r2, 3 * r2, 1), f2, r2, rsem2
    )
    reduce1 = Reduce(
        at, wt_a, area(0, 16 * r1, 2), area(16 * r1, 8 * r1, 2), area(24 * r1, 4 * r1, 2), area(28 * r1, 3 * r1, 2), f1, r1, rsem1
    )
    pl.semaphore_wait(ready.at[0], 1)
    reduce2.go(0)

    split(dos[:, extra_lanes].astype(F32), oxn)

    def attend_back(i, carry):
        lanes = lanes_of(i)

        def slopes(h):
            rows = slice(h * HD, (h + 1) * HD)
            v = heads_of(2 * d, lanes, h)
            do = dos[rows, lanes].astype(F32) * rl_s[i, h : h + 1, :]
            dot_o = jnp.sum(do * att[rows, lanes].astype(F32), 0, keepdims=True)
            dol = do.astype(BF16)
            dp = mm(jnp.concatenate([v[:, :t].T, vxn[h]], 0), dol)
            return dol, dot_o, dp, mm(oxn[h], v)

        def scores_back(h, dol, dot_o, dp, dpq):
            p = probs[i * HEADS + h]
            ds = (p.astype(F32) * (dp - dot_o)).astype(BF16)
            eq = exq[i * HEADS + h]
            eqf = eq.astype(F32)
            dsq = eqf * (dpq - jnp.sum(eqf * dpq, 1, keepdims=True))
            return dol, p, ds, eq, dsq.astype(BF16)

        def heads_back(h, dol, p, ds, eq, dsq):
            rows = slice(h * HD, (h + 1) * HD)
            q = qkv[rows, lanes]
            k = heads_of(d, lanes, h)
            scale = HD**-0.5
            dq = mm(k, ds) * scale
            dqx = mm(k, dsq, NT) * scale
            dk = mm(q, ds, NT) + mm(qkv[rows, last], dsq)
            dv = mm(dol, p, NT) + mm(dos[rows, last], eq)
            dqkvx[rows, :PAD] += dqx
            for base, value in ((d, dk), (2 * d, dv)):
                dqkvx[base + h * HD : base + (h + 1) * HD, :PAD] += value[:, t:]
            return dq, dk, dv

        def keep_heads(h, dq, dk, dv):
            for base, value in ((0, dq), (d, dk), (2 * d, dv)):
                qkv[base + h * HD : base + (h + 1) * HD, lanes] = value[:, :t].astype(BF16)

        first = [slopes(0)]
        second = []
        for h in range(HEADS):
            if h + 1 < HEADS:
                first.append(slopes(h + 1))
            second.append(scores_back(h, *first[h]))
            if h >= 1:
                keep_heads(h - 1, *heads_back(h - 1, *second[h - 1]))
        keep_heads(HEADS - 1, *heads_back(HEADS - 1, *second[HEADS - 1]))

        for step, when in ((1, 1), (2, 5), (3, 7)):

            @pl.when(i == when)
            def _(step=step):
                if step < 4:
                    pl.semaphore_wait(ready.at[step], 1 if step < 3 else NZ - 1)
                reduce2.go(step)

        return carry

    lax.fori_loop(0, images, attend_back, 0)
    qkv[:, extra_lanes] = dqkvx[...].astype(BF16)

    scale1 = jnp.zeros((d, 128), F32)
    shift1 = jnp.zeros((d, 128), F32)
    gain1, bias1 = c_ln1g[:, :1], c_ln1b[:, :1]

    def put(group, k, part):
        part = part.astype(BF16)
        for p in every:
            start = 2 * shard * slot_of(p, group) + shard * k
            wt_a[group, start : start + shard, :] = part[shard * p : shard * (p + 1)]

    for k in range(3):
        rows = slice(k * d, (k + 1) * d)
        g = mm(n1[...], qkv[rows, :], NT)
        sums = g[d : d + 1]
        gvec[BQKV : BQKV + 1, rows] = sums
        weight = wqkv[:, rows].astype(F32)
        scale1 = scale1 + fold(weight * (g[:d] - bias1 * sums))
        shift1 = shift1 + fold(weight * sums)
        put(k // 2, k % 2, g[:d])
    g = mm(att[...], db1[...], NT)
    put(1, 1, g[:d])
    gvec[BOUT : BOUT + 1, :d] = g[d : d + 1]
    scale1 = scale1 * (1.0 / c_ln1g[...])
    for row, acc in ((LN1G, scale1), (LN1B, shift1), (LN2G, a_g2[...]), (LN2B, a_b2[...])):
        gvec[row : row + 1, :d] = jnp.sum(acc.T, 0, keepdims=True)
    tv[...] = jnp.zeros_like(tv)
    for p in every:
        s0 = 8 * slot_of(p, 0)
        tv[0, s0 : s0 + 8, :shard] = gvec[:, shard * p : shard * (p + 1)]
        s1 = 8 * slot_of(p, 1)
        lo = 2 * shard * p if p < 8 else 2 * d + 2 * shard * (p - 8)
        parts = [gvec[BQKV : BQKV + 1, lo + shard * k : lo + shard * (k + 1)] for k in range(2)]
        lo = 4 * shard * p
        parts += [gvec[BFC1 : BFC1 + 1, lo + shard * k : lo + shard * (k + 1)] for k in range(4)]
        tv[1, s1 : s1 + 6, :shard] = jnp.concatenate(parts, 0)

    reduce_v = Reduce(at, tv, uv, av, bv, zv, fv, 8, rsemv)
    reduce1.go(0)
    reduce_v.go(0)
    reduce2.go(4)

    def finish(lanes, count, mu, r):
        u = (xs[:, lanes].astype(F32) - mu) * r
        dn = mm(wqkv[...], qkv[:, lanes])
        return (dmid[:, lanes] + norm_back(dn, u, r, wide(c_ln1g[...], count))).T

    def finish_image(i, carry):
        store_image(i, finish(lanes_of(i), t, stat_s[i, 0:1, :], stat_s[i, 1:2, :]))
        for step, when in ((1, 2), (2, 6)):

            @pl.when(i == when)
            def _(step=step):
                reduce_v.go(step)
                reduce1.go(step)

        return carry

    lax.fori_loop(0, images, finish_image, 0)
    store_last(finish(extra_lanes, 128, stat_s[images, 0:1, :128], stat_s[images, 1:2, :128]))
    copies = [
        pltpu.make_async_copy(stage.at[b], gin.at[:, pl.ds(128 * b, 128)], loc_sem.at[1 + b]) for b in range(blocks)
    ]
    for copy in copies:
        copy.start()
    reduce2.go(5)
    o1[...] = jnp.concatenate([f2[0, shard * k : shard * (k + 1)] for k in range(4)], 1)
    o2[...] = f2[1]
    for step in (3, 4, 5):
        reduce_v.go(step)
        reduce1.go(step)
    oqkv[:, :d] = f1[0, :shard]
    oqkv[:, d : 2 * d] = f1[0, shard:]
    oqkv[:, 2 * d :] = f1[1, :shard]
    oout[...] = f1[1, shard:]
    ovec[...] = fv[...]
    for copy in copies:
        copy.wait()
    out_copy.wait()


def block_call(tok, dup, tgt, weights):
    images, seq = dup.shape
    d = tok.shape[1]
    n = d // 16
    ff = 4 * d
    t = seq - 1
    w = images * t + 128
    vm = pltpu.VMEM
    dma = pltpu.SemaphoreType.DMA
    sd = jax.ShapeDtypeStruct
    scratch = [
        vm((seq * images, d), BF16),
        vm((d // 128, seq * images, 128), F32),
        vm((d, w), BF16),
        vm((d + 16, w), BF16),
        vm((3 * d, w), BF16),
        vm((d + 16, w), BF16),
        vm((d + 16, w), BF16),
        vm((ff + 16, w), BF16),
        vm((ff, w), BF16),
        vm((d, w), BF16),
        vm((d, w), BF16),
        vm((d, w), BF16),
        vm((d, w), F32),
        vm((images * HEADS, t + PAD, t), BF16),
        vm((d, 3 * d), BF16),
        vm((d, d), BF16),
        vm((d, ff), BF16),
        vm((d, ff), BF16),
        vm((2, 2 * d, d), BF16),
        vm((2, ff, d), BF16),
        vm((d, 128), F32), vm((d, 128), F32), vm((3 * d, 128), F32), vm((d, 128), F32),
        vm((d, 128), F32), vm((d, 128), F32), vm((ff, 128), F32), vm((d, 128), F32),
        vm((images + 1, 8, t), F32),
        vm((images, 8, t), F32),
        vm((images * HEADS, PAD, t + PAD), BF16),
        vm((HEADS, PAD, HD), BF16), vm((HEADS, PAD, HD), BF16),
        vm((HEADS, PAD, HD), BF16), vm((HEADS, PAD, HD), BF16),
        vm((d, 128), F32),
        vm((3 * d, 128), F32),
        vm((d, 128), F32), vm((d, 128), F32),
        vm((d, 128), F32),
        vm((8, ff), F32),
        vm((2, 128, 128), F32),
        vm((256, 128), F32),
        vm((2, 128, 128), F32),
    ]
    for slots in (16, 8, 4):
        scratch += [vm((slots * 8, 128), F32)]
    scratch += [vm((24, 128), F32)]
    scratch += [vm((2, 2 * n, d), F32), vm((2, 4 * n, d), F32), vm((2, 8, 128), F32)]
    scratch += [dma((4,))] + [dma((2, 7))] * 6 + [pltpu.SemaphoreType.REGULAR((4,))]
    spec = pl.BlockSpec(memory_space=pltpu.VMEM)
    any_spec = pl.BlockSpec(memory_space=pl.ANY)
    return pl.pallas_call(
        block_body,
        out_shape=(
            sd(tok.shape, BF16), sd(tok.shape, F32),
            sd((n, 3 * d), F32), sd((n, d), F32), sd((n, ff), F32), sd((4 * n, d), F32), sd((2, 8, 128), F32),
        ),
        in_specs=[any_spec] + [spec] * 14,
        out_specs=(any_spec, any_spec) + (spec,) * 5,
        scratch_shapes=scratch,
        compiler_params=pltpu.CompilerParams(
            collective_id=0, has_side_effects=True, vmem_limit_bytes=64 * 1024 * 1024
        ),
        name="block16",
    )(tok, dup, tgt, *weights)


def deliver_body(out, gin, gqkv, gout, g1, g2, gv, *refs):
    o_out, o_gin, o_ln1g, o_ln1b, o_qkv, o_qvb, o_w, o_bout, o_ln2g, o_ln2b, o_fc1, o_b1, o_fc2, o_b2 = refs[:14]
    buf_out, buf_gin, sems = refs[14:]
    n = gqkv.shape[0]
    pieces = []
    for k, (src, buf, dst) in enumerate(((out, buf_out, o_out), (gin, buf_gin, o_gin))):
        count = 1 + 3 * k
        size = (src.shape[0] // count) // 16 * 16
        for m in range(count):
            rows = pl.ds(m * size, size if m < count - 1 else src.shape[0] - m * size)
            s = k + m
            pieces.append((
                pltpu.make_async_copy(src.at[rows], buf.at[rows], sems.at[0, s]),
                pltpu.make_async_copy(buf.at[rows], dst.at[rows], sems.at[1, s]),
            ))
    for load, store in pieces:
        load.start()
    o_qkv[...] = gqkv[...]
    o_w[...] = gout[...]
    o_fc1[...] = g1[...]
    o_fc2[...] = g2[...]
    for ref, row in ((o_ln1g, LN1G), (o_ln1b, LN1B), (o_bout, BOUT), (o_ln2g, LN2G), (o_ln2b, LN2B), (o_b2, BFC2)):
        ref[...] = gv[0, row, :n]
    o_qvb[...] = jnp.concatenate([gv[1, k, :n] for k in range(2)], 0)
    o_b1[...] = jnp.concatenate([gv[1, 2 + k, :n] for k in range(4)], 0)
    for load, store in pieces:
        load.wait()
        store.start()
    for load, store in pieces:
        store.wait()


def deliver_call(out, gin, gqkv, gout, g1, g2, gv):
    n, d = gout.shape
    sd = jax.ShapeDtypeStruct
    spec = pl.BlockSpec(memory_space=pltpu.VMEM)
    any_spec = pl.BlockSpec(memory_space=pl.ANY)
    vec = sd((n,), F32)
    return pl.pallas_call(
        deliver_body,
        out_shape=(
            sd(out.shape, BF16), sd(gin.shape, F32), vec, vec, sd((n, 3 * d), F32), sd((2 * n,), F32),
            sd((n, d), F32), vec, vec, vec, sd((n, 4 * d), F32), sd((4 * n,), F32), sd((4 * n, d), F32), vec,
        ),
        in_specs=[any_spec, any_spec] + [spec] * 5,
        out_specs=(any_spec, any_spec) + (spec,) * 12,
        scratch_shapes=[
            pltpu.VMEM(out.shape, BF16), pltpu.VMEM(gin.shape, F32), pltpu.SemaphoreType.DMA((2, 6)),
        ],
        compiler_params=pltpu.CompilerParams(vmem_limit_bytes=64 * 1024 * 1024),
        name="deliver",
    )(out, gin, gqkv, gout, g1, g2, gv)


def gather_all(value):
    return lax.all_gather(value, "fsdp", axis=0, tiled=True)


def vectors(full):
    ln1_gain, ln1_bias, qv_bias, out_bias, ln2_gain, ln2_bias, fc1_bias, fc2_bias = full
    d = ln1_gain.shape[0]
    bias = jnp.concatenate([qv_bias[:d], jnp.zeros((d,), qv_bias.dtype), qv_bias[d:]])
    rows = (ln1_gain, ln1_bias, bias, out_bias, ln2_gain, ln2_bias, fc1_bias, fc2_bias)
    width = fc1_bias.shape[0]
    return jnp.stack([jnp.pad(row.astype(F32), (0, width - row.shape[0])) for row in rows], 0)


def per_device(tokens, duplicate, targets, *weights, block16):
    images, seq, d = tokens.shape
    rows = tokens.transpose(1, 0, 2).reshape(seq * images, d)
    back = lambda v: v.reshape(seq, images, d).transpose(1, 0, 2)
    if block16:
        results = deliver_call(*block_call(rows, duplicate, targets, weights))
        return (back(results[0]), back(results[1])) + tuple(results[2:])

    (
        ln1_gain, ln1_bias, qkv_weight, qv_bias, out_weight, out_bias,
        ln2_gain, ln2_bias, fc1_weight, fc1_bias, fc2_weight, fc2_bias,
    ) = weights
    small = (ln1_gain, ln1_bias, qv_bias, out_bias, ln2_gain, ln2_bias, fc1_bias, fc2_bias)
    wqkv, wout, w1, w2 = map(gather_all, (qkv_weight, out_weight, fc1_weight, fc2_weight))
    vec = vectors(tuple(map(gather_all, small)))
    out, gin, gqkv, gout, g1, g2, gvec = compute(rows, duplicate, targets, vec, wqkv, wout, w1, w2)

    def scatter(value):
        value = lax.psum_scatter(value.astype(F32), "fsdp", scatter_dimension=0, tiled=True)
        return lax.psum(value, "dp")

    gqkv, gout, g1, g2 = map(scatter, (gqkv, gout, g1, g2))
    gvec = lax.psum(gvec, ("fsdp", "dp"))
    p = lax.axis_index("fsdp")

    def shard(value, whole_size):
        count = whole_size // lax.axis_size("fsdp")
        return lax.dynamic_slice(value, (p * count,), (count,))

    qv_grad = jnp.concatenate([gvec[2, :d], gvec[2, 2 * d : 3 * d]])
    return (
        back(out), back(gin),
        shard(gvec[0], d), shard(gvec[1], d), gqkv, shard(qv_grad, 2 * d), gout, shard(gvec[3], d),
        shard(gvec[4], d), shard(gvec[5], d), g1, shard(gvec[6], 4 * d), g2, shard(gvec[7], d),
    )


def solution(mesh):
    block16 = mesh.shape["fsdp"] == 16 and mesh.shape["dp"] == 2
    both = ("fsdp", "dp")
    vector, matrix = P("fsdp"), P("fsdp", None)
    weights = (vector, vector, matrix, vector, matrix, vector, vector, vector, matrix, vector, matrix, vector)
    return jax.shard_map(
        functools.partial(per_device, block16=block16),
        mesh=mesh,
        in_specs=(P(both, None, None), P(both, None), P(both, None)) + weights,
        out_specs=(P(both, None, None), P(both, None, None)) + weights,
        check_vma=False,
    )
```

```python
import functools
import jax
import jax.numpy as jnp
from jax import lax
from jax.experimental import pallas as pl
from jax.experimental.pallas import tpu as pltpu
from jax.sharding import PartitionSpec as P

HEADS = 6
HD = 64
EPS = 1e-06
F32 = jnp.float32
BF16 = jnp.bfloat16

NN = (((1,), (0,)), ((), ()))
NT = (((1,), (1,)), ((), ()))


def mm(a, b, dims=NN):
    return lax.dot_general(a, b, dims, preferred_element_type=F32)


def normalise(v):
    mu = jnp.mean(v, 0, keepdims=True)
    c = v - mu
    r = lax.rsqrt(jnp.mean(c * c, 0, keepdims=True) + EPS)
    return c * r, r


def norm_back(dn, u, r, gain):
    e = dn * gain
    me = jnp.mean(e, 0, keepdims=True)
    meu = jnp.mean(e * u, 0, keepdims=True)
    return r * (e - me - u * meu)


def fold(v):
    lanes = v.shape[1]
    total = v[:, :128]
    for k in range(1, lanes // 128):
        total = total + v[:, 128 * k : 128 * (k + 1)]
    return total


def wide(col, lanes):
    if lanes == 128:
        return col
    return jnp.concatenate([col] * (lanes // 128), 1)


def gelu_pair(x):
    z = x * 0.7071067811865476
    bell = jnp.exp(-(z * z))
    tail = lax.erf(z)
    half = 0.5 * x
    return half + half * tail, 0.5 + (0.5 * tail + (x * 0.3989422804014327) * bell)


LN1G, LN1B, BQKV, BOUT, LN2G, LN2B, BFC1, BFC2 = range(8)


def to_columns(vec, row, count):
    return jnp.broadcast_to(vec[row : row + 1, :count], (128, count)).T


def compute_body(
    tok, dup, tgt, vec, wqkv, wout, w1, w2,
    out, gin, gqkv, gout, g1, g2, gvec,
    xs, n1, qkv, att, n2, act, dpre, db2, db1, dos, dmid, probs,
    wqkv_t, wout_t, w1_t, w2_t,
    c_ln1g, c_ln1b, c_bqkv, c_bout, c_ln2g, c_ln2b, c_b1, c_b2,
    rl_s, ex_s, exq_s, rlx_s, exx_s, attx, dqkvx, a_g1, a_b1, a_g2, a_b2, tgt_t, stage, gin_sem,
):
    images, seq = dup.shape
    d = tok.shape[1]
    t = seq - 1
    x0 = images * t
    ff = w1.shape[1]
    w = x0 + 128
    dqkv = act.at[: 3 * d]

    blocks = d // 128

    def load_image(i):
        return jnp.concatenate([stage[b, pl.ds(i, t, stride=images), :] for b in range(blocks)], 1)

    def store_image(i, values):
        for b in range(blocks):
            stage[b, pl.ds(i, t, stride=images), :] = values[:, 128 * b : 128 * (b + 1)]

    def store_last(values):
        for b in range(blocks):
            stage[b, x0:, :] = values[:images, 128 * b : 128 * (b + 1)]

    def lanes_of(i):
        return pl.ds(pl.multiple_of(i * t, 128), t)

    extra_lanes = pl.ds(x0, 128)

    tok_copy = pltpu.make_async_copy(tok, out, gin_sem.at[0])
    tok_copy.start()
    tok_copy.wait()
    wqkv_t[...] = wqkv[...].T
    wout_t[...] = wout[...].T
    w1_t[...] = w1[...].T
    w2_t[...] = w2[...].T
    c_ln1g[...] = to_columns(vec, LN1G, d)
    c_ln1b[...] = to_columns(vec, LN1B, d)
    c_bqkv[...] = to_columns(vec, BQKV, 3 * d)
    c_bout[...] = to_columns(vec, BOUT, d)
    c_ln2g[...] = to_columns(vec, LN2G, d)
    c_ln2b[...] = to_columns(vec, LN2B, d)
    c_b1[...] = to_columns(vec, BFC1, ff)
    c_b2[...] = to_columns(vec, BFC2, d)
    tgt_t[...] = jnp.concatenate([tgt[...], jnp.zeros((128 - images, d), F32)], 0).T
    ones_row = jnp.where(lax.broadcasted_iota(jnp.int32, (16, w), 0) == 0, 1.0, 0.0).astype(BF16)
    n1[d : d + 16, :] = ones_row
    n2[d : d + 16, :] = ones_row
    att[d : d + 16, :] = ones_row
    act[ff : ff + 16, :] = ones_row
    attx[...] = jnp.zeros_like(attx)
    dqkvx[...] = jnp.zeros_like(dqkvx)
    for acc in (a_g1, a_b1, a_g2, a_b2):
        acc[...] = jnp.zeros_like(acc)

    def project(x_t, lanes, count):
        x = x_t.astype(F32)
        xs[:, lanes] = x_t
        u, r = normalise(x)
        n = (u * wide(c_ln1g[...], count) + wide(c_ln1b[...], count)).astype(BF16)
        n1[:d, lanes] = n
        for k in range(3):
            rows = slice(k * d, (k + 1) * d)
            y = mm(wqkv_t[rows, :], n) + wide(c_bqkv[rows, :], count)
            y = y.astype(BF16)
            if k == 0:
                y = y * jnp.asarray(HD**-0.5, BF16)
            qkv[rows, lanes] = y

    def project_image(i, carry):
        project(load_image(i).astype(BF16).T, lanes_of(i), t)
        return carry

    for b in range(blocks):
        stage[b] = out[:, 128 * b : 128 * (b + 1)].astype(F32)

    lax.fori_loop(0, images, project_image, 0)
    last = jnp.concatenate([out[x0:, :].astype(F32), jnp.zeros((128 - images, d), F32)], 0)
    project(last.astype(BF16).T, extra_lanes, 128)

    lane_ids = lax.broadcasted_iota(jnp.int32, (HD, 128), 1)

    def pick(ref, row, i):
        block = ref[row : row + HD, extra_lanes].astype(F32)
        return jnp.sum(jnp.where(lane_ids == i, block, 0.0), 1, keepdims=True)

    def attend_image(i, carry):
        lanes = lanes_of(i)
        for h in range(HEADS):
            r0 = h * HD
            q = qkv[r0 : r0 + HD, lanes]
            k = qkv[d + r0 : d + r0 + HD, lanes]
            v = qkv[2 * d + r0 : 2 * d + r0 + HD, lanes]
            qx, kx, vx = pick(qkv, r0, i), pick(qkv, d + r0, i), pick(qkv, 2 * d + r0, i)
            s = mm(k.T, q)
            sx = jnp.sum(q.astype(F32) * kx, 0, keepdims=True)
            top = jnp.maximum(jnp.max(s, 0, keepdims=True), sx)
            e = jnp.exp(s - top)
            ex = jnp.exp(sx - top)
            rl = 1.0 / (jnp.sum(e, 0, keepdims=True) + ex)
            e = e.astype(BF16)
            probs[i * HEADS + h] = e
            o = (mm(v, e) + vx * ex) * rl
            att[r0 : r0 + HD, lanes] = o.astype(BF16)
            rl_s[i, h : h + 1, :] = rl
            ex_s[i, h : h + 1, :] = ex
            sq = jnp.sum(k.astype(F32) * qx, 0, keepdims=True)
            sxx = jnp.sum(kx * qx, 0, keepdims=True)
            topx = jnp.maximum(jnp.max(sq, 1, keepdims=True), sxx)
            eq = jnp.exp(sq - topx)
            exx = jnp.exp(sxx - topx)
            rlx = 1.0 / (jnp.sum(eq, 1, keepdims=True) + exx)
            ox = (jnp.sum(v.astype(F32) * eq, 1, keepdims=True) + vx * exx) * rlx
            attx[r0 : r0 + HD, :] = jnp.where(lane_ids == i, ox, attx[r0 : r0 + HD, :])
            exq_s[i, h : h + 1, :] = eq
            rlx_s[i, h : h + 1, :] = jnp.broadcast_to(rlx, (1, 128))
            exx_s[i, h : h + 1, :] = jnp.broadcast_to(exx, (1, 128))
        return carry

    lax.fori_loop(0, images, attend_image, 0)
    att[:d, extra_lanes] = attx[...].astype(BF16)

    def feed(lanes, count, d_final):
        mid = xs[:, lanes].astype(F32) + mm(wout_t[...], att[:d, lanes]) + wide(c_bout[...], count)
        u, r = normalise(mid)
        n = (u * wide(c_ln2g[...], count) + wide(c_ln2b[...], count)).astype(BF16)
        n2[:d, lanes] = n
        db = d_final.astype(BF16)
        db2[:, lanes] = db
        for j in range(ff // 256):
            rows = slice(256 * j, 256 * (j + 1))
            pre = mm(w1_t[rows, :], n) + wide(c_b1[rows, :], count)
            da = mm(w2[rows, :], db)
            value, slope = gelu_pair(pre)
            act[rows, lanes] = value.astype(BF16)
            dpre[rows, lanes] = (slope * da).astype(BF16)
        final = mid + mm(w2_t[...], act[:ff, lanes]) + wide(c_b2[...], count)
        dn = mm(w1[...], dpre[:, lanes])
        a_g2[...] += fold(dn * u)
        a_b2[...] += fold(dn)
        dm = d_final + norm_back(dn, u, r, wide(c_ln2g[...], count))
        dmid[:, lanes] = dm
        low = dm.astype(BF16)
        db1[:, lanes] = low
        dos[:, lanes] = mm(wout[...], low).astype(BF16)
        return final.T

    def keep_row(row):
        first = lax.broadcasted_iota(jnp.int32, row.shape, 1) == 0
        return jnp.where(first, 1.0, 1.0 - row.astype(F32))

    def feed_image(i, carry):
        keep = keep_row(dup[pl.ds(i, 1), :])
        count = jnp.sum(keep, 1, keepdims=True)
        scale = seq * keep[:, :t] / count
        ids = lax.broadcasted_iota(jnp.int32, (d, 128), 1)
        target = jnp.sum(jnp.where(ids == i, tgt_t[...], 0.0), 1, keepdims=True)
        store_image(i, feed(lanes_of(i), t, target * scale))
        return carry

    lax.fori_loop(0, images, feed_image, 0)
    keep_all = keep_row(dup[...])
    scale_x = seq * keep_all[:, t:] / jnp.sum(keep_all, 1, keepdims=True)
    scale_x = jnp.broadcast_to(scale_x, (images, 128))
    scale_x = jnp.concatenate([scale_x, jnp.zeros((128 - images, 128), F32)], 0).T[:1, :]
    store_last(feed(extra_lanes, 128, tgt_t[...] * scale_x))
    for b in range(blocks):
        out[:, 128 * b : 128 * (b + 1)] = stage[b].astype(BF16)

    for j in range(ff // 256):
        rows = slice(256 * j, 256 * (j + 1))
        g = mm(n2[...], dpre[rows, :], NT)
        g1[:, rows] = g[:d].astype(BF16)
        gvec[BFC1 : BFC1 + 1, rows] = g[d : d + 1]
        g2[rows, :] = mm(act[rows, :], db2[...], NT).astype(BF16)
    g = mm(act[ff : ff + 16, :], db2[...], NT)
    gvec[BFC2 : BFC2 + 1, :d] = g[:1]

    def attend_back(i, carry):
        lanes = lanes_of(i)
        for h in range(HEADS):
            r0 = h * HD
            q = qkv[r0 : r0 + HD, lanes]
            k = qkv[d + r0 : d + r0 + HD, lanes]
            v = qkv[2 * d + r0 : 2 * d + r0 + HD, lanes]
            qx, kx, vx = pick(qkv, r0, i), pick(qkv, d + r0, i), pick(qkv, 2 * d + r0, i)
            rl = rl_s[i, h : h + 1, :]
            ex = ex_s[i, h : h + 1, :]
            do = dos[r0 : r0 + HD, lanes].astype(F32) * rl
            dot_o = jnp.sum(do * att[r0 : r0 + HD, lanes].astype(F32), 0, keepdims=True)
            dol = do.astype(BF16)
            p = probs[i * HEADS + h]
            ds = (p.astype(F32) * (mm(v.T, dol) - dot_o)).astype(BF16)
            dsx = ex * (jnp.sum(do * vx, 0, keepdims=True) - dot_o)
            dq = mm(k, ds) + kx * dsx
            dk = mm(q, ds, NT)
            dv = mm(dol, p, NT)
            qf = q.astype(F32)
            kf = k.astype(F32)
            vf = v.astype(F32)
            dkx = jnp.sum(qf * dsx, 1, keepdims=True)
            dvx = jnp.sum(do * ex, 1, keepdims=True)
            eq = exq_s[i, h : h + 1, :]
            rlx = rlx_s[i, h : h + 1, :1]
            exx = exx_s[i, h : h + 1, :1]
            dox = pick(dos, r0, i) * rlx
            dotx = jnp.sum(dox * pick(att, r0, i), 0, keepdims=True)
            dsq = eq * (jnp.sum(vf * dox, 0, keepdims=True) - dotx)
            dsxx = exx * (jnp.sum(vx * dox, 0, keepdims=True) - dotx)
            dqx = jnp.sum(kf * dsq, 1, keepdims=True) + kx * dsxx
            dk = dk + qx * dsq
            dv = dv + dox * eq
            dkx = dkx + qx * dsxx
            dvx = dvx + dox * exx
            scale = HD**-0.5
            for base, main, tail in ((0, dq * scale, dqx * scale), (d, dk, dkx), (2 * d, dv, dvx)):
                rows = slice(base + r0, base + r0 + HD)
                dqkv[rows, lanes] = main.astype(BF16)
                dqkvx[rows, :] = jnp.where(lane_ids == i, tail, dqkvx[rows, :])
        return carry

    lax.fori_loop(0, images, attend_back, 0)
    dqkv[:, extra_lanes] = dqkvx[...].astype(BF16)

    for k in range(3):
        rows = slice(k * d, (k + 1) * d)
        g = mm(n1[...], dqkv[rows, :], NT)
        gqkv[:, rows] = g[:d].astype(BF16)
        gvec[BQKV : BQKV + 1, rows] = g[d : d + 1]
    g = mm(att[...], db1[...], NT)
    gout[...] = g[:d].astype(BF16)
    gvec[BOUT : BOUT + 1, :d] = g[d : d + 1]

    def finish(lanes, count):
        u, r = normalise(xs[:, lanes].astype(F32))
        dn = mm(wqkv[...], dqkv[:, lanes])
        a_g1[...] += fold(dn * u)
        a_b1[...] += fold(dn)
        return (dmid[:, lanes] + norm_back(dn, u, r, wide(c_ln1g[...], count))).T

    def finish_image(i, carry):
        store_image(i, finish(lanes_of(i), t))
        return carry

    lax.fori_loop(0, images, finish_image, 0)
    store_last(finish(extra_lanes, 128))
    copies = [
        pltpu.make_async_copy(stage.at[b], gin.at[:, pl.ds(128 * b, 128)], gin_sem.at[b]) for b in range(blocks)
    ]
    for copy in copies:
        copy.start()

    for row, acc in ((LN1G, a_g1), (LN1B, a_b1), (LN2G, a_g2), (LN2B, a_b2)):
        gvec[row : row + 1, :d] = jnp.sum(acc[...].T, 0, keepdims=True)
    for copy in copies:
        copy.wait()


def compute(tok, dup, tgt, vec, wqkv, wout, w1, w2):
    images, seq = dup.shape
    d = tok.shape[1]
    ff = w1.shape[1]
    t = seq - 1
    w = images * t + 128
    vm = pltpu.VMEM
    scratch = [
        vm((d, w), BF16),
        vm((d + 16, w), BF16),
        vm((3 * d, w), BF16),
        vm((d + 16, w), BF16),
        vm((d + 16, w), BF16),
        vm((ff + 16, w), BF16),
        vm((ff, w), BF16),
        vm((d, w), BF16),
        vm((d, w), BF16),
        vm((d, w), BF16),
        vm((d, w), F32),
        vm((images * HEADS, t, t), BF16),
        vm((3 * d, d), BF16),
        vm((d, d), BF16),
        vm((ff, d), BF16),
        vm((d, ff), BF16),
        vm((d, 128), F32), vm((d, 128), F32), vm((3 * d, 128), F32), vm((d, 128), F32),
        vm((d, 128), F32), vm((d, 128), F32), vm((ff, 128), F32), vm((d, 128), F32),
        vm((images, 8, t), F32),
        vm((images, 8, t), F32),
        vm((images, 8, t), F32),
        vm((images, 8, 128), F32),
        vm((images, 8, 128), F32),
        vm((d, 128), F32),
        vm((3 * d, 128), F32),
        vm((d, 128), F32), vm((d, 128), F32), vm((d, 128), F32), vm((d, 128), F32),
        vm((d, 128), F32),
        vm((d // 128, images * seq, 128), F32),
        pltpu.SemaphoreType.DMA((d // 128,)),
    ]
    outs = (
        jax.ShapeDtypeStruct(tok.shape, BF16),
        jax.ShapeDtypeStruct(tok.shape, F32),
        jax.ShapeDtypeStruct((d, 3 * d), BF16),
        jax.ShapeDtypeStruct((d, d), BF16),
        jax.ShapeDtypeStruct((d, ff), BF16),
        jax.ShapeDtypeStruct((ff, d), BF16),
        jax.ShapeDtypeStruct((8, ff), F32),
    )
    spec = pl.BlockSpec(memory_space=pltpu.VMEM)
    return pl.pallas_call(
        compute_body,
        out_shape=outs,
        in_specs=[pl.BlockSpec(memory_space=pl.ANY)] + [spec] * 7,
        out_specs=(spec, pl.BlockSpec(memory_space=pl.ANY)) + (spec,) * 5,
        scratch_shapes=scratch,
        compiler_params=pltpu.CompilerParams(vmem_limit_bytes=64 * 1024 * 1024),
        name="block",
    )(tok, dup, tgt, vec, wqkv, wout, w1, w2)

MESH_ID = pl.DeviceIdType.MESH
NZ = 4
UNITS = 2
UNITS1 = 1
UNITS2 = 2
CHUNK = 2
FFB = 128


class Place:
    def __init__(self):
        p = lax.axis_index("fsdp")
        self.p = p
        self.c = lax.axis_index("dp")
        self.x = lax.rem(p, 2)
        self.y = lax.rem(lax.div(p, 2), 2)
        self.z = lax.div(p, 4)
        self.a = self.y + self.c * (self.x - self.y)
        self.b = self.x + self.c * (self.y - self.x)

    def device(self, x, y, z):
        return ((z * 2 + y) * 2 + x, self.c)

    def along_a(self):
        c = self.c
        return self.device(self.x + c * (1 - 2 * self.x), self.y + (1 - c) * (1 - 2 * self.y), self.z)

    def along_b(self):
        c = self.c
        return self.device(self.x + (1 - c) * (1 - 2 * self.x), self.y + c * (1 - 2 * self.y), self.z)

    def along_z(self, step):
        return lax.rem(self.z + step, NZ)

    def sibling(self):
        return (self.p, 1 - self.c)


def slot_of(p, group):
    x, y, z = p % 2, (p // 2) % 2, p // 4
    a, b = (y, x) if group == 0 else (x, y)
    return (a * 2 + b) * NZ + z


def greet(at):
    barrier = pltpu.get_barrier_semaphore()
    others = [at.along_a(), at.along_b(), at.sibling()]
    others += [at.device(at.x, at.y, at.along_z(step)) for step in range(1, NZ)]
    for device in others:
        pl.semaphore_signal(barrier, inc=1, device_id=device, device_id_type=MESH_ID)
    pl.semaphore_wait(barrier, len(others))


def remote(src, dst, sems, k, device):
    return pltpu.make_async_remote_copy(
        src_ref=src, dst_ref=dst, send_sem=sems.at[0, k], recv_sem=sems.at[1, k],
        device_id=device, device_id_type=MESH_ID,
    )


def span(start, size):
    return pl.ds(pl.multiple_of(start, size), size)


class Gather:
    def __init__(self, at, buf, r, sems, swap):
        self.at, self.buf, self.r, self.sems, self.shared = at, buf, r, sems, swap

    def part(self, rows, k, device):
        piece = self.buf.at[rows]
        return remote(piece, piece, self.sems, k, device)

    def line(self):
        at, r = self.at, self.r
        rows = span(((at.a * 2 + at.b) * NZ + at.z) * r, r)
        return [
            self.part(rows, step - 1, at.device(at.x, at.y, at.along_z(step))) for step in range(1, NZ)
        ]

    def over_b(self):
        at, r = self.at, self.r
        return [self.part(span((at.a * 2 + at.b) * NZ * r, NZ * r), 3, at.along_b())]

    def over_a(self):
        at, r = self.at, self.r
        return [self.part(span(at.a * 2 * NZ * r, 2 * NZ * r), 4, at.along_a())]

    def swap(self):
        return [remote(self.buf, self.buf, self.sems, 5, self.at.sibling())] if self.shared else []

    def go(self, step):
        steps = (self.line, self.over_b, self.over_a, self.swap)
        if step > 0:
            for copy in steps[step - 1]():
                copy.wait()
        if step < 4:
            for copy in steps[step]():
                copy.start()


class Reduce:
    def __init__(self, at, full, got, from_a, from_b, from_z, total, r, sems):
        self.at, self.full, self.got = at, full, got
        self.from_a, self.from_b, self.from_z, self.total = from_a, from_b, from_z, total
        self.r, self.sems = r, sems

    def first(self):
        return [remote(self.full.at[1 - self.at.c], self.got, self.sems, 0, self.at.sibling())]

    def over_a(self):
        at, r = self.at, self.r
        rows = span((1 - at.a) * 2 * NZ * r, 2 * NZ * r)
        return [remote(self.full.at[at.c, rows], self.from_a, self.sems, 1, at.along_a())]

    def over_b(self):
        at, r = self.at, self.r
        rows = span((at.a * 2 + 1 - at.b) * NZ * r, NZ * r)
        return [remote(self.full.at[at.c, rows], self.from_b, self.sems, 2, at.along_b())]

    def line(self):
        at, r = self.at, self.r
        copies = []
        for step in range(1, NZ):
            other = at.along_z(step)
            rows = span(((at.a * 2 + at.b) * NZ + other) * r, r)
            copies.append(
                remote(self.full.at[at.c, rows], self.from_z.at[pl.ds((step - 1) * r, r)], self.sems, 2 + step, at.device(at.x, at.y, other))
            )
        return copies

    def last(self):
        piece = self.total.at[self.at.c]
        return [remote(piece, piece, self.sems, 6, self.at.sibling())]

    def add(self, rows, values):
        ref = self.full.at[self.at.c, rows]
        ref[...] = (ref[...].astype(F32) + values.astype(F32)).astype(ref.dtype)

    def go(self, step):
        at, r = self.at, self.r
        steps = (self.first, self.over_a, self.over_b, self.line, self.last)
        if step > 0:
            for copy in steps[step - 1]():
                copy.wait()
        if step == 1:
            for half in range(2):
                rows = pl.ds(half * 2 * NZ * r, 2 * NZ * r)
                self.add(rows, self.got[rows, :])
        elif step == 2:
            self.add(span(at.a * 2 * NZ * r, 2 * NZ * r), self.from_a[...])
        elif step == 3:
            self.add(span((at.a * 2 + at.b) * NZ * r, NZ * r), self.from_b[...])
        elif step == 4:
            total = self.full[at.c, span(((at.a * 2 + at.b) * NZ + at.z) * r, r), :].astype(F32)
            for k in range(NZ - 1):
                total = total + self.from_z[k * r : (k + 1) * r, :].astype(F32)
            self.total[at.c] = total
        if step < 5:
            for copy in steps[step]():
                copy.start()


V_LN1G, V_LN1B, V_QV, V_BOUT, V_LN2G, V_LN2B, V_BFC2, V_BFC1 = 0, 1, 2, 4, 5, 6, 7, 8


def block_body(
    tok, dup, tgt, s_ln1g, s_ln1b, s_qkv, s_qvb, s_out, s_bout, s_ln2g, s_ln2b, s_fc1, s_b1, s_fc2, s_b2,
    out, gin, oqkv, oout, o1, o2, ovec,
    tokb, stage, xs, n1, qkv, att, n2, act, dpre, db2, db1, dos, dmid, probs,
    wqkv, wout, wout_t, w1, w2_t, wt_a, wf,
    c_ln1g, c_ln1b, c_q, c_v, c_bout, c_ln2g, c_ln2b, c_b1, c_b2,
    stat_s, rl_s, ex_s, pq_s, pxq_s, attx, dqkvx, a_g1, a_b1, a_g2, a_b2, tgt_t, gvec, allc, vec_s,
    tail_s, tv, uv, av, bv, zv, f_a, f_b, f_c, f_d, f_v,
    loc_sem, gsem0, gsem1, gsem2, gsem3, rsem_a, rsem_b, rsem_c, rsem_d, rsem_v, ready,
):
    images, seq = dup.shape
    d = tok.shape[1]
    t = seq - 1
    x0 = images * t
    ff = w1.shape[1]
    w = x0 + 128
    n = d // 16
    blocks = d // 128
    at = Place()
    every = range(16)
    pairs = HEADS // 2
    mine = pl.ds(pl.multiple_of(at.c * d, 128), d)
    own = (at.a * 2 + at.b) * NZ + at.z

    def lanes_of(i, count=1):
        return pl.ds(pl.multiple_of(i * t, 128), t * count)

    extra_lanes = pl.ds(x0, 128)

    def load_image(i):
        return jnp.concatenate([stage[b, pl.ds(i, t, stride=images), :] for b in range(blocks)], 1)

    def store_image(i, values):
        for b in range(blocks):
            stage[b, pl.ds(i, t, stride=images), :] = values[:, 128 * b : 128 * (b + 1)]

    def store_last(values):
        for b in range(blocks):
            stage[b, x0:, :] = values[:images, 128 * b : 128 * (b + 1)]

    tok_copy = pltpu.make_async_copy(tok, tokb, loc_sem.at[0])
    tok_copy.start()

    r0, r2, r3 = n + 8, 2 * n, 2 * n + 16
    slots0 = act.at[: 16 * r0, :d]
    slots1 = act.at[16 * r0 : 32 * r0]
    slots2 = act.at[: 16 * r2]
    slots3 = dpre.at[: 16 * r3]
    group = [pl.ds(k * d, d) for k in range(4)]
    later_mine = pl.ds(pl.multiple_of((2 + at.c) * d, 128), d)
    q = s_qkv[...].astype(F32)

    def pair_of(p):
        return jnp.concatenate([q[:, d * k + 128 * p : d * k + 128 * (p + 1)] for k in range(3)], 1)

    vec_s[...] = jnp.zeros_like(vec_s)
    flat = [s_ln1g[...], s_ln1b[...], s_qvb[:n], s_qvb[n:], s_bout[...], s_ln2g[...], s_ln2b[...], s_b2[...]]
    flat += [s_b1[n * k : n * (k + 1)] for k in range(4)]
    for k, line in enumerate(flat):
        lo = 128 * (k // 8)
        vec_s[k % 8 : k % 8 + 1, lo : lo + n] = line.astype(F32).reshape(1, n)
    slots0[span(own * r0, r0), :] = jnp.concatenate([pair_of(0), vec_s[...]], 0).astype(BF16)
    own1, own2, own3 = (span(own * r, r) for r in (r0, r2, r3))
    w_out = s_out[...].astype(F32)
    blank = jnp.zeros((8, d), F32)

    @pl.when(at.c == 0)
    def _():
        f = s_fc1[...].astype(F32)
        slots1[own1, group[0]] = jnp.concatenate([pair_of(1), blank], 0).astype(BF16)
        slots2[own2, group[2]] = jnp.concatenate([f[:, :d], f[:, d : 2 * d]], 0).astype(BF16)
        parts = [f[:, 2 * d : 3 * d], f[:, 3 * d :], w_out[:16]]
        slots3[own3, group[0]] = jnp.concatenate(parts, 0).astype(BF16)

    @pl.when(at.c == 1)
    def _():
        slots1[own1, group[1]] = jnp.concatenate([pair_of(2), blank], 0).astype(BF16)
        slots2[own2, group[3]] = s_fc2[:r2]
        parts = [s_fc2[r2:].astype(F32), w_out[16:], blank]
        slots3[own3, group[1]] = jnp.concatenate(parts, 0).astype(BF16)

    greet(at)
    g0 = Gather(at, slots0, r0, gsem0, False)
    g1 = Gather(at, slots1.at[:, mine], r0, gsem1, True)
    g2 = Gather(at, slots2.at[:, later_mine], r2, gsem2, True)
    g3 = Gather(at, slots3.at[:, mine], r3, gsem3, True)
    g0.go(0)

    tok_copy.wait()
    for b in range(blocks):
        stage[b] = tokb[:, 128 * b : 128 * (b + 1)].astype(F32)

    def statistics(x):
        mu = jnp.mean(x, 0, keepdims=True)
        c = x - mu
        return mu, lax.rsqrt(jnp.mean(c * c, 0, keepdims=True) + EPS)

    def turn(i, carry):
        x = load_image(i).astype(BF16).T
        xs[:, lanes_of(i)] = x
        mu, r = statistics(x.astype(F32))
        stat_s[i, 0:1, :] = mu
        stat_s[i, 1:2, :] = r
        return carry

    lax.fori_loop(0, images // 2, turn, 0)
    g1.go(0)
    lax.fori_loop(images // 2, images, turn, 0)
    last = jnp.concatenate([tokb[x0:, :].astype(F32), jnp.zeros((128 - images, d), F32)], 0)
    x = last.astype(BF16).T
    xs[:, extra_lanes] = x
    mu, r = statistics(x.astype(F32))
    stat_s[images, 0:1, :128] = mu
    stat_s[images, 1:2, :128] = r
    tgt_t[...] = jnp.concatenate([tgt[...], jnp.zeros((128 - images, d), F32)], 0).T
    ones_row = jnp.where(lax.broadcasted_iota(jnp.int32, (16, w), 0) == 0, 1.0, 0.0).astype(BF16)
    n1[d : d + 16, :] = ones_row
    n2[d : d + 16, :] = ones_row
    att[d : d + 16, :] = ones_row
    for ref in (attx, dqkvx, a_g1, a_b1, a_g2, a_b2):
        ref[...] = jnp.zeros_like(ref)
    g2.go(0)
    g0.go(1)
    g0.go(2)
    g3.go(0)
    g1.go(1)
    g0.go(3)
    g1.go(2)
    g2.go(1)

    def slot_of_chip(p):
        px, py, pz = p % 2, (p // 2) % 2, p // 4
        pa = py + at.c * (px - py)
        pb = px + at.c * (py - px)
        return slots0[span(((pa * 2 + pb) * NZ + pz) * r0, r0), :].astype(F32)

    first = [slot_of_chip(p) for p in every]
    for half in range(2):
        rows = [s[n:, 128 * half : 128 * (half + 1)] for s in first]
        allc[half] = jnp.concatenate(rows, 0).T
    lane_ids = lax.broadcasted_iota(jnp.int32, (n, 128), 1)
    ones = jnp.ones((128, 128), BF16)

    def column(ref, entries):
        runs = [jnp.where(lane_ids == 8 * p + k % 8, allc[k // 8, :n, :], 0.0) for p, k in entries]
        ref[...] = mm(jnp.concatenate(runs, 0).astype(BF16), ones)

    column(c_ln1g, [(p, V_LN1G) for p in every])
    column(c_ln1b, [(p, V_LN1B) for p in every])
    column(c_q, [(p, V_QV + k) for p in range(8) for k in range(2)])
    column(c_v, [(p, V_QV + k) for p in range(8, 16) for k in range(2)])

    def put_pair(p, block):
        block = block.astype(BF16)
        wqkv[:, p * d : (p + 1) * d] = block
        wt_a[p // 2, (p % 2) * d : (p % 2 + 1) * d, :] = block.T

    put_pair(0, jnp.concatenate([s[:n] for s in first], 0))

    def unpack(slots, which, lanes, r, lo, hi):
        runs = []
        for p in every:
            s = slot_of(p, which)
            runs.append(slots[r * s : r * (s + 1), lanes].astype(F32)[lo:hi])
        return runs

    def project(p, lanes, count, mu=None, r=None):
        if p == 0:
            u = (xs[:, lanes].astype(F32) - mu) * r
            y = (u * wide(c_ln1g[...], count) + wide(c_ln1b[...], count)).astype(BF16)
            n1[:d, lanes] = y
        else:
            y = n1[:d, lanes]
        y = mm(wt_a[p // 2, (p % 2) * d : (p % 2 + 1) * d, :], y)
        heads = slice(128 * p, 128 * (p + 1))
        query = (y[:128] + wide(c_q[heads, :], count)).astype(BF16) * jnp.asarray(HD**-0.5, BF16)
        value = (y[256:] + wide(c_v[heads, :], count)).astype(BF16)
        qkv[p * d : (p + 1) * d, lanes] = jnp.concatenate([query, y[128:256].astype(BF16), value], 0)

    def rows_of(part, h):
        row = (h // 2) * d + part * 128 + (h % 2) * HD
        return slice(row, row + HD)

    head_lanes = lax.broadcasted_iota(jnp.int32, (HD, 128), 1)

    def pick(ref, rows, i):
        return jnp.sum(jnp.where(head_lanes == i, ref[rows, extra_lanes].astype(F32), 0.0), 1, keepdims=True)

    def row_dot(a, column):
        return jnp.sum(a.astype(F32) * column, 0, keepdims=True)

    def column_dot(a, row):
        return jnp.sum(a.astype(F32) * row, 1, keepdims=True)

    def place_column(ref, rows, i, column):
        ref[rows, :] = jnp.where(head_lanes == i, column, ref[rows, :])

    def score(i, h):
        q, k = (qkv[rows_of(part, h), lanes_of(i)] for part in range(2))
        qx, kx = (pick(qkv, rows_of(part, h), i) for part in range(2))
        return mm(k.T, q), row_dot(q, kx), row_dot(k, qx), jnp.sum(qx * kx, 0, keepdims=True)

    def share(i, h, s, sx, sq, sxq):
        top = jnp.maximum(jnp.max(s, 0, keepdims=True), sx)
        e = jnp.exp(s - top)
        ex = jnp.exp(sx - top)
        rl = 1.0 / (jnp.sum(e, 0, keepdims=True) + ex)
        e = e.astype(BF16)
        probs[i * HEADS + h] = e
        rl_s[i, h : h + 1, :] = rl
        ex_s[i, h : h + 1, :] = ex
        top = jnp.maximum(jnp.max(sq, 1, keepdims=True), sxq)
        eq = jnp.exp(sq - top)
        exq = jnp.exp(sxq - top)
        rlq = 1.0 / (jnp.sum(eq, 1, keepdims=True) + exq)
        pq = eq * rlq
        pxq = exq * rlq
        pq_s[i, h : h + 1, :] = pq
        pxq_s[i, h : h + 1, :] = jnp.broadcast_to(pxq, (1, 128))
        return e, ex, rl, pq, pxq

    def mix(i, h, e, ex, rl, pq, pxq):
        v = qkv[rows_of(2, h), lanes_of(i)]
        vx = pick(qkv, rows_of(2, h), i)
        rows = slice(h * HD, (h + 1) * HD)
        att[rows, lanes_of(i)] = ((mm(v, e) + vx * ex) * rl).astype(BF16)
        place_column(attx, rows, i, column_dot(v, pq) + vx * pxq)

    def attend(units):
        scores = [score(*units[0])]
        shares = []
        for k, unit in enumerate(units):
            if k + 1 < len(units):
                scores.append(score(*units[k + 1]))
            shares.append(share(*unit, *scores[k]))
            if k >= 1:
                mix(*units[k - 1], *shares[k - 1])
        mix(*units[-1], *shares[-1])

    def forward_pair(p, steps):
        if p == 0:

            def project_image(i, carry):
                project(0, lanes_of(i), t, stat_s[i, 0:1, :], stat_s[i, 1:2, :])
                return carry

            lax.fori_loop(0, images, project_image, 0)
            project(0, extra_lanes, 128, stat_s[images, 0:1, :128], stat_s[images, 1:2, :128])
        else:

            def project_images(i, carry):
                project(p, lanes_of(2 * i, 2), 2 * t)
                return carry

            lax.fori_loop(0, images // 2, project_images, 0)
            project(p, extra_lanes, 128)
        for step in steps[0]:
            step()

        def attend_images(i, carry):
            attend([(UNITS * i + k, 2 * p + h) for k in range(UNITS) for h in range(2)])
            for when in range(images // UNITS):

                @pl.when(i == when)
                def _(when=when):
                    for step in steps[1 + when]:
                        step()

            return carry

        lax.fori_loop(0, images // UNITS, attend_images, 0)

    def later(item, step):
        return lambda: item.go(step)

    forward_pair(0, [[later(g3, 1)], [], [later(g1, 3), later(g2, 2)], [], []])
    g1.go(4)
    for k in range(2):
        put_pair(1 + k, jnp.concatenate(unpack(slots1, k, group[k], r0, 0, n), 0))
    forward_pair(1, [[], [later(g3, 2)], [], [later(g2, 3)], []])
    forward_pair(2, [[], [later(g3, 3)], [], [], [later(g2, 4)]])
    att[:d, extra_lanes] = attx[...].astype(BF16)
    column(c_bout, [(p, V_BOUT) for p in every])
    column(c_ln2g, [(p, V_LN2G) for p in every])
    column(c_ln2b, [(p, V_LN2B) for p in every])
    column(c_b2, [(p, V_BFC2) for p in every])
    column(c_b1, [(p, V_BFC1 + k) for p in every for k in range(4)])
    g3.go(4)
    runs = zip(unpack(slots3, 0, group[0], r3, r2, r3), unpack(slots3, 1, group[1], r3, r2, r2 + 8))
    block = jnp.concatenate([part for run in runs for part in run], 0).astype(BF16)
    wout[...] = block
    wout_t[...] = block.T
    for k in range(4):
        slots, lanes, r = (slots2, group[2], r2) if k < 2 else (slots3, group[0], r3)
        block = jnp.concatenate(unpack(slots, 0, lanes, r, (k % 2) * n, (k % 2 + 1) * n), 0).astype(BF16)
        w1[:, k * d : (k + 1) * d] = block
        wf[0, k * d : (k + 1) * d, :] = block.T
    for p in every:
        s = slot_of(p, 1)
        for k, (slots, lanes, r) in enumerate(((slots2, group[3], r2), (slots3, group[1], r3))):
            start = 4 * n * p + r2 * k
            wf[1, start : start + r2, :] = slots[r * s : r * s + r2, lanes]
    w2_t[...] = wf[1].T
    act[ff : ff + 16, :] = ones_row

    def middle(lanes, count):
        return xs[:, lanes].astype(F32) + mm(wout_t[...], att[:d, lanes]) + wide(c_bout[...], count)

    def feed(lanes, count, d_final):
        u, r = normalise(middle(lanes, count))
        y = (u * wide(c_ln2g[...], count) + wide(c_ln2b[...], count)).astype(BF16)
        n2[:d, lanes] = y
        db = d_final.astype(BF16)
        db2[:, lanes] = db
        for j in range(ff // FFB):
            rows = slice(FFB * j, FFB * (j + 1))
            pre = mm(wf[0, rows, :], y) + wide(c_b1[rows, :], count)
            da = mm(wf[1, rows, :], db)
            value, slope = gelu_pair(pre)
            act[rows, lanes] = value.astype(BF16)
            dpre[rows, lanes] = (slope * da).astype(BF16)
        dn = mm(w1[...], dpre[:, lanes])
        a_g2[...] += fold(dn * u)
        a_b2[...] += fold(dn)
        dm = d_final + norm_back(dn, u, r, wide(c_ln2g[...], count))
        dmid[:, lanes] = dm
        low = dm.astype(BF16)
        db1[:, lanes] = low
        dos[:, lanes] = mm(wout[...], low).astype(BF16)

    def keep_row(row):
        position = lax.broadcasted_iota(jnp.int32, row.shape, 1) == 0
        return jnp.where(position, 1.0, 1.0 - row.astype(F32))

    def cotangent(i):
        keep = keep_row(dup[pl.ds(i, 1), :])
        scale = seq * keep[:, :t] / jnp.sum(keep, 1, keepdims=True)
        ids = lax.broadcasted_iota(jnp.int32, (d, 128), 1)
        return jnp.sum(jnp.where(ids == i, tgt_t[...], 0.0), 1, keepdims=True) * scale

    def feed_images(k, carry):
        d_final = jnp.concatenate([cotangent(CHUNK * k + m) for m in range(CHUNK)], 1)
        feed(lanes_of(CHUNK * k, CHUNK), CHUNK * t, d_final)
        return carry

    lax.fori_loop(0, images // CHUNK, feed_images, 0)
    keep_all = keep_row(dup[...])
    scale_x = seq * keep_all[:, t:] / jnp.sum(keep_all, 1, keepdims=True)
    scale_x = jnp.broadcast_to(scale_x, (images, 128))
    scale_x = jnp.concatenate([scale_x, jnp.zeros((128 - images, 128), F32)], 0).T[:1, :]
    feed(extra_lanes, 128, tgt_t[...] * scale_x)

    def put(buf, which, parts, lo=0, step=None):
        for p in every:
            slot = jnp.concatenate([part[n * p + a : n * p + b] for part, a, b in parts], 0).astype(BF16)
            start = step * slot_of(p, which) + lo
            buf[which, start : start + slot.shape[0], :] = slot

    for j in range(ff // 256):
        rows = slice(256 * j, 256 * (j + 1))
        g = mm(act[rows, :], db2[...], NT).astype(BF16)
        for lo in range(256 * j, 256 * (j + 1), 16):
            p, off = lo // (4 * n), lo % (4 * n)
            buf, r = (wf, r2) if off < r2 else (wt_a, r3)
            start = r * slot_of(p, 1) + off % r2
            buf[1, start : start + 16, :] = g[lo - 256 * j : lo - 256 * j + 16]
    g = mm(act[ff : ff + 16, :], db2[...], NT)
    gvec[BFC2 : BFC2 + 1, :d] = g[:1]

    def reducer(full, total, r, sems, width, places):
        refs = []
        for (row, lane), count in zip(places, (16, 8, 4, 3)):
            refs.append(dpre.at[row : row + count * r, lane : lane + width])
        return Reduce(at, full, *refs, total, r, sems)

    ra = reducer(wf.at[:, : 16 * r2], f_a, r2, rsem_a, d, [(k * r2, 0) for k in (0, 16, 24, 28)])
    rb = reducer(wt_a, f_b, r3, rsem_b, d, [(0, d), (16 * r3, d), (0, 2 * d), (4 * r3, 2 * d)])
    rc = reducer(
        wf.at[:, 16 * r2 : 16 * r2 + 16 * r0], f_c, r0, rsem_c, d, [(k * r0, 3 * d) for k in (0, 16, 24, 28)]
    )
    rd = reducer(tail_s, f_d, r2, rsem_d, 128, [(k * r2, 4 * d) for k in (0, 16, 24, 28)])
    rv = Reduce(at, tv, uv, av, bv, zv, f_v, 8, rsem_v)
    gw = mm(att[...], db1[...], NT)
    gvec[BOUT : BOUT + 1, :d] = gw[d : d + 1]
    gw = gw[:d]
    for j in range(2):
        rows = slice(2 * d * j, 2 * d * (j + 1))
        g = mm(n2[...], dpre[rows, :], NT)
        gvec[BFC1 : BFC1 + 1, rows] = g[d : d + 1]
        parts = [(g[:d, :d], 0, n), (g[:d, d:], 0, n)]
        if j == 0:
            put(wf, 0, parts, step=r2)
        else:
            put(wt_a, 0, parts + [(gw, 0, 16)], step=r3)
    for p in every:
        start = r3 * slot_of(p, 1) + r2
        wt_a[1, start : start + 16, :] = jnp.concatenate([gw[n * p + 16 : n * (p + 1)], blank], 0).astype(BF16)

    partners = [at.sibling(), at.along_a(), at.along_b()]
    partners += [at.device(at.x, at.y, at.along_z(step)) for step in range(1, NZ)]
    for k, device in enumerate(partners):
        pl.semaphore_signal(ready.at[min(k, 3)], inc=1, device_id=device, device_id_type=MESH_ID)
    pl.semaphore_wait(ready.at[0], 1)
    ra.go(0)
    rb.go(0)

    def allowed(k):
        return lambda: pl.semaphore_wait(ready.at[k], 1 if k < 3 else NZ - 1)

    def slopes(i, h):
        rows = slice(h * HD, (h + 1) * HD)
        v = qkv[rows_of(2, h), lanes_of(i)]
        vx = pick(qkv, rows_of(2, h), i)
        do = dos[rows, lanes_of(i)].astype(F32) * rl_s[i, h : h + 1, :]
        doq = pick(dos, rows, i)
        dot_o = jnp.sum(do * att[rows, lanes_of(i)].astype(F32), 0, keepdims=True)
        dol = do.astype(BF16)
        dp = mm(v.T, dol)
        return dol, dot_o, dp, row_dot(do, vx), doq, row_dot(v, doq), jnp.sum(vx * doq, 0, keepdims=True)

    def scores_back(i, h, dol, dot_o, dp, dpx, doq, dpq, dpxq):
        p = probs[i * HEADS + h]
        ex = ex_s[i, h : h + 1, :]
        ds = (p.astype(F32) * (dp - dot_o)).astype(BF16)
        dsx = ex * (dpx - dot_o)
        pq = pq_s[i, h : h + 1, :]
        pxq = pxq_s[i, h : h + 1, :1]
        total = jnp.sum(pq * dpq, 1, keepdims=True) + pxq * dpxq
        return dol, p, ex, ds, dsx, doq, pq, pxq, pq * (dpq - total), pxq * (dpxq - total)

    def heads_back(i, h, dol, p, ex, ds, dsx, doq, pq, pxq, dsq, dsxq):
        q, k = (qkv[rows_of(part, h), lanes_of(i)] for part in range(2))
        qx, kx = (pick(qkv, rows_of(part, h), i) for part in range(2))
        scale = HD**-0.5
        dq = (mm(k, ds) + kx * dsx) * scale
        dk = mm(q, ds, NT) + qx * dsq
        dv = mm(dol, p, NT) + doq * pq
        place_column(dqkvx, rows_of(0, h), i, (column_dot(k, dsq) + kx * dsxq) * scale)
        place_column(dqkvx, rows_of(1, h), i, column_dot(q, dsx) + qx * dsxq)
        place_column(dqkvx, rows_of(2, h), i, column_dot(dol, ex) + doq * pxq)
        for part, value in enumerate((dq, dk, dv)):
            qkv[rows_of(part, h), lanes_of(i)] = value.astype(BF16)

    def attend_back(units):
        one = [slopes(*units[0])]
        two = []
        for k, unit in enumerate(units):
            if k + 1 < len(units):
                one.append(slopes(*units[k + 1]))
            two.append(scores_back(*unit, *one[k]))
            if k >= 1:
                heads_back(*units[k - 1], *two[k - 1])
        heads_back(*units[-1], *two[-1])

    def run_steps(i, steps):
        for when, todo in steps:

            @pl.when(i == when)
            def _(todo=todo):
                for step in todo:
                    step()

    def back_first(i, carry):
        attend_back([(UNITS1 * i + k, h) for k in range(UNITS1) for h in range(4)])
        run_steps(i, (
            (2, [allowed(1), later(ra, 1)]),
            (3, [later(rb, 1)]),
            (7, [allowed(2), later(ra, 2)]),
        ))
        return carry

    lax.fori_loop(0, images // UNITS1, back_first, 0)
    qkv[: 2 * d, extra_lanes] = dqkvx[: 2 * d, :].astype(BF16)

    gain1, bias1 = c_ln1g[:, :1], c_ln1b[:, :1]

    def weight_sums(first_pair, count):
        rows = slice(first_pair * d, (first_pair + count) * d)
        g = mm(n1[...], qkv[rows, :], NT)
        sums = g[d : d + 1]
        weight = wqkv[:, rows].astype(F32)
        a_g1[...] += fold(weight * (g[:d] - bias1 * sums))
        a_b1[...] += fold(weight * sums)
        for m in range(count):
            p = first_pair + m
            gvec[BQKV : BQKV + 1, 128 * p : 128 * (p + 1)] = sums[:, m * d : m * d + 128]
            gvec[BQKV : BQKV + 1, 2 * d + 128 * p : 2 * d + 128 * (p + 1)] = sums[:, m * d + 256 : (m + 1) * d]
        return g[:d]

    g = weight_sums(0, 2)
    for p in range(2):
        put(wf, p, [(g[:, p * d : (p + 1) * d], 0, n)], 16 * r2, r0)
    rc.go(0)

    def back_second(i, carry):
        attend_back([(UNITS2 * i + k, h) for k in range(UNITS2) for h in range(4, 6)])
        run_steps(i, (
            (0, [allowed(3), later(ra, 3), later(rb, 2)]),
            (1, [later(rc, 1)]),
            (3, [later(rb, 3)]),
        ))
        return carry

    lax.fori_loop(0, images // UNITS2, back_second, 0)
    qkv[2 * d :, extra_lanes] = dqkvx[2 * d :, :].astype(BF16)
    g = weight_sums(2, 1)
    put(tail_s, 0, [(g[:, :128], 0, n), (g[:, 128:256], 0, n)], step=r2)
    put(tail_s, 1, [(g[:, 256:], 0, n), (jnp.zeros((d, 128), F32), 0, n)], step=r2)
    scale1 = a_g1[...] * (1.0 / c_ln1g[...])
    for row, acc in ((LN1G, scale1), (LN1B, a_b1[...]), (LN2G, a_g2[...]), (LN2B, a_b2[...])):
        gvec[row : row + 1, :d] = jnp.sum(acc.T, 0, keepdims=True)
    tv[...] = jnp.zeros_like(tv)
    for p in every:
        s0 = 8 * slot_of(p, 0)
        tv[0, s0 : s0 + 8, :n] = gvec[:, n * p : n * (p + 1)]
        s1 = 8 * slot_of(p, 1)
        lo = 2 * n * p if p < 8 else 2 * d + 2 * n * (p - 8)
        parts = [gvec[BQKV : BQKV + 1, lo + n * k : lo + n * (k + 1)] for k in range(2)]
        lo = 4 * n * p
        parts += [gvec[BFC1 : BFC1 + 1, lo + n * k : lo + n * (k + 1)] for k in range(4)]
        tv[1, s1 : s1 + 6, :n] = jnp.concatenate(parts, 0)
    rd.go(0)
    rv.go(0)
    ra.go(4)

    def finals(lanes, count):
        return middle(lanes, count) + mm(w2_t[...], act[:ff, lanes]) + wide(c_b2[...], count)

    def final_images(k, carry):
        final = finals(lanes_of(CHUNK * k, CHUNK), CHUNK * t)
        for m in range(CHUNK):
            store_image(CHUNK * k + m, final[:, m * t : (m + 1) * t].T)
        run_steps(k * CHUNK, (
            (2, [later(rc, 2), later(rd, 1), later(rv, 1)]),
            (6, [later(rb, 4), later(rc, 3)]),
        ))
        return carry

    lax.fori_loop(0, images // CHUNK, final_images, 0)
    store_last(finals(extra_lanes, 128).T)
    for b in range(blocks):
        tokb[:, 128 * b : 128 * (b + 1)] = stage[b].astype(BF16)
    out_copy = pltpu.make_async_copy(tokb, out, loc_sem.at[0])
    out_copy.start()

    def finish(lanes, count, mu, r):
        u = (xs[:, lanes].astype(F32) - mu) * r
        dn = mm(wqkv[...], qkv[:, lanes])
        return dmid[:, lanes] + norm_back(dn, u, r, wide(c_ln1g[...], count))

    def finish_images(k, carry):
        mu, r = (
            jnp.concatenate([stat_s[CHUNK * k + m, row : row + 1, :] for m in range(CHUNK)], 1) for row in range(2)
        )
        grad = finish(lanes_of(CHUNK * k, CHUNK), CHUNK * t, mu, r)
        for m in range(CHUNK):
            store_image(CHUNK * k + m, grad[:, m * t : (m + 1) * t].T)
        run_steps(k * CHUNK, (
            (0, [later(rd, 2), later(rv, 2)]),
            (6, [later(rd, 3), later(rv, 3)]),
        ))
        return carry

    lax.fori_loop(0, images // CHUNK, finish_images, 0)
    store_last(finish(extra_lanes, 128, stat_s[images, 0:1, :128], stat_s[images, 1:2, :128]).T)
    copies = [
        pltpu.make_async_copy(stage.at[b], gin.at[:, pl.ds(128 * b, 128)], loc_sem.at[1 + b]) for b in range(blocks)
    ]
    for copy in copies:
        copy.start()
    rc.go(4)
    ra.go(5)
    rb.go(5)
    o1[...] = jnp.concatenate([f[0, n * k : n * (k + 1)] for f in (f_a, f_b) for k in range(2)], 1)
    o2[:r2] = f_a[1]
    o2[r2:] = f_b[1, :r2]
    oout[:16] = f_b[0, r2:]
    oout[16:] = f_b[1, r2 : r2 + 8]
    rd.go(4)
    rv.go(4)
    rc.go(5)
    for k in range(3):
        for p in range(2):
            oqkv[:, d * k + 128 * p : d * k + 128 * (p + 1)] = f_c[p, :n, 128 * k : 128 * (k + 1)]
    rd.go(5)
    rv.go(5)
    for k in range(3):
        oqkv[:, d * k + 256 : d * (k + 1)] = f_d[k // 2, (k % 2) * n : (k % 2 + 1) * n]
    ovec[...] = f_v[...]
    for copy in copies:
        copy.wait()
    out_copy.wait()


def block_call(tok, dup, tgt, weights):
    images, seq = dup.shape
    d = tok.shape[1]
    n = d // 16
    ff = 4 * d
    t = seq - 1
    w = images * t + 128
    vm = pltpu.VMEM
    dma = pltpu.SemaphoreType.DMA
    sd = jax.ShapeDtypeStruct
    column = vm((d, 128), F32)
    scratch = [
        vm((seq * images, d), BF16),
        vm((d // 128, seq * images, 128), F32),
        vm((d, w), BF16),
        vm((d + 16, w), BF16),
        vm((3 * d, w), BF16),
        vm((d + 16, w), BF16),
        vm((d + 16, w), BF16),
        vm((ff + 16, w), BF16),
        vm((ff, w), BF16),
        vm((d, w), BF16),
        vm((d, w), BF16),
        vm((d, w), BF16),
        vm((d, w), F32),
        vm((images * HEADS, t, t), BF16),
        vm((d, 3 * d), BF16),
        vm((d, d), BF16), vm((d, d), BF16),
        vm((d, ff), BF16),
        vm((d, ff), BF16),
        vm((2, 32 * n + 256, d), BF16),
        vm((2, ff, d), BF16),
        column, column, column, column, column, column, column, vm((ff, 128), F32), column,
        vm((images + 1, 8, t), F32),
        vm((images, 8, t), F32),
        vm((images, 8, t), F32),
        vm((images, 8, t), F32),
        vm((images, 8, 128), F32),
        column,
        vm((3 * d, 128), F32),
        column, column, column, column,
        column,
        vm((8, ff), F32),
        vm((2, 128, 128), F32),
        vm((8, d), F32),
        vm((2, 32 * n, 128), BF16),
        vm((2, 128, 128), F32),
    ]
    scratch += [vm((slots * 8, 128), F32) for slots in (16, 8, 4, 3)]
    scratch += [vm((2, r, d), F32) for r in (2 * n, 2 * n + 16, n + 8)] + [vm((2, 2 * n, 128), F32), vm((2, 8, 128), F32)]
    scratch += [dma((4,))] + [dma((2, 7))] * 9 + [pltpu.SemaphoreType.REGULAR((4,))]
    spec = pl.BlockSpec(memory_space=pltpu.VMEM)
    any_spec = pl.BlockSpec(memory_space=pl.ANY)
    return pl.pallas_call(
        block_body,
        out_shape=(
            sd(tok.shape, BF16), sd(tok.shape, F32),
            sd((n, 3 * d), F32), sd((n, d), F32), sd((n, ff), F32), sd((4 * n, d), F32), sd((2, 8, 128), F32),
        ),
        in_specs=[any_spec] + [spec] * 14,
        out_specs=(any_spec, any_spec) + (spec,) * 5,
        scratch_shapes=scratch,
        compiler_params=pltpu.CompilerParams(
            collective_id=0, has_side_effects=True, vmem_limit_bytes=64 * 1024 * 1024
        ),
        name="block16",
    )(tok, dup, tgt, *weights)


def deliver_body(out, gin, gqkv, gout, g1, g2, gv, *refs):
    o_out, o_gin, o_ln1g, o_ln1b, o_qkv, o_qvb, o_w, o_bout, o_ln2g, o_ln2b, o_fc1, o_b1, o_fc2, o_b2 = refs[:14]
    buf_out, buf_gin, sems = refs[14:]
    n = gqkv.shape[0]
    pieces = []
    for k, (src, buf, dst) in enumerate(((out, buf_out, o_out), (gin, buf_gin, o_gin))):
        count = 1 + 3 * k
        size = (src.shape[0] // count) // 16 * 16
        for m in range(count):
            rows = pl.ds(m * size, size if m < count - 1 else src.shape[0] - m * size)
            s = k + m
            pieces.append((
                pltpu.make_async_copy(src.at[rows], buf.at[rows], sems.at[0, s]),
                pltpu.make_async_copy(buf.at[rows], dst.at[rows], sems.at[1, s]),
            ))
    for load, store in pieces:
        load.start()
    o_qkv[...] = gqkv[...]
    o_w[...] = gout[...]
    o_fc1[...] = g1[...]
    o_fc2[...] = g2[...]
    for ref, row in ((o_ln1g, LN1G), (o_ln1b, LN1B), (o_bout, BOUT), (o_ln2g, LN2G), (o_ln2b, LN2B), (o_b2, BFC2)):
        ref[...] = gv[0, row, :n]
    o_qvb[...] = jnp.concatenate([gv[1, k, :n] for k in range(2)], 0)
    o_b1[...] = jnp.concatenate([gv[1, 2 + k, :n] for k in range(4)], 0)
    for load, store in pieces:
        load.wait()
        store.start()
    for load, store in pieces:
        store.wait()


def deliver_call(out, gin, gqkv, gout, g1, g2, gv):
    n, d = gout.shape
    sd = jax.ShapeDtypeStruct
    spec = pl.BlockSpec(memory_space=pltpu.VMEM)
    any_spec = pl.BlockSpec(memory_space=pl.ANY)
    vec = sd((n,), F32)
    return pl.pallas_call(
        deliver_body,
        out_shape=(
            sd(out.shape, BF16), sd(gin.shape, F32), vec, vec, sd((n, 3 * d), F32), sd((2 * n,), F32),
            sd((n, d), F32), vec, vec, vec, sd((n, 4 * d), F32), sd((4 * n,), F32), sd((4 * n, d), F32), vec,
        ),
        in_specs=[any_spec, any_spec] + [spec] * 5,
        out_specs=(any_spec, any_spec) + (spec,) * 12,
        scratch_shapes=[
            pltpu.VMEM(out.shape, BF16), pltpu.VMEM(gin.shape, F32), pltpu.SemaphoreType.DMA((2, 6)),
        ],
        compiler_params=pltpu.CompilerParams(vmem_limit_bytes=64 * 1024 * 1024),
        name="deliver",
    )(out, gin, gqkv, gout, g1, g2, gv)


def gather_all(value):
    return lax.all_gather(value, "fsdp", axis=0, tiled=True)


def vectors(full):
    ln1_gain, ln1_bias, qv_bias, out_bias, ln2_gain, ln2_bias, fc1_bias, fc2_bias = full
    d = ln1_gain.shape[0]
    bias = jnp.concatenate([qv_bias[:d], jnp.zeros((d,), qv_bias.dtype), qv_bias[d:]])
    rows = (ln1_gain, ln1_bias, bias, out_bias, ln2_gain, ln2_bias, fc1_bias, fc2_bias)
    width = fc1_bias.shape[0]
    return jnp.stack([jnp.pad(row.astype(F32), (0, width - row.shape[0])) for row in rows], 0)


def per_device(tokens, duplicate, targets, *weights, block16):
    images, seq, d = tokens.shape
    rows = tokens.transpose(1, 0, 2).reshape(seq * images, d)
    back = lambda v: v.reshape(seq, images, d).transpose(1, 0, 2)
    if block16:
        results = deliver_call(*block_call(rows, duplicate, targets, weights))
        return (back(results[0]), back(results[1])) + tuple(results[2:])

    (
        ln1_gain, ln1_bias, qkv_weight, qv_bias, out_weight, out_bias,
        ln2_gain, ln2_bias, fc1_weight, fc1_bias, fc2_weight, fc2_bias,
    ) = weights
    small = (ln1_gain, ln1_bias, qv_bias, out_bias, ln2_gain, ln2_bias, fc1_bias, fc2_bias)
    wqkv, wout, w1, w2 = map(gather_all, (qkv_weight, out_weight, fc1_weight, fc2_weight))
    vec = vectors(tuple(map(gather_all, small)))
    out, gin, gqkv, gout, g1, g2, gvec = compute(rows, duplicate, targets, vec, wqkv, wout, w1, w2)

    def scatter(value):
        value = lax.psum_scatter(value.astype(F32), "fsdp", scatter_dimension=0, tiled=True)
        return lax.psum(value, "dp")

    gqkv, gout, g1, g2 = map(scatter, (gqkv, gout, g1, g2))
    gvec = lax.psum(gvec, ("fsdp", "dp"))
    p = lax.axis_index("fsdp")

    def shard(value, whole_size):
        count = whole_size // lax.axis_size("fsdp")
        return lax.dynamic_slice(value, (p * count,), (count,))

    qv_grad = jnp.concatenate([gvec[2, :d], gvec[2, 2 * d : 3 * d]])
    return (
        back(out), back(gin),
        shard(gvec[0], d), shard(gvec[1], d), gqkv, shard(qv_grad, 2 * d), gout, shard(gvec[3], d),
        shard(gvec[4], d), shard(gvec[5], d), g1, shard(gvec[6], 4 * d), g2, shard(gvec[7], d),
    )


def solution(mesh):
    block16 = mesh.shape["fsdp"] == 16 and mesh.shape["dp"] == 2
    both = ("fsdp", "dp")
    vector, matrix = P("fsdp"), P("fsdp", None)
    weights = (vector, vector, matrix, vector, matrix, vector, vector, vector, matrix, vector, matrix, vector)
    return jax.shard_map(
        functools.partial(per_device, block16=block16),
        mesh=mesh,
        in_specs=(P(both, None, None), P(both, None), P(both, None)) + weights,
        out_specs=(P(both, None, None), P(both, None, None)) + weights,
        check_vma=False,
    )
```

```python
import functools
import jax
import jax.numpy as jnp
from jax import lax
from jax.experimental import pallas as pl
from jax.experimental.pallas import tpu as pltpu
from jax.sharding import PartitionSpec as P

HEADS = 6
HD = 64
EPS = 1e-06
F32 = jnp.float32
BF16 = jnp.bfloat16

NN = (((1,), (0,)), ((), ()))
NT = (((1,), (1,)), ((), ()))


def mm(a, b, dims=NN):
    return lax.dot_general(a, b, dims, preferred_element_type=F32)


def normalise(v):
    mu = jnp.mean(v, 0, keepdims=True)
    c = v - mu
    r = lax.rsqrt(jnp.mean(c * c, 0, keepdims=True) + EPS)
    return c * r, r


def norm_back(dn, u, r, gain):
    e = dn * gain
    me = jnp.mean(e, 0, keepdims=True)
    meu = jnp.mean(e * u, 0, keepdims=True)
    return r * (e - me - u * meu)


def fold(v):
    lanes = v.shape[1]
    total = v[:, :128]
    for k in range(1, lanes // 128):
        total = total + v[:, 128 * k : 128 * (k + 1)]
    return total


def wide(col, lanes):
    if lanes == 128:
        return col
    return jnp.concatenate([col] * (lanes // 128), 1)


def gelu_pair(x):
    z = x * 0.7071067811865476
    bell = jnp.exp(-(z * z))
    tail = lax.erf(z)
    half = 0.5 * x
    return half + half * tail, 0.5 + (0.5 * tail + (x * 0.3989422804014327) * bell)


LN1G, LN1B, BQKV, BOUT, LN2G, LN2B, BFC1, BFC2 = range(8)


def to_columns(vec, row, count):
    return jnp.broadcast_to(vec[row : row + 1, :count], (128, count)).T


def compute_body(
    tok, dup, tgt, vec, wqkv, wout, w1, w2,
    out, gin, gqkv, gout, g1, g2, gvec,
    xs, n1, qkv, att, n2, act, dpre, db2, db1, dos, dmid, probs,
    wqkv_t, wout_t, w1_t, w2_t,
    c_ln1g, c_ln1b, c_bqkv, c_bout, c_ln2g, c_ln2b, c_b1, c_b2,
    rl_s, ex_s, exq_s, rlx_s, exx_s, attx, dqkvx, a_g1, a_b1, a_g2, a_b2, tgt_t, stage, gin_sem,
):
    images, seq = dup.shape
    d = tok.shape[1]
    t = seq - 1
    x0 = images * t
    ff = w1.shape[1]
    w = x0 + 128
    dqkv = act.at[: 3 * d]

    blocks = d // 128

    def load_image(i):
        return jnp.concatenate([stage[b, pl.ds(i, t, stride=images), :] for b in range(blocks)], 1)

    def store_image(i, values):
        for b in range(blocks):
            stage[b, pl.ds(i, t, stride=images), :] = values[:, 128 * b : 128 * (b + 1)]

    def store_last(values):
        for b in range(blocks):
            stage[b, x0:, :] = values[:images, 128 * b : 128 * (b + 1)]

    def lanes_of(i):
        return pl.ds(pl.multiple_of(i * t, 128), t)

    extra_lanes = pl.ds(x0, 128)

    tok_copy = pltpu.make_async_copy(tok, out, gin_sem.at[0])
    tok_copy.start()
    tok_copy.wait()
    wqkv_t[...] = wqkv[...].T
    wout_t[...] = wout[...].T
    w1_t[...] = w1[...].T
    w2_t[...] = w2[...].T
    c_ln1g[...] = to_columns(vec, LN1G, d)
    c_ln1b[...] = to_columns(vec, LN1B, d)
    c_bqkv[...] = to_columns(vec, BQKV, 3 * d)
    c_bout[...] = to_columns(vec, BOUT, d)
    c_ln2g[...] = to_columns(vec, LN2G, d)
    c_ln2b[...] = to_columns(vec, LN2B, d)
    c_b1[...] = to_columns(vec, BFC1, ff)
    c_b2[...] = to_columns(vec, BFC2, d)
    tgt_t[...] = jnp.concatenate([tgt[...], jnp.zeros((128 - images, d), F32)], 0).T
    ones_row = jnp.where(lax.broadcasted_iota(jnp.int32, (16, w), 0) == 0, 1.0, 0.0).astype(BF16)
    n1[d : d + 16, :] = ones_row
    n2[d : d + 16, :] = ones_row
    att[d : d + 16, :] = ones_row
    act[ff : ff + 16, :] = ones_row
    attx[...] = jnp.zeros_like(attx)
    dqkvx[...] = jnp.zeros_like(dqkvx)
    for acc in (a_g1, a_b1, a_g2, a_b2):
        acc[...] = jnp.zeros_like(acc)

    def project(x_t, lanes, count):
        x = x_t.astype(F32)
        xs[:, lanes] = x_t
        u, r = normalise(x)
        n = (u * wide(c_ln1g[...], count) + wide(c_ln1b[...], count)).astype(BF16)
        n1[:d, lanes] = n
        for k in range(3):
            rows = slice(k * d, (k + 1) * d)
            y = mm(wqkv_t[rows, :], n) + wide(c_bqkv[rows, :], count)
            y = y.astype(BF16)
            if k == 0:
                y = y * jnp.asarray(HD**-0.5, BF16)
            qkv[rows, lanes] = y

    def project_image(i, carry):
        project(load_image(i).astype(BF16).T, lanes_of(i), t)
        return carry

    for b in range(blocks):
        stage[b] = out[:, 128 * b : 128 * (b + 1)].astype(F32)

    lax.fori_loop(0, images, project_image, 0)
    last = jnp.concatenate([out[x0:, :].astype(F32), jnp.zeros((128 - images, d), F32)], 0)
    project(last.astype(BF16).T, extra_lanes, 128)

    lane_ids = lax.broadcasted_iota(jnp.int32, (HD, 128), 1)

    def pick(ref, row, i):
        block = ref[row : row + HD, extra_lanes].astype(F32)
        return jnp.sum(jnp.where(lane_ids == i, block, 0.0), 1, keepdims=True)

    def attend_image(i, carry):
        lanes = lanes_of(i)
        for h in range(HEADS):
            r0 = h * HD
            q = qkv[r0 : r0 + HD, lanes]
            k = qkv[d + r0 : d + r0 + HD, lanes]
            v = qkv[2 * d + r0 : 2 * d + r0 + HD, lanes]
            qx, kx, vx = pick(qkv, r0, i), pick(qkv, d + r0, i), pick(qkv, 2 * d + r0, i)
            s = mm(k.T, q)
            sx = jnp.sum(q.astype(F32) * kx, 0, keepdims=True)
            top = jnp.maximum(jnp.max(s, 0, keepdims=True), sx)
            e = jnp.exp(s - top)
            ex = jnp.exp(sx - top)
            rl = 1.0 / (jnp.sum(e, 0, keepdims=True) + ex)
            e = e.astype(BF16)
            probs[i * HEADS + h] = e
            o = (mm(v, e) + vx * ex) * rl
            att[r0 : r0 + HD, lanes] = o.astype(BF16)
            rl_s[i, h : h + 1, :] = rl
            ex_s[i, h : h + 1, :] = ex
            sq = jnp.sum(k.astype(F32) * qx, 0, keepdims=True)
            sxx = jnp.sum(kx * qx, 0, keepdims=True)
            topx = jnp.maximum(jnp.max(sq, 1, keepdims=True), sxx)
            eq = jnp.exp(sq - topx)
            exx = jnp.exp(sxx - topx)
            rlx = 1.0 / (jnp.sum(eq, 1, keepdims=True) + exx)
            ox = (jnp.sum(v.astype(F32) * eq, 1, keepdims=True) + vx * exx) * rlx
            attx[r0 : r0 + HD, :] = jnp.where(lane_ids == i, ox, attx[r0 : r0 + HD, :])
            exq_s[i, h : h + 1, :] = eq
            rlx_s[i, h : h + 1, :] = jnp.broadcast_to(rlx, (1, 128))
            exx_s[i, h : h + 1, :] = jnp.broadcast_to(exx, (1, 128))
        return carry

    lax.fori_loop(0, images, attend_image, 0)
    att[:d, extra_lanes] = attx[...].astype(BF16)

    def feed(lanes, count, d_final):
        mid = xs[:, lanes].astype(F32) + mm(wout_t[...], att[:d, lanes]) + wide(c_bout[...], count)
        u, r = normalise(mid)
        n = (u * wide(c_ln2g[...], count) + wide(c_ln2b[...], count)).astype(BF16)
        n2[:d, lanes] = n
        db = d_final.astype(BF16)
        db2[:, lanes] = db
        for j in range(ff // 256):
            rows = slice(256 * j, 256 * (j + 1))
            pre = mm(w1_t[rows, :], n) + wide(c_b1[rows, :], count)
            da = mm(w2[rows, :], db)
            value, slope = gelu_pair(pre)
            act[rows, lanes] = value.astype(BF16)
            dpre[rows, lanes] = (slope * da).astype(BF16)
        final = mid + mm(w2_t[...], act[:ff, lanes]) + wide(c_b2[...], count)
        dn = mm(w1[...], dpre[:, lanes])
        a_g2[...] += fold(dn * u)
        a_b2[...] += fold(dn)
        dm = d_final + norm_back(dn, u, r, wide(c_ln2g[...], count))
        dmid[:, lanes] = dm
        low = dm.astype(BF16)
        db1[:, lanes] = low
        dos[:, lanes] = mm(wout[...], low).astype(BF16)
        return final.T

    def keep_row(row):
        first = lax.broadcasted_iota(jnp.int32, row.shape, 1) == 0
        return jnp.where(first, 1.0, 1.0 - row.astype(F32))

    def feed_image(i, carry):
        keep = keep_row(dup[pl.ds(i, 1), :])
        count = jnp.sum(keep, 1, keepdims=True)
        scale = seq * keep[:, :t] / count
        ids = lax.broadcasted_iota(jnp.int32, (d, 128), 1)
        target = jnp.sum(jnp.where(ids == i, tgt_t[...], 0.0), 1, keepdims=True)
        store_image(i, feed(lanes_of(i), t, target * scale))
        return carry

    lax.fori_loop(0, images, feed_image, 0)
    keep_all = keep_row(dup[...])
    scale_x = seq * keep_all[:, t:] / jnp.sum(keep_all, 1, keepdims=True)
    scale_x = jnp.broadcast_to(scale_x, (images, 128))
    scale_x = jnp.concatenate([scale_x, jnp.zeros((128 - images, 128), F32)], 0).T[:1, :]
    store_last(feed(extra_lanes, 128, tgt_t[...] * scale_x))
    for b in range(blocks):
        out[:, 128 * b : 128 * (b + 1)] = stage[b].astype(BF16)

    for j in range(ff // 256):
        rows = slice(256 * j, 256 * (j + 1))
        g = mm(n2[...], dpre[rows, :], NT)
        g1[:, rows] = g[:d].astype(BF16)
        gvec[BFC1 : BFC1 + 1, rows] = g[d : d + 1]
        g2[rows, :] = mm(act[rows, :], db2[...], NT).astype(BF16)
    g = mm(act[ff : ff + 16, :], db2[...], NT)
    gvec[BFC2 : BFC2 + 1, :d] = g[:1]

    def attend_back(i, carry):
        lanes = lanes_of(i)
        for h in range(HEADS):
            r0 = h * HD
            q = qkv[r0 : r0 + HD, lanes]
            k = qkv[d + r0 : d + r0 + HD, lanes]
            v = qkv[2 * d + r0 : 2 * d + r0 + HD, lanes]
            qx, kx, vx = pick(qkv, r0, i), pick(qkv, d + r0, i), pick(qkv, 2 * d + r0, i)
            rl = rl_s[i, h : h + 1, :]
            ex = ex_s[i, h : h + 1, :]
            do = dos[r0 : r0 + HD, lanes].astype(F32) * rl
            dot_o = jnp.sum(do * att[r0 : r0 + HD, lanes].astype(F32), 0, keepdims=True)
            dol = do.astype(BF16)
            p = probs[i * HEADS + h]
            ds = (p.astype(F32) * (mm(v.T, dol) - dot_o)).astype(BF16)
            dsx = ex * (jnp.sum(do * vx, 0, keepdims=True) - dot_o)
            dq = mm(k, ds) + kx * dsx
            dk = mm(q, ds, NT)
            dv = mm(dol, p, NT)
            qf = q.astype(F32)
            kf = k.astype(F32)
            vf = v.astype(F32)
            dkx = jnp.sum(qf * dsx, 1, keepdims=True)
            dvx = jnp.sum(do * ex, 1, keepdims=True)
            eq = exq_s[i, h : h + 1, :]
            rlx = rlx_s[i, h : h + 1, :1]
            exx = exx_s[i, h : h + 1, :1]
            dox = pick(dos, r0, i) * rlx
            dotx = jnp.sum(dox * pick(att, r0, i), 0, keepdims=True)
            dsq = eq * (jnp.sum(vf * dox, 0, keepdims=True) - dotx)
            dsxx = exx * (jnp.sum(vx * dox, 0, keepdims=True) - dotx)
            dqx = jnp.sum(kf * dsq, 1, keepdims=True) + kx * dsxx
            dk = dk + qx * dsq
            dv = dv + dox * eq
            dkx = dkx + qx * dsxx
            dvx = dvx + dox * exx
            scale = HD**-0.5
            for base, main, tail in ((0, dq * scale, dqx * scale), (d, dk, dkx), (2 * d, dv, dvx)):
                rows = slice(base + r0, base + r0 + HD)
                dqkv[rows, lanes] = main.astype(BF16)
                dqkvx[rows, :] = jnp.where(lane_ids == i, tail, dqkvx[rows, :])
        return carry

    lax.fori_loop(0, images, attend_back, 0)
    dqkv[:, extra_lanes] = dqkvx[...].astype(BF16)

    for k in range(3):
        rows = slice(k * d, (k + 1) * d)
        g = mm(n1[...], dqkv[rows, :], NT)
        gqkv[:, rows] = g[:d].astype(BF16)
        gvec[BQKV : BQKV + 1, rows] = g[d : d + 1]
    g = mm(att[...], db1[...], NT)
    gout[...] = g[:d].astype(BF16)
    gvec[BOUT : BOUT + 1, :d] = g[d : d + 1]

    def finish(lanes, count):
        u, r = normalise(xs[:, lanes].astype(F32))
        dn = mm(wqkv[...], dqkv[:, lanes])
        a_g1[...] += fold(dn * u)
        a_b1[...] += fold(dn)
        return (dmid[:, lanes] + norm_back(dn, u, r, wide(c_ln1g[...], count))).T

    def finish_image(i, carry):
        store_image(i, finish(lanes_of(i), t))
        return carry

    lax.fori_loop(0, images, finish_image, 0)
    store_last(finish(extra_lanes, 128))
    copies = [
        pltpu.make_async_copy(stage.at[b], gin.at[:, pl.ds(128 * b, 128)], gin_sem.at[b]) for b in range(blocks)
    ]
    for copy in copies:
        copy.start()

    for row, acc in ((LN1G, a_g1), (LN1B, a_b1), (LN2G, a_g2), (LN2B, a_b2)):
        gvec[row : row + 1, :d] = jnp.sum(acc[...].T, 0, keepdims=True)
    for copy in copies:
        copy.wait()


def compute(tok, dup, tgt, vec, wqkv, wout, w1, w2):
    images, seq = dup.shape
    d = tok.shape[1]
    ff = w1.shape[1]
    t = seq - 1
    w = images * t + 128
    vm = pltpu.VMEM
    scratch = [
        vm((d, w), BF16),
        vm((d + 16, w), BF16),
        vm((3 * d, w), BF16),
        vm((d + 16, w), BF16),
        vm((d + 16, w), BF16),
        vm((ff + 16, w), BF16),
        vm((ff, w), BF16),
        vm((d, w), BF16),
        vm((d, w), BF16),
        vm((d, w), BF16),
        vm((d, w), F32),
        vm((images * HEADS, t, t), BF16),
        vm((3 * d, d), BF16),
        vm((d, d), BF16),
        vm((ff, d), BF16),
        vm((d, ff), BF16),
        vm((d, 128), F32), vm((d, 128), F32), vm((3 * d, 128), F32), vm((d, 128), F32),
        vm((d, 128), F32), vm((d, 128), F32), vm((ff, 128), F32), vm((d, 128), F32),
        vm((images, 8, t), F32),
        vm((images, 8, t), F32),
        vm((images, 8, t), F32),
        vm((images, 8, 128), F32),
        vm((images, 8, 128), F32),
        vm((d, 128), F32),
        vm((3 * d, 128), F32),
        vm((d, 128), F32), vm((d, 128), F32), vm((d, 128), F32), vm((d, 128), F32),
        vm((d, 128), F32),
        vm((d // 128, images * seq, 128), F32),
        pltpu.SemaphoreType.DMA((d // 128,)),
    ]
    outs = (
        jax.ShapeDtypeStruct(tok.shape, BF16),
        jax.ShapeDtypeStruct(tok.shape, F32),
        jax.ShapeDtypeStruct((d, 3 * d), BF16),
        jax.ShapeDtypeStruct((d, d), BF16),
        jax.ShapeDtypeStruct((d, ff), BF16),
        jax.ShapeDtypeStruct((ff, d), BF16),
        jax.ShapeDtypeStruct((8, ff), F32),
    )
    spec = pl.BlockSpec(memory_space=pltpu.VMEM)
    return pl.pallas_call(
        compute_body,
        out_shape=outs,
        in_specs=[pl.BlockSpec(memory_space=pl.ANY)] + [spec] * 7,
        out_specs=(spec, pl.BlockSpec(memory_space=pl.ANY)) + (spec,) * 5,
        scratch_shapes=scratch,
        compiler_params=pltpu.CompilerParams(vmem_limit_bytes=64 * 1024 * 1024),
        name="block",
    )(tok, dup, tgt, vec, wqkv, wout, w1, w2)

MESH_ID = pl.DeviceIdType.MESH
NZ = 4
UNITS = 2
UNITS1 = 1
UNITS2 = 2
CHUNK = 2
FFB = 128


class Place:
    def __init__(self):
        p = lax.axis_index("fsdp")
        self.p = p
        self.c = lax.axis_index("dp")
        self.x = lax.rem(p, 2)
        self.y = lax.rem(lax.div(p, 2), 2)
        self.z = lax.div(p, 4)
        self.a = self.y + self.c * (self.x - self.y)
        self.b = self.x + self.c * (self.y - self.x)

    def device(self, x, y, z):
        return ((z * 2 + y) * 2 + x, self.c)

    def along_a(self):
        c = self.c
        return self.device(self.x + c * (1 - 2 * self.x), self.y + (1 - c) * (1 - 2 * self.y), self.z)

    def along_b(self):
        c = self.c
        return self.device(self.x + (1 - c) * (1 - 2 * self.x), self.y + c * (1 - 2 * self.y), self.z)

    def along_z(self, step):
        return lax.rem(self.z + step, NZ)

    def sibling(self):
        return (self.p, 1 - self.c)

    def everyone(self):
        return [(lax.rem(self.p + k, 16), self.c) for k in range(1, 16)]


def slot_of(p, group):
    x, y, z = p % 2, (p // 2) % 2, p // 4
    a, b = (y, x) if group == 0 else (x, y)
    return (a * 2 + b) * NZ + z


def greet(at):
    barrier = pltpu.get_barrier_semaphore()
    others = [at.sibling()] + at.everyone()
    for device in others:
        pl.semaphore_signal(barrier, inc=1, device_id=device, device_id_type=MESH_ID)


def remote(src, dst, sems, k, device):
    return pltpu.make_async_remote_copy(
        src_ref=src, dst_ref=dst, send_sem=sems.at[0, k], recv_sem=sems.at[1, k],
        device_id=device, device_id_type=MESH_ID,
    )


def span(start, size):
    return pl.ds(pl.multiple_of(start, size), size)


class Gather:
    def __init__(self, at, buf, r, sems, swap):
        self.at, self.buf, self.r, self.sems, self.shared = at, buf, r, sems, swap

    def part(self, rows, k, device):
        piece = self.buf.at[rows]
        return remote(piece, piece, self.sems, k, device)

    def line(self):
        at, r = self.at, self.r
        rows = span(((at.a * 2 + at.b) * NZ + at.z) * r, r)
        return [
            self.part(rows, step - 1, at.device(at.x, at.y, at.along_z(step))) for step in range(1, NZ)
        ]

    def over_b(self):
        at, r = self.at, self.r
        return [self.part(span((at.a * 2 + at.b) * NZ * r, NZ * r), 3, at.along_b())]

    def over_a(self):
        at, r = self.at, self.r
        return [self.part(span(at.a * 2 * NZ * r, 2 * NZ * r), 4, at.along_a())]

    def swap(self):
        return [remote(self.buf, self.buf, self.sems, 5, self.at.sibling())] if self.shared else []

    def go(self, step):
        steps = (self.line, self.over_b, self.over_a, self.swap)
        if step > 0:
            for copy in steps[step - 1]():
                copy.wait()
        if step < 4:
            for copy in steps[step]():
                copy.start()


class Spread:
    def __init__(self, at, buf, r, sems):
        self.at, self.buf, self.r, self.sems = at, buf, r, sems

    def direct(self):
        at, r = self.at, self.r
        piece = self.buf.at[span((at.c * 16 + at.p) * r, r)]
        return [remote(piece, piece, self.sems, k, device) for k, device in enumerate(at.everyone())]

    def swap(self):
        piece = self.buf.at[span(self.at.c * 16 * self.r, 16 * self.r)]
        return [remote(piece, piece, self.sems, 15, self.at.sibling())]

    def go(self, step):
        steps = (self.direct, self.swap)
        if step > 0:
            for copy in steps[step - 1]():
                copy.wait()
        if step < 2:
            for copy in steps[step]():
                copy.start()


class Reduce:
    def __init__(self, at, full, got, from_a, from_b, from_z, total, r, sems):
        self.at, self.full, self.got = at, full, got
        self.from_a, self.from_b, self.from_z, self.total = from_a, from_b, from_z, total
        self.r, self.sems = r, sems

    def first(self):
        return [remote(self.full.at[1 - self.at.c], self.got, self.sems, 0, self.at.sibling())]

    def over_a(self):
        at, r = self.at, self.r
        rows = span((1 - at.a) * 2 * NZ * r, 2 * NZ * r)
        return [remote(self.full.at[at.c, rows], self.from_a, self.sems, 1, at.along_a())]

    def over_b(self):
        at, r = self.at, self.r
        rows = span((at.a * 2 + 1 - at.b) * NZ * r, NZ * r)
        return [remote(self.full.at[at.c, rows], self.from_b, self.sems, 2, at.along_b())]

    def line(self):
        at, r = self.at, self.r
        copies = []
        for step in range(1, NZ):
            other = at.along_z(step)
            rows = span(((at.a * 2 + at.b) * NZ + other) * r, r)
            copies.append(
                remote(self.full.at[at.c, rows], self.from_z.at[pl.ds((step - 1) * r, r)], self.sems, 2 + step, at.device(at.x, at.y, other))
            )
        return copies

    def last(self):
        piece = self.total.at[self.at.c]
        return [remote(piece, piece, self.sems, 6, self.at.sibling())]

    def add(self, rows, values):
        ref = self.full.at[self.at.c, rows]
        ref[...] = (ref[...].astype(F32) + values.astype(F32)).astype(ref.dtype)

    def go(self, step):
        at, r = self.at, self.r
        steps = (self.first, self.over_a, self.over_b, self.line, self.last)
        if step > 0:
            for copy in steps[step - 1]():
                copy.wait()
        if step == 1:
            for half in range(2):
                rows = pl.ds(half * 2 * NZ * r, 2 * NZ * r)
                self.add(rows, self.got[rows, :])
        elif step == 2:
            self.add(span(at.a * 2 * NZ * r, 2 * NZ * r), self.from_a[...])
        elif step == 3:
            self.add(span((at.a * 2 + at.b) * NZ * r, NZ * r), self.from_b[...])
        elif step == 4:
            total = self.full[at.c, span(((at.a * 2 + at.b) * NZ + at.z) * r, r), :].astype(F32)
            for k in range(NZ - 1):
                total = total + self.from_z[k * r : (k + 1) * r, :].astype(F32)
            self.total[at.c] = total
        if step < 5:
            for copy in steps[step]():
                copy.start()


V_LN1G, V_LN1B, V_QV, V_BOUT, V_LN2G, V_LN2B, V_BFC2, V_BFC1 = 0, 1, 2, 4, 5, 6, 7, 8


def block_body(
    tok, dup, tgt, s_ln1g, s_ln1b, s_qkv, s_qvb, s_out, s_bout, s_ln2g, s_ln2b, s_fc1, s_b1, s_fc2, s_b2,
    out, gin, oqkv, oout, o1, o2, ovec,
    tokb, stage, xs, n1, qkv, att, n2, act, dpre, db2, db1, dos, dmid, probs,
    wqkv, wout, wout_t, w1, w2_t, wt_a, wf,
    c_ln1g, c_ln1b, c_q, c_v, c_bout, c_ln2g, c_ln2b, c_b1, c_b2,
    stat_s, rl_s, ex_s, pq_s, pxq_s, attx, dqkvx, a_g1, a_b1, a_g2, a_b2, tgt_t, gvec, allc, vec_s,
    tail_s, tv, uv, av, bv, zv, f_a, f_b, f_c, f_d, f_v,
    loc_sem, gsem0, gsem1, gsem2, gsem3, rsem_a, rsem_b, rsem_c, rsem_d, rsem_v, ready,
):
    images, seq = dup.shape
    d = tok.shape[1]
    t = seq - 1
    x0 = images * t
    ff = w1.shape[1]
    w = x0 + 128
    n = d // 16
    blocks = d // 128
    at = Place()
    every = range(16)
    pairs = HEADS // 2
    mine = pl.ds(pl.multiple_of(at.c * d, 128), d)
    own = (at.a * 2 + at.b) * NZ + at.z

    def lanes_of(i, count=1):
        return pl.ds(pl.multiple_of(i * t, 128), t * count)

    extra_lanes = pl.ds(x0, 128)

    def load_image(i):
        return jnp.concatenate([stage[b, pl.ds(i, t, stride=images), :] for b in range(blocks)], 1)

    def store_image(i, values):
        for b in range(blocks):
            stage[b, pl.ds(i, t, stride=images), :] = values[:, 128 * b : 128 * (b + 1)]

    def store_last(values):
        for b in range(blocks):
            stage[b, x0:, :] = values[:images, 128 * b : 128 * (b + 1)]

    greet(at)
    tok_copy = pltpu.make_async_copy(tok, tokb, loc_sem.at[0])
    tok_copy.start()

    r0, r2, r3 = n + 8, 2 * n, 2 * n + 16
    slots0 = act.at[: 16 * r0, :d]
    slots1 = act.at[16 * r0 : 32 * r0]
    slots2 = act.at[: 16 * r2]
    slots3 = dpre.at[: 16 * r3]
    group = [pl.ds(k * d, d) for k in range(4)]
    later_mine = pl.ds(pl.multiple_of((2 + at.c) * d, 128), d)
    q = s_qkv[...].astype(F32)

    def pair_of(p):
        return jnp.concatenate([q[:, d * k + 128 * p : d * k + 128 * (p + 1)] for k in range(3)], 1)

    vec_s[...] = jnp.zeros_like(vec_s)
    flat = [s_ln1g[...], s_ln1b[...], s_qvb[:n], s_qvb[n:], s_bout[...], s_ln2g[...], s_ln2b[...], s_b2[...]]
    flat += [s_b1[n * k : n * (k + 1)] for k in range(4)]
    for k, line in enumerate(flat):
        lo = 128 * (k // 8)
        vec_s[k % 8 : k % 8 + 1, lo : lo + n] = line.astype(F32).reshape(1, n)
    slot = jnp.concatenate([pair_of(0), vec_s[...]], 0)
    half = r0 // 2
    slots0[span((at.c * 16 + at.p) * half, half), :] = jnp.where(at.c == 0, slot[:half], slot[half:]).astype(BF16)
    own1, own2, own3 = (span(own * r, r) for r in (r0, r2, r3))
    w_out = s_out[...].astype(F32)
    blank = jnp.zeros((8, d), F32)

    @pl.when(at.c == 0)
    def _():
        f = s_fc1[...].astype(F32)
        slots1[own1, group[0]] = jnp.concatenate([pair_of(1), blank], 0).astype(BF16)
        slots2[own2, group[2]] = jnp.concatenate([f[:, :d], f[:, d : 2 * d]], 0).astype(BF16)
        parts = [f[:, 2 * d : 3 * d], f[:, 3 * d :], w_out[:16]]
        slots3[own3, group[0]] = jnp.concatenate(parts, 0).astype(BF16)

    @pl.when(at.c == 1)
    def _():
        slots1[own1, group[1]] = jnp.concatenate([pair_of(2), blank], 0).astype(BF16)
        slots2[own2, group[3]] = s_fc2[:r2]
        parts = [s_fc2[r2:].astype(F32), w_out[16:], blank]
        slots3[own3, group[1]] = jnp.concatenate(parts, 0).astype(BF16)

    pl.semaphore_wait(pltpu.get_barrier_semaphore(), 16)
    g0 = Spread(at, slots0, half, gsem0)
    g1 = Gather(at, slots1.at[:, mine], r0, gsem1, True)
    g2 = Gather(at, slots2.at[:, later_mine], r2, gsem2, True)
    g3 = Gather(at, slots3.at[:, mine], r3, gsem3, True)
    g0.go(0)

    tok_copy.wait()
    for b in range(blocks):
        stage[b] = tokb[:, 128 * b : 128 * (b + 1)].astype(F32)

    def statistics(x):
        mu = jnp.mean(x, 0, keepdims=True)
        c = x - mu
        return mu, lax.rsqrt(jnp.mean(c * c, 0, keepdims=True) + EPS)

    def turn(i, carry):
        x = load_image(i).astype(BF16).T
        xs[:, lanes_of(i)] = x
        mu, r = statistics(x.astype(F32))
        stat_s[i, 0:1, :] = mu
        stat_s[i, 1:2, :] = r
        return carry

    lax.fori_loop(0, images // 2, turn, 0)
    g1.go(0)
    lax.fori_loop(images // 2, images, turn, 0)
    last = jnp.concatenate([tokb[x0:, :].astype(F32), jnp.zeros((128 - images, d), F32)], 0)
    x = last.astype(BF16).T
    xs[:, extra_lanes] = x
    mu, r = statistics(x.astype(F32))
    stat_s[images, 0:1, :128] = mu
    stat_s[images, 1:2, :128] = r
    tgt_t[...] = jnp.concatenate([tgt[...], jnp.zeros((128 - images, d), F32)], 0).T
    ones_row = jnp.where(lax.broadcasted_iota(jnp.int32, (16, w), 0) == 0, 1.0, 0.0).astype(BF16)
    n1[d : d + 16, :] = ones_row
    n2[d : d + 16, :] = ones_row
    att[d : d + 16, :] = ones_row
    for ref in (attx, dqkvx, a_g1, a_b1, a_g2, a_b2):
        ref[...] = jnp.zeros_like(ref)
    g0.go(1)
    g1.go(1)
    g2.go(0)
    g0.go(2)
    g3.go(0)

    def slot_of_chip(p):
        parts = [slots0[(16 * k + p) * half : (16 * k + p + 1) * half, :].astype(F32) for k in range(2)]
        return jnp.concatenate(parts, 0)

    first = [slot_of_chip(p) for p in every]
    for half in range(2):
        rows = [s[n:, 128 * half : 128 * (half + 1)] for s in first]
        allc[half] = jnp.concatenate(rows, 0).T
    lane_ids = lax.broadcasted_iota(jnp.int32, (n, 128), 1)
    ones = jnp.ones((128, 128), BF16)

    def column(ref, entries):
        runs = [jnp.where(lane_ids == 8 * p + k % 8, allc[k // 8, :n, :], 0.0) for p, k in entries]
        ref[...] = mm(jnp.concatenate(runs, 0).astype(BF16), ones)

    column(c_ln1g, [(p, V_LN1G) for p in every])
    column(c_ln1b, [(p, V_LN1B) for p in every])
    column(c_q, [(p, V_QV + k) for p in range(8) for k in range(2)])
    column(c_v, [(p, V_QV + k) for p in range(8, 16) for k in range(2)])

    def put_pair(p, block):
        block = block.astype(BF16)
        wqkv[:, p * d : (p + 1) * d] = block
        wt_a[p // 2, (p % 2) * d : (p % 2 + 1) * d, :] = block.T

    put_pair(0, jnp.concatenate([s[:n] for s in first], 0))

    def unpack(slots, which, lanes, r, lo, hi):
        runs = []
        for p in every:
            s = slot_of(p, which)
            runs.append(slots[r * s : r * (s + 1), lanes].astype(F32)[lo:hi])
        return runs

    def project(p, lanes, count, mu=None, r=None):
        if p == 0:
            u = (xs[:, lanes].astype(F32) - mu) * r
            y = (u * wide(c_ln1g[...], count) + wide(c_ln1b[...], count)).astype(BF16)
            n1[:d, lanes] = y
        else:
            y = n1[:d, lanes]
        y = mm(wt_a[p // 2, (p % 2) * d : (p % 2 + 1) * d, :], y)
        heads = slice(128 * p, 128 * (p + 1))
        query = (y[:128] + wide(c_q[heads, :], count)).astype(BF16) * jnp.asarray(HD**-0.5, BF16)
        value = (y[256:] + wide(c_v[heads, :], count)).astype(BF16)
        qkv[p * d : (p + 1) * d, lanes] = jnp.concatenate([query, y[128:256].astype(BF16), value], 0)

    def rows_of(part, h):
        row = (h // 2) * d + part * 128 + (h % 2) * HD
        return slice(row, row + HD)

    head_lanes = lax.broadcasted_iota(jnp.int32, (HD, 128), 1)

    def pick(ref, rows, i):
        return jnp.sum(jnp.where(head_lanes == i, ref[rows, extra_lanes].astype(F32), 0.0), 1, keepdims=True)

    def row_dot(a, column):
        return jnp.sum(a.astype(F32) * column, 0, keepdims=True)

    def column_dot(a, row):
        return jnp.sum(a.astype(F32) * row, 1, keepdims=True)

    def place_column(ref, rows, i, column):
        ref[rows, :] = jnp.where(head_lanes == i, column, ref[rows, :])

    def score(i, h):
        q, k = (qkv[rows_of(part, h), lanes_of(i)] for part in range(2))
        qx, kx = (pick(qkv, rows_of(part, h), i) for part in range(2))
        return mm(k.T, q), row_dot(q, kx), row_dot(k, qx), jnp.sum(qx * kx, 0, keepdims=True)

    def share(i, h, s, sx, sq, sxq):
        top = jnp.maximum(jnp.max(s, 0, keepdims=True), sx)
        e = jnp.exp(s - top)
        ex = jnp.exp(sx - top)
        rl = 1.0 / (jnp.sum(e, 0, keepdims=True) + ex)
        e = e.astype(BF16)
        probs[i * HEADS + h] = e
        rl_s[i, h : h + 1, :] = rl
        ex_s[i, h : h + 1, :] = ex
        top = jnp.maximum(jnp.max(sq, 1, keepdims=True), sxq)
        eq = jnp.exp(sq - top)
        exq = jnp.exp(sxq - top)
        rlq = 1.0 / (jnp.sum(eq, 1, keepdims=True) + exq)
        pq = eq * rlq
        pxq = exq * rlq
        pq_s[i, h : h + 1, :] = pq
        pxq_s[i, h : h + 1, :] = jnp.broadcast_to(pxq, (1, 128))
        return e, ex, rl, pq, pxq

    def mix(i, h, e, ex, rl, pq, pxq):
        v = qkv[rows_of(2, h), lanes_of(i)]
        vx = pick(qkv, rows_of(2, h), i)
        rows = slice(h * HD, (h + 1) * HD)
        att[rows, lanes_of(i)] = ((mm(v, e) + vx * ex) * rl).astype(BF16)
        place_column(attx, rows, i, column_dot(v, pq) + vx * pxq)

    def attend(units):
        scores = [score(*units[0])]
        shares = []
        for k, unit in enumerate(units):
            if k + 1 < len(units):
                scores.append(score(*units[k + 1]))
            shares.append(share(*unit, *scores[k]))
            if k >= 1:
                mix(*units[k - 1], *shares[k - 1])
        mix(*units[-1], *shares[-1])

    def forward_pair(p, steps):
        if p == 0:

            def project_image(i, carry):
                project(0, lanes_of(i), t, stat_s[i, 0:1, :], stat_s[i, 1:2, :])
                return carry

            lax.fori_loop(0, images, project_image, 0)
            project(0, extra_lanes, 128, stat_s[images, 0:1, :128], stat_s[images, 1:2, :128])
        else:

            def project_images(i, carry):
                project(p, lanes_of(2 * i, 2), 2 * t)
                return carry

            lax.fori_loop(0, images // 2, project_images, 0)
            project(p, extra_lanes, 128)
        for step in steps[0]:
            step()

        def attend_images(i, carry):
            attend([(UNITS * i + k, 2 * p + h) for k in range(UNITS) for h in range(2)])
            for when in range(images // UNITS):

                @pl.when(i == when)
                def _(when=when):
                    for step in steps[1 + when]:
                        step()

            return carry

        lax.fori_loop(0, images // UNITS, attend_images, 0)

    def later(item, step):
        return lambda: item.go(step)

    forward_pair(0, [[later(g1, 2), later(g2, 1)], [], [later(g3, 1)], [], [later(g1, 3), later(g2, 2)]])
    g1.go(4)
    for k in range(2):
        put_pair(1 + k, jnp.concatenate(unpack(slots1, k, group[k], r0, 0, n), 0))
    forward_pair(1, [[], [later(g3, 2)], [], [later(g2, 3)], []])
    forward_pair(2, [[], [later(g3, 3)], [], [], [later(g2, 4)]])
    att[:d, extra_lanes] = attx[...].astype(BF16)
    column(c_bout, [(p, V_BOUT) for p in every])
    column(c_ln2g, [(p, V_LN2G) for p in every])
    column(c_ln2b, [(p, V_LN2B) for p in every])
    column(c_b2, [(p, V_BFC2) for p in every])
    column(c_b1, [(p, V_BFC1 + k) for p in every for k in range(4)])
    g3.go(4)
    runs = zip(unpack(slots3, 0, group[0], r3, r2, r3), unpack(slots3, 1, group[1], r3, r2, r2 + 8))
    block = jnp.concatenate([part for run in runs for part in run], 0).astype(BF16)
    wout[...] = block
    wout_t[...] = block.T
    for k in range(4):
        slots, lanes, r = (slots2, group[2], r2) if k < 2 else (slots3, group[0], r3)
        block = jnp.concatenate(unpack(slots, 0, lanes, r, (k % 2) * n, (k % 2 + 1) * n), 0).astype(BF16)
        w1[:, k * d : (k + 1) * d] = block
        wf[0, k * d : (k + 1) * d, :] = block.T
    for p in every:
        s = slot_of(p, 1)
        for k, (slots, lanes, r) in enumerate(((slots2, group[3], r2), (slots3, group[1], r3))):
            start = 4 * n * p + r2 * k
            wf[1, start : start + r2, :] = slots[r * s : r * s + r2, lanes]
    w2_t[...] = wf[1].T
    act[ff : ff + 16, :] = ones_row

    def middle(lanes, count):
        return xs[:, lanes].astype(F32) + mm(wout_t[...], att[:d, lanes]) + wide(c_bout[...], count)

    def feed(lanes, count, d_final):
        u, r = normalise(middle(lanes, count))
        y = (u * wide(c_ln2g[...], count) + wide(c_ln2b[...], count)).astype(BF16)
        n2[:d, lanes] = y
        db = d_final.astype(BF16)
        db2[:, lanes] = db
        for j in range(ff // FFB):
            rows = slice(FFB * j, FFB * (j + 1))
            pre = mm(wf[0, rows, :], y) + wide(c_b1[rows, :], count)
            da = mm(wf[1, rows, :], db)
            value, slope = gelu_pair(pre)
            act[rows, lanes] = value.astype(BF16)
            dpre[rows, lanes] = (slope * da).astype(BF16)
        dn = mm(w1[...], dpre[:, lanes])
        a_g2[...] += fold(dn * u)
        a_b2[...] += fold(dn)
        dm = d_final + norm_back(dn, u, r, wide(c_ln2g[...], count))
        dmid[:, lanes] = dm
        low = dm.astype(BF16)
        db1[:, lanes] = low
        dos[:, lanes] = mm(wout[...], low).astype(BF16)

    def keep_row(row):
        position = lax.broadcasted_iota(jnp.int32, row.shape, 1) == 0
        return jnp.where(position, 1.0, 1.0 - row.astype(F32))

    def cotangent(i):
        keep = keep_row(dup[pl.ds(i, 1), :])
        scale = seq * keep[:, :t] / jnp.sum(keep, 1, keepdims=True)
        ids = lax.broadcasted_iota(jnp.int32, (d, 128), 1)
        return jnp.sum(jnp.where(ids == i, tgt_t[...], 0.0), 1, keepdims=True) * scale

    def feed_images(k, carry):
        d_final = jnp.concatenate([cotangent(CHUNK * k + m) for m in range(CHUNK)], 1)
        feed(lanes_of(CHUNK * k, CHUNK), CHUNK * t, d_final)
        return carry

    lax.fori_loop(0, images // CHUNK, feed_images, 0)
    keep_all = keep_row(dup[...])
    scale_x = seq * keep_all[:, t:] / jnp.sum(keep_all, 1, keepdims=True)
    scale_x = jnp.broadcast_to(scale_x, (images, 128))
    scale_x = jnp.concatenate([scale_x, jnp.zeros((128 - images, 128), F32)], 0).T[:1, :]
    feed(extra_lanes, 128, tgt_t[...] * scale_x)

    def put(buf, which, parts, lo=0, step=None):
        for p in every:
            slot = jnp.concatenate([part[n * p + a : n * p + b] for part, a, b in parts], 0).astype(BF16)
            start = step * slot_of(p, which) + lo
            buf[which, start : start + slot.shape[0], :] = slot

    for j in range(ff // 256):
        rows = slice(256 * j, 256 * (j + 1))
        g = mm(act[rows, :], db2[...], NT).astype(BF16)
        for lo in range(256 * j, 256 * (j + 1), 16):
            p, off = lo // (4 * n), lo % (4 * n)
            buf, r = (wf, r2) if off < r2 else (wt_a, r3)
            start = r * slot_of(p, 1) + off % r2
            buf[1, start : start + 16, :] = g[lo - 256 * j : lo - 256 * j + 16]
    g = mm(act[ff : ff + 16, :], db2[...], NT)
    gvec[BFC2 : BFC2 + 1, :d] = g[:1]

    def reducer(full, total, r, sems, width, places):
        refs = []
        for (row, lane), count in zip(places, (16, 8, 4, 3)):
            refs.append(dpre.at[row : row + count * r, lane : lane + width])
        return Reduce(at, full, *refs, total, r, sems)

    ra = reducer(wf.at[:, : 16 * r2], f_a, r2, rsem_a, d, [(k * r2, 0) for k in (0, 16, 24, 28)])
    rb = reducer(wt_a, f_b, r3, rsem_b, d, [(0, d), (16 * r3, d), (0, 2 * d), (4 * r3, 2 * d)])
    rc = reducer(
        wf.at[:, 16 * r2 : 16 * r2 + 16 * r0], f_c, r0, rsem_c, d, [(k * r0, 3 * d) for k in (0, 16, 24, 28)]
    )
    rd = reducer(tail_s, f_d, r2, rsem_d, 128, [(k * r2, 4 * d) for k in (0, 16, 24, 28)])
    rv = Reduce(at, tv, uv, av, bv, zv, f_v, 8, rsem_v)
    gw = mm(att[...], db1[...], NT)
    gvec[BOUT : BOUT + 1, :d] = gw[d : d + 1]
    gw = gw[:d]
    for j in range(2):
        rows = slice(2 * d * j, 2 * d * (j + 1))
        g = mm(n2[...], dpre[rows, :], NT)
        gvec[BFC1 : BFC1 + 1, rows] = g[d : d + 1]
        parts = [(g[:d, :d], 0, n), (g[:d, d:], 0, n)]
        if j == 0:
            put(wf, 0, parts, step=r2)
        else:
            put(wt_a, 0, parts + [(gw, 0, 16)], step=r3)
    for p in every:
        start = r3 * slot_of(p, 1) + r2
        wt_a[1, start : start + 16, :] = jnp.concatenate([gw[n * p + 16 : n * (p + 1)], blank], 0).astype(BF16)

    partners = [at.sibling(), at.along_a(), at.along_b()]
    partners += [at.device(at.x, at.y, at.along_z(step)) for step in range(1, NZ)]
    for k, device in enumerate(partners):
        pl.semaphore_signal(ready.at[min(k, 3)], inc=1, device_id=device, device_id_type=MESH_ID)
    pl.semaphore_wait(ready.at[0], 1)
    ra.go(0)
    rb.go(0)

    def allowed(k):
        return lambda: pl.semaphore_wait(ready.at[k], 1 if k < 3 else NZ - 1)

    def slopes(i, h):
        rows = slice(h * HD, (h + 1) * HD)
        v = qkv[rows_of(2, h), lanes_of(i)]
        vx = pick(qkv, rows_of(2, h), i)
        do = dos[rows, lanes_of(i)].astype(F32) * rl_s[i, h : h + 1, :]
        doq = pick(dos, rows, i)
        dot_o = jnp.sum(do * att[rows, lanes_of(i)].astype(F32), 0, keepdims=True)
        dol = do.astype(BF16)
        dp = mm(v.T, dol)
        return dol, dot_o, dp, row_dot(do, vx), doq, row_dot(v, doq), jnp.sum(vx * doq, 0, keepdims=True)

    def scores_back(i, h, dol, dot_o, dp, dpx, doq, dpq, dpxq):
        p = probs[i * HEADS + h]
        ex = ex_s[i, h : h + 1, :]
        ds = (p.astype(F32) * (dp - dot_o)).astype(BF16)
        dsx = ex * (dpx - dot_o)
        pq = pq_s[i, h : h + 1, :]
        pxq = pxq_s[i, h : h + 1, :1]
        total = jnp.sum(pq * dpq, 1, keepdims=True) + pxq * dpxq
        return dol, p, ex, ds, dsx, doq, pq, pxq, pq * (dpq - total), pxq * (dpxq - total)

    def heads_back(i, h, dol, p, ex, ds, dsx, doq, pq, pxq, dsq, dsxq):
        q, k = (qkv[rows_of(part, h), lanes_of(i)] for part in range(2))
        qx, kx = (pick(qkv, rows_of(part, h), i) for part in range(2))
        scale = HD**-0.5
        dq = (mm(k, ds) + kx * dsx) * scale
        dk = mm(q, ds, NT) + qx * dsq
        dv = mm(dol, p, NT) + doq * pq
        place_column(dqkvx, rows_of(0, h), i, (column_dot(k, dsq) + kx * dsxq) * scale)
        place_column(dqkvx, rows_of(1, h), i, column_dot(q, dsx) + qx * dsxq)
        place_column(dqkvx, rows_of(2, h), i, column_dot(dol, ex) + doq * pxq)
        for part, value in enumerate((dq, dk, dv)):
            qkv[rows_of(part, h), lanes_of(i)] = value.astype(BF16)

    def attend_back(units):
        one = [slopes(*units[0])]
        two = []
        for k, unit in enumerate(units):
            if k + 1 < len(units):
                one.append(slopes(*units[k + 1]))
            two.append(scores_back(*unit, *one[k]))
            if k >= 1:
                heads_back(*units[k - 1], *two[k - 1])
        heads_back(*units[-1], *two[-1])

    def run_steps(i, steps):
        for when, todo in steps:

            @pl.when(i == when)
            def _(todo=todo):
                for step in todo:
                    step()

    def back_first(i, carry):
        attend_back([(UNITS1 * i + k, h) for k in range(UNITS1) for h in range(4)])
        run_steps(i, (
            (3, [allowed(1), later(ra, 1)]),
            (4, [later(rb, 1)]),
        ))
        return carry

    lax.fori_loop(0, images // UNITS1, back_first, 0)
    pl.semaphore_wait(ready.at[2], 1)
    ra.go(2)
    qkv[: 2 * d, extra_lanes] = dqkvx[: 2 * d, :].astype(BF16)

    gain1, bias1 = c_ln1g[:, :1], c_ln1b[:, :1]

    def weight_sums(first_pair, count):
        rows = slice(first_pair * d, (first_pair + count) * d)
        g = mm(n1[...], qkv[rows, :], NT)
        sums = g[d : d + 1]
        weight = wqkv[:, rows].astype(F32)
        a_g1[...] += fold(weight * (g[:d] - bias1 * sums))
        a_b1[...] += fold(weight * sums)
        for m in range(count):
            p = first_pair + m
            gvec[BQKV : BQKV + 1, 128 * p : 128 * (p + 1)] = sums[:, m * d : m * d + 128]
            gvec[BQKV : BQKV + 1, 2 * d + 128 * p : 2 * d + 128 * (p + 1)] = sums[:, m * d + 256 : (m + 1) * d]
        return g[:d]

    g = weight_sums(0, 2)
    for p in range(2):
        put(wf, p, [(g[:, p * d : (p + 1) * d], 0, n)], 16 * r2, r0)
    rc.go(0)

    def back_second(i, carry):
        attend_back([(UNITS2 * i + k, h) for k in range(UNITS2) for h in range(4, 6)])
        run_steps(i, (
            (0, [allowed(3), later(ra, 3)]),
            (1, [later(rb, 2), later(rc, 1)]),
        ))
        return carry

    lax.fori_loop(0, images // UNITS2, back_second, 0)
    qkv[2 * d :, extra_lanes] = dqkvx[2 * d :, :].astype(BF16)
    g = weight_sums(2, 1)
    put(tail_s, 0, [(g[:, :128], 0, n), (g[:, 128:256], 0, n)], step=r2)
    put(tail_s, 1, [(g[:, 256:], 0, n), (jnp.zeros((d, 128), F32), 0, n)], step=r2)
    scale1 = a_g1[...] * (1.0 / c_ln1g[...])
    for row, acc in ((LN1G, scale1), (LN1B, a_b1[...]), (LN2G, a_g2[...]), (LN2B, a_b2[...])):
        gvec[row : row + 1, :d] = jnp.sum(acc.T, 0, keepdims=True)
    tv[...] = jnp.zeros_like(tv)
    for p in every:
        s0 = 8 * slot_of(p, 0)
        tv[0, s0 : s0 + 8, :n] = gvec[:, n * p : n * (p + 1)]
        s1 = 8 * slot_of(p, 1)
        lo = 2 * n * p if p < 8 else 2 * d + 2 * n * (p - 8)
        parts = [gvec[BQKV : BQKV + 1, lo + n * k : lo + n * (k + 1)] for k in range(2)]
        lo = 4 * n * p
        parts += [gvec[BFC1 : BFC1 + 1, lo + n * k : lo + n * (k + 1)] for k in range(4)]
        tv[1, s1 : s1 + 6, :n] = jnp.concatenate(parts, 0)
    rd.go(0)
    rv.go(0)
    ra.go(4)
    rb.go(3)

    def finals(lanes, count):
        return middle(lanes, count) + mm(w2_t[...], act[:ff, lanes]) + wide(c_b2[...], count)

    def final_images(k, carry):
        final = finals(lanes_of(CHUNK * k, CHUNK), CHUNK * t)
        for m in range(CHUNK):
            store_image(CHUNK * k + m, final[:, m * t : (m + 1) * t].T)
        run_steps(k * CHUNK, (
            (0, [later(rd, 1), later(rv, 1)]),
            (2, [later(rc, 2)]),
            (6, [later(rd, 2), later(rv, 2)]),
        ))
        return carry

    lax.fori_loop(0, images // CHUNK, final_images, 0)
    store_last(finals(extra_lanes, 128).T)
    for b in range(blocks):
        tokb[:, 128 * b : 128 * (b + 1)] = stage[b].astype(BF16)
    out_copy = pltpu.make_async_copy(tokb, out, loc_sem.at[0])
    out_copy.start()

    def finish(lanes, count, mu, r):
        u = (xs[:, lanes].astype(F32) - mu) * r
        dn = mm(wqkv[...], qkv[:, lanes])
        return dmid[:, lanes] + norm_back(dn, u, r, wide(c_ln1g[...], count))

    def finish_images(k, carry):
        mu, r = (
            jnp.concatenate([stat_s[CHUNK * k + m, row : row + 1, :] for m in range(CHUNK)], 1) for row in range(2)
        )
        grad = finish(lanes_of(CHUNK * k, CHUNK), CHUNK * t, mu, r)
        for m in range(CHUNK):
            store_image(CHUNK * k + m, grad[:, m * t : (m + 1) * t].T)
        run_steps(k * CHUNK, (
            (0, [later(rc, 3)]),
            (2, [later(rb, 4)]),
            (4, [later(rd, 3), later(rv, 3)]),
        ))
        return carry

    lax.fori_loop(0, images // CHUNK, finish_images, 0)
    store_last(finish(extra_lanes, 128, stat_s[images, 0:1, :128], stat_s[images, 1:2, :128]).T)
    copies = [
        pltpu.make_async_copy(stage.at[b], gin.at[:, pl.ds(128 * b, 128)], loc_sem.at[1 + b]) for b in range(blocks)
    ]
    for copy in copies:
        copy.start()
    rc.go(4)
    ra.go(5)
    rb.go(5)
    o1[...] = jnp.concatenate([f[0, n * k : n * (k + 1)] for f in (f_a, f_b) for k in range(2)], 1)
    o2[:r2] = f_a[1]
    o2[r2:] = f_b[1, :r2]
    oout[:16] = f_b[0, r2:]
    oout[16:] = f_b[1, r2 : r2 + 8]
    rd.go(4)
    rv.go(4)
    rc.go(5)
    for k in range(3):
        for p in range(2):
            oqkv[:, d * k + 128 * p : d * k + 128 * (p + 1)] = f_c[p, :n, 128 * k : 128 * (k + 1)]
    rd.go(5)
    rv.go(5)
    for k in range(3):
        oqkv[:, d * k + 256 : d * (k + 1)] = f_d[k // 2, (k % 2) * n : (k % 2 + 1) * n]
    ovec[...] = f_v[...]
    for copy in copies:
        copy.wait()
    out_copy.wait()


def block_call(tok, dup, tgt, weights):
    images, seq = dup.shape
    d = tok.shape[1]
    n = d // 16
    ff = 4 * d
    t = seq - 1
    w = images * t + 128
    vm = pltpu.VMEM
    dma = pltpu.SemaphoreType.DMA
    sd = jax.ShapeDtypeStruct
    column = vm((d, 128), F32)
    scratch = [
        vm((seq * images, d), BF16),
        vm((d // 128, seq * images, 128), F32),
        vm((d, w), BF16),
        vm((d + 16, w), BF16),
        vm((3 * d, w), BF16),
        vm((d + 16, w), BF16),
        vm((d + 16, w), BF16),
        vm((ff + 16, w), BF16),
        vm((ff, w), BF16),
        vm((d, w), BF16),
        vm((d, w), BF16),
        vm((d, w), BF16),
        vm((d, w), F32),
        vm((images * HEADS, t, t), BF16),
        vm((d, 3 * d), BF16),
        vm((d, d), BF16), vm((d, d), BF16),
        vm((d, ff), BF16),
        vm((d, ff), BF16),
        vm((2, 32 * n + 256, d), BF16),
        vm((2, ff, d), BF16),
        column, column, column, column, column, column, column, vm((ff, 128), F32), column,
        vm((images + 1, 8, t), F32),
        vm((images, 8, t), F32),
        vm((images, 8, t), F32),
        vm((images, 8, t), F32),
        vm((images, 8, 128), F32),
        column,
        vm((3 * d, 128), F32),
        column, column, column, column,
        column,
        vm((8, ff), F32),
        vm((2, 128, 128), F32),
        vm((8, d), F32),
        vm((2, 32 * n, 128), BF16),
        vm((2, 128, 128), F32),
    ]
    scratch += [vm((slots * 8, 128), F32) for slots in (16, 8, 4, 3)]
    scratch += [vm((2, r, d), F32) for r in (2 * n, 2 * n + 16, n + 8)] + [vm((2, 2 * n, 128), F32), vm((2, 8, 128), F32)]
    scratch += [dma((4,)), dma((2, 16))] + [dma((2, 7))] * 8 + [pltpu.SemaphoreType.REGULAR((4,))]
    spec = pl.BlockSpec(memory_space=pltpu.VMEM)
    any_spec = pl.BlockSpec(memory_space=pl.ANY)
    return pl.pallas_call(
        block_body,
        out_shape=(
            sd(tok.shape, BF16), sd(tok.shape, F32),
            sd((n, 3 * d), F32), sd((n, d), F32), sd((n, ff), F32), sd((4 * n, d), F32), sd((2, 8, 128), F32),
        ),
        in_specs=[any_spec] + [spec] * 14,
        out_specs=(any_spec, any_spec) + (spec,) * 5,
        scratch_shapes=scratch,
        compiler_params=pltpu.CompilerParams(
            collective_id=0, has_side_effects=True, vmem_limit_bytes=64 * 1024 * 1024
        ),
        name="block16",
    )(tok, dup, tgt, *weights)


def deliver_body(out, gin, gqkv, gout, g1, g2, gv, *refs):
    o_out, o_gin, o_ln1g, o_ln1b, o_qkv, o_qvb, o_w, o_bout, o_ln2g, o_ln2b, o_fc1, o_b1, o_fc2, o_b2 = refs[:14]
    buf_out, buf_gin, sems = refs[14:]
    n = gqkv.shape[0]
    pieces = []
    for k, (src, buf, dst) in enumerate(((out, buf_out, o_out), (gin, buf_gin, o_gin))):
        count = 1 + 3 * k
        size = (src.shape[0] // count) // 16 * 16
        for m in range(count):
            rows = pl.ds(m * size, size if m < count - 1 else src.shape[0] - m * size)
            s = k + m
            pieces.append((
                pltpu.make_async_copy(src.at[rows], buf.at[rows], sems.at[0, s]),
                pltpu.make_async_copy(buf.at[rows], dst.at[rows], sems.at[1, s]),
            ))
    for load, store in pieces:
        load.start()
    o_qkv[...] = gqkv[...]
    o_w[...] = gout[...]
    o_fc1[...] = g1[...]
    o_fc2[...] = g2[...]
    for ref, row in ((o_ln1g, LN1G), (o_ln1b, LN1B), (o_bout, BOUT), (o_ln2g, LN2G), (o_ln2b, LN2B), (o_b2, BFC2)):
        ref[...] = gv[0, row, :n]
    o_qvb[...] = jnp.concatenate([gv[1, k, :n] for k in range(2)], 0)
    o_b1[...] = jnp.concatenate([gv[1, 2 + k, :n] for k in range(4)], 0)
    for load, store in pieces:
        load.wait()
        store.start()
    for load, store in pieces:
        store.wait()


def deliver_call(out, gin, gqkv, gout, g1, g2, gv):
    n, d = gout.shape
    sd = jax.ShapeDtypeStruct
    spec = pl.BlockSpec(memory_space=pltpu.VMEM)
    any_spec = pl.BlockSpec(memory_space=pl.ANY)
    vec = sd((n,), F32)
    return pl.pallas_call(
        deliver_body,
        out_shape=(
            sd(out.shape, BF16), sd(gin.shape, F32), vec, vec, sd((n, 3 * d), F32), sd((2 * n,), F32),
            sd((n, d), F32), vec, vec, vec, sd((n, 4 * d), F32), sd((4 * n,), F32), sd((4 * n, d), F32), vec,
        ),
        in_specs=[any_spec, any_spec] + [spec] * 5,
        out_specs=(any_spec, any_spec) + (spec,) * 12,
        scratch_shapes=[
            pltpu.VMEM(out.shape, BF16), pltpu.VMEM(gin.shape, F32), pltpu.SemaphoreType.DMA((2, 6)),
        ],
        compiler_params=pltpu.CompilerParams(vmem_limit_bytes=64 * 1024 * 1024),
        name="deliver",
    )(out, gin, gqkv, gout, g1, g2, gv)


def gather_all(value):
    return lax.all_gather(value, "fsdp", axis=0, tiled=True)


def vectors(full):
    ln1_gain, ln1_bias, qv_bias, out_bias, ln2_gain, ln2_bias, fc1_bias, fc2_bias = full
    d = ln1_gain.shape[0]
    bias = jnp.concatenate([qv_bias[:d], jnp.zeros((d,), qv_bias.dtype), qv_bias[d:]])
    rows = (ln1_gain, ln1_bias, bias, out_bias, ln2_gain, ln2_bias, fc1_bias, fc2_bias)
    width = fc1_bias.shape[0]
    return jnp.stack([jnp.pad(row.astype(F32), (0, width - row.shape[0])) for row in rows], 0)


def per_device(tokens, duplicate, targets, *weights, block16):
    images, seq, d = tokens.shape
    rows = tokens.transpose(1, 0, 2).reshape(seq * images, d)
    back = lambda v: v.reshape(seq, images, d).transpose(1, 0, 2)
    if block16:
        results = deliver_call(*block_call(rows, duplicate, targets, weights))
        return (back(results[0]), back(results[1])) + tuple(results[2:])

    (
        ln1_gain, ln1_bias, qkv_weight, qv_bias, out_weight, out_bias,
        ln2_gain, ln2_bias, fc1_weight, fc1_bias, fc2_weight, fc2_bias,
    ) = weights
    small = (ln1_gain, ln1_bias, qv_bias, out_bias, ln2_gain, ln2_bias, fc1_bias, fc2_bias)
    wqkv, wout, w1, w2 = map(gather_all, (qkv_weight, out_weight, fc1_weight, fc2_weight))
    vec = vectors(tuple(map(gather_all, small)))
    out, gin, gqkv, gout, g1, g2, gvec = compute(rows, duplicate, targets, vec, wqkv, wout, w1, w2)

    def scatter(value):
        value = lax.psum_scatter(value.astype(F32), "fsdp", scatter_dimension=0, tiled=True)
        return lax.psum(value, "dp")

    gqkv, gout, g1, g2 = map(scatter, (gqkv, gout, g1, g2))
    gvec = lax.psum(gvec, ("fsdp", "dp"))
    p = lax.axis_index("fsdp")

    def shard(value, whole_size):
        count = whole_size // lax.axis_size("fsdp")
        return lax.dynamic_slice(value, (p * count,), (count,))

    qv_grad = jnp.concatenate([gvec[2, :d], gvec[2, 2 * d : 3 * d]])
    return (
        back(out), back(gin),
        shard(gvec[0], d), shard(gvec[1], d), gqkv, shard(qv_grad, 2 * d), gout, shard(gvec[3], d),
        shard(gvec[4], d), shard(gvec[5], d), g1, shard(gvec[6], 4 * d), g2, shard(gvec[7], d),
    )


def solution(mesh):
    block16 = mesh.shape["fsdp"] == 16 and mesh.shape["dp"] == 2
    both = ("fsdp", "dp")
    vector, matrix = P("fsdp"), P("fsdp", None)
    weights = (vector, vector, matrix, vector, matrix, vector, vector, vector, matrix, vector, matrix, vector)
    return jax.shard_map(
        functools.partial(per_device, block16=block16),
        mesh=mesh,
        in_specs=(P(both, None, None), P(both, None), P(both, None)) + weights,
        out_specs=(P(both, None, None), P(both, None, None)) + weights,
        check_vma=False,
    )
```

```python
import functools
import jax
import jax.numpy as jnp
from jax import lax
from jax.experimental import pallas as pl
from jax.experimental.pallas import tpu as pltpu
from jax.sharding import PartitionSpec as P

HEADS = 6
HD = 64
EPS = 1e-06
F32 = jnp.float32
BF16 = jnp.bfloat16

NN = (((1,), (0,)), ((), ()))
NT = (((1,), (1,)), ((), ()))


def mm(a, b, dims=NN):
    return lax.dot_general(a, b, dims, preferred_element_type=F32)


def normalise(v):
    mu = jnp.mean(v, 0, keepdims=True)
    c = v - mu
    r = lax.rsqrt(jnp.mean(c * c, 0, keepdims=True) + EPS)
    return c * r, r


def norm_back(dn, u, r, gain):
    e = dn * gain
    me = jnp.mean(e, 0, keepdims=True)
    meu = jnp.mean(e * u, 0, keepdims=True)
    return r * (e - me - u * meu)


def fold(v):
    lanes = v.shape[1]
    total = v[:, :128]
    for k in range(1, lanes // 128):
        total = total + v[:, 128 * k : 128 * (k + 1)]
    return total


def wide(col, lanes):
    if lanes == 128:
        return col
    return jnp.concatenate([col] * (lanes // 128), 1)


def gelu_pair(x):
    z = x * 0.7071067811865476
    bell = jnp.exp(-(z * z))
    tail = lax.erf(z)
    half = 0.5 * x
    return half + half * tail, 0.5 + (0.5 * tail + (x * 0.3989422804014327) * bell)


LN1G, LN1B, BQKV, BOUT, LN2G, LN2B, BFC1, BFC2 = range(8)


def to_columns(vec, row, count):
    return jnp.broadcast_to(vec[row : row + 1, :count], (128, count)).T


def compute_body(
    tok, dup, tgt, vec, wqkv, wout, w1, w2,
    out, gin, gqkv, gout, g1, g2, gvec,
    xs, n1, qkv, att, n2, act, dpre, db2, db1, dos, dmid, probs,
    wqkv_t, wout_t, w1_t, w2_t,
    c_ln1g, c_ln1b, c_bqkv, c_bout, c_ln2g, c_ln2b, c_b1, c_b2,
    rl_s, ex_s, exq_s, rlx_s, exx_s, attx, dqkvx, a_g1, a_b1, a_g2, a_b2, tgt_t, stage, gin_sem,
):
    images, seq = dup.shape
    d = tok.shape[1]
    t = seq - 1
    x0 = images * t
    ff = w1.shape[1]
    w = x0 + 128
    dqkv = act.at[: 3 * d]

    blocks = d // 128

    def load_image(i):
        return jnp.concatenate([stage[b, pl.ds(i, t, stride=images), :] for b in range(blocks)], 1)

    def store_image(i, values):
        for b in range(blocks):
            stage[b, pl.ds(i, t, stride=images), :] = values[:, 128 * b : 128 * (b + 1)]

    def store_last(values):
        for b in range(blocks):
            stage[b, x0:, :] = values[:images, 128 * b : 128 * (b + 1)]

    def lanes_of(i):
        return pl.ds(pl.multiple_of(i * t, 128), t)

    extra_lanes = pl.ds(x0, 128)

    tok_copy = pltpu.make_async_copy(tok, out, gin_sem.at[0])
    tok_copy.start()
    tok_copy.wait()
    wqkv_t[...] = wqkv[...].T
    wout_t[...] = wout[...].T
    w1_t[...] = w1[...].T
    w2_t[...] = w2[...].T
    c_ln1g[...] = to_columns(vec, LN1G, d)
    c_ln1b[...] = to_columns(vec, LN1B, d)
    c_bqkv[...] = to_columns(vec, BQKV, 3 * d)
    c_bout[...] = to_columns(vec, BOUT, d)
    c_ln2g[...] = to_columns(vec, LN2G, d)
    c_ln2b[...] = to_columns(vec, LN2B, d)
    c_b1[...] = to_columns(vec, BFC1, ff)
    c_b2[...] = to_columns(vec, BFC2, d)
    tgt_t[...] = jnp.concatenate([tgt[...], jnp.zeros((128 - images, d), F32)], 0).T
    ones_row = jnp.where(lax.broadcasted_iota(jnp.int32, (16, w), 0) == 0, 1.0, 0.0).astype(BF16)
    n1[d : d + 16, :] = ones_row
    n2[d : d + 16, :] = ones_row
    att[d : d + 16, :] = ones_row
    act[ff : ff + 16, :] = ones_row
    attx[...] = jnp.zeros_like(attx)
    dqkvx[...] = jnp.zeros_like(dqkvx)
    for acc in (a_g1, a_b1, a_g2, a_b2):
        acc[...] = jnp.zeros_like(acc)

    def project(x_t, lanes, count):
        x = x_t.astype(F32)
        xs[:, lanes] = x_t
        u, r = normalise(x)
        n = (u * wide(c_ln1g[...], count) + wide(c_ln1b[...], count)).astype(BF16)
        n1[:d, lanes] = n
        for k in range(3):
            rows = slice(k * d, (k + 1) * d)
            y = mm(wqkv_t[rows, :], n) + wide(c_bqkv[rows, :], count)
            y = y.astype(BF16)
            if k == 0:
                y = y * jnp.asarray(HD**-0.5, BF16)
            qkv[rows, lanes] = y

    def project_image(i, carry):
        project(load_image(i).astype(BF16).T, lanes_of(i), t)
        return carry

    for b in range(blocks):
        stage[b] = out[:, 128 * b : 128 * (b + 1)].astype(F32)

    lax.fori_loop(0, images, project_image, 0)
    last = jnp.concatenate([out[x0:, :].astype(F32), jnp.zeros((128 - images, d), F32)], 0)
    project(last.astype(BF16).T, extra_lanes, 128)

    lane_ids = lax.broadcasted_iota(jnp.int32, (HD, 128), 1)

    def pick(ref, row, i):
        block = ref[row : row + HD, extra_lanes].astype(F32)
        return jnp.sum(jnp.where(lane_ids == i, block, 0.0), 1, keepdims=True)

    def attend_image(i, carry):
        lanes = lanes_of(i)
        for h in range(HEADS):
            r0 = h * HD
            q = qkv[r0 : r0 + HD, lanes]
            k = qkv[d + r0 : d + r0 + HD, lanes]
            v = qkv[2 * d + r0 : 2 * d + r0 + HD, lanes]
            qx, kx, vx = pick(qkv, r0, i), pick(qkv, d + r0, i), pick(qkv, 2 * d + r0, i)
            s = mm(k.T, q)
            sx = jnp.sum(q.astype(F32) * kx, 0, keepdims=True)
            top = jnp.maximum(jnp.max(s, 0, keepdims=True), sx)
            e = jnp.exp(s - top)
            ex = jnp.exp(sx - top)
            rl = 1.0 / (jnp.sum(e, 0, keepdims=True) + ex)
            e = e.astype(BF16)
            probs[i * HEADS + h] = e
            o = (mm(v, e) + vx * ex) * rl
            att[r0 : r0 + HD, lanes] = o.astype(BF16)
            rl_s[i, h : h + 1, :] = rl
            ex_s[i, h : h + 1, :] = ex
            sq = jnp.sum(k.astype(F32) * qx, 0, keepdims=True)
            sxx = jnp.sum(kx * qx, 0, keepdims=True)
            topx = jnp.maximum(jnp.max(sq, 1, keepdims=True), sxx)
            eq = jnp.exp(sq - topx)
            exx = jnp.exp(sxx - topx)
            rlx = 1.0 / (jnp.sum(eq, 1, keepdims=True) + exx)
            ox = (jnp.sum(v.astype(F32) * eq, 1, keepdims=True) + vx * exx) * rlx
            attx[r0 : r0 + HD, :] = jnp.where(lane_ids == i, ox, attx[r0 : r0 + HD, :])
            exq_s[i, h : h + 1, :] = eq
            rlx_s[i, h : h + 1, :] = jnp.broadcast_to(rlx, (1, 128))
            exx_s[i, h : h + 1, :] = jnp.broadcast_to(exx, (1, 128))
        return carry

    lax.fori_loop(0, images, attend_image, 0)
    att[:d, extra_lanes] = attx[...].astype(BF16)

    def feed(lanes, count, d_final):
        mid = xs[:, lanes].astype(F32) + mm(wout_t[...], att[:d, lanes]) + wide(c_bout[...], count)
        u, r = normalise(mid)
        n = (u * wide(c_ln2g[...], count) + wide(c_ln2b[...], count)).astype(BF16)
        n2[:d, lanes] = n
        db = d_final.astype(BF16)
        db2[:, lanes] = db
        for j in range(ff // 256):
            rows = slice(256 * j, 256 * (j + 1))
            pre = mm(w1_t[rows, :], n) + wide(c_b1[rows, :], count)
            da = mm(w2[rows, :], db)
            value, slope = gelu_pair(pre)
            act[rows, lanes] = value.astype(BF16)
            dpre[rows, lanes] = (slope * da).astype(BF16)
        final = mid + mm(w2_t[...], act[:ff, lanes]) + wide(c_b2[...], count)
        dn = mm(w1[...], dpre[:, lanes])
        a_g2[...] += fold(dn * u)
        a_b2[...] += fold(dn)
        dm = d_final + norm_back(dn, u, r, wide(c_ln2g[...], count))
        dmid[:, lanes] = dm
        low = dm.astype(BF16)
        db1[:, lanes] = low
        dos[:, lanes] = mm(wout[...], low).astype(BF16)
        return final.T

    def keep_row(row):
        first = lax.broadcasted_iota(jnp.int32, row.shape, 1) == 0
        return jnp.where(first, 1.0, 1.0 - row.astype(F32))

    def feed_image(i, carry):
        keep = keep_row(dup[pl.ds(i, 1), :])
        count = jnp.sum(keep, 1, keepdims=True)
        scale = seq * keep[:, :t] / count
        ids = lax.broadcasted_iota(jnp.int32, (d, 128), 1)
        target = jnp.sum(jnp.where(ids == i, tgt_t[...], 0.0), 1, keepdims=True)
        store_image(i, feed(lanes_of(i), t, target * scale))
        return carry

    lax.fori_loop(0, images, feed_image, 0)
    keep_all = keep_row(dup[...])
    scale_x = seq * keep_all[:, t:] / jnp.sum(keep_all, 1, keepdims=True)
    scale_x = jnp.broadcast_to(scale_x, (images, 128))
    scale_x = jnp.concatenate([scale_x, jnp.zeros((128 - images, 128), F32)], 0).T[:1, :]
    store_last(feed(extra_lanes, 128, tgt_t[...] * scale_x))
    for b in range(blocks):
        out[:, 128 * b : 128 * (b + 1)] = stage[b].astype(BF16)

    for j in range(ff // 256):
        rows = slice(256 * j, 256 * (j + 1))
        g = mm(n2[...], dpre[rows, :], NT)
        g1[:, rows] = g[:d].astype(BF16)
        gvec[BFC1 : BFC1 + 1, rows] = g[d : d + 1]
        g2[rows, :] = mm(act[rows, :], db2[...], NT).astype(BF16)
    g = mm(act[ff : ff + 16, :], db2[...], NT)
    gvec[BFC2 : BFC2 + 1, :d] = g[:1]

    def attend_back(i, carry):
        lanes = lanes_of(i)
        for h in range(HEADS):
            r0 = h * HD
            q = qkv[r0 : r0 + HD, lanes]
            k = qkv[d + r0 : d + r0 + HD, lanes]
            v = qkv[2 * d + r0 : 2 * d + r0 + HD, lanes]
            qx, kx, vx = pick(qkv, r0, i), pick(qkv, d + r0, i), pick(qkv, 2 * d + r0, i)
            rl = rl_s[i, h : h + 1, :]
            ex = ex_s[i, h : h + 1, :]
            do = dos[r0 : r0 + HD, lanes].astype(F32) * rl
            dot_o = jnp.sum(do * att[r0 : r0 + HD, lanes].astype(F32), 0, keepdims=True)
            dol = do.astype(BF16)
            p = probs[i * HEADS + h]
            ds = (p.astype(F32) * (mm(v.T, dol) - dot_o)).astype(BF16)
            dsx = ex * (jnp.sum(do * vx, 0, keepdims=True) - dot_o)
            dq = mm(k, ds) + kx * dsx
            dk = mm(q, ds, NT)
            dv = mm(dol, p, NT)
            qf = q.astype(F32)
            kf = k.astype(F32)
            vf = v.astype(F32)
            dkx = jnp.sum(qf * dsx, 1, keepdims=True)
            dvx = jnp.sum(do * ex, 1, keepdims=True)
            eq = exq_s[i, h : h + 1, :]
            rlx = rlx_s[i, h : h + 1, :1]
            exx = exx_s[i, h : h + 1, :1]
            dox = pick(dos, r0, i) * rlx
            dotx = jnp.sum(dox * pick(att, r0, i), 0, keepdims=True)
            dsq = eq * (jnp.sum(vf * dox, 0, keepdims=True) - dotx)
            dsxx = exx * (jnp.sum(vx * dox, 0, keepdims=True) - dotx)
            dqx = jnp.sum(kf * dsq, 1, keepdims=True) + kx * dsxx
            dk = dk + qx * dsq
            dv = dv + dox * eq
            dkx = dkx + qx * dsxx
            dvx = dvx + dox * exx
            scale = HD**-0.5
            for base, main, tail in ((0, dq * scale, dqx * scale), (d, dk, dkx), (2 * d, dv, dvx)):
                rows = slice(base + r0, base + r0 + HD)
                dqkv[rows, lanes] = main.astype(BF16)
                dqkvx[rows, :] = jnp.where(lane_ids == i, tail, dqkvx[rows, :])
        return carry

    lax.fori_loop(0, images, attend_back, 0)
    dqkv[:, extra_lanes] = dqkvx[...].astype(BF16)

    for k in range(3):
        rows = slice(k * d, (k + 1) * d)
        g = mm(n1[...], dqkv[rows, :], NT)
        gqkv[:, rows] = g[:d].astype(BF16)
        gvec[BQKV : BQKV + 1, rows] = g[d : d + 1]
    g = mm(att[...], db1[...], NT)
    gout[...] = g[:d].astype(BF16)
    gvec[BOUT : BOUT + 1, :d] = g[d : d + 1]

    def finish(lanes, count):
        u, r = normalise(xs[:, lanes].astype(F32))
        dn = mm(wqkv[...], dqkv[:, lanes])
        a_g1[...] += fold(dn * u)
        a_b1[...] += fold(dn)
        return (dmid[:, lanes] + norm_back(dn, u, r, wide(c_ln1g[...], count))).T

    def finish_image(i, carry):
        store_image(i, finish(lanes_of(i), t))
        return carry

    lax.fori_loop(0, images, finish_image, 0)
    store_last(finish(extra_lanes, 128))
    copies = [
        pltpu.make_async_copy(stage.at[b], gin.at[:, pl.ds(128 * b, 128)], gin_sem.at[b]) for b in range(blocks)
    ]
    for copy in copies:
        copy.start()

    for row, acc in ((LN1G, a_g1), (LN1B, a_b1), (LN2G, a_g2), (LN2B, a_b2)):
        gvec[row : row + 1, :d] = jnp.sum(acc[...].T, 0, keepdims=True)
    for copy in copies:
        copy.wait()


def compute(tok, dup, tgt, vec, wqkv, wout, w1, w2):
    images, seq = dup.shape
    d = tok.shape[1]
    ff = w1.shape[1]
    t = seq - 1
    w = images * t + 128
    vm = pltpu.VMEM
    scratch = [
        vm((d, w), BF16),
        vm((d + 16, w), BF16),
        vm((3 * d, w), BF16),
        vm((d + 16, w), BF16),
        vm((d + 16, w), BF16),
        vm((ff + 16, w), BF16),
        vm((ff, w), BF16),
        vm((d, w), BF16),
        vm((d, w), BF16),
        vm((d, w), BF16),
        vm((d, w), F32),
        vm((images * HEADS, t, t), BF16),
        vm((3 * d, d), BF16),
        vm((d, d), BF16),
        vm((ff, d), BF16),
        vm((d, ff), BF16),
        vm((d, 128), F32), vm((d, 128), F32), vm((3 * d, 128), F32), vm((d, 128), F32),
        vm((d, 128), F32), vm((d, 128), F32), vm((ff, 128), F32), vm((d, 128), F32),
        vm((images, 8, t), F32),
        vm((images, 8, t), F32),
        vm((images, 8, t), F32),
        vm((images, 8, 128), F32),
        vm((images, 8, 128), F32),
        vm((d, 128), F32),
        vm((3 * d, 128), F32),
        vm((d, 128), F32), vm((d, 128), F32), vm((d, 128), F32), vm((d, 128), F32),
        vm((d, 128), F32),
        vm((d // 128, images * seq, 128), F32),
        pltpu.SemaphoreType.DMA((d // 128,)),
    ]
    outs = (
        jax.ShapeDtypeStruct(tok.shape, BF16),
        jax.ShapeDtypeStruct(tok.shape, F32),
        jax.ShapeDtypeStruct((d, 3 * d), BF16),
        jax.ShapeDtypeStruct((d, d), BF16),
        jax.ShapeDtypeStruct((d, ff), BF16),
        jax.ShapeDtypeStruct((ff, d), BF16),
        jax.ShapeDtypeStruct((8, ff), F32),
    )
    spec = pl.BlockSpec(memory_space=pltpu.VMEM)
    return pl.pallas_call(
        compute_body,
        out_shape=outs,
        in_specs=[pl.BlockSpec(memory_space=pl.ANY)] + [spec] * 7,
        out_specs=(spec, pl.BlockSpec(memory_space=pl.ANY)) + (spec,) * 5,
        scratch_shapes=scratch,
        compiler_params=pltpu.CompilerParams(vmem_limit_bytes=64 * 1024 * 1024),
        name="block",
    )(tok, dup, tgt, vec, wqkv, wout, w1, w2)

MESH_ID = pl.DeviceIdType.MESH
NZ = 4
UNITS = 2
UNITS1 = 1
UNITS2 = 2
CHUNK = 2
FFB = 128


class Place:
    def __init__(self):
        p = lax.axis_index("fsdp")
        self.p = p
        self.c = lax.axis_index("dp")
        self.x = lax.rem(p, 2)
        self.y = lax.rem(lax.div(p, 2), 2)
        self.z = lax.div(p, 4)
        self.a = self.y + self.c * (self.x - self.y)
        self.b = self.x + self.c * (self.y - self.x)

    def device(self, x, y, z):
        return ((z * 2 + y) * 2 + x, self.c)

    def along_a(self):
        c = self.c
        return self.device(self.x + c * (1 - 2 * self.x), self.y + (1 - c) * (1 - 2 * self.y), self.z)

    def along_b(self):
        c = self.c
        return self.device(self.x + (1 - c) * (1 - 2 * self.x), self.y + c * (1 - 2 * self.y), self.z)

    def along_z(self, step):
        return lax.rem(self.z + step, NZ)

    def sibling(self):
        return (self.p, 1 - self.c)

    def everyone(self):
        return [(lax.rem(self.p + k, 16), self.c) for k in range(1, 16)]


def slot_of(p, group):
    x, y, z = p % 2, (p // 2) % 2, p // 4
    a, b = (y, x) if group == 0 else (x, y)
    return (a * 2 + b) * NZ + z


def greet(at):
    barrier = pltpu.get_barrier_semaphore()
    others = [at.sibling()] + at.everyone()
    for device in others:
        pl.semaphore_signal(barrier, inc=1, device_id=device, device_id_type=MESH_ID)


def remote(src, dst, sems, k, device):
    return pltpu.make_async_remote_copy(
        src_ref=src, dst_ref=dst, send_sem=sems.at[0, k], recv_sem=sems.at[1, k],
        device_id=device, device_id_type=MESH_ID,
    )


def span(start, size):
    return pl.ds(pl.multiple_of(start, size), size)


class Gather:
    def __init__(self, at, buf, r, sems, swap):
        self.at, self.buf, self.r, self.sems, self.shared = at, buf, r, sems, swap

    def part(self, rows, k, device):
        piece = self.buf.at[rows]
        return remote(piece, piece, self.sems, k, device)

    def line(self):
        at, r = self.at, self.r
        rows = span(((at.a * 2 + at.b) * NZ + at.z) * r, r)
        return [
            self.part(rows, step - 1, at.device(at.x, at.y, at.along_z(step))) for step in range(1, NZ)
        ]

    def over_b(self):
        at, r = self.at, self.r
        return [self.part(span((at.a * 2 + at.b) * NZ * r, NZ * r), 3, at.along_b())]

    def over_a(self):
        at, r = self.at, self.r
        return [self.part(span(at.a * 2 * NZ * r, 2 * NZ * r), 4, at.along_a())]

    def swap(self):
        return [remote(self.buf, self.buf, self.sems, 5, self.at.sibling())] if self.shared else []

    def go(self, step):
        steps = (self.line, self.over_b, self.over_a, self.swap)
        if step > 0:
            for copy in steps[step - 1]():
                copy.wait()
        if step < 4:
            for copy in steps[step]():
                copy.start()


class Spread:
    def __init__(self, at, buf, r, sems):
        self.at, self.buf, self.r, self.sems = at, buf, r, sems

    def direct(self):
        at, r = self.at, self.r
        piece = self.buf.at[span((at.c * 16 + at.p) * r, r)]
        return [remote(piece, piece, self.sems, k, device) for k, device in enumerate(at.everyone())]

    def swap(self):
        piece = self.buf.at[span(self.at.c * 16 * self.r, 16 * self.r)]
        return [remote(piece, piece, self.sems, 15, self.at.sibling())]

    def go(self, step):
        steps = (self.direct, self.swap)
        if step > 0:
            for copy in steps[step - 1]():
                copy.wait()
        if step < 2:
            for copy in steps[step]():
                copy.start()


class Reduce:
    def __init__(self, at, full, got, from_a, from_b, from_z, total, r, sems):
        self.at, self.full, self.got = at, full, got
        self.from_a, self.from_b, self.from_z, self.total = from_a, from_b, from_z, total
        self.r, self.sems = r, sems

    def first(self):
        return [remote(self.full.at[1 - self.at.c], self.got, self.sems, 0, self.at.sibling())]

    def over_a(self):
        at, r = self.at, self.r
        rows = span((1 - at.a) * 2 * NZ * r, 2 * NZ * r)
        return [remote(self.full.at[at.c, rows], self.from_a, self.sems, 1, at.along_a())]

    def over_b(self):
        at, r = self.at, self.r
        rows = span((at.a * 2 + 1 - at.b) * NZ * r, NZ * r)
        return [remote(self.full.at[at.c, rows], self.from_b, self.sems, 2, at.along_b())]

    def line(self):
        at, r = self.at, self.r
        copies = []
        for step in range(1, NZ):
            other = at.along_z(step)
            rows = span(((at.a * 2 + at.b) * NZ + other) * r, r)
            copies.append(
                remote(self.full.at[at.c, rows], self.from_z.at[pl.ds((step - 1) * r, r)], self.sems, 2 + step, at.device(at.x, at.y, other))
            )
        return copies

    def last(self):
        piece = self.total.at[self.at.c]
        return [remote(piece, piece, self.sems, 6, self.at.sibling())]

    def add(self, rows, values):
        ref = self.full.at[self.at.c, rows]
        ref[...] = (ref[...].astype(F32) + values.astype(F32)).astype(ref.dtype)

    def go(self, step):
        at, r = self.at, self.r
        steps = (self.first, self.over_a, self.over_b, self.line, self.last)
        if step > 0:
            for copy in steps[step - 1]():
                copy.wait()
        if step == 1:
            for half in range(2):
                rows = pl.ds(half * 2 * NZ * r, 2 * NZ * r)
                self.add(rows, self.got[rows, :])
        elif step == 2:
            self.add(span(at.a * 2 * NZ * r, 2 * NZ * r), self.from_a[...])
        elif step == 3:
            self.add(span((at.a * 2 + at.b) * NZ * r, NZ * r), self.from_b[...])
        elif step == 4:
            total = self.full[at.c, span(((at.a * 2 + at.b) * NZ + at.z) * r, r), :].astype(F32)
            for k in range(NZ - 1):
                total = total + self.from_z[k * r : (k + 1) * r, :].astype(F32)
            self.total[at.c] = total
        if step < 5:
            for copy in steps[step]():
                copy.start()


V_LN1G, V_LN1B, V_QV, V_BOUT, V_LN2G, V_LN2B, V_BFC2, V_BFC1 = 0, 1, 2, 4, 5, 6, 7, 8


def block_body(
    tok, dup, tgt, s_ln1g, s_ln1b, s_qkv, s_qvb, s_out, s_bout, s_ln2g, s_ln2b, s_fc1, s_b1, s_fc2, s_b2,
    out, gin, oqkv, oout, o1, o2, ovec,
    tokb, stage, xs, n1, qkv, att, n2, act, dpre, db2, db1, dos, dmid, probs,
    wqkv, wout, wout_t, w1, w2_t, wt_a, wf,
    c_ln1g, c_ln1b, c_q, c_v, c_bout, c_ln2g, c_ln2b, c_b1, c_b2,
    stat_s, rl_s, ex_s, pq_s, pxq_s, attx, dqkvx, a_g1, a_b1, a_g2, a_b2, tgt_t, gvec, allc, vec_s,
    tail_s, tv, uv, av, bv, zv, f_a, f_b, f_c, f_d, f_v,
    loc_sem, gsem0, gsem1, gsem2, gsem3, rsem_a, rsem_b, rsem_c, rsem_d, rsem_v, ready,
):
    images, seq = dup.shape
    d = tok.shape[1]
    t = seq - 1
    x0 = images * t
    ff = w1.shape[1]
    w = x0 + 128
    n = d // 16
    blocks = d // 128
    at = Place()
    every = range(16)
    pairs = HEADS // 2
    mine = pl.ds(pl.multiple_of(at.c * d, 128), d)
    own = (at.a * 2 + at.b) * NZ + at.z

    def lanes_of(i, count=1):
        return pl.ds(pl.multiple_of(i * t, 128), t * count)

    extra_lanes = pl.ds(x0, 128)

    def load_image(i):
        return jnp.concatenate([stage[b, pl.ds(i, t, stride=images), :] for b in range(blocks)], 1)

    def store_image(i, values):
        for b in range(blocks):
            stage[b, pl.ds(i, t, stride=images), :] = values[:, 128 * b : 128 * (b + 1)]

    def store_last(values):
        for b in range(blocks):
            stage[b, x0:, :] = values[:images, 128 * b : 128 * (b + 1)]

    greet(at)
    tok_copy = pltpu.make_async_copy(tok, tokb, loc_sem.at[0])
    tok_copy.start()

    r0, r2, r3 = n + 8, 2 * n, 2 * n + 16
    slots0 = act.at[: 16 * r0, :d]
    slots1 = act.at[16 * r0 : 32 * r0]
    slots2 = act.at[: 16 * r2]
    slots3 = dpre.at[: 16 * r3]
    group = [pl.ds(k * d, d) for k in range(4)]
    later_mine = pl.ds(pl.multiple_of((2 + at.c) * d, 128), d)
    q = s_qkv[...].astype(F32)

    def pair_of(p):
        return jnp.concatenate([q[:, d * k + 128 * p : d * k + 128 * (p + 1)] for k in range(3)], 1)

    vec_s[...] = jnp.zeros_like(vec_s)
    flat = [s_ln1g[...], s_ln1b[...], s_qvb[:n], s_qvb[n:], s_bout[...], s_ln2g[...], s_ln2b[...], s_b2[...]]
    flat += [s_b1[n * k : n * (k + 1)] for k in range(4)]
    for k, line in enumerate(flat):
        lo = 128 * (k // 8)
        vec_s[k % 8 : k % 8 + 1, lo : lo + n] = line.astype(F32).reshape(1, n)
    slot = jnp.concatenate([pair_of(0), vec_s[...]], 0)
    half = r0 // 2
    slots0[span((at.c * 16 + at.p) * half, half), :] = jnp.where(at.c == 0, slot[:half], slot[half:]).astype(BF16)
    own1, own2, own3 = (span(own * r, r) for r in (r0, r2, r3))
    w_out = s_out[...].astype(F32)
    blank = jnp.zeros((8, d), F32)

    @pl.when(at.c == 0)
    def _():
        f = s_fc1[...].astype(F32)
        slots1[own1, group[0]] = jnp.concatenate([pair_of(1), blank], 0).astype(BF16)
        slots2[own2, group[2]] = jnp.concatenate([f[:, :d], f[:, d : 2 * d]], 0).astype(BF16)
        parts = [f[:, 2 * d : 3 * d], f[:, 3 * d :], w_out[:16]]
        slots3[own3, group[0]] = jnp.concatenate(parts, 0).astype(BF16)

    @pl.when(at.c == 1)
    def _():
        slots1[own1, group[1]] = jnp.concatenate([pair_of(2), blank], 0).astype(BF16)
        slots2[own2, group[3]] = s_fc2[:r2]
        parts = [s_fc2[r2:].astype(F32), w_out[16:], blank]
        slots3[own3, group[1]] = jnp.concatenate(parts, 0).astype(BF16)

    pl.semaphore_wait(pltpu.get_barrier_semaphore(), 16)
    g0 = Spread(at, slots0, half, gsem0)
    g1 = Gather(at, slots1.at[:, mine], r0, gsem1, True)
    g2 = Gather(at, slots2.at[:, later_mine], r2, gsem2, True)
    g3 = Gather(at, slots3.at[:, mine], r3, gsem3, True)
    g0.go(0)

    tok_copy.wait()
    for b in range(blocks):
        stage[b] = tokb[:, 128 * b : 128 * (b + 1)].astype(F32)

    def statistics(x):
        mu = jnp.mean(x, 0, keepdims=True)
        c = x - mu
        return mu, lax.rsqrt(jnp.mean(c * c, 0, keepdims=True) + EPS)

    def turn(i, carry):
        x = load_image(i).astype(BF16).T
        xs[:, lanes_of(i)] = x
        mu, r = statistics(x.astype(F32))
        stat_s[i, 0:1, :] = mu
        stat_s[i, 1:2, :] = r
        return carry

    lax.fori_loop(0, images // 2, turn, 0)
    g1.go(0)
    lax.fori_loop(images // 2, images, turn, 0)
    last = jnp.concatenate([tokb[x0:, :].astype(F32), jnp.zeros((128 - images, d), F32)], 0)
    x = last.astype(BF16).T
    xs[:, extra_lanes] = x
    mu, r = statistics(x.astype(F32))
    stat_s[images, 0:1, :128] = mu
    stat_s[images, 1:2, :128] = r
    tgt_t[...] = jnp.concatenate([tgt[...], jnp.zeros((128 - images, d), F32)], 0).T
    ones_row = jnp.where(lax.broadcasted_iota(jnp.int32, (16, w), 0) == 0, 1.0, 0.0).astype(BF16)
    n1[d : d + 16, :] = ones_row
    n2[d : d + 16, :] = ones_row
    att[d : d + 16, :] = ones_row
    for ref in (attx, dqkvx, a_g1, a_b1, a_g2, a_b2):
        ref[...] = jnp.zeros_like(ref)
    g0.go(1)
    g1.go(1)
    g2.go(0)
    g0.go(2)
    g3.go(0)

    def slot_of_chip(p):
        parts = [slots0[(16 * k + p) * half : (16 * k + p + 1) * half, :].astype(F32) for k in range(2)]
        return jnp.concatenate(parts, 0)

    first = [slot_of_chip(p) for p in every]
    for half in range(2):
        rows = [s[n:, 128 * half : 128 * (half + 1)] for s in first]
        allc[half] = jnp.concatenate(rows, 0).T
    lane_ids = lax.broadcasted_iota(jnp.int32, (n, 128), 1)
    ones = jnp.ones((128, 128), BF16)

    def column(ref, entries):
        runs = [jnp.where(lane_ids == 8 * p + k % 8, allc[k // 8, :n, :], 0.0) for p, k in entries]
        ref[...] = mm(jnp.concatenate(runs, 0).astype(BF16), ones)

    column(c_ln1g, [(p, V_LN1G) for p in every])
    column(c_ln1b, [(p, V_LN1B) for p in every])
    column(c_q, [(p, V_QV + k) for p in range(8) for k in range(2)])
    column(c_v, [(p, V_QV + k) for p in range(8, 16) for k in range(2)])

    def put_pair(p, block):
        block = block.astype(BF16)
        wqkv[:, p * d : (p + 1) * d] = block
        wt_a[p // 2, (p % 2) * d : (p % 2 + 1) * d, :] = block.T

    put_pair(0, jnp.concatenate([s[:n] for s in first], 0))

    def unpack(slots, which, lanes, r, lo, hi):
        runs = []
        for p in every:
            s = slot_of(p, which)
            runs.append(slots[r * s : r * (s + 1), lanes].astype(F32)[lo:hi])
        return runs

    def project(p, lanes, count, mu=None, r=None):
        if p == 0:
            u = (xs[:, lanes].astype(F32) - mu) * r
            y = (u * wide(c_ln1g[...], count) + wide(c_ln1b[...], count)).astype(BF16)
            n1[:d, lanes] = y
        else:
            y = n1[:d, lanes]
        y = mm(wt_a[p // 2, (p % 2) * d : (p % 2 + 1) * d, :], y)
        heads = slice(128 * p, 128 * (p + 1))
        query = (y[:128] + wide(c_q[heads, :], count)).astype(BF16) * jnp.asarray(HD**-0.5, BF16)
        value = (y[256:] + wide(c_v[heads, :], count)).astype(BF16)
        qkv[p * d : (p + 1) * d, lanes] = jnp.concatenate([query, y[128:256].astype(BF16), value], 0)

    def rows_of(part, h):
        row = (h // 2) * d + part * 128 + (h % 2) * HD
        return slice(row, row + HD)

    head_lanes = lax.broadcasted_iota(jnp.int32, (HD, 128), 1)

    def pick(ref, rows, i):
        return jnp.sum(jnp.where(head_lanes == i, ref[rows, extra_lanes].astype(F32), 0.0), 1, keepdims=True)

    def row_dot(a, column):
        return jnp.sum(a.astype(F32) * column, 0, keepdims=True)

    def column_dot(a, row):
        return jnp.sum(a.astype(F32) * row, 1, keepdims=True)

    def place_column(ref, rows, i, column):
        ref[rows, :] = jnp.where(head_lanes == i, column, ref[rows, :])

    def score(i, h):
        q, k = (qkv[rows_of(part, h), lanes_of(i)] for part in range(2))
        qx, kx = (pick(qkv, rows_of(part, h), i) for part in range(2))
        vx = pick(qkv, rows_of(2, h), i)
        return mm(k.T, q), row_dot(q, kx), row_dot(k, qx), jnp.sum(qx * kx, 0, keepdims=True), vx

    def share(i, h, s, sx, sq, sxq, vx):
        top = jnp.maximum(jnp.max(s, 0, keepdims=True), sx)
        e = jnp.exp(s - top)
        ex = jnp.exp(sx - top)
        rl = 1.0 / (jnp.sum(e, 0, keepdims=True) + ex)
        e = e.astype(BF16)
        probs[i * HEADS + h] = e
        rl_s[i, h : h + 1, :] = rl
        ex_s[i, h : h + 1, :] = ex
        top = jnp.maximum(jnp.max(sq, 1, keepdims=True), sxq)
        eq = jnp.exp(sq - top)
        exq = jnp.exp(sxq - top)
        rlq = 1.0 / (jnp.sum(eq, 1, keepdims=True) + exq)
        pq = eq * rlq
        pxq = exq * rlq
        pq_s[i, h : h + 1, :] = pq
        pxq_s[i, h : h + 1, :] = jnp.broadcast_to(pxq, (1, 128))
        return e, ex, rl, pq, pxq, vx

    def mix(i, h, e, ex, rl, pq, pxq, vx):
        v = qkv[rows_of(2, h), lanes_of(i)]
        rows = slice(h * HD, (h + 1) * HD)
        att[rows, lanes_of(i)] = ((mm(v, e) + vx * ex) * rl).astype(BF16)
        place_column(attx, rows, i, column_dot(v, pq) + vx * pxq)

    def attend(units):
        scores = [score(*units[0])]
        shares = []
        for k, unit in enumerate(units):
            if k + 1 < len(units):
                scores.append(score(*units[k + 1]))
            shares.append(share(*unit, *scores[k]))
            if k >= 1:
                mix(*units[k - 1], *shares[k - 1])
        mix(*units[-1], *shares[-1])

    def forward_pair(p, steps):
        if p == 0:

            def project_image(i, carry):
                project(0, lanes_of(i), t, stat_s[i, 0:1, :], stat_s[i, 1:2, :])
                return carry

            lax.fori_loop(0, images, project_image, 0)
            project(0, extra_lanes, 128, stat_s[images, 0:1, :128], stat_s[images, 1:2, :128])
        else:

            def project_images(i, carry):
                project(p, lanes_of(2 * i, 2), 2 * t)
                return carry

            lax.fori_loop(0, images // 2, project_images, 0)
            project(p, extra_lanes, 128)
        for step in steps[0]:
            step()

        def attend_images(i, carry):
            attend([(UNITS * i + k, 2 * p + h) for k in range(UNITS) for h in range(2)])
            for when in range(images // UNITS):

                @pl.when(i == when)
                def _(when=when):
                    for step in steps[1 + when]:
                        step()

            return carry

        lax.fori_loop(0, images // UNITS, attend_images, 0)

    def later(item, step):
        return lambda: item.go(step)

    forward_pair(0, [[later(g1, 2), later(g2, 1)], [], [later(g3, 1)], [], [later(g1, 3), later(g2, 2)]])
    g1.go(4)
    for k in range(2):
        put_pair(1 + k, jnp.concatenate(unpack(slots1, k, group[k], r0, 0, n), 0))
    forward_pair(1, [[], [later(g3, 2)], [], [later(g2, 3)], []])
    forward_pair(2, [[], [later(g3, 3)], [], [], [later(g2, 4)]])
    att[:d, extra_lanes] = attx[...].astype(BF16)
    column(c_bout, [(p, V_BOUT) for p in every])
    column(c_ln2g, [(p, V_LN2G) for p in every])
    column(c_ln2b, [(p, V_LN2B) for p in every])
    column(c_b2, [(p, V_BFC2) for p in every])
    column(c_b1, [(p, V_BFC1 + k) for p in every for k in range(4)])
    g3.go(4)
    runs = zip(unpack(slots3, 0, group[0], r3, r2, r3), unpack(slots3, 1, group[1], r3, r2, r2 + 8))
    block = jnp.concatenate([part for run in runs for part in run], 0).astype(BF16)
    wout[...] = block
    wout_t[...] = block.T
    for k in range(4):
        slots, lanes, r = (slots2, group[2], r2) if k < 2 else (slots3, group[0], r3)
        block = jnp.concatenate(unpack(slots, 0, lanes, r, (k % 2) * n, (k % 2 + 1) * n), 0).astype(BF16)
        w1[:, k * d : (k + 1) * d] = block
        wf[0, k * d : (k + 1) * d, :] = block.T
    for p in every:
        s = slot_of(p, 1)
        for k, (slots, lanes, r) in enumerate(((slots2, group[3], r2), (slots3, group[1], r3))):
            start = 4 * n * p + r2 * k
            wf[1, start : start + r2, :] = slots[r * s : r * s + r2, lanes]
    w2_t[...] = wf[1].T
    act[ff : ff + 16, :] = ones_row

    def middle(lanes, count):
        return xs[:, lanes].astype(F32) + mm(wout_t[...], att[:d, lanes]) + wide(c_bout[...], count)

    def feed(lanes, count, d_final):
        u, r = normalise(middle(lanes, count))
        y = (u * wide(c_ln2g[...], count) + wide(c_ln2b[...], count)).astype(BF16)
        n2[:d, lanes] = y
        db = d_final.astype(BF16)
        db2[:, lanes] = db
        for j in range(ff // FFB):
            rows = slice(FFB * j, FFB * (j + 1))
            pre = mm(wf[0, rows, :], y) + wide(c_b1[rows, :], count)
            da = mm(wf[1, rows, :], db)
            value, slope = gelu_pair(pre)
            act[rows, lanes] = value.astype(BF16)
            dpre[rows, lanes] = (slope * da).astype(BF16)
        dn = mm(w1[...], dpre[:, lanes])
        a_g2[...] += fold(dn * u)
        a_b2[...] += fold(dn)
        dm = d_final + norm_back(dn, u, r, wide(c_ln2g[...], count))
        dmid[:, lanes] = dm
        low = dm.astype(BF16)
        db1[:, lanes] = low
        dos[:, lanes] = mm(wout[...], low).astype(BF16)

    def keep_row(row):
        position = lax.broadcasted_iota(jnp.int32, row.shape, 1) == 0
        return jnp.where(position, 1.0, 1.0 - row.astype(F32))

    def cotangent(i):
        keep = keep_row(dup[pl.ds(i, 1), :])
        scale = seq * keep[:, :t] / jnp.sum(keep, 1, keepdims=True)
        ids = lax.broadcasted_iota(jnp.int32, (d, 128), 1)
        return jnp.sum(jnp.where(ids == i, tgt_t[...], 0.0), 1, keepdims=True) * scale

    def feed_images(k, carry):
        d_final = jnp.concatenate([cotangent(CHUNK * k + m) for m in range(CHUNK)], 1)
        feed(lanes_of(CHUNK * k, CHUNK), CHUNK * t, d_final)
        return carry

    lax.fori_loop(0, images // CHUNK, feed_images, 0)
    keep_all = keep_row(dup[...])
    scale_x = seq * keep_all[:, t:] / jnp.sum(keep_all, 1, keepdims=True)
    scale_x = jnp.broadcast_to(scale_x, (images, 128))
    scale_x = jnp.concatenate([scale_x, jnp.zeros((128 - images, 128), F32)], 0).T[:1, :]
    feed(extra_lanes, 128, tgt_t[...] * scale_x)

    def put(buf, which, parts, lo=0, step=None):
        for p in every:
            slot = jnp.concatenate([part[n * p + a : n * p + b] for part, a, b in parts], 0).astype(BF16)
            start = step * slot_of(p, which) + lo
            buf[which, start : start + slot.shape[0], :] = slot

    for j in range(ff // 256):
        rows = slice(256 * j, 256 * (j + 1))
        g = mm(act[rows, :], db2[...], NT).astype(BF16)
        for lo in range(256 * j, 256 * (j + 1), 16):
            p, off = lo // (4 * n), lo % (4 * n)
            buf, r = (wf, r2) if off < r2 else (wt_a, r3)
            start = r * slot_of(p, 1) + off % r2
            buf[1, start : start + 16, :] = g[lo - 256 * j : lo - 256 * j + 16]
    g = mm(act[ff : ff + 16, :], db2[...], NT)
    gvec[BFC2 : BFC2 + 1, :d] = g[:1]

    def reducer(full, total, r, sems, width, places):
        refs = []
        for (row, lane), count in zip(places, (16, 8, 4, 3)):
            refs.append(dpre.at[row : row + count * r, lane : lane + width])
        return Reduce(at, full, *refs, total, r, sems)

    ra = reducer(wf.at[:, : 16 * r2], f_a, r2, rsem_a, d, [(k * r2, 0) for k in (0, 16, 24, 28)])
    rb = reducer(wt_a, f_b, r3, rsem_b, d, [(0, d), (16 * r3, d), (0, 2 * d), (4 * r3, 2 * d)])
    rc = reducer(
        wf.at[:, 16 * r2 : 16 * r2 + 16 * r0], f_c, r0, rsem_c, d, [(k * r0, 3 * d) for k in (0, 16, 24, 28)]
    )
    rd = reducer(tail_s, f_d, r2, rsem_d, 128, [(k * r2, 4 * d) for k in (0, 16, 24, 28)])
    rv = Reduce(at, tv, uv, av, bv, zv, f_v, 8, rsem_v)
    gw = mm(att[...], db1[...], NT)
    gvec[BOUT : BOUT + 1, :d] = gw[d : d + 1]
    gw = gw[:d]
    for j in range(2):
        rows = slice(2 * d * j, 2 * d * (j + 1))
        g = mm(n2[...], dpre[rows, :], NT)
        gvec[BFC1 : BFC1 + 1, rows] = g[d : d + 1]
        parts = [(g[:d, :d], 0, n), (g[:d, d:], 0, n)]
        if j == 0:
            put(wf, 0, parts, step=r2)
        else:
            put(wt_a, 0, parts + [(gw, 0, 16)], step=r3)
    for p in every:
        start = r3 * slot_of(p, 1) + r2
        wt_a[1, start : start + 16, :] = jnp.concatenate([gw[n * p + 16 : n * (p + 1)], blank], 0).astype(BF16)

    partners = [at.sibling(), at.along_a(), at.along_b()]
    partners += [at.device(at.x, at.y, at.along_z(step)) for step in range(1, NZ)]
    for k, device in enumerate(partners):
        pl.semaphore_signal(ready.at[min(k, 3)], inc=1, device_id=device, device_id_type=MESH_ID)
    pl.semaphore_wait(ready.at[0], 1)
    ra.go(0)
    rb.go(0)

    def allowed(k):
        return lambda: pl.semaphore_wait(ready.at[k], 1 if k < 3 else NZ - 1)

    def slopes(i, h):
        rows = slice(h * HD, (h + 1) * HD)
        v = qkv[rows_of(2, h), lanes_of(i)]
        vx = pick(qkv, rows_of(2, h), i)
        do = dos[rows, lanes_of(i)].astype(F32) * rl_s[i, h : h + 1, :]
        doq = pick(dos, rows, i)
        dot_o = jnp.sum(do * att[rows, lanes_of(i)].astype(F32), 0, keepdims=True)
        dol = do.astype(BF16)
        dp = mm(v.T, dol)
        qx, kx = (pick(qkv, rows_of(part, h), i) for part in range(2))
        return qx, kx, dol, dot_o, dp, row_dot(do, vx), doq, row_dot(v, doq), jnp.sum(vx * doq, 0, keepdims=True)

    def scores_back(i, h, qx, kx, dol, dot_o, dp, dpx, doq, dpq, dpxq):
        p = probs[i * HEADS + h]
        ex = ex_s[i, h : h + 1, :]
        ds = (p.astype(F32) * (dp - dot_o)).astype(BF16)
        dsx = ex * (dpx - dot_o)
        pq = pq_s[i, h : h + 1, :]
        pxq = pxq_s[i, h : h + 1, :1]
        total = jnp.sum(pq * dpq, 1, keepdims=True) + pxq * dpxq
        return qx, kx, dol, p, ex, ds, dsx, doq, pq, pxq, pq * (dpq - total), pxq * (dpxq - total)

    def heads_back(i, h, qx, kx, dol, p, ex, ds, dsx, doq, pq, pxq, dsq, dsxq):
        q, k = (qkv[rows_of(part, h), lanes_of(i)] for part in range(2))
        scale = HD**-0.5
        dq = (mm(k, ds) + kx * dsx) * scale
        dk = mm(q, ds, NT) + qx * dsq
        dv = mm(dol, p, NT) + doq * pq
        place_column(dqkvx, rows_of(0, h), i, (column_dot(k, dsq) + kx * dsxq) * scale)
        place_column(dqkvx, rows_of(1, h), i, column_dot(q, dsx) + qx * dsxq)
        place_column(dqkvx, rows_of(2, h), i, column_dot(dol, ex) + doq * pxq)
        for part, value in enumerate((dq, dk, dv)):
            qkv[rows_of(part, h), lanes_of(i)] = value.astype(BF16)

    def attend_back(units):
        one = [slopes(*units[0])]
        two = []
        for k, unit in enumerate(units):
            if k + 1 < len(units):
                one.append(slopes(*units[k + 1]))
            two.append(scores_back(*unit, *one[k]))
            if k >= 1:
                heads_back(*units[k - 1], *two[k - 1])
        heads_back(*units[-1], *two[-1])

    def run_steps(i, steps):
        for when, todo in steps:

            @pl.when(i == when)
            def _(todo=todo):
                for step in todo:
                    step()

    def back_first(i, carry):
        attend_back([(UNITS1 * i + k, h) for k in range(UNITS1) for h in range(4)])
        run_steps(i, (
            (3, [allowed(1), later(ra, 1)]),
            (4, [later(rb, 1)]),
        ))
        return carry

    lax.fori_loop(0, images // UNITS1, back_first, 0)
    pl.semaphore_wait(ready.at[2], 1)
    ra.go(2)
    qkv[: 2 * d, extra_lanes] = dqkvx[: 2 * d, :].astype(BF16)

    gain1, bias1 = c_ln1g[:, :1], c_ln1b[:, :1]

    def weight_sums(first_pair, count):
        rows = slice(first_pair * d, (first_pair + count) * d)
        g = mm(n1[...], qkv[rows, :], NT)
        sums = g[d : d + 1]
        weight = wqkv[:, rows].astype(F32)
        a_g1[...] += fold(weight * (g[:d] - bias1 * sums))
        a_b1[...] += fold(weight * sums)
        for m in range(count):
            p = first_pair + m
            gvec[BQKV : BQKV + 1, 128 * p : 128 * (p + 1)] = sums[:, m * d : m * d + 128]
            gvec[BQKV : BQKV + 1, 2 * d + 128 * p : 2 * d + 128 * (p + 1)] = sums[:, m * d + 256 : (m + 1) * d]
        return g[:d]

    g = weight_sums(0, 2)
    for p in range(2):
        put(wf, p, [(g[:, p * d : (p + 1) * d], 0, n)], 16 * r2, r0)
    rc.go(0)

    def back_second(i, carry):
        attend_back([(UNITS2 * i + k, h) for k in range(UNITS2) for h in range(4, 6)])
        run_steps(i, (
            (0, [allowed(3), later(ra, 3)]),
            (1, [later(rb, 2), later(rc, 1)]),
        ))
        return carry

    lax.fori_loop(0, images // UNITS2, back_second, 0)
    qkv[2 * d :, extra_lanes] = dqkvx[2 * d :, :].astype(BF16)
    g = weight_sums(2, 1)
    put(tail_s, 0, [(g[:, :128], 0, n), (g[:, 128:256], 0, n)], step=r2)
    put(tail_s, 1, [(g[:, 256:], 0, n), (jnp.zeros((d, 128), F32), 0, n)], step=r2)
    scale1 = a_g1[...] * (1.0 / c_ln1g[...])
    for row, acc in ((LN1G, scale1), (LN1B, a_b1[...]), (LN2G, a_g2[...]), (LN2B, a_b2[...])):
        gvec[row : row + 1, :d] = jnp.sum(acc.T, 0, keepdims=True)
    tv[...] = jnp.zeros_like(tv)
    for p in every:
        s0 = 8 * slot_of(p, 0)
        tv[0, s0 : s0 + 8, :n] = gvec[:, n * p : n * (p + 1)]
        s1 = 8 * slot_of(p, 1)
        lo = 2 * n * p if p < 8 else 2 * d + 2 * n * (p - 8)
        parts = [gvec[BQKV : BQKV + 1, lo + n * k : lo + n * (k + 1)] for k in range(2)]
        lo = 4 * n * p
        parts += [gvec[BFC1 : BFC1 + 1, lo + n * k : lo + n * (k + 1)] for k in range(4)]
        tv[1, s1 : s1 + 6, :n] = jnp.concatenate(parts, 0)
    rd.go(0)
    rv.go(0)
    ra.go(4)
    rb.go(3)

    def finals(lanes, count):
        return middle(lanes, count) + mm(w2_t[...], act[:ff, lanes]) + wide(c_b2[...], count)

    def final_images(k, carry):
        final = finals(lanes_of(CHUNK * k, CHUNK), CHUNK * t)
        for m in range(CHUNK):
            store_image(CHUNK * k + m, final[:, m * t : (m + 1) * t].T)
        run_steps(k * CHUNK, (
            (0, [later(rd, 1), later(rv, 1)]),
            (2, [later(rc, 2)]),
            (6, [later(rd, 2), later(rv, 2)]),
        ))
        return carry

    lax.fori_loop(0, images // CHUNK, final_images, 0)
    store_last(finals(extra_lanes, 128).T)
    for b in range(blocks):
        tokb[:, 128 * b : 128 * (b + 1)] = stage[b].astype(BF16)
    out_copy = pltpu.make_async_copy(tokb, out, loc_sem.at[0])
    out_copy.start()

    def finish(lanes, count, mu, r):
        u = (xs[:, lanes].astype(F32) - mu) * r
        dn = mm(wqkv[...], qkv[:, lanes])
        return dmid[:, lanes] + norm_back(dn, u, r, wide(c_ln1g[...], count))

    def finish_images(k, carry):
        mu, r = (
            jnp.concatenate([stat_s[CHUNK * k + m, row : row + 1, :] for m in range(CHUNK)], 1) for row in range(2)
        )
        grad = finish(lanes_of(CHUNK * k, CHUNK), CHUNK * t, mu, r)
        for m in range(CHUNK):
            store_image(CHUNK * k + m, grad[:, m * t : (m + 1) * t].T)
        run_steps(k * CHUNK, (
            (0, [later(rc, 3)]),
            (2, [later(rb, 4)]),
            (4, [later(rd, 3), later(rv, 3)]),
        ))
        return carry

    lax.fori_loop(0, images // CHUNK, finish_images, 0)
    store_last(finish(extra_lanes, 128, stat_s[images, 0:1, :128], stat_s[images, 1:2, :128]).T)
    copies = [
        pltpu.make_async_copy(stage.at[b], gin.at[:, pl.ds(128 * b, 128)], loc_sem.at[1 + b]) for b in range(blocks)
    ]
    for copy in copies:
        copy.start()
    rc.go(4)
    ra.go(5)
    rb.go(5)
    o1[...] = jnp.concatenate([f[0, n * k : n * (k + 1)] for f in (f_a, f_b) for k in range(2)], 1)
    o2[:r2] = f_a[1]
    o2[r2:] = f_b[1, :r2]
    oout[:16] = f_b[0, r2:]
    oout[16:] = f_b[1, r2 : r2 + 8]
    rd.go(4)
    rv.go(4)
    rc.go(5)
    for k in range(3):
        for p in range(2):
            oqkv[:, d * k + 128 * p : d * k + 128 * (p + 1)] = f_c[p, :n, 128 * k : 128 * (k + 1)]
    rd.go(5)
    rv.go(5)
    for k in range(3):
        oqkv[:, d * k + 256 : d * (k + 1)] = f_d[k // 2, (k % 2) * n : (k % 2 + 1) * n]
    ovec[...] = f_v[...]
    for copy in copies:
        copy.wait()
    out_copy.wait()


def block_call(tok, dup, tgt, weights):
    images, seq = dup.shape
    d = tok.shape[1]
    n = d // 16
    ff = 4 * d
    t = seq - 1
    w = images * t + 128
    vm = pltpu.VMEM
    dma = pltpu.SemaphoreType.DMA
    sd = jax.ShapeDtypeStruct
    column = vm((d, 128), F32)
    scratch = [
        vm((seq * images, d), BF16),
        vm((d // 128, seq * images, 128), F32),
        vm((d, w), BF16),
        vm((d + 16, w), BF16),
        vm((3 * d, w), BF16),
        vm((d + 16, w), BF16),
        vm((d + 16, w), BF16),
        vm((ff + 16, w), BF16),
        vm((ff, w), BF16),
        vm((d, w), BF16),
        vm((d, w), BF16),
        vm((d, w), BF16),
        vm((d, w), F32),
        vm((images * HEADS, t, t), BF16),
        vm((d, 3 * d), BF16),
        vm((d, d), BF16), vm((d, d), BF16),
        vm((d, ff), BF16),
        vm((d, ff), BF16),
        vm((2, 32 * n + 256, d), BF16),
        vm((2, ff, d), BF16),
        column, column, column, column, column, column, column, vm((ff, 128), F32), column,
        vm((images + 1, 8, t), F32),
        vm((images, 8, t), F32),
        vm((images, 8, t), F32),
        vm((images, 8, t), F32),
        vm((images, 8, 128), F32),
        column,
        vm((3 * d, 128), F32),
        column, column, column, column,
        column,
        vm((8, ff), F32),
        vm((2, 128, 128), F32),
        vm((8, d), F32),
        vm((2, 32 * n, 128), BF16),
        vm((2, 128, 128), F32),
    ]
    scratch += [vm((slots * 8, 128), F32) for slots in (16, 8, 4, 3)]
    scratch += [vm((2, r, d), F32) for r in (2 * n, 2 * n + 16, n + 8)] + [vm((2, 2 * n, 128), F32), vm((2, 8, 128), F32)]
    scratch += [dma((4,)), dma((2, 16))] + [dma((2, 7))] * 8 + [pltpu.SemaphoreType.REGULAR((4,))]
    spec = pl.BlockSpec(memory_space=pltpu.VMEM)
    any_spec = pl.BlockSpec(memory_space=pl.ANY)
    return pl.pallas_call(
        block_body,
        out_shape=(
            sd(tok.shape, BF16), sd(tok.shape, F32),
            sd((n, 3 * d), F32), sd((n, d), F32), sd((n, ff), F32), sd((4 * n, d), F32), sd((2, 8, 128), F32),
        ),
        in_specs=[any_spec] + [spec] * 14,
        out_specs=(any_spec, any_spec) + (spec,) * 5,
        scratch_shapes=scratch,
        compiler_params=pltpu.CompilerParams(
            collective_id=0, has_side_effects=True, vmem_limit_bytes=64 * 1024 * 1024
        ),
        name="block16",
    )(tok, dup, tgt, *weights)


def deliver_body(out, gin, gqkv, gout, g1, g2, gv, *refs):
    o_out, o_gin, o_ln1g, o_ln1b, o_qkv, o_qvb, o_w, o_bout, o_ln2g, o_ln2b, o_fc1, o_b1, o_fc2, o_b2 = refs[:14]
    buf_out, buf_gin, sems = refs[14:]
    n = gqkv.shape[0]
    pieces = []
    for k, (src, buf, dst) in enumerate(((out, buf_out, o_out), (gin, buf_gin, o_gin))):
        count = 1 + 3 * k
        size = (src.shape[0] // count) // 16 * 16
        for m in range(count):
            rows = pl.ds(m * size, size if m < count - 1 else src.shape[0] - m * size)
            s = k + m
            pieces.append((
                pltpu.make_async_copy(src.at[rows], buf.at[rows], sems.at[0, s]),
                pltpu.make_async_copy(buf.at[rows], dst.at[rows], sems.at[1, s]),
            ))
    for load, store in pieces:
        load.start()
    o_qkv[...] = gqkv[...]
    o_w[...] = gout[...]
    o_fc1[...] = g1[...]
    o_fc2[...] = g2[...]
    for ref, row in ((o_ln1g, LN1G), (o_ln1b, LN1B), (o_bout, BOUT), (o_ln2g, LN2G), (o_ln2b, LN2B), (o_b2, BFC2)):
        ref[...] = gv[0, row, :n]
    o_qvb[...] = jnp.concatenate([gv[1, k, :n] for k in range(2)], 0)
    o_b1[...] = jnp.concatenate([gv[1, 2 + k, :n] for k in range(4)], 0)
    for load, store in pieces:
        load.wait()
        store.start()
    for load, store in pieces:
        store.wait()


def deliver_call(out, gin, gqkv, gout, g1, g2, gv):
    n, d = gout.shape
    sd = jax.ShapeDtypeStruct
    spec = pl.BlockSpec(memory_space=pltpu.VMEM)
    any_spec = pl.BlockSpec(memory_space=pl.ANY)
    vec = sd((n,), F32)
    return pl.pallas_call(
        deliver_body,
        out_shape=(
            sd(out.shape, BF16), sd(gin.shape, F32), vec, vec, sd((n, 3 * d), F32), sd((2 * n,), F32),
            sd((n, d), F32), vec, vec, vec, sd((n, 4 * d), F32), sd((4 * n,), F32), sd((4 * n, d), F32), vec,
        ),
        in_specs=[any_spec, any_spec] + [spec] * 5,
        out_specs=(any_spec, any_spec) + (spec,) * 12,
        scratch_shapes=[
            pltpu.VMEM(out.shape, BF16), pltpu.VMEM(gin.shape, F32), pltpu.SemaphoreType.DMA((2, 6)),
        ],
        compiler_params=pltpu.CompilerParams(vmem_limit_bytes=64 * 1024 * 1024),
        name="deliver",
    )(out, gin, gqkv, gout, g1, g2, gv)


def gather_all(value):
    return lax.all_gather(value, "fsdp", axis=0, tiled=True)


def vectors(full):
    ln1_gain, ln1_bias, qv_bias, out_bias, ln2_gain, ln2_bias, fc1_bias, fc2_bias = full
    d = ln1_gain.shape[0]
    bias = jnp.concatenate([qv_bias[:d], jnp.zeros((d,), qv_bias.dtype), qv_bias[d:]])
    rows = (ln1_gain, ln1_bias, bias, out_bias, ln2_gain, ln2_bias, fc1_bias, fc2_bias)
    width = fc1_bias.shape[0]
    return jnp.stack([jnp.pad(row.astype(F32), (0, width - row.shape[0])) for row in rows], 0)


def per_device(tokens, duplicate, targets, *weights, block16):
    images, seq, d = tokens.shape
    rows = tokens.transpose(1, 0, 2).reshape(seq * images, d)
    back = lambda v: v.reshape(seq, images, d).transpose(1, 0, 2)
    if block16:
        results = deliver_call(*block_call(rows, duplicate, targets, weights))
        return (back(results[0]), back(results[1])) + tuple(results[2:])

    (
        ln1_gain, ln1_bias, qkv_weight, qv_bias, out_weight, out_bias,
        ln2_gain, ln2_bias, fc1_weight, fc1_bias, fc2_weight, fc2_bias,
    ) = weights
    small = (ln1_gain, ln1_bias, qv_bias, out_bias, ln2_gain, ln2_bias, fc1_bias, fc2_bias)
    wqkv, wout, w1, w2 = map(gather_all, (qkv_weight, out_weight, fc1_weight, fc2_weight))
    vec = vectors(tuple(map(gather_all, small)))
    out, gin, gqkv, gout, g1, g2, gvec = compute(rows, duplicate, targets, vec, wqkv, wout, w1, w2)

    def scatter(value):
        value = lax.psum_scatter(value.astype(F32), "fsdp", scatter_dimension=0, tiled=True)
        return lax.psum(value, "dp")

    gqkv, gout, g1, g2 = map(scatter, (gqkv, gout, g1, g2))
    gvec = lax.psum(gvec, ("fsdp", "dp"))
    p = lax.axis_index("fsdp")

    def shard(value, whole_size):
        count = whole_size // lax.axis_size("fsdp")
        return lax.dynamic_slice(value, (p * count,), (count,))

    qv_grad = jnp.concatenate([gvec[2, :d], gvec[2, 2 * d : 3 * d]])
    return (
        back(out), back(gin),
        shard(gvec[0], d), shard(gvec[1], d), gqkv, shard(qv_grad, 2 * d), gout, shard(gvec[3], d),
        shard(gvec[4], d), shard(gvec[5], d), g1, shard(gvec[6], 4 * d), g2, shard(gvec[7], d),
    )


def solution(mesh):
    block16 = mesh.shape["fsdp"] == 16 and mesh.shape["dp"] == 2
    both = ("fsdp", "dp")
    vector, matrix = P("fsdp"), P("fsdp", None)
    weights = (vector, vector, matrix, vector, matrix, vector, vector, vector, matrix, vector, matrix, vector)
    return jax.shard_map(
        functools.partial(per_device, block16=block16),
        mesh=mesh,
        in_specs=(P(both, None, None), P(both, None), P(both, None)) + weights,
        out_specs=(P(both, None, None), P(both, None, None)) + weights,
        check_vma=False,
    )
```

```python
import functools
import jax
import jax.numpy as jnp
from jax import lax
from jax.experimental import pallas as pl
from jax.experimental.pallas import tpu as pltpu
from jax.sharding import PartitionSpec as P

HEADS = 6
HD = 64
EPS = 1e-06
F32 = jnp.float32
BF16 = jnp.bfloat16

NN = (((1,), (0,)), ((), ()))
NT = (((1,), (1,)), ((), ()))


def mm(a, b, dims=NN):
    return lax.dot_general(a, b, dims, preferred_element_type=F32)


def normalise(v):
    mu = jnp.mean(v, 0, keepdims=True)
    c = v - mu
    r = lax.rsqrt(jnp.mean(c * c, 0, keepdims=True) + EPS)
    return c * r, r


def norm_back(dn, u, r, gain):
    e = dn * gain
    me = jnp.mean(e, 0, keepdims=True)
    meu = jnp.mean(e * u, 0, keepdims=True)
    return r * (e - me - u * meu)


def fold(v):
    lanes = v.shape[1]
    total = v[:, :128]
    for k in range(1, lanes // 128):
        total = total + v[:, 128 * k : 128 * (k + 1)]
    return total


def wide(col, lanes):
    if lanes == 128:
        return col
    return jnp.concatenate([col] * (lanes // 128), 1)


def gelu_pair(x):
    z = x * 0.7071067811865476
    bell = jnp.exp(-(z * z))
    tail = lax.erf(z)
    half = 0.5 * x
    return half + half * tail, 0.5 + (0.5 * tail + (x * 0.3989422804014327) * bell)


LN1G, LN1B, BQKV, BOUT, LN2G, LN2B, BFC1, BFC2 = range(8)


def to_columns(vec, row, count):
    return jnp.broadcast_to(vec[row : row + 1, :count], (128, count)).T


def compute_body(
    tok, dup, tgt, vec, wqkv, wout, w1, w2,
    out, gin, gqkv, gout, g1, g2, gvec,
    xs, n1, qkv, att, n2, act, dpre, db2, db1, dos, dmid, probs,
    wqkv_t, wout_t, w1_t, w2_t,
    c_ln1g, c_ln1b, c_bqkv, c_bout, c_ln2g, c_ln2b, c_b1, c_b2,
    rl_s, ex_s, exq_s, rlx_s, exx_s, attx, dqkvx, a_g1, a_b1, a_g2, a_b2, tgt_t, stage, gin_sem,
):
    images, seq = dup.shape
    d = tok.shape[1]
    t = seq - 1
    x0 = images * t
    ff = w1.shape[1]
    w = x0 + 128
    dqkv = act.at[: 3 * d]

    blocks = d // 128

    def load_image(i):
        return jnp.concatenate([stage[b, pl.ds(i, t, stride=images), :] for b in range(blocks)], 1)

    def store_image(i, values):
        for b in range(blocks):
            stage[b, pl.ds(i, t, stride=images), :] = values[:, 128 * b : 128 * (b + 1)]

    def store_last(values):
        for b in range(blocks):
            stage[b, x0:, :] = values[:images, 128 * b : 128 * (b + 1)]

    def lanes_of(i):
        return pl.ds(pl.multiple_of(i * t, 128), t)

    extra_lanes = pl.ds(x0, 128)

    tok_copy = pltpu.make_async_copy(tok, out, gin_sem.at[0])
    tok_copy.start()
    tok_copy.wait()
    wqkv_t[...] = wqkv[...].T
    wout_t[...] = wout[...].T
    w1_t[...] = w1[...].T
    w2_t[...] = w2[...].T
    c_ln1g[...] = to_columns(vec, LN1G, d)
    c_ln1b[...] = to_columns(vec, LN1B, d)
    c_bqkv[...] = to_columns(vec, BQKV, 3 * d)
    c_bout[...] = to_columns(vec, BOUT, d)
    c_ln2g[...] = to_columns(vec, LN2G, d)
    c_ln2b[...] = to_columns(vec, LN2B, d)
    c_b1[...] = to_columns(vec, BFC1, ff)
    c_b2[...] = to_columns(vec, BFC2, d)
    tgt_t[...] = jnp.concatenate([tgt[...], jnp.zeros((128 - images, d), F32)], 0).T
    ones_row = jnp.where(lax.broadcasted_iota(jnp.int32, (16, w), 0) == 0, 1.0, 0.0).astype(BF16)
    n1[d : d + 16, :] = ones_row
    n2[d : d + 16, :] = ones_row
    att[d : d + 16, :] = ones_row
    act[ff : ff + 16, :] = ones_row
    attx[...] = jnp.zeros_like(attx)
    dqkvx[...] = jnp.zeros_like(dqkvx)
    for acc in (a_g1, a_b1, a_g2, a_b2):
        acc[...] = jnp.zeros_like(acc)

    def project(x_t, lanes, count):
        x = x_t.astype(F32)
        xs[:, lanes] = x_t
        u, r = normalise(x)
        n = (u * wide(c_ln1g[...], count) + wide(c_ln1b[...], count)).astype(BF16)
        n1[:d, lanes] = n
        for k in range(3):
            rows = slice(k * d, (k + 1) * d)
            y = mm(wqkv_t[rows, :], n) + wide(c_bqkv[rows, :], count)
            y = y.astype(BF16)
            if k == 0:
                y = y * jnp.asarray(HD**-0.5, BF16)
            qkv[rows, lanes] = y

    def project_image(i, carry):
        project(load_image(i).astype(BF16).T, lanes_of(i), t)
        return carry

    for b in range(blocks):
        stage[b] = out[:, 128 * b : 128 * (b + 1)].astype(F32)

    lax.fori_loop(0, images, project_image, 0)
    last = jnp.concatenate([out[x0:, :].astype(F32), jnp.zeros((128 - images, d), F32)], 0)
    project(last.astype(BF16).T, extra_lanes, 128)

    lane_ids = lax.broadcasted_iota(jnp.int32, (HD, 128), 1)

    def pick(ref, row, i):
        block = ref[row : row + HD, extra_lanes].astype(F32)
        return jnp.sum(jnp.where(lane_ids == i, block, 0.0), 1, keepdims=True)

    def attend_image(i, carry):
        lanes = lanes_of(i)
        for h in range(HEADS):
            r0 = h * HD
            q = qkv[r0 : r0 + HD, lanes]
            k = qkv[d + r0 : d + r0 + HD, lanes]
            v = qkv[2 * d + r0 : 2 * d + r0 + HD, lanes]
            qx, kx, vx = pick(qkv, r0, i), pick(qkv, d + r0, i), pick(qkv, 2 * d + r0, i)
            s = mm(k.T, q)
            sx = jnp.sum(q.astype(F32) * kx, 0, keepdims=True)
            top = jnp.maximum(jnp.max(s, 0, keepdims=True), sx)
            e = jnp.exp(s - top)
            ex = jnp.exp(sx - top)
            rl = 1.0 / (jnp.sum(e, 0, keepdims=True) + ex)
            e = e.astype(BF16)
            probs[i * HEADS + h] = e
            o = (mm(v, e) + vx * ex) * rl
            att[r0 : r0 + HD, lanes] = o.astype(BF16)
            rl_s[i, h : h + 1, :] = rl
            ex_s[i, h : h + 1, :] = ex
            sq = jnp.sum(k.astype(F32) * qx, 0, keepdims=True)
            sxx = jnp.sum(kx * qx, 0, keepdims=True)
            topx = jnp.maximum(jnp.max(sq, 1, keepdims=True), sxx)
            eq = jnp.exp(sq - topx)
            exx = jnp.exp(sxx - topx)
            rlx = 1.0 / (jnp.sum(eq, 1, keepdims=True) + exx)
            ox = (jnp.sum(v.astype(F32) * eq, 1, keepdims=True) + vx * exx) * rlx
            attx[r0 : r0 + HD, :] = jnp.where(lane_ids == i, ox, attx[r0 : r0 + HD, :])
            exq_s[i, h : h + 1, :] = eq
            rlx_s[i, h : h + 1, :] = jnp.broadcast_to(rlx, (1, 128))
            exx_s[i, h : h + 1, :] = jnp.broadcast_to(exx, (1, 128))
        return carry

    lax.fori_loop(0, images, attend_image, 0)
    att[:d, extra_lanes] = attx[...].astype(BF16)

    def feed(lanes, count, d_final):
        mid = xs[:, lanes].astype(F32) + mm(wout_t[...], att[:d, lanes]) + wide(c_bout[...], count)
        u, r = normalise(mid)
        n = (u * wide(c_ln2g[...], count) + wide(c_ln2b[...], count)).astype(BF16)
        n2[:d, lanes] = n
        db = d_final.astype(BF16)
        db2[:, lanes] = db
        for j in range(ff // 256):
            rows = slice(256 * j, 256 * (j + 1))
            pre = mm(w1_t[rows, :], n) + wide(c_b1[rows, :], count)
            da = mm(w2[rows, :], db)
            value, slope = gelu_pair(pre)
            act[rows, lanes] = value.astype(BF16)
            dpre[rows, lanes] = (slope * da).astype(BF16)
        final = mid + mm(w2_t[...], act[:ff, lanes]) + wide(c_b2[...], count)
        dn = mm(w1[...], dpre[:, lanes])
        a_g2[...] += fold(dn * u)
        a_b2[...] += fold(dn)
        dm = d_final + norm_back(dn, u, r, wide(c_ln2g[...], count))
        dmid[:, lanes] = dm
        low = dm.astype(BF16)
        db1[:, lanes] = low
        dos[:, lanes] = mm(wout[...], low).astype(BF16)
        return final.T

    def keep_row(row):
        first = lax.broadcasted_iota(jnp.int32, row.shape, 1) == 0
        return jnp.where(first, 1.0, 1.0 - row.astype(F32))

    def feed_image(i, carry):
        keep = keep_row(dup[pl.ds(i, 1), :])
        count = jnp.sum(keep, 1, keepdims=True)
        scale = seq * keep[:, :t] / count
        ids = lax.broadcasted_iota(jnp.int32, (d, 128), 1)
        target = jnp.sum(jnp.where(ids == i, tgt_t[...], 0.0), 1, keepdims=True)
        store_image(i, feed(lanes_of(i), t, target * scale))
        return carry

    lax.fori_loop(0, images, feed_image, 0)
    keep_all = keep_row(dup[...])
    scale_x = seq * keep_all[:, t:] / jnp.sum(keep_all, 1, keepdims=True)
    scale_x = jnp.broadcast_to(scale_x, (images, 128))
    scale_x = jnp.concatenate([scale_x, jnp.zeros((128 - images, 128), F32)], 0).T[:1, :]
    store_last(feed(extra_lanes, 128, tgt_t[...] * scale_x))
    for b in range(blocks):
        out[:, 128 * b : 128 * (b + 1)] = stage[b].astype(BF16)

    for j in range(ff // 256):
        rows = slice(256 * j, 256 * (j + 1))
        g = mm(n2[...], dpre[rows, :], NT)
        g1[:, rows] = g[:d].astype(BF16)
        gvec[BFC1 : BFC1 + 1, rows] = g[d : d + 1]
        g2[rows, :] = mm(act[rows, :], db2[...], NT).astype(BF16)
    g = mm(act[ff : ff + 16, :], db2[...], NT)
    gvec[BFC2 : BFC2 + 1, :d] = g[:1]

    def attend_back(i, carry):
        lanes = lanes_of(i)
        for h in range(HEADS):
            r0 = h * HD
            q = qkv[r0 : r0 + HD, lanes]
            k = qkv[d + r0 : d + r0 + HD, lanes]
            v = qkv[2 * d + r0 : 2 * d + r0 + HD, lanes]
            qx, kx, vx = pick(qkv, r0, i), pick(qkv, d + r0, i), pick(qkv, 2 * d + r0, i)
            rl = rl_s[i, h : h + 1, :]
            ex = ex_s[i, h : h + 1, :]
            do = dos[r0 : r0 + HD, lanes].astype(F32) * rl
            dot_o = jnp.sum(do * att[r0 : r0 + HD, lanes].astype(F32), 0, keepdims=True)
            dol = do.astype(BF16)
            p = probs[i * HEADS + h]
            ds = (p.astype(F32) * (mm(v.T, dol) - dot_o)).astype(BF16)
            dsx = ex * (jnp.sum(do * vx, 0, keepdims=True) - dot_o)
            dq = mm(k, ds) + kx * dsx
            dk = mm(q, ds, NT)
            dv = mm(dol, p, NT)
            qf = q.astype(F32)
            kf = k.astype(F32)
            vf = v.astype(F32)
            dkx = jnp.sum(qf * dsx, 1, keepdims=True)
            dvx = jnp.sum(do * ex, 1, keepdims=True)
            eq = exq_s[i, h : h + 1, :]
            rlx = rlx_s[i, h : h + 1, :1]
            exx = exx_s[i, h : h + 1, :1]
            dox = pick(dos, r0, i) * rlx
            dotx = jnp.sum(dox * pick(att, r0, i), 0, keepdims=True)
            dsq = eq * (jnp.sum(vf * dox, 0, keepdims=True) - dotx)
            dsxx = exx * (jnp.sum(vx * dox, 0, keepdims=True) - dotx)
            dqx = jnp.sum(kf * dsq, 1, keepdims=True) + kx * dsxx
            dk = dk + qx * dsq
            dv = dv + dox * eq
            dkx = dkx + qx * dsxx
            dvx = dvx + dox * exx
            scale = HD**-0.5
            for base, main, tail in ((0, dq * scale, dqx * scale), (d, dk, dkx), (2 * d, dv, dvx)):
                rows = slice(base + r0, base + r0 + HD)
                dqkv[rows, lanes] = main.astype(BF16)
                dqkvx[rows, :] = jnp.where(lane_ids == i, tail, dqkvx[rows, :])
        return carry

    lax.fori_loop(0, images, attend_back, 0)
    dqkv[:, extra_lanes] = dqkvx[...].astype(BF16)

    for k in range(3):
        rows = slice(k * d, (k + 1) * d)
        g = mm(n1[...], dqkv[rows, :], NT)
        gqkv[:, rows] = g[:d].astype(BF16)
        gvec[BQKV : BQKV + 1, rows] = g[d : d + 1]
    g = mm(att[...], db1[...], NT)
    gout[...] = g[:d].astype(BF16)
    gvec[BOUT : BOUT + 1, :d] = g[d : d + 1]

    def finish(lanes, count):
        u, r = normalise(xs[:, lanes].astype(F32))
        dn = mm(wqkv[...], dqkv[:, lanes])
        a_g1[...] += fold(dn * u)
        a_b1[...] += fold(dn)
        return (dmid[:, lanes] + norm_back(dn, u, r, wide(c_ln1g[...], count))).T

    def finish_image(i, carry):
        store_image(i, finish(lanes_of(i), t))
        return carry

    lax.fori_loop(0, images, finish_image, 0)
    store_last(finish(extra_lanes, 128))
    copies = [
        pltpu.make_async_copy(stage.at[b], gin.at[:, pl.ds(128 * b, 128)], gin_sem.at[b]) for b in range(blocks)
    ]
    for copy in copies:
        copy.start()

    for row, acc in ((LN1G, a_g1), (LN1B, a_b1), (LN2G, a_g2), (LN2B, a_b2)):
        gvec[row : row + 1, :d] = jnp.sum(acc[...].T, 0, keepdims=True)
    for copy in copies:
        copy.wait()


def compute(tok, dup, tgt, vec, wqkv, wout, w1, w2):
    images, seq = dup.shape
    d = tok.shape[1]
    ff = w1.shape[1]
    t = seq - 1
    w = images * t + 128
    vm = pltpu.VMEM
    scratch = [
        vm((d, w), BF16),
        vm((d + 16, w), BF16),
        vm((3 * d, w), BF16),
        vm((d + 16, w), BF16),
        vm((d + 16, w), BF16),
        vm((ff + 16, w), BF16),
        vm((ff, w), BF16),
        vm((d, w), BF16),
        vm((d, w), BF16),
        vm((d, w), BF16),
        vm((d, w), F32),
        vm((images * HEADS, t, t), BF16),
        vm((3 * d, d), BF16),
        vm((d, d), BF16),
        vm((ff, d), BF16),
        vm((d, ff), BF16),
        vm((d, 128), F32), vm((d, 128), F32), vm((3 * d, 128), F32), vm((d, 128), F32),
        vm((d, 128), F32), vm((d, 128), F32), vm((ff, 128), F32), vm((d, 128), F32),
        vm((images, 8, t), F32),
        vm((images, 8, t), F32),
        vm((images, 8, t), F32),
        vm((images, 8, 128), F32),
        vm((images, 8, 128), F32),
        vm((d, 128), F32),
        vm((3 * d, 128), F32),
        vm((d, 128), F32), vm((d, 128), F32), vm((d, 128), F32), vm((d, 128), F32),
        vm((d, 128), F32),
        vm((d // 128, images * seq, 128), F32),
        pltpu.SemaphoreType.DMA((d // 128,)),
    ]
    outs = (
        jax.ShapeDtypeStruct(tok.shape, BF16),
        jax.ShapeDtypeStruct(tok.shape, F32),
        jax.ShapeDtypeStruct((d, 3 * d), BF16),
        jax.ShapeDtypeStruct((d, d), BF16),
        jax.ShapeDtypeStruct((d, ff), BF16),
        jax.ShapeDtypeStruct((ff, d), BF16),
        jax.ShapeDtypeStruct((8, ff), F32),
    )
    spec = pl.BlockSpec(memory_space=pltpu.VMEM)
    return pl.pallas_call(
        compute_body,
        out_shape=outs,
        in_specs=[pl.BlockSpec(memory_space=pl.ANY)] + [spec] * 7,
        out_specs=(spec, pl.BlockSpec(memory_space=pl.ANY)) + (spec,) * 5,
        scratch_shapes=scratch,
        compiler_params=pltpu.CompilerParams(vmem_limit_bytes=64 * 1024 * 1024),
        name="block",
    )(tok, dup, tgt, vec, wqkv, wout, w1, w2)

MESH_ID = pl.DeviceIdType.MESH
NZ = 4
UNITS = 2
UNITS1 = 1
UNITS2 = 2
CHUNK = 2
FFB = 128


class Place:
    def __init__(self):
        p = lax.axis_index("fsdp")
        self.p = p
        self.c = lax.axis_index("dp")
        self.x = lax.rem(p, 2)
        self.y = lax.rem(lax.div(p, 2), 2)
        self.z = lax.div(p, 4)
        self.a = self.y + self.c * (self.x - self.y)
        self.b = self.x + self.c * (self.y - self.x)

    def device(self, x, y, z):
        return ((z * 2 + y) * 2 + x, self.c)

    def along_a(self):
        c = self.c
        return self.device(self.x + c * (1 - 2 * self.x), self.y + (1 - c) * (1 - 2 * self.y), self.z)

    def along_b(self):
        c = self.c
        return self.device(self.x + (1 - c) * (1 - 2 * self.x), self.y + c * (1 - 2 * self.y), self.z)

    def along_z(self, step):
        return lax.rem(self.z + step, NZ)

    def sibling(self):
        return (self.p, 1 - self.c)

    def everyone(self):
        return [(lax.rem(self.p + k, 16), self.c) for k in range(1, 16)]


def slot_of(p, group):
    x, y, z = p % 2, (p // 2) % 2, p // 4
    a, b = (y, x) if group == 0 else (x, y)
    return (a * 2 + b) * NZ + z


def greet(at):
    barrier = pltpu.get_barrier_semaphore()
    others = [at.sibling()] + at.everyone()
    for device in others:
        pl.semaphore_signal(barrier, inc=1, device_id=device, device_id_type=MESH_ID)


def remote(src, dst, sems, k, device):
    return pltpu.make_async_remote_copy(
        src_ref=src, dst_ref=dst, send_sem=sems.at[0, k], recv_sem=sems.at[1, k],
        device_id=device, device_id_type=MESH_ID,
    )


def span(start, size):
    return pl.ds(pl.multiple_of(start, size), size)


class Gather:
    def __init__(self, at, buf, r, sems, swap):
        self.at, self.buf, self.r, self.sems, self.shared = at, buf, r, sems, swap

    def part(self, rows, k, device):
        piece = self.buf.at[rows]
        return remote(piece, piece, self.sems, k, device)

    def line(self):
        at, r = self.at, self.r
        rows = span(((at.a * 2 + at.b) * NZ + at.z) * r, r)
        return [
            self.part(rows, step - 1, at.device(at.x, at.y, at.along_z(step))) for step in range(1, NZ)
        ]

    def over_b(self):
        at, r = self.at, self.r
        return [self.part(span((at.a * 2 + at.b) * NZ * r, NZ * r), 3, at.along_b())]

    def over_a(self):
        at, r = self.at, self.r
        return [self.part(span(at.a * 2 * NZ * r, 2 * NZ * r), 4, at.along_a())]

    def swap(self):
        return [remote(self.buf, self.buf, self.sems, 5, self.at.sibling())] if self.shared else []

    def go(self, step):
        steps = (self.line, self.over_b, self.over_a, self.swap)
        if step > 0:
            for copy in steps[step - 1]():
                copy.wait()
        if step < 4:
            for copy in steps[step]():
                copy.start()


class Spread:
    def __init__(self, at, buf, r, sems):
        self.at, self.buf, self.r, self.sems = at, buf, r, sems

    def direct(self):
        at, r = self.at, self.r
        piece = self.buf.at[span((at.c * 16 + at.p) * r, r)]
        return [remote(piece, piece, self.sems, k, device) for k, device in enumerate(at.everyone())]

    def swap(self):
        piece = self.buf.at[span(self.at.c * 16 * self.r, 16 * self.r)]
        return [remote(piece, piece, self.sems, 15, self.at.sibling())]

    def go(self, step):
        steps = (self.direct, self.swap)
        if step > 0:
            for copy in steps[step - 1]():
                copy.wait()
        if step < 2:
            for copy in steps[step]():
                copy.start()


class Reduce:
    def __init__(self, at, full, got, from_a, from_b, from_z, total, r, sems):
        self.at, self.full, self.got = at, full, got
        self.from_a, self.from_b, self.from_z, self.total = from_a, from_b, from_z, total
        self.r, self.sems = r, sems

    def first(self):
        return [remote(self.full.at[1 - self.at.c], self.got, self.sems, 0, self.at.sibling())]

    def over_a(self):
        at, r = self.at, self.r
        rows = span((1 - at.a) * 2 * NZ * r, 2 * NZ * r)
        return [remote(self.full.at[at.c, rows], self.from_a, self.sems, 1, at.along_a())]

    def over_b(self):
        at, r = self.at, self.r
        rows = span((at.a * 2 + 1 - at.b) * NZ * r, NZ * r)
        return [remote(self.full.at[at.c, rows], self.from_b, self.sems, 2, at.along_b())]

    def line(self):
        at, r = self.at, self.r
        copies = []
        for step in range(1, NZ):
            other = at.along_z(step)
            rows = span(((at.a * 2 + at.b) * NZ + other) * r, r)
            copies.append(
                remote(self.full.at[at.c, rows], self.from_z.at[pl.ds((step - 1) * r, r)], self.sems, 2 + step, at.device(at.x, at.y, other))
            )
        return copies

    def last(self):
        piece = self.total.at[self.at.c]
        return [remote(piece, piece, self.sems, 6, self.at.sibling())]

    def add(self, rows, values):
        ref = self.full.at[self.at.c, rows]
        ref[...] = (ref[...].astype(F32) + values.astype(F32)).astype(ref.dtype)

    def go(self, step):
        at, r = self.at, self.r
        steps = (self.first, self.over_a, self.over_b, self.line, self.last)
        if step > 0:
            for copy in steps[step - 1]():
                copy.wait()
        if step == 1:
            for half in range(2):
                rows = pl.ds(half * 2 * NZ * r, 2 * NZ * r)
                self.add(rows, self.got[rows, :])
        elif step == 2:
            self.add(span(at.a * 2 * NZ * r, 2 * NZ * r), self.from_a[...])
        elif step == 3:
            self.add(span((at.a * 2 + at.b) * NZ * r, NZ * r), self.from_b[...])
        elif step == 4:
            total = self.full[at.c, span(((at.a * 2 + at.b) * NZ + at.z) * r, r), :].astype(F32)
            for k in range(NZ - 1):
                total = total + self.from_z[k * r : (k + 1) * r, :].astype(F32)
            self.total[at.c] = total
        if step < 5:
            for copy in steps[step]():
                copy.start()


class ReduceAtOnce:
    def __init__(self, at, full, got, landing, total, r, sems):
        self.at, self.full, self.got, self.landing, self.total = at, full, got, landing, total
        self.r, self.sems = r, sems

    def first(self):
        return [remote(self.full.at[1 - self.at.c], self.got, self.sems, 15, self.at.sibling())]

    def direct(self):
        at, r = self.at, self.r
        return [
            remote(self.full.at[at.c, span(device[0] * r, r)], self.landing.at[pl.ds(k * r, r)], self.sems, k, device)
            for k, device in enumerate(at.everyone())
        ]

    def last(self):
        piece = self.total.at[self.at.c]
        return [remote(piece, piece, self.sems, 16, self.at.sibling())]

    def go(self, step):
        at, r = self.at, self.r
        steps = (self.first, self.direct, self.last)
        if step > 0:
            for copy in steps[step - 1]():
                copy.wait()
        if step == 1:
            ref = self.full.at[at.c]
            ref[...] = (ref[...].astype(F32) + self.got[...].astype(F32)).astype(ref.dtype)
        elif step == 2:
            total = self.full[at.c, span(at.p * r, r), :].astype(F32)
            for k in range(15):
                total = total + self.landing[k * r : (k + 1) * r, :].astype(F32)
            self.total[at.c] = total
        if step < 3:
            for copy in steps[step]():
                copy.start()


V_LN1G, V_LN1B, V_QV, V_BOUT, V_LN2G, V_LN2B, V_BFC2, V_BFC1 = 0, 1, 2, 4, 5, 6, 7, 8


def block_body(
    tok, dup, tgt, s_ln1g, s_ln1b, s_qkv, s_qvb, s_out, s_bout, s_ln2g, s_ln2b, s_fc1, s_b1, s_fc2, s_b2,
    out, gin, oqkv, oout, o1, o2, ovec,
    tokb, stage, xs, n1, qkv, att, n2, act, dpre, db2, db1, dos, dmid, probs,
    wqkv, wout, wout_t, w1, w2_t, wt_a, wf,
    c_ln1g, c_ln1b, c_q, c_v, c_bout, c_ln2g, c_ln2b, c_b1, c_b2,
    stat_s, rl_s, ex_s, pq_s, pxq_s, attx, dqkvx, a_g1, a_b1, a_g2, a_b2, tgt_t, gvec, allc, vec_s,
    tail_s, tail_g, tail_l, tv, uv, av, f_a, f_b, f_c, f_d, f_v,
    loc_sem, gsem0, gsem1, gsem2, gsem3, rsem_a, rsem_b, rsem_c, rsem_d, rsem_v, ready,
):
    images, seq = dup.shape
    d = tok.shape[1]
    t = seq - 1
    x0 = images * t
    ff = w1.shape[1]
    w = x0 + 128
    n = d // 16
    blocks = d // 128
    at = Place()
    every = range(16)
    pairs = HEADS // 2
    mine = pl.ds(pl.multiple_of(at.c * d, 128), d)
    own = (at.a * 2 + at.b) * NZ + at.z

    def lanes_of(i, count=1):
        return pl.ds(pl.multiple_of(i * t, 128), t * count)

    extra_lanes = pl.ds(x0, 128)

    def load_image(i):
        return jnp.concatenate([stage[b, pl.ds(i, t, stride=images), :] for b in range(blocks)], 1)

    def store_image(i, values):
        for b in range(blocks):
            stage[b, pl.ds(i, t, stride=images), :] = values[:, 128 * b : 128 * (b + 1)]

    def store_last(values):
        for b in range(blocks):
            stage[b, x0:, :] = values[:images, 128 * b : 128 * (b + 1)]

    greet(at)
    tok_copy = pltpu.make_async_copy(tok, tokb, loc_sem.at[0])
    tok_copy.start()

    r0, r2, r3 = n + 8, 2 * n, 2 * n + 16
    slots0 = act.at[: 16 * r0, :d]
    slots1 = act.at[16 * r0 : 32 * r0]
    slots2 = act.at[: 16 * r2]
    slots3 = dpre.at[: 16 * r3]
    group = [pl.ds(k * d, d) for k in range(4)]
    later_mine = pl.ds(pl.multiple_of((2 + at.c) * d, 128), d)
    q = s_qkv[...].astype(F32)

    def pair_of(p):
        return jnp.concatenate([q[:, d * k + 128 * p : d * k + 128 * (p + 1)] for k in range(3)], 1)

    vec_s[...] = jnp.zeros_like(vec_s)
    flat = [s_ln1g[...], s_ln1b[...], s_qvb[:n], s_qvb[n:], s_bout[...], s_ln2g[...], s_ln2b[...], s_b2[...]]
    flat += [s_b1[n * k : n * (k + 1)] for k in range(4)]
    for k, line in enumerate(flat):
        lo = 128 * (k // 8)
        vec_s[k % 8 : k % 8 + 1, lo : lo + n] = line.astype(F32).reshape(1, n)
    slot = jnp.concatenate([pair_of(0), vec_s[...]], 0)
    half = r0 // 2
    slots0[span((at.c * 16 + at.p) * half, half), :] = jnp.where(at.c == 0, slot[:half], slot[half:]).astype(BF16)
    own1, own2, own3 = (span(own * r, r) for r in (r0, r2, r3))
    w_out = s_out[...].astype(F32)
    blank = jnp.zeros((8, d), F32)

    @pl.when(at.c == 0)
    def _():
        f = s_fc1[...].astype(F32)
        slots1[own1, group[0]] = jnp.concatenate([pair_of(1), blank], 0).astype(BF16)
        slots2[own2, group[2]] = jnp.concatenate([f[:, :d], f[:, d : 2 * d]], 0).astype(BF16)
        parts = [f[:, 2 * d : 3 * d], f[:, 3 * d :], w_out[:16]]
        slots3[own3, group[0]] = jnp.concatenate(parts, 0).astype(BF16)

    @pl.when(at.c == 1)
    def _():
        slots1[own1, group[1]] = jnp.concatenate([pair_of(2), blank], 0).astype(BF16)
        slots2[own2, group[3]] = s_fc2[:r2]
        parts = [s_fc2[r2:].astype(F32), w_out[16:], blank]
        slots3[own3, group[1]] = jnp.concatenate(parts, 0).astype(BF16)

    pl.semaphore_wait(pltpu.get_barrier_semaphore(), 16)
    g0 = Spread(at, slots0, half, gsem0)
    g1 = Gather(at, slots1.at[:, mine], r0, gsem1, True)
    g2 = Gather(at, slots2.at[:, later_mine], r2, gsem2, True)
    g3 = Gather(at, slots3.at[:, mine], r3, gsem3, True)
    g0.go(0)

    tok_copy.wait()
    for b in range(blocks):
        stage[b] = tokb[:, 128 * b : 128 * (b + 1)].astype(F32)

    def statistics(x):
        mu = jnp.mean(x, 0, keepdims=True)
        c = x - mu
        return mu, lax.rsqrt(jnp.mean(c * c, 0, keepdims=True) + EPS)

    def turn(i, carry):
        x = load_image(i).astype(BF16).T
        xs[:, lanes_of(i)] = x
        mu, r = statistics(x.astype(F32))
        stat_s[i, 0:1, :] = mu
        stat_s[i, 1:2, :] = r
        return carry

    lax.fori_loop(0, images // 2, turn, 0)
    g1.go(0)
    lax.fori_loop(images // 2, images, turn, 0)
    last = jnp.concatenate([tokb[x0:, :].astype(F32), jnp.zeros((128 - images, d), F32)], 0)
    x = last.astype(BF16).T
    xs[:, extra_lanes] = x
    mu, r = statistics(x.astype(F32))
    stat_s[images, 0:1, :128] = mu
    stat_s[images, 1:2, :128] = r
    tgt_t[...] = jnp.concatenate([tgt[...], jnp.zeros((128 - images, d), F32)], 0).T
    ones_row = jnp.where(lax.broadcasted_iota(jnp.int32, (16, w), 0) == 0, 1.0, 0.0).astype(BF16)
    n1[d : d + 16, :] = ones_row
    n2[d : d + 16, :] = ones_row
    att[d : d + 16, :] = ones_row
    for ref in (attx, dqkvx, a_g1, a_b1, a_g2, a_b2):
        ref[...] = jnp.zeros_like(ref)
    g0.go(1)
    g1.go(1)
    g2.go(0)
    g0.go(2)
    g3.go(0)

    def slot_of_chip(p):
        parts = [slots0[(16 * k + p) * half : (16 * k + p + 1) * half, :].astype(F32) for k in range(2)]
        return jnp.concatenate(parts, 0)

    first = [slot_of_chip(p) for p in every]
    for half in range(2):
        rows = [s[n:, 128 * half : 128 * (half + 1)] for s in first]
        allc[half] = jnp.concatenate(rows, 0).T
    lane_ids = lax.broadcasted_iota(jnp.int32, (n, 128), 1)
    ones = jnp.ones((128, 128), BF16)

    def column(ref, entries):
        runs = [jnp.where(lane_ids == 8 * p + k % 8, allc[k // 8, :n, :], 0.0) for p, k in entries]
        ref[...] = mm(jnp.concatenate(runs, 0).astype(BF16), ones)

    column(c_ln1g, [(p, V_LN1G) for p in every])
    column(c_ln1b, [(p, V_LN1B) for p in every])
    column(c_q, [(p, V_QV + k) for p in range(8) for k in range(2)])
    column(c_v, [(p, V_QV + k) for p in range(8, 16) for k in range(2)])

    def put_pair(p, block):
        block = block.astype(BF16)
        wqkv[:, p * d : (p + 1) * d] = block
        wt_a[p // 2, (p % 2) * d : (p % 2 + 1) * d, :] = block.T

    put_pair(0, jnp.concatenate([s[:n] for s in first], 0))

    def unpack(slots, which, lanes, r, lo, hi):
        runs = []
        for p in every:
            s = slot_of(p, which)
            runs.append(slots[r * s : r * (s + 1), lanes].astype(F32)[lo:hi])
        return runs

    def project(p, lanes, count, mu=None, r=None):
        if p == 0:
            u = (xs[:, lanes].astype(F32) - mu) * r
            y = (u * wide(c_ln1g[...], count) + wide(c_ln1b[...], count)).astype(BF16)
            n1[:d, lanes] = y
        else:
            y = n1[:d, lanes]
        y = mm(wt_a[p // 2, (p % 2) * d : (p % 2 + 1) * d, :], y)
        heads = slice(128 * p, 128 * (p + 1))
        query = (y[:128] + wide(c_q[heads, :], count)).astype(BF16) * jnp.asarray(HD**-0.5, BF16)
        value = (y[256:] + wide(c_v[heads, :], count)).astype(BF16)
        qkv[p * d : (p + 1) * d, lanes] = jnp.concatenate([query, y[128:256].astype(BF16), value], 0)

    def rows_of(part, h):
        row = (h // 2) * d + part * 128 + (h % 2) * HD
        return slice(row, row + HD)

    head_lanes = lax.broadcasted_iota(jnp.int32, (HD, 128), 1)

    def pick(ref, rows, i):
        return jnp.sum(jnp.where(head_lanes == i, ref[rows, extra_lanes].astype(F32), 0.0), 1, keepdims=True)

    def row_dot(a, column):
        return jnp.sum(a.astype(F32) * column, 0, keepdims=True)

    def column_dot(a, row):
        return jnp.sum(a.astype(F32) * row, 1, keepdims=True)

    def place_column(ref, rows, i, column):
        ref[rows, :] = jnp.where(head_lanes == i, column, ref[rows, :])

    def score(i, h):
        q, k = (qkv[rows_of(part, h), lanes_of(i)] for part in range(2))
        qx, kx = (pick(qkv, rows_of(part, h), i) for part in range(2))
        vx = pick(qkv, rows_of(2, h), i)
        return mm(k.T, q), row_dot(q, kx), row_dot(k, qx), jnp.sum(qx * kx, 0, keepdims=True), vx

    def share(i, h, s, sx, sq, sxq, vx):
        top = jnp.maximum(jnp.max(s, 0, keepdims=True), sx)
        e = jnp.exp(s - top)
        ex = jnp.exp(sx - top)
        rl = 1.0 / (jnp.sum(e, 0, keepdims=True) + ex)
        e = e.astype(BF16)
        probs[i * HEADS + h] = e
        rl_s[i, h : h + 1, :] = rl
        ex_s[i, h : h + 1, :] = ex
        top = jnp.maximum(jnp.max(sq, 1, keepdims=True), sxq)
        eq = jnp.exp(sq - top)
        exq = jnp.exp(sxq - top)
        rlq = 1.0 / (jnp.sum(eq, 1, keepdims=True) + exq)
        pq = eq * rlq
        pxq = exq * rlq
        pq_s[i, h : h + 1, :] = pq
        pxq_s[i, h : h + 1, :] = jnp.broadcast_to(pxq, (1, 128))
        return e, ex, rl, pq, pxq, vx

    def mix(i, h, e, ex, rl, pq, pxq, vx):
        v = qkv[rows_of(2, h), lanes_of(i)]
        rows = slice(h * HD, (h + 1) * HD)
        att[rows, lanes_of(i)] = ((mm(v, e) + vx * ex) * rl).astype(BF16)
        place_column(attx, rows, i, column_dot(v, pq) + vx * pxq)

    def attend(units):
        scores = [score(*units[0])]
        shares = []
        for k, unit in enumerate(units):
            if k + 1 < len(units):
                scores.append(score(*units[k + 1]))
            shares.append(share(*unit, *scores[k]))
            if k >= 1:
                mix(*units[k - 1], *shares[k - 1])
        mix(*units[-1], *shares[-1])

    def forward_pair(p, steps):
        if p == 0:

            def project_image(i, carry):
                project(0, lanes_of(i), t, stat_s[i, 0:1, :], stat_s[i, 1:2, :])
                return carry

            lax.fori_loop(0, images, project_image, 0)
            project(0, extra_lanes, 128, stat_s[images, 0:1, :128], stat_s[images, 1:2, :128])
        else:

            def project_images(i, carry):
                project(p, lanes_of(2 * i, 2), 2 * t)
                return carry

            lax.fori_loop(0, images // 2, project_images, 0)
            project(p, extra_lanes, 128)
        for step in steps[0]:
            step()

        def attend_images(i, carry):
            attend([(UNITS * i + k, 2 * p + h) for k in range(UNITS) for h in range(2)])
            for when in range(images // UNITS):

                @pl.when(i == when)
                def _(when=when):
                    for step in steps[1 + when]:
                        step()

            return carry

        lax.fori_loop(0, images // UNITS, attend_images, 0)

    def later(item, step):
        return lambda: item.go(step)

    forward_pair(0, [[later(g1, 2), later(g2, 1)], [], [later(g3, 1)], [], [later(g1, 3), later(g2, 2)]])
    g1.go(4)
    for k in range(2):
        put_pair(1 + k, jnp.concatenate(unpack(slots1, k, group[k], r0, 0, n), 0))
    forward_pair(1, [[], [later(g3, 2)], [], [later(g2, 3)], []])
    forward_pair(2, [[], [later(g3, 3)], [], [], [later(g2, 4)]])
    att[:d, extra_lanes] = attx[...].astype(BF16)
    column(c_bout, [(p, V_BOUT) for p in every])
    column(c_ln2g, [(p, V_LN2G) for p in every])
    column(c_ln2b, [(p, V_LN2B) for p in every])
    column(c_b2, [(p, V_BFC2) for p in every])
    column(c_b1, [(p, V_BFC1 + k) for p in every for k in range(4)])
    g3.go(4)
    runs = zip(unpack(slots3, 0, group[0], r3, r2, r3), unpack(slots3, 1, group[1], r3, r2, r2 + 8))
    block = jnp.concatenate([part for run in runs for part in run], 0).astype(BF16)
    wout[...] = block
    wout_t[...] = block.T
    for k in range(4):
        slots, lanes, r = (slots2, group[2], r2) if k < 2 else (slots3, group[0], r3)
        block = jnp.concatenate(unpack(slots, 0, lanes, r, (k % 2) * n, (k % 2 + 1) * n), 0).astype(BF16)
        w1[:, k * d : (k + 1) * d] = block
        wf[0, k * d : (k + 1) * d, :] = block.T
    for p in every:
        s = slot_of(p, 1)
        for k, (slots, lanes, r) in enumerate(((slots2, group[3], r2), (slots3, group[1], r3))):
            start = 4 * n * p + r2 * k
            wf[1, start : start + r2, :] = slots[r * s : r * s + r2, lanes]
    w2_t[...] = wf[1].T
    act[ff : ff + 16, :] = ones_row

    def middle(lanes, count):
        return xs[:, lanes].astype(F32) + mm(wout_t[...], att[:d, lanes]) + wide(c_bout[...], count)

    def feed(lanes, count, d_final):
        u, r = normalise(middle(lanes, count))
        y = (u * wide(c_ln2g[...], count) + wide(c_ln2b[...], count)).astype(BF16)
        n2[:d, lanes] = y
        db = d_final.astype(BF16)
        db2[:, lanes] = db
        for j in range(ff // FFB):
            rows = slice(FFB * j, FFB * (j + 1))
            pre = mm(wf[0, rows, :], y) + wide(c_b1[rows, :], count)
            da = mm(wf[1, rows, :], db)
            value, slope = gelu_pair(pre)
            act[rows, lanes] = value.astype(BF16)
            dpre[rows, lanes] = (slope * da).astype(BF16)
        dn = mm(w1[...], dpre[:, lanes])
        a_g2[...] += fold(dn * u)
        a_b2[...] += fold(dn)
        dm = d_final + norm_back(dn, u, r, wide(c_ln2g[...], count))
        dmid[:, lanes] = dm
        low = dm.astype(BF16)
        db1[:, lanes] = low
        dos[:, lanes] = mm(wout[...], low).astype(BF16)

    def keep_row(row):
        position = lax.broadcasted_iota(jnp.int32, row.shape, 1) == 0
        return jnp.where(position, 1.0, 1.0 - row.astype(F32))

    def cotangent(i):
        keep = keep_row(dup[pl.ds(i, 1), :])
        scale = seq * keep[:, :t] / jnp.sum(keep, 1, keepdims=True)
        ids = lax.broadcasted_iota(jnp.int32, (d, 128), 1)
        return jnp.sum(jnp.where(ids == i, tgt_t[...], 0.0), 1, keepdims=True) * scale

    def feed_images(k, carry):
        d_final = jnp.concatenate([cotangent(CHUNK * k + m) for m in range(CHUNK)], 1)
        feed(lanes_of(CHUNK * k, CHUNK), CHUNK * t, d_final)
        return carry

    lax.fori_loop(0, images // CHUNK, feed_images, 0)
    keep_all = keep_row(dup[...])
    scale_x = seq * keep_all[:, t:] / jnp.sum(keep_all, 1, keepdims=True)
    scale_x = jnp.broadcast_to(scale_x, (images, 128))
    scale_x = jnp.concatenate([scale_x, jnp.zeros((128 - images, 128), F32)], 0).T[:1, :]
    feed(extra_lanes, 128, tgt_t[...] * scale_x)

    def put(buf, which, parts, lo=0, step=None, slot_at=slot_of):
        for p in every:
            slot = jnp.concatenate([part[n * p + a : n * p + b] for part, a, b in parts], 0).astype(BF16)
            start = step * slot_at(p, which) + lo
            buf[which, start : start + slot.shape[0], :] = slot

    for j in range(ff // 256):
        rows = slice(256 * j, 256 * (j + 1))
        g = mm(act[rows, :], db2[...], NT).astype(BF16)
        for lo in range(256 * j, 256 * (j + 1), 16):
            p, off = lo // (4 * n), lo % (4 * n)
            buf, r = (wf, r2) if off < r2 else (wt_a, r3)
            start = r * slot_of(p, 1) + off % r2
            buf[1, start : start + 16, :] = g[lo - 256 * j : lo - 256 * j + 16]
    g = mm(act[ff : ff + 16, :], db2[...], NT)
    gvec[BFC2 : BFC2 + 1, :d] = g[:1]

    def reducer(full, total, r, sems, width, places):
        refs = []
        for (row, lane), count in zip(places, (16, 8, 4, 3)):
            refs.append(dpre.at[row : row + count * r, lane : lane + width])
        return Reduce(at, full, *refs, total, r, sems)

    ra = reducer(wf.at[:, : 16 * r2], f_a, r2, rsem_a, d, [(k * r2, 0) for k in (0, 16, 24, 28)])
    rb = reducer(wt_a, f_b, r3, rsem_b, d, [(0, d), (16 * r3, d), (0, 2 * d), (4 * r3, 2 * d)])
    rc = reducer(
        wf.at[:, 16 * r2 : 16 * r2 + 16 * r0], f_c, r0, rsem_c, d, [(k * r0, 3 * d) for k in (0, 16, 24, 28)]
    )
    rd = ReduceAtOnce(at, tail_s, tail_g, tail_l, f_d, r2, rsem_d)
    rv = ReduceAtOnce(at, tv, uv, av, f_v, 8, rsem_v)
    gw = mm(att[...], db1[...], NT)
    gvec[BOUT : BOUT + 1, :d] = gw[d : d + 1]
    gw = gw[:d]
    for j in range(2):
        rows = slice(2 * d * j, 2 * d * (j + 1))
        g = mm(n2[...], dpre[rows, :], NT)
        gvec[BFC1 : BFC1 + 1, rows] = g[d : d + 1]
        parts = [(g[:d, :d], 0, n), (g[:d, d:], 0, n)]
        if j == 0:
            put(wf, 0, parts, step=r2)
        else:
            put(wt_a, 0, parts + [(gw, 0, 16)], step=r3)
    for p in every:
        start = r3 * slot_of(p, 1) + r2
        wt_a[1, start : start + 16, :] = jnp.concatenate([gw[n * p + 16 : n * (p + 1)], blank], 0).astype(BF16)

    partners = [at.sibling(), at.along_a(), at.along_b()]
    partners += [at.device(at.x, at.y, at.along_z(step)) for step in range(1, NZ)]
    for k, device in enumerate(partners):
        pl.semaphore_signal(ready.at[min(k, 3)], inc=1, device_id=device, device_id_type=MESH_ID)
    pl.semaphore_wait(ready.at[0], 1)
    ra.go(0)
    rb.go(0)

    def allowed(k):
        return lambda: pl.semaphore_wait(ready.at[k], 1 if k < 3 else NZ - 1)

    def slopes(i, h):
        rows = slice(h * HD, (h + 1) * HD)
        v = qkv[rows_of(2, h), lanes_of(i)]
        vx = pick(qkv, rows_of(2, h), i)
        do = dos[rows, lanes_of(i)].astype(F32) * rl_s[i, h : h + 1, :]
        doq = pick(dos, rows, i)
        dot_o = jnp.sum(do * att[rows, lanes_of(i)].astype(F32), 0, keepdims=True)
        dol = do.astype(BF16)
        dp = mm(v.T, dol)
        qx, kx = (pick(qkv, rows_of(part, h), i) for part in range(2))
        return qx, kx, dol, dot_o, dp, row_dot(do, vx), doq, row_dot(v, doq), jnp.sum(vx * doq, 0, keepdims=True)

    def scores_back(i, h, qx, kx, dol, dot_o, dp, dpx, doq, dpq, dpxq):
        p = probs[i * HEADS + h]
        ex = ex_s[i, h : h + 1, :]
        ds = (p.astype(F32) * (dp - dot_o)).astype(BF16)
        dsx = ex * (dpx - dot_o)
        pq = pq_s[i, h : h + 1, :]
        pxq = pxq_s[i, h : h + 1, :1]
        total = jnp.sum(pq * dpq, 1, keepdims=True) + pxq * dpxq
        return qx, kx, dol, p, ex, ds, dsx, doq, pq, pxq, pq * (dpq - total), pxq * (dpxq - total)

    def heads_back(i, h, qx, kx, dol, p, ex, ds, dsx, doq, pq, pxq, dsq, dsxq):
        q, k = (qkv[rows_of(part, h), lanes_of(i)] for part in range(2))
        scale = HD**-0.5
        dq = (mm(k, ds) + kx * dsx) * scale
        dk = mm(q, ds, NT) + qx * dsq
        dv = mm(dol, p, NT) + doq * pq
        place_column(dqkvx, rows_of(0, h), i, (column_dot(k, dsq) + kx * dsxq) * scale)
        place_column(dqkvx, rows_of(1, h), i, column_dot(q, dsx) + qx * dsxq)
        place_column(dqkvx, rows_of(2, h), i, column_dot(dol, ex) + doq * pxq)
        for part, value in enumerate((dq, dk, dv)):
            qkv[rows_of(part, h), lanes_of(i)] = value.astype(BF16)

    def attend_back(units):
        one = [slopes(*units[0])]
        two = []
        for k, unit in enumerate(units):
            if k + 1 < len(units):
                one.append(slopes(*units[k + 1]))
            two.append(scores_back(*unit, *one[k]))
            if k >= 1:
                heads_back(*units[k - 1], *two[k - 1])
        heads_back(*units[-1], *two[-1])

    def run_steps(i, steps):
        for when, todo in steps:

            @pl.when(i == when)
            def _(todo=todo):
                for step in todo:
                    step()

    def back_first(i, carry):
        attend_back([(UNITS1 * i + k, h) for k in range(UNITS1) for h in range(4)])
        run_steps(i, (
            (3, [allowed(1), later(ra, 1)]),
            (4, [later(rb, 1)]),
        ))
        return carry

    lax.fori_loop(0, images // UNITS1, back_first, 0)
    pl.semaphore_wait(ready.at[2], 1)
    ra.go(2)
    qkv[: 2 * d, extra_lanes] = dqkvx[: 2 * d, :].astype(BF16)

    gain1, bias1 = c_ln1g[:, :1], c_ln1b[:, :1]

    def weight_sums(first_pair, count):
        rows = slice(first_pair * d, (first_pair + count) * d)
        g = mm(n1[...], qkv[rows, :], NT)
        sums = g[d : d + 1]
        weight = wqkv[:, rows].astype(F32)
        a_g1[...] += fold(weight * (g[:d] - bias1 * sums))
        a_b1[...] += fold(weight * sums)
        for m in range(count):
            p = first_pair + m
            gvec[BQKV : BQKV + 1, 128 * p : 128 * (p + 1)] = sums[:, m * d : m * d + 128]
            gvec[BQKV : BQKV + 1, 2 * d + 128 * p : 2 * d + 128 * (p + 1)] = sums[:, m * d + 256 : (m + 1) * d]
        return g[:d]

    g = weight_sums(0, 2)
    for p in range(2):
        put(wf, p, [(g[:, p * d : (p + 1) * d], 0, n)], 16 * r2, r0)
    rc.go(0)

    def back_second(i, carry):
        attend_back([(UNITS2 * i + k, h) for k in range(UNITS2) for h in range(4, 6)])
        run_steps(i, (
            (0, [allowed(3), later(ra, 3)]),
            (1, [later(rb, 2), later(rc, 1)]),
        ))
        return carry

    lax.fori_loop(0, images // UNITS2, back_second, 0)
    qkv[2 * d :, extra_lanes] = dqkvx[2 * d :, :].astype(BF16)
    g = weight_sums(2, 1)
    put(tail_s, 0, [(g[:, :128], 0, n), (g[:, 128:256], 0, n)], step=r2, slot_at=lambda p, which: p)
    put(tail_s, 1, [(g[:, 256:], 0, n), (jnp.zeros((d, 128), F32), 0, n)], step=r2, slot_at=lambda p, which: p)
    scale1 = a_g1[...] * (1.0 / c_ln1g[...])
    for row, acc in ((LN1G, scale1), (LN1B, a_b1[...]), (LN2G, a_g2[...]), (LN2B, a_b2[...])):
        gvec[row : row + 1, :d] = jnp.sum(acc.T, 0, keepdims=True)
    tv[...] = jnp.zeros_like(tv)
    for p in every:
        s0 = 8 * p
        tv[0, s0 : s0 + 8, :n] = gvec[:, n * p : n * (p + 1)]
        s1 = 8 * p
        lo = 2 * n * p if p < 8 else 2 * d + 2 * n * (p - 8)
        parts = [gvec[BQKV : BQKV + 1, lo + n * k : lo + n * (k + 1)] for k in range(2)]
        lo = 4 * n * p
        parts += [gvec[BFC1 : BFC1 + 1, lo + n * k : lo + n * (k + 1)] for k in range(4)]
        tv[1, s1 : s1 + 6, :n] = jnp.concatenate(parts, 0)
    rd.go(0)
    rv.go(0)
    ra.go(4)
    rb.go(3)
    rc.go(2)

    def finals(lanes, count):
        return middle(lanes, count) + mm(w2_t[...], act[:ff, lanes]) + wide(c_b2[...], count)

    def final_images(k, carry):
        final = finals(lanes_of(CHUNK * k, CHUNK), CHUNK * t)
        for m in range(CHUNK):
            store_image(CHUNK * k + m, final[:, m * t : (m + 1) * t].T)
        run_steps(k * CHUNK, (
            (0, [later(rd, 1), later(rv, 1)]),
            (4, [later(rc, 3)]),
        ))
        return carry

    lax.fori_loop(0, images // CHUNK, final_images, 0)
    store_last(finals(extra_lanes, 128).T)
    for b in range(blocks):
        tokb[:, 128 * b : 128 * (b + 1)] = stage[b].astype(BF16)
    out_copy = pltpu.make_async_copy(tokb, out, loc_sem.at[0])
    out_copy.start()

    def finish(lanes, count, mu, r):
        u = (xs[:, lanes].astype(F32) - mu) * r
        dn = mm(wqkv[...], qkv[:, lanes])
        return dmid[:, lanes] + norm_back(dn, u, r, wide(c_ln1g[...], count))

    def finish_images(k, carry):
        mu, r = (
            jnp.concatenate([stat_s[CHUNK * k + m, row : row + 1, :] for m in range(CHUNK)], 1) for row in range(2)
        )
        grad = finish(lanes_of(CHUNK * k, CHUNK), CHUNK * t, mu, r)
        for m in range(CHUNK):
            store_image(CHUNK * k + m, grad[:, m * t : (m + 1) * t].T)
        run_steps(k * CHUNK, (
            (0, [later(rb, 4)]),

        ))
        return carry

    lax.fori_loop(0, images // CHUNK, finish_images, 0)
    store_last(finish(extra_lanes, 128, stat_s[images, 0:1, :128], stat_s[images, 1:2, :128]).T)
    copies = [
        pltpu.make_async_copy(stage.at[b], gin.at[:, pl.ds(128 * b, 128)], loc_sem.at[1 + b]) for b in range(blocks)
    ]
    for copy in copies:
        copy.start()
    rc.go(4)
    ra.go(5)
    rb.go(5)
    o1[...] = jnp.concatenate([f[0, n * k : n * (k + 1)] for f in (f_a, f_b) for k in range(2)], 1)
    o2[:r2] = f_a[1]
    o2[r2:] = f_b[1, :r2]
    oout[:16] = f_b[0, r2:]
    oout[16:] = f_b[1, r2 : r2 + 8]
    rd.go(2)
    rv.go(2)
    rc.go(5)
    for k in range(3):
        for p in range(2):
            oqkv[:, d * k + 128 * p : d * k + 128 * (p + 1)] = f_c[p, :n, 128 * k : 128 * (k + 1)]
    rd.go(3)
    rv.go(3)
    for k in range(3):
        oqkv[:, d * k + 256 : d * (k + 1)] = f_d[k // 2, (k % 2) * n : (k % 2 + 1) * n]
    ovec[...] = f_v[...]
    for copy in copies:
        copy.wait()
    out_copy.wait()


def block_call(tok, dup, tgt, weights):
    images, seq = dup.shape
    d = tok.shape[1]
    n = d // 16
    ff = 4 * d
    t = seq - 1
    w = images * t + 128
    vm = pltpu.VMEM
    dma = pltpu.SemaphoreType.DMA
    sd = jax.ShapeDtypeStruct
    column = vm((d, 128), F32)
    scratch = [
        vm((seq * images, d), BF16),
        vm((d // 128, seq * images, 128), F32),
        vm((d, w), BF16),
        vm((d + 16, w), BF16),
        vm((3 * d, w), BF16),
        vm((d + 16, w), BF16),
        vm((d + 16, w), BF16),
        vm((ff + 16, w), BF16),
        vm((ff, w), BF16),
        vm((d, w), BF16),
        vm((d, w), BF16),
        vm((d, w), BF16),
        vm((d, w), F32),
        vm((images * HEADS, t, t), BF16),
        vm((d, 3 * d), BF16),
        vm((d, d), BF16), vm((d, d), BF16),
        vm((d, ff), BF16),
        vm((d, ff), BF16),
        vm((2, 32 * n + 256, d), BF16),
        vm((2, ff, d), BF16),
        column, column, column, column, column, column, column, vm((ff, 128), F32), column,
        vm((images + 1, 8, t), F32),
        vm((images, 8, t), F32),
        vm((images, 8, t), F32),
        vm((images, 8, t), F32),
        vm((images, 8, 128), F32),
        column,
        vm((3 * d, 128), F32),
        column, column, column, column,
        column,
        vm((8, ff), F32),
        vm((2, 128, 128), F32),
        vm((8, d), F32),
        vm((2, 32 * n, 128), BF16), vm((32 * n, 128), BF16), vm((30 * n, 128), BF16),
        vm((2, 128, 128), F32),
    ]
    scratch += [vm((128, 128), F32), vm((120, 128), F32)]
    scratch += [vm((2, r, d), F32) for r in (2 * n, 2 * n + 16, n + 8)] + [vm((2, 2 * n, 128), F32), vm((2, 8, 128), F32)]
    scratch += [dma((4,)), dma((2, 16))] + [dma((2, 7))] * 6 + [dma((2, 17))] * 2 + [pltpu.SemaphoreType.REGULAR((4,))]
    spec = pl.BlockSpec(memory_space=pltpu.VMEM)
    any_spec = pl.BlockSpec(memory_space=pl.ANY)
    return pl.pallas_call(
        block_body,
        out_shape=(
            sd(tok.shape, BF16), sd(tok.shape, F32),
            sd((n, 3 * d), F32), sd((n, d), F32), sd((n, ff), F32), sd((4 * n, d), F32), sd((2, 8, 128), F32),
        ),
        in_specs=[any_spec] + [spec] * 14,
        out_specs=(any_spec, any_spec) + (spec,) * 5,
        scratch_shapes=scratch,
        compiler_params=pltpu.CompilerParams(
            collective_id=0, has_side_effects=True, vmem_limit_bytes=64 * 1024 * 1024
        ),
        name="block16",
    )(tok, dup, tgt, *weights)


def deliver_body(out, gin, gqkv, gout, g1, g2, gv, *refs):
    o_out, o_gin, o_ln1g, o_ln1b, o_qkv, o_qvb, o_w, o_bout, o_ln2g, o_ln2b, o_fc1, o_b1, o_fc2, o_b2 = refs[:14]
    buf_out, buf_gin, sems = refs[14:]
    n = gqkv.shape[0]
    pieces = []
    for k, (src, buf, dst) in enumerate(((out, buf_out, o_out), (gin, buf_gin, o_gin))):
        count = 1 + 3 * k
        size = (src.shape[0] // count) // 16 * 16
        for m in range(count):
            rows = pl.ds(m * size, size if m < count - 1 else src.shape[0] - m * size)
            s = k + m
            pieces.append((
                pltpu.make_async_copy(src.at[rows], buf.at[rows], sems.at[0, s]),
                pltpu.make_async_copy(buf.at[rows], dst.at[rows], sems.at[1, s]),
            ))
    for load, store in pieces:
        load.start()
    o_qkv[...] = gqkv[...]
    o_w[...] = gout[...]
    o_fc1[...] = g1[...]
    o_fc2[...] = g2[...]
    for ref, row in ((o_ln1g, LN1G), (o_ln1b, LN1B), (o_bout, BOUT), (o_ln2g, LN2G), (o_ln2b, LN2B), (o_b2, BFC2)):
        ref[...] = gv[0, row, :n]
    o_qvb[...] = jnp.concatenate([gv[1, k, :n] for k in range(2)], 0)
    o_b1[...] = jnp.concatenate([gv[1, 2 + k, :n] for k in range(4)], 0)
    for load, store in pieces:
        load.wait()
        store.start()
    for load, store in pieces:
        store.wait()


def deliver_call(out, gin, gqkv, gout, g1, g2, gv):
    n, d = gout.shape
    sd = jax.ShapeDtypeStruct
    spec = pl.BlockSpec(memory_space=pltpu.VMEM)
    any_spec = pl.BlockSpec(memory_space=pl.ANY)
    vec = sd((n,), F32)
    return pl.pallas_call(
        deliver_body,
        out_shape=(
            sd(out.shape, BF16), sd(gin.shape, F32), vec, vec, sd((n, 3 * d), F32), sd((2 * n,), F32),
            sd((n, d), F32), vec, vec, vec, sd((n, 4 * d), F32), sd((4 * n,), F32), sd((4 * n, d), F32), vec,
        ),
        in_specs=[any_spec, any_spec] + [spec] * 5,
        out_specs=(any_spec, any_spec) + (spec,) * 12,
        scratch_shapes=[
            pltpu.VMEM(out.shape, BF16), pltpu.VMEM(gin.shape, F32), pltpu.SemaphoreType.DMA((2, 6)),
        ],
        compiler_params=pltpu.CompilerParams(vmem_limit_bytes=64 * 1024 * 1024),
        name="deliver",
    )(out, gin, gqkv, gout, g1, g2, gv)


def gather_all(value):
    return lax.all_gather(value, "fsdp", axis=0, tiled=True)


def vectors(full):
    ln1_gain, ln1_bias, qv_bias, out_bias, ln2_gain, ln2_bias, fc1_bias, fc2_bias = full
    d = ln1_gain.shape[0]
    bias = jnp.concatenate([qv_bias[:d], jnp.zeros((d,), qv_bias.dtype), qv_bias[d:]])
    rows = (ln1_gain, ln1_bias, bias, out_bias, ln2_gain, ln2_bias, fc1_bias, fc2_bias)
    width = fc1_bias.shape[0]
    return jnp.stack([jnp.pad(row.astype(F32), (0, width - row.shape[0])) for row in rows], 0)


def per_device(tokens, duplicate, targets, *weights, block16):
    images, seq, d = tokens.shape
    rows = tokens.transpose(1, 0, 2).reshape(seq * images, d)
    back = lambda v: v.reshape(seq, images, d).transpose(1, 0, 2)
    if block16:
        results = deliver_call(*block_call(rows, duplicate, targets, weights))
        return (back(results[0]), back(results[1])) + tuple(results[2:])

    (
        ln1_gain, ln1_bias, qkv_weight, qv_bias, out_weight, out_bias,
        ln2_gain, ln2_bias, fc1_weight, fc1_bias, fc2_weight, fc2_bias,
    ) = weights
    small = (ln1_gain, ln1_bias, qv_bias, out_bias, ln2_gain, ln2_bias, fc1_bias, fc2_bias)
    wqkv, wout, w1, w2 = map(gather_all, (qkv_weight, out_weight, fc1_weight, fc2_weight))
    vec = vectors(tuple(map(gather_all, small)))
    out, gin, gqkv, gout, g1, g2, gvec = compute(rows, duplicate, targets, vec, wqkv, wout, w1, w2)

    def scatter(value):
        value = lax.psum_scatter(value.astype(F32), "fsdp", scatter_dimension=0, tiled=True)
        return lax.psum(value, "dp")

    gqkv, gout, g1, g2 = map(scatter, (gqkv, gout, g1, g2))
    gvec = lax.psum(gvec, ("fsdp", "dp"))
    p = lax.axis_index("fsdp")

    def shard(value, whole_size):
        count = whole_size // lax.axis_size("fsdp")
        return lax.dynamic_slice(value, (p * count,), (count,))

    qv_grad = jnp.concatenate([gvec[2, :d], gvec[2, 2 * d : 3 * d]])
    return (
        back(out), back(gin),
        shard(gvec[0], d), shard(gvec[1], d), gqkv, shard(qv_grad, 2 * d), gout, shard(gvec[3], d),
        shard(gvec[4], d), shard(gvec[5], d), g1, shard(gvec[6], 4 * d), g2, shard(gvec[7], d),
    )


def solution(mesh):
    block16 = mesh.shape["fsdp"] == 16 and mesh.shape["dp"] == 2
    both = ("fsdp", "dp")
    vector, matrix = P("fsdp"), P("fsdp", None)
    weights = (vector, vector, matrix, vector, matrix, vector, vector, vector, matrix, vector, matrix, vector)
    return jax.shard_map(
        functools.partial(per_device, block16=block16),
        mesh=mesh,
        in_specs=(P(both, None, None), P(both, None), P(both, None)) + weights,
        out_specs=(P(both, None, None), P(both, None, None)) + weights,
        check_vma=False,
    )
```
